32 devices in a mesh: fsdp: 4 (over y, x), ctx: 4 (over z), tp: 2 (over core).
Axes of the slice: x: 2, y: 2, z: 4, core: 2. Of those that a mesh axis runs over, the one named last changes fastest.
Arguments:
- tokens: bfloat16 [4096, 2048], P(('fsdp', 'ctx')), may hold values from -6 to 6
- cotangent: bfloat16 [4096, 2048], P(('fsdp', 'ctx')), may hold values from -6 to 6
- segments: int32 [4096], P(('fsdp', 'ctx')), may hold values from 0 to 12, as said below
- depths: int32 [4096], P(('fsdp', 'ctx')), may hold values from 0 to 542, as said below
- parents: int32 [4, 13], P('fsdp'), may hold values from 0 to 4, as said below
- tree_adapter_index: int32 [4], P('fsdp'), may hold values from 0 to 7
- layer_norm_gains: float32 [2, 2, 2048], replicated, may hold values from 0.5 to 1.5
- difference_lambda: float32 [2, 8], P(None, 'tp'), may hold values from 0.2 to 0.8
- query_key_value_weight: bfloat16 [2, 2048, 3, 2048], P(None, ('fsdp', 'ctx'), None, 'tp'), may hold values from -0.125 to 0.125
- output_weight: bfloat16 [2, 2048, 2048], P(None, ('fsdp', 'ctx'), 'tp'), may hold values from -0.125 to 0.125
- gate_up_weight: bfloat16 [2, 2048, 2, 5632], P(None, ('fsdp', 'ctx'), None, 'tp'), may hold values from -0.125 to 0.125
- down_weight: bfloat16 [2, 2048, 5632], P(None, ('fsdp', 'ctx'), 'tp'), may hold values from -0.078125 to 0.078125
- adapter_model_factors: bfloat16 [2, 11, 8, 16, 2048], replicated, may hold values from -0.29882812 to 0.29882812
- adapter_hidden_factors: bfloat16 [2, 3, 8, 16, 5632], replicated, may hold values from -0.29882812 to 0.29882812
Outputs:
- outputs: bfloat16 [4096, 2048], P(('fsdp', 'ctx'))
- tokens_grad: float32 [4096, 2048], P(('fsdp', 'ctx'))
- grad_lora_model: float32 [2, 11, 8, 16, 2048], P(None, None, 'fsdp', None, ('ctx', 'tp'))
- grad_lora_hidden: float32 [2, 3, 8, 16, 5632], P(None, None, 'fsdp', None, ('ctx', 'tp'))
The draws below stay inside these ranges and needn't reach their ends.
Inputs may be any that keep to these rules, and one draw needn't show every extreme that they name: `parents`: segment 0 is a tree's trunk and its own parent; segments 1 to 4 are branches with parent 0; segments 5 to 12 are leaves, two on each branch. `segments`: within each tree of 1024 tokens the segment numbers never fall, every segment is nonempty and the trunk fills the first 384 tokens; each branch with its two leaves holds (640) / 4 tokens. `depths`: A token's depth is the total length of its proper ancestor segments plus its offset within its own segment; the largest is reached in every tree.
All inputs are finite; a program needn't handle non-finite values.
Results may differ from the reference program's by a relative error of at most 0.028.
Values may be sent and summed in bfloat16 or wider, within the bound.
A program may use at most 320 MiB of HBM per device.

```python
import math
import jax
import jax.numpy as jnp
from jax import lax

MODEL_WIDTH = 2048
H = 8
HD = 128
VD = 256
HIDDEN_UNITS = 5632
ADAPTER_RANK = 16
ADAPTER_COUNT = 8
NSEG = 13
LAYER_COUNT = 2
TOK_DEV = 256
TREE = 1024
TRUNK = 384
TREES = 4
TOKENS = 4096


def tree_layout(key):
    group_size = (TREE - TRUNK) // 4

    def one_group(group_key):
        cuts = jnp.sort(jax.random.permutation(group_key, group_size - 1)[:2] + 1).astype(jnp.int32)
        return (cuts[0], cuts[1] - cuts[0], group_size - cuts[1])

    def one_tree(tree_key):
        group_key, leaf_key, force_key, branch_key = jax.random.split(tree_key, 4)
        branch_len, first_leaf, second_leaf = jax.vmap(one_group)(jax.random.split(group_key, 4))
        forced = jax.random.randint(force_key, (), 0, 4)
        forced_branch = jax.random.randint(branch_key, (), 1, group_size - 1).astype(jnp.int32)
        is_forced = jnp.arange(4) == forced
        branch_len = jnp.where(is_forced, forced_branch, branch_len).astype(jnp.int32)
        first_leaf = jnp.where(is_forced, 1, first_leaf).astype(jnp.int32)
        second_leaf = jnp.where(is_forced, group_size - 1 - forced_branch, second_leaf).astype(jnp.int32)
        pairing = jax.random.permutation(leaf_key, NSEG - 5).astype(jnp.int32)
        leaf_branch = pairing // 2
        leaf_lengths = jnp.where(pairing % 2 == 0, first_leaf[leaf_branch], second_leaf[leaf_branch])
        lengths = jnp.concatenate([jnp.full((1,), TRUNK, jnp.int32), branch_len, leaf_lengths.astype(jnp.int32)])
        tree_parents = jnp.concatenate([jnp.zeros((5,), jnp.int32), 1 + leaf_branch])
        starts = jnp.cumsum(lengths) - lengths
        places = jnp.arange(TREE, dtype=jnp.int32)
        tree_segments = jnp.sum((places[:, None] >= starts[None, 1:]).astype(jnp.int32), axis=1)
        numbers = jnp.arange(NSEG, dtype=jnp.int32)
        above = jnp.where(numbers == 0, 0, TRUNK) + jnp.where(numbers >= 5, lengths[tree_parents], 0)
        tree_depths = above[tree_segments] + places - starts[tree_segments]
        return (tree_parents, tree_segments, tree_depths)
    tree_keys = jax.random.split(key, TREES)
    all_parents, all_segments, all_depths = jax.vmap(one_tree)(tree_keys)
    return (all_parents, all_segments.reshape(TOKENS), all_depths.reshape(TOKENS))


def draw_parents(key, part):
    layout = tree_layout(key)
    return layout[0]


def draw_segments(key, part):
    layout = tree_layout(key)
    return layout[1]


def draw_depths(key, part):
    layout = tree_layout(key)
    return layout[2]


def set_ends(values, stream_key, least, top_value):
    dims = values.shape
    spot = [jax.random.randint(jax.random.fold_in(stream_key, axis), (), 0, dims[axis]) for axis in range(len(dims))]
    values = values.at[tuple(spot)].set(least)
    longest = dims.index(max(dims))
    spot[longest] = (spot[longest] + 1) % dims[longest]
    return values.at[tuple(spot)].set(top_value)


def level_of(rng, extent, pieces, smallest, high):
    def one(position, shards_of):
        heights = jax.random.uniform(jax.random.fold_in(jax.random.fold_in(rng, 6), position), (shards_of,), jnp.float32, smallest / len(pieces), high / len(pieces))
        return jnp.repeat(jnp.exp(heights), extent[position] // shards_of).reshape((-1,) + (1,) * (len(extent) - position - 1))

    gain = one(*pieces[0])
    for cut in pieces[1:]:
        gain = gain * one(*cut)
    return gain


def bell_draw(own_key, extent, deviation, limit, cuts=(), kind=jnp.bfloat16):
    drawn = deviation * jax.random.normal(own_key, extent, jnp.float32)
    if cuts:
        drawn = drawn * level_of(own_key, extent, cuts, -0.22, 0.18)
    return jnp.clip(drawn, -limit, limit).astype(kind)


def setup_inputs(seed: int = 0) -> dict:
    arg_keys = jax.random.split(jax.random.key(seed), 15)
    return {
        "tokens": bell_draw(arg_keys[0], (TOKENS, MODEL_WIDTH), 1.0, 6.0, ((0, 16),)),
        "cotangent": bell_draw(arg_keys[1], (TOKENS, MODEL_WIDTH), 1.0, 6.0, ((0, 16),)),
        "segments": draw_segments(jax.random.fold_in(arg_keys[14], 71), 0),
        "depths": draw_depths(jax.random.fold_in(arg_keys[14], 71), 0),
        "parents": draw_parents(jax.random.fold_in(arg_keys[14], 71), 0),
        "tree_adapter_index": set_ends(jax.random.randint(arg_keys[5], (TREES,), 0, ADAPTER_COUNT), jax.random.fold_in(arg_keys[5], 1), 0, ADAPTER_COUNT - 1).astype(jnp.int32),
        "layer_norm_gains": jnp.clip(1.0 + 0.1 * jax.random.normal(arg_keys[6], (LAYER_COUNT, 2, MODEL_WIDTH), jnp.float32), 0.5, 1.5),
        "difference_lambda": jnp.clip(0.2 + 0.6 * jax.random.uniform(arg_keys[7], (LAYER_COUNT, H), jnp.float32) ** level_of(arg_keys[7], (LAYER_COUNT, H), ((1, 2),), -0.2, 0.2), 0.2, 0.8),
        "query_key_value_weight": bell_draw(arg_keys[8], (LAYER_COUNT, MODEL_WIDTH, 3, MODEL_WIDTH), MODEL_WIDTH ** -0.5, 0.125, ((1, 16), (3, 2))),
        "output_weight": bell_draw(arg_keys[9], (LAYER_COUNT, MODEL_WIDTH, MODEL_WIDTH), MODEL_WIDTH ** -0.5, 0.125, ((1, 16), (2, 2))),
        "gate_up_weight": bell_draw(arg_keys[10], (LAYER_COUNT, MODEL_WIDTH, 2, HIDDEN_UNITS), MODEL_WIDTH ** -0.5, 0.125, ((1, 16), (3, 2))),
        "down_weight": bell_draw(arg_keys[11], (LAYER_COUNT, MODEL_WIDTH, HIDDEN_UNITS), HIDDEN_UNITS ** -0.5, 0.078125, ((1, 16), (2, 2))),
        "adapter_model_factors": bell_draw(arg_keys[12], (LAYER_COUNT, 11, ADAPTER_COUNT, ADAPTER_RANK, MODEL_WIDTH), 0.05, 0.29882812),
        "adapter_hidden_factors": bell_draw(arg_keys[13], (LAYER_COUNT, 3, ADAPTER_COUNT, ADAPTER_RANK, HIDDEN_UNITS), 0.05, 0.29882812),
    }


@jax.custom_vjp
def low(v):
    return lax.optimization_barrier(v.astype(jnp.bfloat16)).astype(jnp.float32)

@jax.custom_vjp
def low_back(v):
    return v

def low_keep(v):
    return (low(v), None)

def low_pass(kept, grad):
    return (grad,)

def back_keep(v):
    return (v, None)

def back_low(kept, grad):
    return (low(grad),)
low.defvjp(low_keep, low_pass)
low_back.defvjp(back_keep, back_low)
EPSILON = 1e-05
ADAPTER_SCALE = 0.5
NEGATIVE_BIG = -1e+30
PRECISION_HIGH = lax.Precision.HIGHEST

def matrix_product(left_side, right_side):
    return jnp.dot(left_side, right_side, precision=PRECISION_HIGH)

def einsum_precise(formula, left_side, right_side):
    return jnp.einsum(formula, left_side, right_side, precision=PRECISION_HIGH)

def rms_scale(values):
    return lax.rsqrt(lax.optimization_barrier(jnp.mean(values * values, axis=-1, keepdims=True)) + EPSILON)

def angles_of(depths):
    half_width = HD // 2
    frequency = 10000.0 ** (-jnp.arange(half_width).astype(jnp.float32) / half_width)
    return depths.astype(jnp.float32)[:, None] * frequency[None, :]

def rotate(vectors, angles, direction):
    half_width = vectors.shape[-1] // 2
    cosine = jnp.cos(angles)[:, None, None, :]
    sine_part = direction * jnp.sin(angles)[:, None, None, :]
    first_half = vectors[..., :half_width]
    second_half = vectors[..., half_width:]
    return jnp.concatenate([first_half * cosine - second_half * sine_part, first_half * sine_part + second_half * cosine], axis=-1)

def ancestors(parents):
    parent_table = (parents[:, None] == jnp.arange(NSEG)[None, :]).astype(jnp.float32)
    identity = jnp.eye(NSEG, dtype=jnp.float32)
    return jnp.minimum(identity + parent_table + jnp.dot(parent_table, parent_table), 1.0)

def keep_factor(current_layer_index):
    return 0.2 + 0.6 * math.exp(-0.3 * current_layer_index)

def attend(queries, key_vectors, values, tree_segments, reach_table, lambdas):
    onehot = (tree_segments[:, None] == jnp.arange(NSEG)[None, :]).astype(jnp.float32)
    reach_rows = jnp.dot(onehot, reach_table, precision=PRECISION_HIGH)
    key_index = jnp.arange(TREE)

    def score_block(block_item):
        query_block, segment_block, reach_block, index_block = block_item
        scores = low_back(einsum_precise('qhcd,khcd->hcqk', query_block, key_vectors) * HD ** (-0.5))
        allowed = jnp.dot(reach_block, onehot.T, precision=PRECISION_HIGH) > 0.5
        same_segment = segment_block[:, None] == tree_segments[None, :]
        causal = index_block[:, None] >= key_index[None, :]
        visible = allowed & (causal | jnp.logical_not(same_segment))
        scores = jnp.where(visible, scores, NEGATIVE_BIG)
        row_max = lax.optimization_barrier(jnp.max(scores, axis=-1, keepdims=True))
        weights_raw = jnp.exp(scores - row_max)
        probability = low(weights_raw / lax.optimization_barrier(jnp.sum(weights_raw, axis=-1, keepdims=True)))
        mixed_block = einsum_precise('hcqk,khv->hcqv', probability, values)
        return mixed_block[:, 0] - lambdas[:, None, None] * mixed_block[:, 1]
    blocks = TREE // TOK_DEV
    block_items = (queries.reshape(blocks, TOK_DEV, H, 2, HD), tree_segments.reshape(blocks, TOK_DEV), reach_rows.reshape(blocks, TOK_DEV, NSEG), key_index.reshape(blocks, TOK_DEV))
    gathered_blocks = lax.map(jax.checkpoint(score_block), block_items)
    return gathered_blocks.transpose(0, 2, 1, 3).reshape(TREE, H, VD)

def reference(tokens, cotangent, segments, depths, parents, tree_adapter_index, layer_norm_gains, difference_lambda, query_key_value_weight, output_weight, gate_up_weight, down_weight, adapter_model_factors, adapter_hidden_factors):
    query_key_value_matrices = query_key_value_weight.astype(jnp.float32)
    output_matrix = output_weight.astype(jnp.float32)
    gate_up_matrix = gate_up_weight.astype(jnp.float32)
    down_matrix = down_weight.astype(jnp.float32)
    model_adapter_factors = adapter_model_factors.astype(jnp.float32)
    hidden_adapter_factors = adapter_hidden_factors.astype(jnp.float32)

    def tree_forward(tree_tokens, model_all, hidden_all, tree_segments, tree_depths, reach_table, adapter_slot):
        residual_stream = tree_tokens
        angles = angles_of(tree_depths)
        for current_layer_index in range(LAYER_COUNT):
            model_portion = model_all[current_layer_index, :, adapter_slot]
            hidden_portion = hidden_all[current_layer_index, :, adapter_slot]
            normed_attention_input = low(residual_stream * rms_scale(residual_stream) * layer_norm_gains[current_layer_index, 0])
            reduced_query_key_value = low_back(low(matrix_product(normed_attention_input, model_portion[0:3].reshape(3 * ADAPTER_RANK, MODEL_WIDTH).T))).reshape(TREE, 3, ADAPTER_RANK)
            projected_rows = einsum_precise('zs,sxw->zxw', normed_attention_input, query_key_value_matrices[current_layer_index]) + ADAPTER_SCALE * einsum_precise('gwy,wyk->gwk', reduced_query_key_value, model_portion[6:9])
            projected_rows = low_back(projected_rows)
            queries = low(rotate(projected_rows[:, 0].reshape(TREE, H, 2, HD), angles, 1.0))
            key_vectors = low(rotate(projected_rows[:, 1].reshape(TREE, H, 2, HD), angles, 1.0))
            values = low(projected_rows[:, 2].reshape(TREE, H, VD))
            mixed_heads = low_back(attend(queries, key_vectors, values, tree_segments, reach_table, difference_lambda[current_layer_index]))
            per_head_rows = low((mixed_heads * rms_scale(mixed_heads) * keep_factor(current_layer_index)).reshape(TREE, MODEL_WIDTH))
            adapter_attention = low_back(low(matrix_product(per_head_rows, model_portion[3].T)))
            branch_output = low_back(matrix_product(per_head_rows, output_matrix[current_layer_index].T) + ADAPTER_SCALE * matrix_product(adapter_attention, model_portion[9]))
            residual_stream = residual_stream + branch_output
            normed_feedforward_input = low(residual_stream * rms_scale(residual_stream) * layer_norm_gains[current_layer_index, 1])
            reduced_feedforward = low_back(low(matrix_product(normed_feedforward_input, model_portion[4:6].reshape(2 * ADAPTER_RANK, MODEL_WIDTH).T))).reshape(TREE, 2, ADAPTER_RANK)
            gate_up_values = einsum_precise('im,mqg->iqg', normed_feedforward_input, gate_up_matrix[current_layer_index]) + ADAPTER_SCALE * einsum_precise('jvi,vin->jvn', reduced_feedforward, hidden_portion[0:2])
            gate_up_values = low_back(gate_up_values)
            hidden_activation = low(jax.nn.silu(gate_up_values[:, 0]) * gate_up_values[:, 1])
            adapter_feedforward = low_back(low(matrix_product(hidden_activation, hidden_portion[2].T)))
            branch_feedforward = low_back(matrix_product(hidden_activation, down_matrix[current_layer_index].T) + ADAPTER_SCALE * matrix_product(adapter_feedforward, model_portion[10]))
            residual_stream = residual_stream + branch_feedforward
        return residual_stream

    def per_tree(totals, tree_item):
        tree_tokens, tree_cot, tree_segments, tree_depths, tree_parents, adapter_slot = tree_item
        reach_table = ancestors(tree_parents)

        def forward(tokens_value, model_value, hidden_value):
            return tree_forward(tokens_value, model_value, hidden_value, tree_segments, tree_depths, reach_table, adapter_slot)
        tree_out, pullback = jax.vjp(forward, tree_tokens, model_adapter_factors, hidden_adapter_factors)
        grad_tokens, grad_model, grad_hidden = pullback(tree_cot)
        return ((totals[0] + grad_model, totals[1] + grad_hidden), (tree_out, grad_tokens))
    tree_items = (tokens.astype(jnp.float32).reshape(TREES, TREE, MODEL_WIDTH), cotangent.astype(jnp.float32).reshape(TREES, TREE, MODEL_WIDTH), segments.reshape(TREES, TREE), depths.reshape(TREES, TREE), parents, tree_adapter_index)
    empty_totals = (jnp.zeros(adapter_model_factors.shape, jnp.float32), jnp.zeros(adapter_hidden_factors.shape, jnp.float32))
    (grad_model, grad_hidden), (tree_outs, grad_tokens) = lax.scan(per_tree, empty_totals, tree_items)
    return (tree_outs.reshape(TOKENS, MODEL_WIDTH).astype(jnp.bfloat16), grad_tokens.reshape(TOKENS, MODEL_WIDTH), grad_model, grad_hidden)
```

```python
import functools
import math

import jax
import jax.numpy as jnp
from jax import lax
from jax.experimental import pallas as pl
from jax.experimental.pallas import tpu as pltpu
from jax.sharding import PartitionSpec as P

HD = 128
VD = 256
NSEG = 13
EPSILON = 1e-05
ADAPTER_SCALE = 0.5
NEGATIVE_BIG = -1e30
MESH = pl.DeviceIdType.MESH
BF = jnp.bfloat16
F32 = jnp.float32


class Place:
    def __init__(self, n):
        self.n, self.h = n, n // 2
        self.f, self.c, self.t = lax.axis_index("fsdp"), lax.axis_index("ctx"), lax.axis_index("tp")
        self.f_hi, self.f_lo = self.f // 2, self.f % 2
        self.c_hi, self.c_lo = self.c // self.h, self.c % self.h
        self.q = self.f_lo * self.h + self.c_lo
        self.pos = self.f_lo * (n - 1) + (1 - 2 * self.f_lo) * self.c_lo

    def ring(self, k):
        n, h = self.n, self.h
        p = lax.rem(self.pos + k + 2 * n, n)
        low = p // h
        column = (1 - low) * p + low * (n - 1 - p)
        device = {"fsdp": self.f_hi * 2 + low, "ctx": self.c_hi * h + column}
        return low * h + column, device


def enter(place):
    bar = pltpu.get_barrier_semaphore()
    for device in (place.ring(1)[1], place.ring(-1)[1], {"tp": 1 - place.t}):
        pl.semaphore_signal(bar, inc=1, device_id=device, device_id_type=MESH)
    pl.semaphore_wait(bar, 3)


def remote(src, dst, send, recv, device):
    copy = pltpu.make_async_remote_copy(
        src_ref=src, dst_ref=dst, send_sem=send, recv_sem=recv, device_id=device, device_id_type=MESH
    )
    copy.start()
    return copy


class Gather:
    def __init__(self, place, x, send_r, recv_r, send_l, recv_l, core_send, core_recv):
        self.place, self.x = place, x
        self.sems = (send_r, recv_r, send_l, recv_l, core_send, core_recv)
        self.to_right, self.to_left, self.across = [], [], []

    @staticmethod
    def semaphores(n):
        dma = pltpu.SemaphoreType.DMA
        return [dma((n // 2,))] * 4 + [dma((n,))] * 2

    def _pass_on(self, s):
        place, x = self.place, self.x
        send_r, recv_r, send_l, recv_l = self.sems[:4]
        rows, half, t = x.shape[2], place.n // 2, place.t
        top = rows // 2
        part_r = pl.ds(0, top) if s == half - 1 else pl.ds(0, rows)
        part_l = pl.ds(top, top) if s == half - 1 else pl.ds(0, rows)
        right_at = x.at[place.ring(-s)[0], t, part_r]
        left_at = x.at[place.ring(s)[0], t, part_l]
        self.to_right.append(remote(right_at, right_at, send_r.at[s], recv_r.at[s], place.ring(1)[1]))
        self.to_left.append(remote(left_at, left_at, send_l.at[s], recv_l.at[s], place.ring(-1)[1]))

    def _cross(self, q):
        core_send, core_recv = self.sems[4:]
        slot, at = len(self.across), self.x.at[q, self.place.t]
        other = {"tp": 1 - self.place.t}
        self.across.append(remote(at, at, core_send.at[slot], core_recv.at[slot], other))

    def begin(self):
        self._pass_on(0)
        self._cross(self.place.q)

    def chunks(self):
        place, half = self.place, self.place.n // 2
        self.across[0].wait_recv()
        yield place.q
        for s in range(half):
            self.to_right[s].wait_recv()
            self.to_left[s].wait_recv()
            arrived = [place.ring(half)[0]] if s == half - 1 else [place.ring(-s - 1)[0], place.ring(s + 1)[0]]
            if s < half - 1:
                self._pass_on(s + 1)
            first = len(self.across)
            for q in arrived:
                self._cross(q)
            for i, q in enumerate(arrived):
                self.across[first + i].wait_recv()
                yield q

    def finish(self):
        for copy in self.to_right + self.to_left + self.across:
            copy.wait_send()


def by_rows(count, body, step=16):
    def one(i, carry):
        body(pl.ds(pl.multiple_of(i * step, step), step))
        return carry

    lax.fori_loop(0, count // step, one, 0)


class Reduce:
    def __init__(self, place, p, from_core, in_r, in_l, send_r, recv_r, send_l, recv_l, core_send, core_recv):
        self.place, self.p, self.from_core, self.in_r, self.in_l = place, p, from_core, in_r, in_l
        self.sems = (send_r, recv_r, send_l, recv_l, core_send, core_recv)
        half = place.n // 2
        self.order = [half] + [k for j in range(half - 1, 0, -1) for k in (j, -j)] + [0]
        self.chips = {k: place.ring(k)[0] for k in self.order}
        self.across, self.to_right, self.to_left = {}, [], []

    @staticmethod
    def scratch(n, rows, width):
        dma = pltpu.SemaphoreType.DMA
        wide = [pltpu.VMEM((n, rows, width), BF)] + [pltpu.VMEM((n // 2, rows, width), BF)] * 2
        return wide + [dma((n // 2,))] * 4 + [dma((n,))] * 2

    def offer(self, k):
        core_send, core_recv = self.sems[4:]
        slot, q, t = len(self.across), self.chips[k], self.place.t
        self.across[k] = remote(
            self.p.at[q, 1 - t], self.from_core.at[q], core_send.at[slot], core_recv.at[slot], {"tp": 1 - t}
        )

    def _local(self, k, at):
        q = self.chips[k]
        return self.p[q, self.place.t, at].astype(F32) + self.from_core[q, at].astype(F32)

    def _add(self, k, start, count, extra=None):
        def body(at):
            whole = pl.ds(pl.multiple_of(start + at.start, 16), at.size)
            total = self._local(k, whole)
            if extra is not None:
                total = total + extra[whole].astype(F32)
            self.from_core[self.chips[k], whole] = total.astype(BF)

        by_rows(count, body)

    def far(self):
        send_r, recv_r, send_l, recv_l = self.sems[:4]
        place, half = self.place, self.place.n // 2
        rows = self.p.shape[2]
        top = rows // 2
        self.across[half].wait_recv()
        self._add(half, 0, rows)
        low, high = pl.ds(0, top), pl.ds(top, top)
        sums = self.from_core.at[self.chips[half]]
        right, left = place.ring(1)[1], place.ring(-1)[1]
        self.to_right.append(remote(sums.at[low], self.in_r.at[0, low], send_r.at[0], recv_r.at[0], right))
        self.to_left.append(remote(sums.at[high], self.in_l.at[0, high], send_l.at[0], recv_l.at[0], left))

    def near(self, s):
        send_r, recv_r, send_l, recv_l = self.sems[:4]
        place, k = self.place, self.place.n // 2 - s
        rows = self.p.shape[2]
        top = rows // 2
        self.across[k].wait_recv()
        self.across[-k].wait_recv()
        if s == 1:
            self._add(k, top, top)
            self._add(-k, 0, top)
        start = 0 if s == 1 else None
        self.to_right[-1].wait_recv()
        self._add(k, 0, top if s == 1 else rows, self.in_r.at[s - 1])
        self.to_right.append(
            remote(self.from_core.at[self.chips[k]], self.in_r.at[s], send_r.at[s], recv_r.at[s], place.ring(1)[1])
        )
        self.to_left[-1].wait_recv()
        self._add(-k, top if s == 1 else 0, top if s == 1 else rows, self.in_l.at[s - 1])
        self.to_left.append(
            remote(self.from_core.at[self.chips[-k]], self.in_l.at[s], send_l.at[s], recv_l.at[s], place.ring(-1)[1])
        )

    def end(self, use):
        half = self.place.n // 2
        self.across[0].wait_recv()
        self.to_right[-1].wait_recv()
        self.to_left[-1].wait_recv()

        def body(at):
            use(at, self._local(0, at) + self.in_r[half - 1, at].astype(F32) + self.in_l[half - 1, at].astype(F32))

        by_rows(self.p.shape[2], body)

    def finish(self):
        for copy in self.to_right + self.to_left + list(self.across.values()):
            copy.wait_send()

    def run(self, use, before=None):
        for k in self.order:
            self.offer(k)
        self.far()
        for s in range(1, self.place.n // 2):
            self.near(s)
        if before is not None:
            before()
        self.end(use)


def rs_kernel(n, p_ref, out_ref, *scratch):
    place = Place(n)
    reduce = Reduce(place, p_ref, *scratch)
    enter(place)

    def use(at, total):
        out_ref[at] = total

    reduce.run(use)
    reduce.finish()


def group_reduce(p, n, collective):
    vmem = pl.BlockSpec(memory_space=pltpu.VMEM)
    rows, width = p.shape[2:]
    return pl.pallas_call(
        functools.partial(rs_kernel, n),
        out_shape=jax.ShapeDtypeStruct((rows, width), F32),
        in_specs=[vmem],
        out_specs=vmem,
        scratch_shapes=Reduce.scratch(n, rows, width),
        compiler_params=pltpu.CompilerParams(
            collective_id=collective, has_side_effects=True, vmem_limit_bytes=60 << 20
        ),
    )(p)


def mm(a, b):
    return jnp.dot(a, b, preferred_element_type=F32)


def mm_t(a, b):
    return lax.dot_general(a, b, (((1,), (1,)), ((), ())), preferred_element_type=F32)


def t_mm(a, b):
    return lax.dot_general(a, b, (((0,), (0,)), ((), ())), preferred_element_type=F32)


def rms_scale(values):
    return lax.rsqrt(jnp.mean(values * values, axis=-1, keepdims=True) + EPSILON)


def norm_back(grad_normed, inputs, scale_rows, gain):
    unit = inputs * scale_rows
    scaled = grad_normed * gain
    return scale_rows * (scaled - unit * jnp.mean(scaled * unit, axis=-1, keepdims=True))


def tiles(count, width, body):
    def one(j, carry):
        body(pl.ds(pl.multiple_of(j * width, width), width))
        return carry

    lax.fori_loop(0, count // width, one, 0)


def tile_of(count):
    return 256 if count % 256 == 0 else 128


def turn(v, cosine, sine):
    return v * cosine + pltpu.roll(v, HD // 2, 1) * sine


def block_diagonal(out, parts, rank, width):
    out[...] = jnp.zeros(out.shape, out.dtype)
    for i in range(parts[1]):
        out[i * rank : (i + 1) * rank, i * width : (i + 1) * width] = parts[0][i * rank : (i + 1) * rank, :]


def write_norm(x_rows, source, gain):
    def body(at):
        v = source[at]
        x_rows[at] = (v * rms_scale(v) * gain[...]).astype(BF)

    by_rows(source.shape[0], body)


ROW_BLOCK = 128
KEY_STEP = 256


def row_blocks(tree, body):
    for j in range(tree // KEY_STEP):

        def one(i, carry, j=j):
            body(pl.ds(pl.multiple_of(j * KEY_STEP + i * ROW_BLOCK, ROW_BLOCK), ROW_BLOCK), (j + 1) * KEY_STEP)
            return carry

        lax.fori_loop(0, KEY_STEP // ROW_BLOCK, one, 0)


def seen(rows, keys, query_bits, key_bits):
    shared = (query_bits[rows] & key_bits[:, :keys]) != 0
    i = rows.start + lax.broadcasted_iota(jnp.int32, (ROW_BLOCK, keys), 0)
    j = lax.broadcasted_iota(jnp.int32, (ROW_BLOCK, keys), 1)
    return shared & (j <= i)


def attention_forward(
    n, layer, part, rank,
    residual, gain, w_hbm, a_model, a_head, cosine, sine, query_bits, key_bits, lam,
    middle, x_hbm, queries, keys, values, small, log_total, mixed, headed, side,
    x, p, w, raised, copy_sems, *sems,
):
    place = Place(n)
    chip_rows, width = 2 * x_hbm.shape[2], x_hbm.shape[3]
    tree = n * chip_rows
    load = pltpu.make_async_copy(w_hbm, w, copy_sems.at[0])
    load.start()
    gather, reduce = Gather(place, x, *sems[:6]), Reduce(place, p, *sems[6:])
    write_norm(x.at[place.q, place.t], residual, gain)
    block_diagonal(raised, (a_head[rank : 4 * rank], 3), rank, VD)
    enter(place)
    gather.begin()
    load.wait()

    def project(q):
        rows = pl.ds(pl.multiple_of(q * chip_rows, chip_rows), chip_rows)
        v = x[q].reshape(chip_rows, width)
        low = mm_t(v, a_model[: 3 * rank]).astype(BF)
        small[rows] = low
        for i, out in enumerate((queries, keys, values)):
            at = slice(i * VD, (i + 1) * VD)
            made = mm(v, w[:, at]) + ADAPTER_SCALE * mm(low, raised[:, at])
            if i < 2:
                for c in range(2):
                    half = slice(c * HD, (c + 1) * HD)
                    out[rows, half] = turn(made[:, half], cosine[rows], sine[rows]).astype(BF)
            else:
                out[rows] = made.astype(BF)

    for q in gather.chunks():
        project(q)
    keep = pltpu.make_async_copy(x, x_hbm, copy_sems.at[1])
    keep.start()
    score_scale = HD ** (-0.5)
    weight = lam[...]

    def attend(rows, count):
        visible = seen(rows, count, query_bits, key_bits)
        both = []
        for c in range(2):
            at = slice(c * HD, (c + 1) * HD)
            scores = mm_t(queries[rows, at], keys[:count, at]) * score_scale
            scores = jnp.where(visible, scores, NEGATIVE_BIG)
            top = jnp.max(scores, axis=-1, keepdims=True)
            raw = jnp.exp(scores - top)
            total = jnp.sum(raw, axis=-1, keepdims=True)
            log_total[rows, c : c + 1] = top + jnp.log(total)
            both.append(raw * (1.0 / total))
        mix = mm((both[0] - weight * both[1]).astype(BF), values[:count])
        mixed[rows] = mix
        head = (mix * rms_scale(mix) * keep_factor(layer)).astype(BF)
        headed[rows] = head
        side[rows] = mm_t(head, a_head[:rank]).astype(BF)

    row_blocks(tree, attend)

    for k in reduce.order:
        q = reduce.chips[k]
        rows = pl.ds(pl.multiple_of(q * chip_rows, chip_rows), chip_rows)
        head, low = headed[rows], side[rows]

        def out_tile(at):
            made = mm_t(head, w[at, 3 * VD :]) + ADAPTER_SCALE * mm(low, a_model[9 * rank : 10 * rank, at])
            p[q, :, :, at] = (made * part).astype(BF).reshape(2, chip_rows // 2, at.size)

        tiles(width, 512, out_tile)
        reduce.offer(k)
        if k == reduce.order[2]:
            reduce.far()
    for s in range(1, n // 2):
        reduce.near(s)

    def use(at, total):
        middle[at] = residual[at] + total

    reduce.end(use)
    keep.wait()
    gather.finish()
    reduce.finish()


def ffn_forward(
    n, units, rank,
    residual, gain, w_hbm, a_model, e_model,
    following, x_hbm, gates, ups, hidden, small, side,
    x, p, w, raised, copy_sems, *sems,
):
    place = Place(n)
    chip_rows, width = 2 * x_hbm.shape[2], x_hbm.shape[3]
    tree = n * chip_rows
    load = pltpu.make_async_copy(w_hbm, w, copy_sems.at[0])
    load.start()
    gather, reduce = Gather(place, x, *sems[:6]), Reduce(place, p, *sems[6:])
    write_norm(x.at[place.q, place.t], residual, gain)
    block_diagonal(raised, (e_model, 2), rank, units)
    enter(place)
    gather.begin()
    load.wait()
    step = tile_of(units)

    for q in gather.chunks():
        rows = pl.ds(pl.multiple_of(q * chip_rows, chip_rows), chip_rows)
        v = x[q].reshape(chip_rows, width)
        low = mm_t(v, a_model[4 * rank : 6 * rank]).astype(BF)
        small[rows] = low

        def unit_tile(at):
            up_at = pl.ds(pl.multiple_of(units + at.start, step), step)
            gate = mm(v, w[:, at]) + ADAPTER_SCALE * mm(low, raised[:, at])
            up = mm(v, w[:, up_at]) + ADAPTER_SCALE * mm(low, raised[:, up_at])
            gates[rows, at] = gate.astype(BF)
            ups[rows, at] = up.astype(BF)
            hidden[rows, at] = (gate / (1.0 + jnp.exp(-gate)) * up).astype(BF)

        tiles(units, step, unit_tile)
        made_hidden = hidden[rows]
        low_hidden = mm_t(made_hidden, e_model[2 * rank : 3 * rank]).astype(BF)
        side[rows] = low_hidden

        def out_tile(at):
            made = mm_t(made_hidden, w[at, 2 * units :])
            made = made + ADAPTER_SCALE * mm(low_hidden, a_model[10 * rank : 11 * rank, at])
            p[q, :, :, at] = made.astype(BF).reshape(2, chip_rows // 2, at.size)

        tiles(width, 512, out_tile)

    keep = pltpu.make_async_copy(x, x_hbm, copy_sems.at[1])
    keep.start()

    def use(at, total):
        following[at] = residual[at] + total

    reduce.run(use)
    keep.wait()
    gather.finish()
    reduce.finish()


def ffn_backward(
    n, units, rank,
    grad, middle, gain, w_hbm, a_model, e_model, x_hbm, gates, ups, hidden, small, side,
    grad_out, grad_up_down, grad_in, grad_units, grad_e2,
    x, p, w, kept, dgu, dsmall, dside, raised, copy_sems, *sems,
):
    place = Place(n)
    chip_rows, width = 2 * x_hbm.shape[2], x_hbm.shape[3]
    tree = n * chip_rows
    load = pltpu.make_async_copy(w_hbm, w, copy_sems.at[0])
    load.start()
    fetch = pltpu.make_async_copy(x_hbm, kept, copy_sems.at[1])
    fetch.start()
    gather, reduce = Gather(place, x, *sems[:6]), Reduce(place, p, *sems[6:])

    def own(at):
        x[place.q, place.t, at] = grad[at].astype(BF)

    by_rows(grad.shape[0], own)
    block_diagonal(raised, (e_model, 2), rank, units)
    enter(place)
    gather.begin()
    load.wait()
    step = tile_of(units)

    for q in gather.chunks():
        rows = pl.ds(pl.multiple_of(q * chip_rows, chip_rows), chip_rows)
        v = x[q].reshape(chip_rows, width)
        low = (ADAPTER_SCALE * mm_t(v, a_model[10 * rank : 11 * rank])).astype(BF)
        dside[rows] = low

        def unit_tile(at):
            up_at = pl.ds(pl.multiple_of(units + at.start, step), step)
            down_at = pl.ds(pl.multiple_of(2 * units + at.start, step), step)
            dhidden = mm(v, w[:, down_at]) + mm(low, e_model[2 * rank : 3 * rank, at])
            gate, up = gates[rows, at].astype(F32), ups[rows, at].astype(F32)
            sig = 1.0 / (1.0 + jnp.exp(-gate))
            dgu[rows, at] = (dhidden * up * sig * (1.0 + gate * (1.0 - sig))).astype(BF)
            dgu[rows, up_at] = (dhidden * gate * sig).astype(BF)

        tiles(units, step, unit_tile)
        back = dgu[rows]
        low_back = (ADAPTER_SCALE * mm_t(back, raised[...])).astype(BF)
        dsmall[rows] = low_back

        def out_tile(at):
            made = mm_t(back, w[at, : 2 * units]) + mm(low_back, a_model[4 * rank : 6 * rank, at])
            p[q, :, :, at] = made.astype(BF).reshape(2, chip_rows // 2, at.size)

        tiles(width, 512, out_tile)

    def use(at, total):
        inputs = middle[at]
        grad_out[at] = grad[at] + norm_back(total, inputs, rms_scale(inputs), gain[...])

    def adapters():
        fetch.wait()

        def model_tile(at):
            flat = x[:, :, :, at].reshape(tree, at.size)
            grad_up_down[:, at] = (ADAPTER_SCALE * t_mm(side[...], flat)).astype(BF)
            flat = kept[:, :, :, at].reshape(tree, at.size)
            grad_in[:, at] = t_mm(dsmall[...], flat).astype(BF)

        tiles(width, 256, model_tile)

        def unit_tile(at):
            up_at = pl.ds(pl.multiple_of(units + at.start, step), step)
            grad_units[:rank, at] = ADAPTER_SCALE * t_mm(small[...], dgu[:, at])[:rank]
            grad_units[rank:, at] = ADAPTER_SCALE * t_mm(small[...], dgu[:, up_at])[rank:]
            grad_e2[:, at] = t_mm(dside[...], hidden[:, at])

        tiles(units, step, unit_tile)

    reduce.run(use, adapters)
    gather.finish()
    reduce.finish()


def attention_backward(
    n, layer, part, rank,
    grad, residual, gain, w_hbm, a_model, a_head, cosine, sine, query_bits, key_bits, lam,
    x_hbm, queries, keys, values, small, log_total, mixed, headed, side,
    grad_out, grad_a9, grad_in, grad_head,
    x, p, w, dmixed, dq, dk, dv, dprojected, dsmall, dside, raised, copy_sems, *sems,
):
    place = Place(n)
    chip_rows, width = 2 * x_hbm.shape[2], x_hbm.shape[3]
    tree = n * chip_rows
    load = pltpu.make_async_copy(w_hbm, w, copy_sems.at[0])
    load.start()
    gather, reduce = Gather(place, x, *sems[:6]), Reduce(place, p, *sems[6:])

    def own(at):
        x[place.q, place.t, at] = grad[at].astype(BF)

    by_rows(grad.shape[0], own)
    block_diagonal(raised, (a_head[rank : 4 * rank], 3), rank, VD)
    enter(place)
    gather.begin()
    dk[...] = jnp.zeros(dk.shape, F32)
    dv[...] = jnp.zeros(dv.shape, F32)
    load.wait()

    for q in gather.chunks():
        rows = pl.ds(pl.multiple_of(q * chip_rows, chip_rows), chip_rows)
        v = x[q].reshape(chip_rows, width)
        low = (ADAPTER_SCALE * mm_t(v, a_model[9 * rank : 10 * rank])).astype(BF)
        dside[rows] = low
        dheaded = mm(v, w[:, 3 * VD :]) + mm(low, a_head[:rank])
        inputs = mixed[rows]
        dmixed[rows] = norm_back(dheaded, inputs, rms_scale(inputs), keep_factor(layer)).astype(BF)

    def out_gradient(at):
        flat = x[:, :, :, at].reshape(tree, at.size)
        grad_a9[:, at] = (ADAPTER_SCALE * part * t_mm(side[...], flat)).astype(BF)

    tiles(width, 256, out_gradient)
    gather.finish()
    fetch = pltpu.make_async_copy(x_hbm, x, copy_sems.at[1])
    fetch.start()
    score_scale = HD ** (-0.5)
    weight = lam[...]

    def attend(rows, count):
        visible = seen(rows, count, query_bits, key_bits)
        dmix = dmixed[rows]
        dweights = mm_t(dmix, values[:count])
        both = []
        for c in range(2):
            at = slice(c * HD, (c + 1) * HD)
            scores = mm_t(queries[rows, at], keys[:count, at]) * score_scale
            probability = jnp.exp(jnp.where(visible, scores - log_total[rows, c : c + 1], NEGATIVE_BIG))
            both.append(probability)
            weighted = probability * dweights
            dscores = weighted - probability * jnp.sum(weighted, axis=-1, keepdims=True)
            dscores = (dscores * -weight if c else dscores).astype(BF)
            dq[rows, at] = mm(dscores, keys[:count, at])
            dk[:count, at] += t_mm(dscores, queries[rows, at])
        dv[:count] += t_mm((both[0] - weight * both[1]).astype(BF), dmix)

    row_blocks(tree, attend)

    for k in reduce.order:
        q = reduce.chips[k]
        rows = pl.ds(pl.multiple_of(q * chip_rows, chip_rows), chip_rows)
        for i, source in enumerate((dq, dk)):
            for c in range(2):
                half = slice(c * HD, (c + 1) * HD)
                turned = turn(source[rows, half] * score_scale, cosine[rows], -sine[rows])
                dprojected[rows, i * VD + c * HD : i * VD + (c + 1) * HD] = turned.astype(BF)
        dprojected[rows, 2 * VD :] = dv[rows].astype(BF)
        back = dprojected[rows]
        low_back = (ADAPTER_SCALE * mm_t(back, raised[...])).astype(BF)
        dsmall[rows] = low_back

        def out_tile(at):
            made = mm_t(back, w[at, : 3 * VD]) + mm(low_back, a_model[: 3 * rank, at])
            p[q, :, :, at] = (made * part).astype(BF).reshape(2, chip_rows // 2, at.size)

        tiles(width, 512, out_tile)
        reduce.offer(k)
        if k == reduce.order[2]:
            reduce.far()
    for s in range(1, n // 2):
        reduce.near(s)

    fetch.wait()

    def model_tile(at):
        flat = x[:, :, :, at].reshape(tree, at.size)
        grad_in[:, at] = (part * t_mm(dsmall[...], flat)).astype(BF)

    tiles(width, 256, model_tile)
    grad_head[:rank] = part * t_mm(dside[...], headed[...])
    for i in range(3):
        made = t_mm(small[...], dprojected[:, i * VD : (i + 1) * VD])[i * rank : (i + 1) * rank]
        grad_head[(i + 1) * rank : (i + 2) * rank] = ADAPTER_SCALE * part * made

    def use(at, total):
        inputs = residual[at]
        grad_out[at] = grad[at] + norm_back(total, inputs, rms_scale(inputs), gain[...])

    reduce.end(use)
    reduce.finish()


def call(kernel, collective, ins, outs, scratch):
    spec = lambda hbm: pl.BlockSpec(memory_space=pl.ANY if hbm else pltpu.VMEM)
    return pl.pallas_call(
        kernel,
        out_shape=[jax.ShapeDtypeStruct(shape, kind) for shape, kind, _ in outs],
        in_specs=[spec(hbm) for _, hbm in ins],
        out_specs=[spec(hbm) for _, _, hbm in outs],
        scratch_shapes=scratch,
        compiler_params=pltpu.CompilerParams(
            collective_id=collective, has_side_effects=True, vmem_limit_bytes=60 << 20
        ),
    )(*[array for array, _ in ins])


def line_bits(parent_row, seg):
    number = jnp.arange(NSEG)
    one = lambda x: lax.shift_left(jnp.ones_like(x), x)
    grand = jnp.sum(jnp.where(parent_row[:, None] == number[None, :], parent_row[None, :], 0), axis=1)
    line = one(number) | one(parent_row) | one(grand)
    mine = jnp.sum(jnp.where(seg[:, None] == number[None, :], line[None, :], 0), axis=1)
    return mine, one(seg)


def keep_factor(layer):
    return 0.2 + 0.6 * math.exp(-0.3 * layer)


def chips_of(nf, nc):
    h = nc // 2
    for f in range(nf):
        for c in range(nc):
            yield f * nc + c, (f // 2, f % 2, c // h, c % h)


def permute(x, nf, nc, target):
    h = nc // 2
    pairs = []
    for source, spot in chips_of(nf, nc):
        f_hi, f_lo, c_hi, c_lo = target(*spot)
        pairs.append((source, (f_hi * 2 + f_lo) * nc + c_hi * h + c_lo))
    return lax.ppermute(x, ("fsdp", "ctx"), pairs)


def swap_trees(x, nf, nc):
    return permute(x, nf, nc, lambda f_hi, f_lo, c_hi, c_lo: (f_hi, c_hi, f_lo, c_lo))


def spread_weights(blocks, q, g, nf, nc):
    n, h = nc, nc // 2
    rows, width = blocks.shape[1:]
    mine = jnp.zeros((n, rows, width), BF)
    for d in range(n):
        part = lax.dynamic_index_in_dim(blocks, q ^ d, 0, keepdims=False)
        if d:

            def exchange(f_hi, f_lo, c_hi, c_lo, d=d):
                to = (f_lo * h + c_lo) ^ d
                return f_hi, to // h, c_hi, to % h

            part = permute(part, nf, nc, exchange)
        mine = lax.dynamic_update_index_in_dim(mine, part, q ^ d, 0)
    gathered = jnp.zeros((nf, n, rows, width), BF)
    gathered = lax.dynamic_update_index_in_dim(gathered, mine, g, 0)
    partner = permute(mine, nf, nc, lambda a, b, c, d: (a, b, c ^ 1, d))
    gathered = lax.dynamic_update_index_in_dim(gathered, partner, g ^ 1, 0)
    for d in range(1, nf // 2):
        for e, held in ((0, mine), (1, partner)):
            moved = permute(held, nf, nc, lambda a, b, c, k, d=d: (a ^ d, b, c, k))
            gathered = lax.dynamic_update_index_in_dim(gathered, moved, g ^ (2 * d + e), 0)
    return gathered.reshape(nf * n * rows, width)


def shards(
    nf,
    nc,
    tokens,
    cotangent,
    segments,
    depths,
    parents,
    tree_adapter_index,
    layer_norm_gains,
    difference_lambda,
    query_key_value_weight,
    output_weight,
    gate_up_weight,
    down_weight,
    adapter_model_factors,
    adapter_hidden_factors,
):
    n = nc
    place = Place(n)
    q, t, g = place.q, place.t, place.f_hi * 2 + place.c_hi
    tokens_dev, width = tokens.shape
    rows = tokens_dev // 2
    tree = tokens_dev * n
    layers, weight_rows = query_key_value_weight.shape[:2]
    heads_tp = difference_lambda.shape[1]
    share = max(1, n // heads_tp)
    head = q // share
    hidden_tp = down_weight.shape[2]
    units = (hidden_tp + n * 128 - 1) // (n * 128) * 128
    rank, adapters = adapter_model_factors.shape[3], adapter_model_factors.shape[2]
    h = n // 2

    def swap_columns(x):
        lead = x.shape[:-1]
        cut = x.reshape(lead + (nf // 2, 2, 2, h * weight_rows))
        return jnp.swapaxes(cut, -3, -2).reshape(lead + (width,))

    of_tree = lax.all_gather(jnp.stack([segments, depths]), "ctx", axis=1, tiled=True)
    notes = jnp.concatenate([of_tree[0], of_tree[1], parents[0], tree_adapter_index])
    notes = swap_trees(notes, nf, nc)
    seg, dep = notes[:tree], notes[tree : 2 * tree]
    parent_row, slot = notes[2 * tree : 2 * tree + NSEG], notes[2 * tree + NSEG]
    own_tokens = lax.dynamic_slice_in_dim(tokens, t * rows, rows, 0)
    own_cotangent = lax.dynamic_slice_in_dim(cotangent, t * rows, rows, 0)
    residual = swap_columns(swap_trees(own_tokens, nf, nc)).astype(F32)
    own_cotangent = swap_columns(swap_trees(own_cotangent, nf, nc))

    query_bits, key_bits = line_bits(parent_row, seg)
    query_bits, key_bits = query_bits[:, None], key_bits[None, :]
    frequency = 10000.0 ** (-jnp.arange(HD // 2).astype(F32) / (HD // 2))
    angles = dep.astype(F32)[:, None] * frequency[None, :]
    cosine, sine = jnp.cos(angles), jnp.sin(angles)
    cosine = jnp.concatenate([cosine, cosine], axis=1)
    sine = jnp.concatenate([-sine, sine], axis=1)
    gains = swap_columns(layer_norm_gains)

    a_all = lax.dynamic_index_in_dim(adapter_model_factors, slot, 2, keepdims=False)
    e_all = lax.dynamic_index_in_dim(adapter_hidden_factors, slot, 2, keepdims=False)
    a_model = swap_columns(a_all).reshape(layers, 11 * rank, width)
    e_all = e_all.reshape(layers, 3 * rank, -1)
    head_at = (t * heads_tp + head) * VD

    heads_of = lax.dynamic_slice_in_dim(a_all, head_at, VD, 3)
    a_head = jnp.concatenate([heads_of[:, 3:4], heads_of[:, 6:9]], axis=1).reshape(layers, 4 * rank, VD)

    def unit_columns(x):
        x = lax.dynamic_slice_in_dim(x, t * hidden_tp, hidden_tp, x.ndim - 1)
        x = jnp.pad(x, ((0, 0),) * (x.ndim - 1) + ((0, n * units - hidden_tp),))
        return lax.dynamic_slice_in_dim(x, q * units, units, x.ndim - 1)

    e_model = unit_columns(e_all)

    def blocks_of(l):
        def heads(x):
            cut = x.reshape(weight_rows, heads_tp, VD).transpose(1, 0, 2)
            return jnp.repeat(cut, share, axis=0) if share > 1 else cut

        def unit(x):
            x = jnp.pad(x, ((0, 0), (0, n * units - hidden_tp)))
            return x.reshape(weight_rows, n, units).transpose(1, 0, 2)

        w = query_key_value_weight[l]
        v = gate_up_weight[l]
        attention = jnp.concatenate([heads(w[:, i]) for i in range(3)] + [heads(output_weight[l])], axis=2)
        forward = jnp.concatenate([unit(v[:, 0]), unit(v[:, 1]), unit(down_weight[l])], axis=2)
        return attention, forward

    weights = []
    for l in range(layers):
        attention, forward = blocks_of(l)
        weights.append((spread_weights(attention, q, g, nf, nc), spread_weights(forward, q, g, nf, nc)))

    part = 1.0 / share
    calls = [0]
    whole_x = ((n, 2, rows, width), BF)
    sems = Gather.semaphores(n) + Reduce.scratch(n, rows, width)
    pair = pltpu.SemaphoreType.DMA((2,))
    vmem = lambda *spec: pltpu.VMEM(*spec)
    big = [vmem(*whole_x), vmem(*whole_x)]

    def run(kernel, ins, outs, scratch):
        calls[0] += 1
        return call(kernel, calls[0], ins, outs, scratch)

    near = lambda *arrays: [(array, False) for array in arrays]
    far = lambda *arrays: [(array, True) for array in arrays]
    out = lambda shape, kind, hbm=False: (shape, kind, hbm)

    saved = []
    for l in range(layers):
        w_attention, w_forward = weights[l]
        lam = lax.dynamic_slice_in_dim(difference_lambda[l], head, 1).reshape(1, 1)
        gain_a, gain_f = gains[l, 0:1], gains[l, 1:2]
        shared = (a_model[l], a_head[l], cosine, sine, query_bits, key_bits, lam)
        got = run(
            functools.partial(attention_forward, n, l, part, rank),
            near(residual, gain_a) + far(w_attention) + near(*shared),
            [
                out((rows, width), F32),
                out(*whole_x, True),
                out((tree, VD), BF),
                out((tree, VD), BF),
                out((tree, VD), BF),
                out((tree, 3 * rank), BF),
                out((tree, 2), F32),
                out((tree, VD), F32),
                out((tree, VD), BF),
                out((tree, rank), BF),
            ],
            big + [vmem((width, 4 * VD), BF), vmem((3 * rank, 3 * VD), BF), pair] + sems,
        )
        middle, kept = got[0], got[1:]
        ffn = run(
            functools.partial(ffn_forward, n, units, rank),
            near(middle, gain_f) + far(w_forward) + near(a_model[l], e_model[l]),
            [
                out((rows, width), F32),
                out(*whole_x, True),
                out((tree, units), BF),
                out((tree, units), BF),
                out((tree, units), BF),
                out((tree, 2 * rank), BF),
                out((tree, rank), BF),
            ],
            big + [vmem((width, 3 * units), BF), vmem((2 * rank, 2 * units), BF), pair] + sems,
        )
        saved.append((residual, middle, gain_a, gain_f, shared, kept, ffn[1:]))
        residual = ffn[0]

    grad = own_cotangent.astype(F32)
    model_grads, hidden_grads = [], []
    for l in reversed(range(layers)):
        w_attention, w_forward = weights[l]
        residual_in, middle, gain_a, gain_f, shared, kept, ffn = saved[l]
        grad, grad_a10, grad_a45, grad_e01, grad_e2 = run(
            functools.partial(ffn_backward, n, units, rank),
            near(grad, middle, gain_f) + far(w_forward) + near(a_model[l], e_model[l]) + far(ffn[0]) + near(*ffn[1:]),
            [
                out((rows, width), F32),
                out((rank, width), BF),
                out((2 * rank, width), BF),
                out((2 * rank, units), F32),
                out((rank, units), F32),
            ],
            big
            + [
                vmem((width, 3 * units), BF),
                vmem(*whole_x),
                vmem((tree, 2 * units), BF),
                vmem((tree, 2 * rank), BF),
                vmem((tree, rank), BF),
                vmem((2 * rank, 2 * units), BF),
                pair,
            ]
            + sems,
        )
        grad, grad_a9, grad_a012, grad_head = run(
            functools.partial(attention_backward, n, l, part, rank),
            near(grad, residual_in, gain_a) + far(w_attention) + near(*shared) + far(kept[0]) + near(*kept[1:]),
            [
                out((rows, width), F32),
                out((rank, width), BF),
                out((3 * rank, width), BF),
                out((4 * rank, VD), F32),
            ],
            big
            + [
                vmem((width, 4 * VD), BF),
                vmem((tree, VD), BF),
                vmem((tree, VD), F32),
                vmem((tree, VD), F32),
                vmem((tree, VD), F32),
                vmem((tree, 3 * VD), BF),
                vmem((tree, 3 * rank), BF),
                vmem((tree, rank), BF),
                vmem((3 * rank, 3 * VD), BF),
                pair,
            ]
            + sems,
        )

        def placed(x):
            empty = jnp.zeros(x.shape[:-1] + (width,), F32)
            return lax.dynamic_update_slice_in_dim(empty, x, head_at, x.ndim - 1).astype(BF)

        def placed_units(x):
            empty = jnp.zeros(x.shape[:-1] + (2, n * units), F32)
            empty = lax.dynamic_update_slice(
                empty, x[..., None, :], (0,) * (x.ndim - 1) + (t, q * units)
            )
            return empty[..., :hidden_tp].reshape(x.shape[:-1] + (2 * hidden_tp,)).astype(BF)

        headed = placed(grad_head)
        model_grads.insert(
            0,
            jnp.concatenate(
                [
                    swap_columns(grad_a012),
                    headed[:rank],
                    swap_columns(grad_a45),
                    headed[rank:],
                    swap_columns(grad_a9),
                    swap_columns(grad_a10),
                ]
            ),
        )
        hidden_grads.insert(0, placed_units(jnp.concatenate([grad_e01, grad_e2])))

    model_all = jnp.stack(model_grads).reshape(layers * 11 * rank, n, 2, width // (2 * n))
    hidden_all = jnp.stack(hidden_grads).reshape(layers * 3 * rank, n, 2, 2 * hidden_tp // (2 * n))
    lanes = 1024
    flat = jnp.concatenate(
        [x.transpose(1, 2, 0, 3).reshape(n, 2, -1) for x in (model_all, hidden_all)], axis=2
    )
    size = flat.shape[2]
    tall = -(-size // (lanes * 32)) * 32
    flat = jnp.pad(flat, ((0, 0), (0, 0), (0, tall * lanes - size))).reshape(n, 2, tall, lanes).astype(BF)
    calls[0] += 1
    summed = swap_trees(group_reduce(flat, n, calls[0]).astype(BF), nf, nc)
    every = lax.all_gather(summed, "fsdp", axis=0).reshape(nf, -1)[:, :size].astype(F32)
    slots = lax.all_gather(tree_adapter_index, "fsdp", axis=0, tiled=True)
    own_adapters = adapters // nf
    chosen = place.f * own_adapters + jnp.arange(own_adapters)
    pick = (slots[None, :] == chosen[:, None]).astype(F32)
    totals = jnp.sum(pick[:, :, None] * every[None], axis=1)
    cut = layers * 11 * rank * (width // (2 * n))
    grad_model = totals[:, :cut].reshape(own_adapters, layers, 11, rank, -1).transpose(1, 2, 0, 3, 4)
    grad_hidden = totals[:, cut:].reshape(own_adapters, layers, 3, rank, -1).transpose(1, 2, 0, 3, 4)

    def home(x):
        mine = swap_trees(swap_columns(x), nf, nc)
        other = lax.ppermute(mine, "tp", ((0, 1), (1, 0)))
        return jnp.where(t == 0, jnp.concatenate([mine, other]), jnp.concatenate([other, mine]))

    return home(residual.astype(BF)), home(grad), grad_model, grad_hidden


def solution(mesh):
    in_specs = (
        P(("fsdp", "ctx"), None),
        P(("fsdp", "ctx"), None),
        P(("fsdp", "ctx")),
        P(("fsdp", "ctx")),
        P("fsdp", None),
        P("fsdp"),
        P(),
        P(None, "tp"),
        P(None, ("fsdp", "ctx"), None, "tp"),
        P(None, ("fsdp", "ctx"), "tp"),
        P(None, ("fsdp", "ctx"), None, "tp"),
        P(None, ("fsdp", "ctx"), "tp"),
        P(),
        P(),
    )
    out_specs = (
        P(("fsdp", "ctx"), None),
        P(("fsdp", "ctx"), None),
        P(None, None, "fsdp", None, ("ctx", "tp")),
        P(None, None, "fsdp", None, ("ctx", "tp")),
    )
    body = functools.partial(shards, mesh.shape["fsdp"], mesh.shape["ctx"])
    return jax.shard_map(body, mesh=mesh, in_specs=in_specs, out_specs=out_specs, check_vma=False)
```

```python
import functools
import math

import jax
import jax.numpy as jnp
from jax import lax
from jax.experimental import pallas as pl
from jax.experimental.pallas import tpu as pltpu
from jax.sharding import PartitionSpec as P

HD = 128
VD = 256
NSEG = 13
EPSILON = 1e-05
ADAPTER_SCALE = 0.5
NEGATIVE_BIG = -1e30
MESH = pl.DeviceIdType.MESH
BF = jnp.bfloat16
F32 = jnp.float32


class Place:
    def __init__(self, n):
        self.n, self.h = n, n // 2
        self.f, self.c, self.t = lax.axis_index("fsdp"), lax.axis_index("ctx"), lax.axis_index("tp")
        self.f_hi, self.f_lo = self.f // 2, self.f % 2
        self.c_hi, self.c_lo = self.c // self.h, self.c % self.h
        self.q = self.f_lo * self.h + self.c_lo
        self.pos = self.f_lo * (n - 1) + (1 - 2 * self.f_lo) * self.c_lo

    def ring(self, k):
        n, h = self.n, self.h
        p = lax.rem(self.pos + k + 2 * n, n)
        low = p // h
        column = (1 - low) * p + low * (n - 1 - p)
        device = {"fsdp": self.f_hi * 2 + low, "ctx": self.c_hi * h + column}
        return low * h + column, device


def remote(src, dst, send, recv, device):
    copy = pltpu.make_async_remote_copy(
        src_ref=src, dst_ref=dst, send_sem=send, recv_sem=recv, device_id=device, device_id_type=MESH
    )
    copy.start()
    return copy


def flip(number, bits):
    b = 1
    while b <= bits:
        if bits & b:
            number = number + b * (1 - 2 * ((number // b) % 2))
        b *= 2
    return number


class Spread:
    def __init__(self, place, nf, w, rows):
        self.place, self.nf, self.w, self.rows = place, nf, w, rows
        self.g = place.f_hi * 2 + place.c_hi
        self.links = range(1, nf // 2)
        self.scattered, self.sent = [], []
        self.to_partner, self.along, self.onward = {}, {}, {}

    @staticmethod
    def scatter_semaphores(n):
        dma = pltpu.SemaphoreType.DMA
        return [dma((n,)), dma((n,))]

    @staticmethod
    def spread_semaphores(n, nf):
        dma = pltpu.SemaphoreType.DMA
        return [dma((n,))] * 2 + [dma((n, max(1, nf // 2 - 1)))] * 4

    def block(self, g, q):
        start = pl.multiple_of((g * self.place.n + q) * self.rows, self.rows)
        return self.w.at[pl.ds(start, self.rows)]

    def chip(self, q):
        place = self.place
        return {"fsdp": place.f_hi * 2 + q // place.h, "ctx": place.c_hi * place.h + q % place.h}

    def partner(self):
        place = self.place
        return {"ctx": (1 - place.c_hi) * place.h + place.c_lo}

    def line(self, e):
        return {"fsdp": flip(self.place.f_hi, e) * 2 + self.place.f_lo}

    def scatter(self, blocks, send, recv):
        q = self.place.q
        own = self.block(self.g, q)
        copy = pltpu.make_async_copy(blocks.at[q], own, recv.at[0])
        copy.start()
        self.scattered.append(copy)
        for d in range(1, self.place.n):
            to = flip(q, d)
            self.scattered.append(remote(blocks.at[to], own, send.at[d], recv.at[d], self.chip(to)))

    def arrived(self, d):
        if d:
            self.scattered[d].wait_recv()
        else:
            self.scattered[0].wait()

    def scatter_sent(self):
        for copy in self.scattered[1:]:
            copy.wait_send()

    def use(self, *sems):
        self.sems = sems

    def spread(self, d):
        send_z, recv_z, send_y, recv_y = self.sems[:4]
        at = self.block(self.g, flip(self.place.q, d))
        self.to_partner[d] = remote(at, at, send_z.at[d], recv_z.at[d], self.partner())
        for e in self.links:
            self.along[d, e] = remote(at, at, send_y.at[d, e - 1], recv_y.at[d, e - 1], self.line(e))

    def forward(self, d):
        send, recv = self.sems[4:]
        self.to_partner[d].wait_recv()
        at = self.block(flip(self.g, 1), flip(self.place.q, d))
        for e in self.links:
            self.onward[d, e] = remote(at, at, send.at[d, e - 1], recv.at[d, e - 1], self.line(e))

    def complete(self):
        for copy in list(self.along.values()) + list(self.onward.values()):
            copy.wait_recv()

    def sent_all(self):
        for copies in (self.to_partner, self.along, self.onward):
            for copy in copies.values():
                copy.wait_send()


def enter(place, nf=0, scatters=False):
    bar = pltpu.get_barrier_semaphore()
    devices = [{"tp": 1 - place.t}]
    guide = Spread(place, nf, None, 0)
    if scatters:
        devices += [guide.chip(flip(place.q, d)) for d in range(1, place.n)]
    else:
        devices += [place.ring(1)[1], place.ring(-1)[1]]
    if nf:
        devices += [guide.partner()] + [guide.line(e) for e in guide.links]
    for device in devices:
        pl.semaphore_signal(bar, inc=1, device_id=device, device_id_type=MESH)
    pl.semaphore_wait(bar, len(devices))


class Work:
    def __init__(self, place, nf, rows, scatters, spreads):
        self.n = place.n
        self.scatters, self.spreads = [], []
        for blocks, w, sems in scatters:
            self.scatters.append((Spread(place, nf, w, rows), blocks, sems))
        for w, sems in spreads:
            piece = Spread(place, nf, w, rows)
            piece.use(*sems)
            self.spreads.append(piece)

    def scatter(self, i):
        if i < len(self.scatters):
            piece, blocks, sems = self.scatters[i]
            piece.scatter(blocks, *sems)

    def spread(self, i, places=None):
        if i < len(self.spreads):
            for d in range(self.n) if places is None else places:
                self.spreads[i].spread(d)

    def forward(self, i, places):
        if i < len(self.spreads):
            for d in places:
                self.spreads[i].forward(d)

    def complete(self, i):
        if i < len(self.spreads):
            self.spreads[i].complete()

    def settle(self, done=()):
        for i in range(len(self.spreads)):
            if i not in done:
                self.complete(i)
            self.spreads[i].sent_all()
        for piece, _, _ in self.scatters:
            for d in range(self.n):
                piece.arrived(d)
            piece.scatter_sent()


def weights_kernel(
    n, nf, units, share, layers,
    qkv, output, gate_up, down, *refs,
):
    place = Place(n)
    rows, hidden = down.shape[1:]
    w_a, w_g = refs[:2]
    later = refs[2 : 2 + 3 * layers - 2]
    a_first, g_first, raw_g, raw_d, cut_sems, raw_sems = refs[3 * layers : 3 * layers + 6]
    sems = refs[3 * layers + 6 :]
    a_blocks = [a_first] + list(later[: layers - 1])
    g_blocks = [g_first] + list(later[layers - 1 : 2 * layers - 2])
    d_blocks = list(later[2 * layers - 2 :])
    cuts = []
    for l in range(layers):
        for q in range(n):
            columns = pl.ds(q // share * VD, VD)
            for i in range(4):
                source = qkv.at[l, i, :, columns] if i < 3 else output.at[l, :, columns]
                target = a_blocks[l].at[q, :, pl.ds(i * VD, VD)]
                cuts.append(pltpu.make_async_copy(source, target, cut_sems.at[l, q, i]))
    for copy in cuts[: 4 * n]:
        copy.start()
    raws = []
    for l in range(layers):
        raws.append(pltpu.make_async_copy(gate_up.at[l], raw_g.at[l], raw_sems.at[l, 0]))
        raws.append(pltpu.make_async_copy(down.at[l], raw_d.at[l], raw_sems.at[l, 1]))
    for copy in raws:
        copy.start()
    attention, forward = Spread(place, nf, w_a, rows), Spread(place, nf, w_g, rows)
    attention.use(*sems[2:8])
    enter(place, nf, True)
    for copy in cuts[: 4 * n]:
        copy.wait()
    attention.scatter(a_first, *sems[:2])
    for copy in cuts[4 * n :]:
        copy.start()

    def fill(target, j, at, value):
        width = min(units, hidden - j * units)
        target[j, :, at : at + width] = value(pl.ds(j * units, width))
        if width < units:
            target[j, :, at + width : at + units] = jnp.zeros((rows, units - width), BF)

    def cut_gate_up(l):
        raws[2 * l].wait()
        for i in range(2):
            for j in range(n):
                fill(g_blocks[l], j, i * units, lambda at, i=i: raw_g[l, :, i, at])

    cut_gate_up(0)
    for d in range(n):
        attention.arrived(d)
        attention.spread(d)
    forward.scatter(g_first, *sems[8:10])
    for l in range(layers):
        if l:
            cut_gate_up(l)
        raws[2 * l + 1].wait()
        for j in range(n):
            fill(d_blocks[l], j, 0, lambda at, l=l: raw_d[l, :, at])
    for copy in cuts[4 * n :]:
        copy.wait()
    for d in range(n):
        attention.forward(d)
    attention.complete()
    attention.scatter_sent()
    attention.sent_all()
    for d in range(n):
        forward.arrived(d)
    forward.scatter_sent()


class Gather:
    def __init__(self, place, x, send_r, recv_r, send_l, recv_l, core_send, core_recv):
        self.place, self.x = place, x
        self.sems = (send_r, recv_r, send_l, recv_l, core_send, core_recv)
        self.to_right, self.to_left, self.across = [], [], []

    @staticmethod
    def semaphores(n):
        dma = pltpu.SemaphoreType.DMA
        return [dma((n // 2,))] * 4 + [dma((n,))] * 2

    def _pass_on(self, s):
        place, x = self.place, self.x
        send_r, recv_r, send_l, recv_l = self.sems[:4]
        rows, half, t = x.shape[2], place.n // 2, place.t
        top = rows // 2
        part_r = pl.ds(0, top) if s == half - 1 else pl.ds(0, rows)
        part_l = pl.ds(top, top) if s == half - 1 else pl.ds(0, rows)
        right_at = x.at[place.ring(-s)[0], t, part_r]
        left_at = x.at[place.ring(s)[0], t, part_l]
        self.to_right.append(remote(right_at, right_at, send_r.at[s], recv_r.at[s], place.ring(1)[1]))
        self.to_left.append(remote(left_at, left_at, send_l.at[s], recv_l.at[s], place.ring(-1)[1]))

    def _cross(self, q):
        core_send, core_recv = self.sems[4:]
        slot, at = len(self.across), self.x.at[q, self.place.t]
        other = {"tp": 1 - self.place.t}
        self.across.append(remote(at, at, core_send.at[slot], core_recv.at[slot], other))

    def begin(self):
        self._pass_on(0)
        self._cross(self.place.q)

    def chunks(self):
        place, half = self.place, self.place.n // 2
        self.across[0].wait_recv()
        yield place.q
        for s in range(half):
            self.to_right[s].wait_recv()
            self.to_left[s].wait_recv()
            arrived = [place.ring(half)[0]] if s == half - 1 else [place.ring(-s - 1)[0], place.ring(s + 1)[0]]
            if s < half - 1:
                self._pass_on(s + 1)
            first = len(self.across)
            for q in arrived:
                self._cross(q)
            for i, q in enumerate(arrived):
                self.across[first + i].wait_recv()
                yield q

    def finish(self):
        for copy in self.to_right + self.to_left + self.across:
            copy.wait_send()


def by_rows(count, body, step=16):
    def one(i, carry):
        body(pl.ds(pl.multiple_of(i * step, step), step))
        return carry

    lax.fori_loop(0, count // step, one, 0)


class Reduce:
    def __init__(self, place, p, from_core, in_r, in_l, send_r, recv_r, send_l, recv_l, core_send, core_recv):
        self.place, self.p, self.from_core, self.in_r, self.in_l = place, p, from_core, in_r, in_l
        self.sems = (send_r, recv_r, send_l, recv_l, core_send, core_recv)
        half = place.n // 2
        self.order = [half] + [k for j in range(half - 1, 0, -1) for k in (j, -j)] + [0]
        self.chips = {k: place.ring(k)[0] for k in self.order}
        self.across, self.to_right, self.to_left = {}, [], []

    @staticmethod
    def scratch(n, rows, width):
        dma = pltpu.SemaphoreType.DMA
        wide = [pltpu.VMEM((n, rows, width), BF)] + [pltpu.VMEM((n // 2, rows, width), BF)] * 2
        return wide + [dma((n // 2,))] * 4 + [dma((n,))] * 2

    def offer(self, k):
        core_send, core_recv = self.sems[4:]
        slot, q, t = len(self.across), self.chips[k], self.place.t
        self.across[k] = remote(
            self.p.at[q, 1 - t], self.from_core.at[q], core_send.at[slot], core_recv.at[slot], {"tp": 1 - t}
        )

    def _local(self, k, at):
        q = self.chips[k]
        return self.p[q, self.place.t, at].astype(F32) + self.from_core[q, at].astype(F32)

    def _add(self, k, start, count, extra=None):
        def body(at):
            whole = pl.ds(pl.multiple_of(start + at.start, 16), at.size)
            total = self._local(k, whole)
            if extra is not None:
                total = total + extra[whole].astype(F32)
            self.from_core[self.chips[k], whole] = total.astype(BF)

        by_rows(count, body)

    def far(self):
        send_r, recv_r, send_l, recv_l = self.sems[:4]
        place, half = self.place, self.place.n // 2
        rows = self.p.shape[2]
        top = rows // 2
        self.across[half].wait_recv()
        self._add(half, 0, rows)
        low, high = pl.ds(0, top), pl.ds(top, top)
        sums = self.from_core.at[self.chips[half]]
        right, left = place.ring(1)[1], place.ring(-1)[1]
        self.to_right.append(remote(sums.at[low], self.in_r.at[0, low], send_r.at[0], recv_r.at[0], right))
        self.to_left.append(remote(sums.at[high], self.in_l.at[0, high], send_l.at[0], recv_l.at[0], left))

    def near(self, s):
        send_r, recv_r, send_l, recv_l = self.sems[:4]
        place, k = self.place, self.place.n // 2 - s
        rows = self.p.shape[2]
        top = rows // 2
        self.across[k].wait_recv()
        self.across[-k].wait_recv()
        if s == 1:
            self._add(k, top, top)
            self._add(-k, 0, top)
        start = 0 if s == 1 else None
        self.to_right[-1].wait_recv()
        self._add(k, 0, top if s == 1 else rows, self.in_r.at[s - 1])
        self.to_right.append(
            remote(self.from_core.at[self.chips[k]], self.in_r.at[s], send_r.at[s], recv_r.at[s], place.ring(1)[1])
        )
        self.to_left[-1].wait_recv()
        self._add(-k, top if s == 1 else 0, top if s == 1 else rows, self.in_l.at[s - 1])
        self.to_left.append(
            remote(self.from_core.at[self.chips[-k]], self.in_l.at[s], send_l.at[s], recv_l.at[s], place.ring(-1)[1])
        )

    def end(self, use):
        half = self.place.n // 2
        self.across[0].wait_recv()
        self.to_right[-1].wait_recv()
        self.to_left[-1].wait_recv()

        def body(at):
            use(at, self._local(0, at) + self.in_r[half - 1, at].astype(F32) + self.in_l[half - 1, at].astype(F32))

        by_rows(self.p.shape[2], body)

    def finish(self):
        for copy in self.to_right + self.to_left + list(self.across.values()):
            copy.wait_send()

    def run(self, use, before=None):
        for k in self.order:
            self.offer(k)
        self.far()
        for s in range(1, self.place.n // 2):
            self.near(s)
        if before is not None:
            before()
        self.end(use)


def rs_kernel(n, p_ref, out_ref, *scratch):
    place = Place(n)
    reduce = Reduce(place, p_ref, *scratch)
    enter(place)

    def use(at, total):
        out_ref[at] = total

    reduce.run(use)
    reduce.finish()


def group_reduce(p, n, collective):
    vmem = pl.BlockSpec(memory_space=pltpu.VMEM)
    rows, width = p.shape[2:]
    return pl.pallas_call(
        functools.partial(rs_kernel, n),
        out_shape=jax.ShapeDtypeStruct((rows, width), F32),
        in_specs=[vmem],
        out_specs=vmem,
        scratch_shapes=Reduce.scratch(n, rows, width),
        compiler_params=pltpu.CompilerParams(
            collective_id=collective, has_side_effects=True, vmem_limit_bytes=60 << 20
        ),
    )(p)


def mm(a, b):
    return jnp.dot(a, b, preferred_element_type=F32)


def mm_t(a, b):
    return lax.dot_general(a, b, (((1,), (1,)), ((), ())), preferred_element_type=F32)


def t_mm(a, b):
    return lax.dot_general(a, b, (((0,), (0,)), ((), ())), preferred_element_type=F32)


def rms_scale(values):
    return lax.rsqrt(jnp.mean(values * values, axis=-1, keepdims=True) + EPSILON)


def norm_back(grad_normed, inputs, scale_rows, gain):
    unit = inputs * scale_rows
    scaled = grad_normed * gain
    return scale_rows * (scaled - unit * jnp.mean(scaled * unit, axis=-1, keepdims=True))


def tiles(count, width, body):
    def one(j, carry):
        body(pl.ds(pl.multiple_of(j * width, width), width))
        return carry

    lax.fori_loop(0, count // width, one, 0)


def tile_of(count):
    return 256 if count % 256 == 0 else 128


def turn(v, cosine, sine):
    return v * cosine + pltpu.roll(v, HD // 2, 1) * sine


def block_diagonal(out, parts, rank, width):
    out[...] = jnp.zeros(out.shape, out.dtype)
    for i in range(parts[1]):
        out[i * rank : (i + 1) * rank, i * width : (i + 1) * width] = parts[0][i * rank : (i + 1) * rank, :]


def write_norm(x_rows, source, gain):
    def body(at):
        v = source[at]
        x_rows[at] = (v * rms_scale(v) * gain[...]).astype(BF)

    by_rows(source.shape[0], body)


ROW_BLOCK = 128
KEY_STEP = 256


def row_blocks(tree, body):
    for j in range(tree // KEY_STEP):

        def one(i, carry, j=j):
            body(pl.ds(pl.multiple_of(j * KEY_STEP + i * ROW_BLOCK, ROW_BLOCK), ROW_BLOCK), (j + 1) * KEY_STEP)
            return carry

        lax.fori_loop(0, KEY_STEP // ROW_BLOCK, one, 0)


def seen(rows, keys, query_bits, key_bits):
    shared = (query_bits[rows] & key_bits[:, :keys]) != 0
    i = rows.start + lax.broadcasted_iota(jnp.int32, (ROW_BLOCK, keys), 0)
    j = lax.broadcasted_iota(jnp.int32, (ROW_BLOCK, keys), 1)
    return shared & (j <= i)


def attention_forward(
    n, nf, layer, part, rank, plan,
    residual, gain, w_hbm, a_model, a_head, cosine, sine, query_bits, key_bits, lam, *refs,
):
    jobs, refs = plan.split(refs)
    (middle, x_hbm, queries, keys, values, small, log_total, mixed, headed, side,
     x, p, w, raised, copy_sems, *sems) = refs
    place = Place(n)
    chip_rows, width = 2 * x_hbm.shape[2], x_hbm.shape[3]
    tree = n * chip_rows
    load = pltpu.make_async_copy(w_hbm, w, copy_sems.at[0])
    load.start()
    gather, reduce = Gather(place, x, *sems[:6]), Reduce(place, p, *sems[6:])
    write_norm(x.at[place.q, place.t], residual, gain)
    block_diagonal(raised, (a_head[rank : 4 * rank], 3), rank, VD)
    work = plan.work(place, nf, jobs)
    enter(place, nf, bool(plan.scatters))
    gather.begin()
    work.spread(0)
    load.wait()

    def project(q):
        rows = pl.ds(pl.multiple_of(q * chip_rows, chip_rows), chip_rows)
        v = x[q].reshape(chip_rows, width)
        low = mm_t(v, a_model[: 3 * rank]).astype(BF)
        small[rows] = low
        for i, out in enumerate((queries, keys, values)):
            at = slice(i * VD, (i + 1) * VD)
            made = mm(v, w[:, at]) + ADAPTER_SCALE * mm(low, raised[:, at])
            if i < 2:
                for c in range(2):
                    half = slice(c * HD, (c + 1) * HD)
                    out[rows, half] = turn(made[:, half], cosine[rows], sine[rows]).astype(BF)
            else:
                out[rows] = made.astype(BF)

    for q in gather.chunks():
        project(q)
    work.forward(0, range(1))
    work.scatter(0)
    keep = pltpu.make_async_copy(x, x_hbm, copy_sems.at[1])
    keep.start()
    score_scale = HD ** (-0.5)
    weight = lam[...]

    def attend(rows, count):
        visible = seen(rows, count, query_bits, key_bits)
        both = []
        for c in range(2):
            at = slice(c * HD, (c + 1) * HD)
            scores = mm_t(queries[rows, at], keys[:count, at]) * score_scale
            scores = jnp.where(visible, scores, NEGATIVE_BIG)
            top = jnp.max(scores, axis=-1, keepdims=True)
            raw = jnp.exp(scores - top)
            total = jnp.sum(raw, axis=-1, keepdims=True)
            log_total[rows, c : c + 1] = top + jnp.log(total)
            both.append(raw * (1.0 / total))
        mix = mm((both[0] - weight * both[1]).astype(BF), values[:count])
        mixed[rows] = mix
        head = (mix * rms_scale(mix) * keep_factor(layer)).astype(BF)
        headed[rows] = head
        side[rows] = mm_t(head, a_head[:rank]).astype(BF)

    row_blocks(tree, attend)
    work.forward(0, range(1, n // 2))
    work.scatter(1)

    for k in reduce.order:
        q = reduce.chips[k]
        rows = pl.ds(pl.multiple_of(q * chip_rows, chip_rows), chip_rows)
        head, low = headed[rows], side[rows]

        def out_tile(at):
            made = mm_t(head, w[at, 3 * VD :]) + ADAPTER_SCALE * mm(low, a_model[9 * rank : 10 * rank, at])
            p[q, :, :, at] = (made * part).astype(BF).reshape(2, chip_rows // 2, at.size)

        tiles(width, 512, out_tile)
        reduce.offer(k)
        if k == reduce.order[2]:
            reduce.far()
    for s in range(1, n // 2):
        reduce.near(s)

    def use(at, total):
        middle[at] = residual[at] + total

    reduce.end(use)
    work.forward(0, range(n // 2, n))
    keep.wait()
    gather.finish()
    reduce.finish()
    work.settle()


def ffn_forward(
    n, nf, units, rank, plan,
    residual, gain, w_hbm, a_model, e_model, *refs,
):
    jobs, refs = plan.split(refs)
    (following, x_hbm, gates, ups, hidden, small, side,
     x, p, w, raised, copy_sems, *sems) = refs
    place = Place(n)
    chip_rows, width = 2 * x_hbm.shape[2], x_hbm.shape[3]
    tree = n * chip_rows
    load = pltpu.make_async_copy(w_hbm, w.at[:, pl.ds(0, 2 * units)], copy_sems.at[0])
    load.start()
    gather, reduce = Gather(place, x, *sems[:6]), Reduce(place, p, *sems[6:])
    write_norm(x.at[place.q, place.t], residual, gain)
    block_diagonal(raised, (e_model, 2), rank, units)
    work = plan.work(place, nf, jobs)
    enter(place, nf, bool(plan.scatters))
    gather.begin()
    work.spread(0)
    load.wait()
    step = tile_of(units)

    for number, q in enumerate(gather.chunks()):
        if number == n - 1:
            work.forward(0, range(1))
        rows = pl.ds(pl.multiple_of(q * chip_rows, chip_rows), chip_rows)
        v = x[q].reshape(chip_rows, width)
        low = mm_t(v, a_model[4 * rank : 6 * rank]).astype(BF)
        small[rows] = low

        def unit_tile(at):
            up_at = pl.ds(pl.multiple_of(units + at.start, step), step)
            gate = mm(v, w[:, at]) + ADAPTER_SCALE * mm(low, raised[:, at])
            up = mm(v, w[:, up_at]) + ADAPTER_SCALE * mm(low, raised[:, up_at])
            gates[rows, at] = gate.astype(BF)
            ups[rows, at] = up.astype(BF)
            hidden[rows, at] = (gate / (1.0 + jnp.exp(-gate)) * up).astype(BF)

        tiles(units, step, unit_tile)

    work.forward(0, range(1, n // 2))
    work.spread(1)
    work.scatter(0)
    keep = pltpu.make_async_copy(x, x_hbm, copy_sems.at[1])
    keep.start()

    work.forward(0, range(n // 2, n))
    work.complete(0)
    load = pltpu.make_async_copy(plan.late(jobs), w.at[:, pl.ds(2 * units, units)], copy_sems.at[0])
    load.start()
    load.wait()
    for k in reduce.order:
        q = reduce.chips[k]
        rows = pl.ds(pl.multiple_of(q * chip_rows, chip_rows), chip_rows)
        made_hidden = hidden[rows]
        low = mm_t(made_hidden, e_model[2 * rank : 3 * rank]).astype(BF)
        side[rows] = low

        def out_tile(at):
            made = mm_t(made_hidden, w[at, 2 * units :])
            made = made + ADAPTER_SCALE * mm(low, a_model[10 * rank : 11 * rank, at])
            p[q, :, :, at] = made.astype(BF).reshape(2, chip_rows // 2, at.size)

        tiles(width, 512, out_tile)
        reduce.offer(k)
        if k == reduce.order[2]:
            reduce.far()
    for s in range(1, n // 2):
        reduce.near(s)

    def use(at, total):
        following[at] = residual[at] + total

    reduce.end(use)
    work.forward(1, range(n))
    keep.wait()
    gather.finish()
    reduce.finish()
    work.settle((0,))


def ffn_backward(
    n, units, rank,
    grad, middle, gain, w_hbm, w_down_hbm, a_model, e_model, x_hbm, gates, ups, hidden, small, side,
    grad_out, grad_up_down, grad_in, grad_units, grad_e2,
    x, p, w, kept, dgu, dsmall, dside, raised, copy_sems, *sems,
):
    place = Place(n)
    chip_rows, width = 2 * x_hbm.shape[2], x_hbm.shape[3]
    tree = n * chip_rows
    load = pltpu.make_async_copy(w_hbm, w.at[:, pl.ds(0, 2 * units)], copy_sems.at[0])
    load.start()
    load_down = pltpu.make_async_copy(w_down_hbm, w.at[:, pl.ds(2 * units, units)], copy_sems.at[2])
    load_down.start()
    fetch = pltpu.make_async_copy(x_hbm, kept, copy_sems.at[1])
    fetch.start()
    gather, reduce = Gather(place, x, *sems[:6]), Reduce(place, p, *sems[6:])

    def own(at):
        x[place.q, place.t, at] = grad[at].astype(BF)

    by_rows(grad.shape[0], own)
    block_diagonal(raised, (e_model, 2), rank, units)
    enter(place)
    gather.begin()
    load.wait()
    load_down.wait()
    step = tile_of(units)

    for q in gather.chunks():
        rows = pl.ds(pl.multiple_of(q * chip_rows, chip_rows), chip_rows)
        v = x[q].reshape(chip_rows, width)
        low = (ADAPTER_SCALE * mm_t(v, a_model[10 * rank : 11 * rank])).astype(BF)
        dside[rows] = low

        def unit_tile(at):
            up_at = pl.ds(pl.multiple_of(units + at.start, step), step)
            down_at = pl.ds(pl.multiple_of(2 * units + at.start, step), step)
            dhidden = mm(v, w[:, down_at]) + mm(low, e_model[2 * rank : 3 * rank, at])
            gate, up = gates[rows, at].astype(F32), ups[rows, at].astype(F32)
            sig = 1.0 / (1.0 + jnp.exp(-gate))
            dgu[rows, at] = (dhidden * up * sig * (1.0 + gate * (1.0 - sig))).astype(BF)
            dgu[rows, up_at] = (dhidden * gate * sig).astype(BF)

        tiles(units, step, unit_tile)
        back = dgu[rows]
        low_back = (ADAPTER_SCALE * mm_t(back, raised[...])).astype(BF)
        dsmall[rows] = low_back

        def out_tile(at):
            made = mm_t(back, w[at, : 2 * units]) + mm(low_back, a_model[4 * rank : 6 * rank, at])
            p[q, :, :, at] = made.astype(BF).reshape(2, chip_rows // 2, at.size)

        tiles(width, 512, out_tile)

    def use(at, total):
        inputs = middle[at]
        grad_out[at] = grad[at] + norm_back(total, inputs, rms_scale(inputs), gain[...])

    def adapters():
        fetch.wait()

        def model_tile(at):
            flat = x[:, :, :, at].reshape(tree, at.size)
            grad_up_down[:, at] = (ADAPTER_SCALE * t_mm(side[...], flat)).astype(BF)
            flat = kept[:, :, :, at].reshape(tree, at.size)
            grad_in[:, at] = t_mm(dsmall[...], flat).astype(BF)

        tiles(width, 256, model_tile)

        def unit_tile(at):
            up_at = pl.ds(pl.multiple_of(units + at.start, step), step)
            grad_units[:rank, at] = ADAPTER_SCALE * t_mm(small[...], dgu[:, at])[:rank]
            grad_units[rank:, at] = ADAPTER_SCALE * t_mm(small[...], dgu[:, up_at])[rank:]
            grad_e2[:, at] = t_mm(dside[...], hidden[:, at])

        tiles(units, step, unit_tile)

    reduce.run(use, adapters)
    gather.finish()
    reduce.finish()


def attention_backward(
    n, layer, part, rank,
    grad, residual, gain, w_hbm, a_model, a_head, cosine, sine, query_bits, key_bits, lam,
    x_hbm, queries, keys, values, small, log_total, mixed, headed, side,
    grad_out, grad_a9, grad_in, grad_head,
    x, p, w, dmixed, dq, dk, dv, dprojected, dsmall, dside, raised, copy_sems, *sems,
):
    place = Place(n)
    chip_rows, width = 2 * x_hbm.shape[2], x_hbm.shape[3]
    tree = n * chip_rows
    load = pltpu.make_async_copy(w_hbm, w, copy_sems.at[0])
    load.start()
    gather, reduce = Gather(place, x, *sems[:6]), Reduce(place, p, *sems[6:])

    def own(at):
        x[place.q, place.t, at] = grad[at].astype(BF)

    by_rows(grad.shape[0], own)
    block_diagonal(raised, (a_head[rank : 4 * rank], 3), rank, VD)
    enter(place)
    gather.begin()
    dk[...] = jnp.zeros(dk.shape, F32)
    dv[...] = jnp.zeros(dv.shape, F32)
    load.wait()

    for q in gather.chunks():
        rows = pl.ds(pl.multiple_of(q * chip_rows, chip_rows), chip_rows)
        v = x[q].reshape(chip_rows, width)
        low = (ADAPTER_SCALE * mm_t(v, a_model[9 * rank : 10 * rank])).astype(BF)
        dside[rows] = low
        dheaded = mm(v, w[:, 3 * VD :]) + mm(low, a_head[:rank])
        inputs = mixed[rows]
        dmixed[rows] = norm_back(dheaded, inputs, rms_scale(inputs), keep_factor(layer)).astype(BF)

    def out_gradient(at):
        flat = x[:, :, :, at].reshape(tree, at.size)
        grad_a9[:, at] = (ADAPTER_SCALE * part * t_mm(side[...], flat)).astype(BF)

    tiles(width, 256, out_gradient)
    gather.finish()
    fetch = pltpu.make_async_copy(x_hbm, x, copy_sems.at[1])
    fetch.start()
    score_scale = HD ** (-0.5)
    weight = lam[...]

    def attend(rows, count):
        visible = seen(rows, count, query_bits, key_bits)
        dmix = dmixed[rows]
        dweights = mm_t(dmix, values[:count])
        both = []
        for c in range(2):
            at = slice(c * HD, (c + 1) * HD)
            scores = mm_t(queries[rows, at], keys[:count, at]) * score_scale
            probability = jnp.exp(jnp.where(visible, scores - log_total[rows, c : c + 1], NEGATIVE_BIG))
            both.append(probability)
            weighted = probability * dweights
            dscores = weighted - probability * jnp.sum(weighted, axis=-1, keepdims=True)
            dscores = (dscores * -weight if c else dscores).astype(BF)
            dq[rows, at] = mm(dscores, keys[:count, at])
            dk[:count, at] += t_mm(dscores, queries[rows, at])
        dv[:count] += t_mm((both[0] - weight * both[1]).astype(BF), dmix)

    row_blocks(tree, attend)

    for k in reduce.order:
        q = reduce.chips[k]
        rows = pl.ds(pl.multiple_of(q * chip_rows, chip_rows), chip_rows)
        for i, source in enumerate((dq, dk)):
            for c in range(2):
                half = slice(c * HD, (c + 1) * HD)
                turned = turn(source[rows, half] * score_scale, cosine[rows], -sine[rows])
                dprojected[rows, i * VD + c * HD : i * VD + (c + 1) * HD] = turned.astype(BF)
        dprojected[rows, 2 * VD :] = dv[rows].astype(BF)
        back = dprojected[rows]
        low_back = (ADAPTER_SCALE * mm_t(back, raised[...])).astype(BF)
        dsmall[rows] = low_back

        def out_tile(at):
            made = mm_t(back, w[at, : 3 * VD]) + mm(low_back, a_model[: 3 * rank, at])
            p[q, :, :, at] = (made * part).astype(BF).reshape(2, chip_rows // 2, at.size)

        tiles(width, 512, out_tile)
        reduce.offer(k)
        if k == reduce.order[2]:
            reduce.far()
    for s in range(1, n // 2):
        reduce.near(s)

    fetch.wait()

    def model_tile(at):
        flat = x[:, :, :, at].reshape(tree, at.size)
        grad_in[:, at] = (part * t_mm(dsmall[...], flat)).astype(BF)

    tiles(width, 256, model_tile)
    grad_head[:rank] = part * t_mm(dside[...], headed[...])
    for i in range(3):
        made = t_mm(small[...], dprojected[:, i * VD : (i + 1) * VD])[i * rank : (i + 1) * rank]
        grad_head[(i + 1) * rank : (i + 2) * rank] = ADAPTER_SCALE * part * made

    def use(at, total):
        inputs = residual[at]
        grad_out[at] = grad[at] + norm_back(total, inputs, rms_scale(inputs), gain[...])

    reduce.end(use)
    reduce.finish()


class Plan:
    def __init__(self, n, nf, rows, scatters, spreads):
        self.n, self.nf, self.rows = n, nf, rows
        self.scatters, self.spreads = scatters, spreads

    def ins(self):
        return [(blocks, True) for blocks, _ in self.scatters] + [(w, True) for w in self.spreads]

    def outs(self):
        made = [(shape, BF, True) for _, shape in self.scatters]
        return made + [(w.shape, BF, True) for w in self.spreads]

    def semaphores(self):
        made = Spread.scatter_semaphores(self.n) * len(self.scatters)
        return made + Spread.spread_semaphores(self.n, self.nf) * len(self.spreads)

    def split(self, refs):
        a, b = len(self.scatters), len(self.spreads)
        count = 2 * a + 6 * b
        refs = list(refs)
        taken = refs[: a + b], refs[a + b : 2 * (a + b)], refs[len(refs) - count :]
        return taken, refs[2 * (a + b) : len(refs) - count]

    def work(self, place, nf, jobs):
        a, b = len(self.scatters), len(self.spreads)
        ins, outs, sems = jobs
        scatters = [(ins[i], outs[i], sems[2 * i : 2 * i + 2]) for i in range(a)]
        spreads = [(outs[a + i], sems[2 * a + 6 * i : 2 * a + 6 * i + 6]) for i in range(b)]
        return Work(place, nf, self.rows, scatters, spreads)

    def late(self, jobs):
        return jobs[1][len(self.scatters)]


def call(kernel, collective, ins, outs, scratch, plan=None):
    spec = lambda hbm: pl.BlockSpec(memory_space=pl.ANY if hbm else pltpu.VMEM)
    aliases = {}
    if plan is not None:
        first_in, count = len(ins), len(plan.scatters)
        aliases = {first_in + count + i: count + i for i in range(len(plan.spreads))}
        ins, outs, scratch = ins + plan.ins(), plan.outs() + outs, scratch + plan.semaphores()
    made = pl.pallas_call(
        kernel,
        out_shape=[jax.ShapeDtypeStruct(shape, kind) for shape, kind, _ in outs],
        in_specs=[spec(hbm) for _, hbm in ins],
        out_specs=[spec(hbm) for _, _, hbm in outs],
        scratch_shapes=scratch,
        input_output_aliases=aliases,
        compiler_params=pltpu.CompilerParams(
            collective_id=collective, has_side_effects=True, vmem_limit_bytes=60 << 20
        ),
    )(*[array for array, _ in ins])
    return list(made)


def line_bits(parent_row, seg):
    number = jnp.arange(NSEG)
    one = lambda x: lax.shift_left(jnp.ones_like(x), x)
    grand = jnp.sum(jnp.where(parent_row[:, None] == number[None, :], parent_row[None, :], 0), axis=1)
    line = one(number) | one(parent_row) | one(grand)
    mine = jnp.sum(jnp.where(seg[:, None] == number[None, :], line[None, :], 0), axis=1)
    return mine, one(seg)


def keep_factor(layer):
    return 0.2 + 0.6 * math.exp(-0.3 * layer)


def chips_of(nf, nc):
    h = nc // 2
    for f in range(nf):
        for c in range(nc):
            yield f * nc + c, (f // 2, f % 2, c // h, c % h)


def permute(x, nf, nc, target):
    h = nc // 2
    pairs = []
    for source, spot in chips_of(nf, nc):
        f_hi, f_lo, c_hi, c_lo = target(*spot)
        pairs.append((source, (f_hi * 2 + f_lo) * nc + c_hi * h + c_lo))
    return lax.ppermute(x, ("fsdp", "ctx"), pairs)


def swap_trees(x, nf, nc):
    return permute(x, nf, nc, lambda f_hi, f_lo, c_hi, c_lo: (f_hi, c_hi, f_lo, c_lo))


def shards(
    nf,
    nc,
    tokens,
    cotangent,
    segments,
    depths,
    parents,
    tree_adapter_index,
    layer_norm_gains,
    difference_lambda,
    query_key_value_weight,
    output_weight,
    gate_up_weight,
    down_weight,
    adapter_model_factors,
    adapter_hidden_factors,
):
    n = nc
    place = Place(n)
    q, t = place.q, place.t
    tokens_dev, width = tokens.shape
    rows = tokens_dev // 2
    tree = tokens_dev * n
    layers, weight_rows = query_key_value_weight.shape[:2]
    heads_tp = difference_lambda.shape[1]
    share = max(1, n // heads_tp)
    head = q // share
    hidden_tp = down_weight.shape[2]
    units = (hidden_tp + n * 128 - 1) // (n * 128) * 128
    rank, adapters = adapter_model_factors.shape[3], adapter_model_factors.shape[2]
    h = n // 2

    def swap_columns(x):
        lead = x.shape[:-1]
        cut = x.reshape(lead + (nf // 2, 2, 2, h * weight_rows))
        return jnp.swapaxes(cut, -3, -2).reshape(lead + (width,))

    of_tree = lax.all_gather(jnp.stack([segments, depths]), "ctx", axis=1, tiled=True)
    notes = jnp.concatenate([of_tree[0], of_tree[1], parents[0], tree_adapter_index])
    notes = swap_trees(notes, nf, nc)
    seg, dep = notes[:tree], notes[tree : 2 * tree]
    parent_row, slot = notes[2 * tree : 2 * tree + NSEG], notes[2 * tree + NSEG]
    own_tokens = lax.dynamic_slice_in_dim(tokens, t * rows, rows, 0)
    own_cotangent = lax.dynamic_slice_in_dim(cotangent, t * rows, rows, 0)
    residual = swap_columns(swap_trees(own_tokens, nf, nc)).astype(F32)
    own_cotangent = swap_columns(swap_trees(own_cotangent, nf, nc))

    query_bits, key_bits = line_bits(parent_row, seg)
    query_bits, key_bits = query_bits[:, None], key_bits[None, :]
    frequency = 10000.0 ** (-jnp.arange(HD // 2).astype(F32) / (HD // 2))
    angles = dep.astype(F32)[:, None] * frequency[None, :]
    cosine, sine = jnp.cos(angles), jnp.sin(angles)
    cosine = jnp.concatenate([cosine, cosine], axis=1)
    sine = jnp.concatenate([-sine, sine], axis=1)
    gains = swap_columns(layer_norm_gains)

    a_all = lax.dynamic_index_in_dim(adapter_model_factors, slot, 2, keepdims=False)
    e_all = lax.dynamic_index_in_dim(adapter_hidden_factors, slot, 2, keepdims=False)
    a_model = swap_columns(a_all).reshape(layers, 11 * rank, width)
    e_all = e_all.reshape(layers, 3 * rank, -1)
    head_at = (t * heads_tp + head) * VD

    heads_of = lax.dynamic_slice_in_dim(a_all, head_at, VD, 3)
    a_head = jnp.concatenate([heads_of[:, 3:4], heads_of[:, 6:9]], axis=1).reshape(layers, 4 * rank, VD)

    def unit_columns(x):
        x = lax.dynamic_slice_in_dim(x, t * hidden_tp, hidden_tp, x.ndim - 1)
        x = jnp.pad(x, ((0, 0),) * (x.ndim - 1) + ((0, n * units - hidden_tp),))
        return lax.dynamic_slice_in_dim(x, q * units, units, x.ndim - 1)

    e_model = unit_columns(e_all)

    part = 1.0 / share
    vmem = lambda *spec: pltpu.VMEM(*spec)
    calls = [0]
    whole_x = ((n, 2, rows, width), BF)
    sems = Gather.semaphores(n) + Reduce.scratch(n, rows, width)
    pair = pltpu.SemaphoreType.DMA((3,))
    big = [vmem(*whole_x), vmem(*whole_x)]

    def run(kernel, ins, outs, scratch, plan=None):
        calls[0] += 1
        return call(kernel, calls[0], ins, outs, scratch, plan)

    near = lambda *arrays: [(array, False) for array in arrays]
    far = lambda *arrays: [(array, True) for array in arrays]
    out = lambda shape, kind, hbm=False: (shape, kind, hbm)

    dma = pltpu.SemaphoreType.DMA
    c_a, c_g, c_d = 4 * VD, 2 * units, units
    tall = nf * n * weight_rows
    cut = lambda columns: out((n, weight_rows, columns), BF)
    calls[0] += 1
    made = call(
        functools.partial(weights_kernel, n, nf, units, share, layers),
        calls[0],
        far(jnp.transpose(query_key_value_weight, (0, 2, 1, 3)), output_weight, gate_up_weight, down_weight),
        [out((tall, c_a), BF, True), out((tall, c_g), BF, True)]
        + [cut(c_a)] * (layers - 1)
        + [cut(c_g)] * (layers - 1)
        + [cut(c_d)] * layers,
        [
            vmem((n, weight_rows, c_a), BF),
            vmem((n, weight_rows, c_g), BF),
            vmem((layers, weight_rows, 2, hidden_tp), BF),
            vmem((layers, weight_rows, hidden_tp), BF),
            dma((layers, n, 4)),
            dma((layers, 2)),
        ]
        + Spread.scatter_semaphores(n)
        + Spread.spread_semaphores(n, nf)
        + Spread.scatter_semaphores(n),
    )
    w_a, w_g = [made[0]], [made[1]]
    w_d = []
    a_blocks = [None] + made[2 : 1 + layers]
    g_blocks = [None] + made[1 + layers : 2 * layers]
    d_blocks = made[2 * layers :]

    def plan_of(scatters, spreads):
        return Plan(n, nf, weight_rows, scatters, spreads)

    saved = []
    for l in range(layers):
        last = l == layers - 1
        w_attention = w_a[l]
        lam = lax.dynamic_slice_in_dim(difference_lambda[l], head, 1).reshape(1, 1)
        gain_a, gain_f = gains[l, 0:1], gains[l, 1:2]
        shared = (a_model[l], a_head[l], cosine, sine, query_bits, key_bits, lam)
        plan = plan_of(
            [(d_blocks[l], (tall, c_d))] + ([] if last else [(a_blocks[l + 1], (tall, c_a))]), [w_g[l]]
        )
        got = run(
            functools.partial(attention_forward, n, nf, l, part, rank, plan),
            near(residual, gain_a) + far(w_attention) + near(*shared),
            [
                out((rows, width), F32),
                out(*whole_x, True),
                out((tree, VD), BF),
                out((tree, VD), BF),
                out((tree, VD), BF),
                out((tree, 3 * rank), BF),
                out((tree, 2), F32),
                out((tree, VD), F32),
                out((tree, VD), BF),
                out((tree, rank), BF),
            ],
            big + [vmem((width, 4 * VD), BF), vmem((3 * rank, 3 * VD), BF), pair] + sems,
            plan,
        )
        w_d.append(got[0])
        if not last:
            w_a.append(got[1])
        w_g[l] = got[2 - last]
        middle, kept = got[3 - last], got[4 - last :]
        plan = plan_of([] if last else [(g_blocks[l + 1], (tall, c_g))], [w_d[l]] + ([] if last else [w_a[l + 1]]))
        ffn = run(
            functools.partial(ffn_forward, n, nf, units, rank, plan),
            near(middle, gain_f) + far(w_g[l]) + near(a_model[l], e_model[l]),
            [
                out((rows, width), F32),
                out(*whole_x, True),
                out((tree, units), BF),
                out((tree, units), BF),
                out((tree, units), BF),
                out((tree, 2 * rank), BF),
                out((tree, rank), BF),
            ],
            big + [vmem((width, 3 * units), BF), vmem((2 * rank, 2 * units), BF), pair] + sems,
            plan,
        )
        if not last:
            w_g.append(ffn[0])
            w_a[l + 1] = ffn[2]
        w_d[l] = ffn[1 - last]
        ffn = ffn[3 - 2 * last :]
        saved.append((residual, middle, gain_a, gain_f, shared, kept, ffn[1:]))
        residual = ffn[0]

    grad = own_cotangent.astype(F32)
    model_grads, hidden_grads = [], []
    for l in reversed(range(layers)):
        residual_in, middle, gain_a, gain_f, shared, kept, ffn = saved[l]
        grad, grad_a10, grad_a45, grad_e01, grad_e2 = run(
            functools.partial(ffn_backward, n, units, rank),
            near(grad, middle, gain_f) + far(w_g[l], w_d[l]) + near(a_model[l], e_model[l]) + far(ffn[0]) + near(*ffn[1:]),
            [
                out((rows, width), F32),
                out((rank, width), BF),
                out((2 * rank, width), BF),
                out((2 * rank, units), F32),
                out((rank, units), F32),
            ],
            big
            + [
                vmem((width, 3 * units), BF),
                vmem(*whole_x),
                vmem((tree, 2 * units), BF),
                vmem((tree, 2 * rank), BF),
                vmem((tree, rank), BF),
                vmem((2 * rank, 2 * units), BF),
                pair,
            ]
            + sems,
        )
        grad, grad_a9, grad_a012, grad_head = run(
            functools.partial(attention_backward, n, l, part, rank),
            near(grad, residual_in, gain_a) + far(w_a[l]) + near(*shared) + far(kept[0]) + near(*kept[1:]),
            [
                out((rows, width), F32),
                out((rank, width), BF),
                out((3 * rank, width), BF),
                out((4 * rank, VD), F32),
            ],
            big
            + [
                vmem((width, 4 * VD), BF),
                vmem((tree, VD), BF),
                vmem((tree, VD), F32),
                vmem((tree, VD), F32),
                vmem((tree, VD), F32),
                vmem((tree, 3 * VD), BF),
                vmem((tree, 3 * rank), BF),
                vmem((tree, rank), BF),
                vmem((3 * rank, 3 * VD), BF),
                pair,
            ]
            + sems,
        )

        def placed(x):
            empty = jnp.zeros(x.shape[:-1] + (width,), F32)
            return lax.dynamic_update_slice_in_dim(empty, x, head_at, x.ndim - 1).astype(BF)

        def placed_units(x):
            empty = jnp.zeros(x.shape[:-1] + (2, n * units), F32)
            empty = lax.dynamic_update_slice(
                empty, x[..., None, :], (0,) * (x.ndim - 1) + (t, q * units)
            )
            return empty[..., :hidden_tp].reshape(x.shape[:-1] + (2 * hidden_tp,)).astype(BF)

        headed = placed(grad_head)
        model_grads.insert(
            0,
            jnp.concatenate(
                [
                    swap_columns(grad_a012),
                    headed[:rank],
                    swap_columns(grad_a45),
                    headed[rank:],
                    swap_columns(grad_a9),
                    swap_columns(grad_a10),
                ]
            ),
        )
        hidden_grads.insert(0, placed_units(jnp.concatenate([grad_e01, grad_e2])))

    model_all = jnp.stack(model_grads).reshape(layers * 11 * rank, n, 2, width // (2 * n))
    hidden_all = jnp.stack(hidden_grads).reshape(layers * 3 * rank, n, 2, 2 * hidden_tp // (2 * n))
    lanes = 1024
    flat = jnp.concatenate(
        [x.transpose(1, 2, 0, 3).reshape(n, 2, -1) for x in (model_all, hidden_all)], axis=2
    )
    size = flat.shape[2]
    tall = -(-size // (lanes * 32)) * 32
    flat = jnp.pad(flat, ((0, 0), (0, 0), (0, tall * lanes - size))).reshape(n, 2, tall, lanes).astype(BF)
    calls[0] += 1
    summed = swap_trees(group_reduce(flat, n, calls[0]).astype(BF), nf, nc)
    every = lax.all_gather(summed, "fsdp", axis=0).reshape(nf, -1)[:, :size].astype(F32)
    slots = lax.all_gather(tree_adapter_index, "fsdp", axis=0, tiled=True)
    own_adapters = adapters // nf
    chosen = place.f * own_adapters + jnp.arange(own_adapters)
    pick = (slots[None, :] == chosen[:, None]).astype(F32)
    totals = jnp.sum(pick[:, :, None] * every[None], axis=1)
    cut = layers * 11 * rank * (width // (2 * n))
    grad_model = totals[:, :cut].reshape(own_adapters, layers, 11, rank, -1).transpose(1, 2, 0, 3, 4)
    grad_hidden = totals[:, cut:].reshape(own_adapters, layers, 3, rank, -1).transpose(1, 2, 0, 3, 4)

    def home(x):
        mine = swap_trees(swap_columns(x), nf, nc)
        other = lax.ppermute(mine, "tp", ((0, 1), (1, 0)))
        return jnp.where(t == 0, jnp.concatenate([mine, other]), jnp.concatenate([other, mine]))

    return home(residual.astype(BF)), home(grad), grad_model, grad_hidden


def solution(mesh):
    in_specs = (
        P(("fsdp", "ctx"), None),
        P(("fsdp", "ctx"), None),
        P(("fsdp", "ctx")),
        P(("fsdp", "ctx")),
        P("fsdp", None),
        P("fsdp"),
        P(),
        P(None, "tp"),
        P(None, ("fsdp", "ctx"), None, "tp"),
        P(None, ("fsdp", "ctx"), "tp"),
        P(None, ("fsdp", "ctx"), None, "tp"),
        P(None, ("fsdp", "ctx"), "tp"),
        P(),
        P(),
    )
    out_specs = (
        P(("fsdp", "ctx"), None),
        P(("fsdp", "ctx"), None),
        P(None, None, "fsdp", None, ("ctx", "tp")),
        P(None, None, "fsdp", None, ("ctx", "tp")),
    )
    body = functools.partial(shards, mesh.shape["fsdp"], mesh.shape["ctx"])
    return jax.shard_map(body, mesh=mesh, in_specs=in_specs, out_specs=out_specs, check_vma=False)
```

```python
import functools
import math

import jax
import jax.numpy as jnp
from jax import lax
from jax.experimental import pallas as pl
from jax.experimental.pallas import tpu as pltpu
from jax.sharding import PartitionSpec as P

HD = 128
VD = 256
NSEG = 13
EPSILON = 1e-05
ADAPTER_SCALE = 0.5
NEGATIVE_BIG = -1e30
MESH = pl.DeviceIdType.MESH
BF = jnp.bfloat16
F32 = jnp.float32


class Place:
    def __init__(self, n):
        self.n, self.h = n, n // 2
        self.f, self.c, self.t = lax.axis_index("fsdp"), lax.axis_index("ctx"), lax.axis_index("tp")
        self.f_hi, self.f_lo = self.f // 2, self.f % 2
        self.c_hi, self.c_lo = self.c // self.h, self.c % self.h
        self.q = self.f_lo * self.h + self.c_lo
        self.away = self.f_lo + self.c_hi - 2 * self.f_lo * self.c_hi
        self.home = {"fsdp": self.f_hi * 2 + self.c_hi, "ctx": self.f_lo * self.h + self.c_lo}
        self.pos = self.f_lo * (n - 1) + (1 - 2 * self.f_lo) * self.c_lo

    def ring(self, k):
        n, h = self.n, self.h
        p = lax.rem(self.pos + k + 2 * n, n)
        low = p // h
        column = (1 - low) * p + low * (n - 1 - p)
        device = {"fsdp": self.f_hi * 2 + low, "ctx": self.c_hi * h + column}
        return low * h + column, device


def remote(src, dst, send, recv, device):
    copy = pltpu.make_async_remote_copy(
        src_ref=src, dst_ref=dst, send_sem=send, recv_sem=recv, device_id=device, device_id_type=MESH
    )
    copy.start()
    return copy


def flip(number, bits):
    b = 1
    while b <= bits:
        if bits & b:
            number = number + b * (1 - 2 * ((number // b) % 2))
        b *= 2
    return number


class Spread:
    def __init__(self, place, nf, w, rows):
        self.place, self.nf, self.w, self.rows = place, nf, w, rows
        self.g = place.f_hi * 2 + place.c_hi
        self.links = range(1, nf // 2)
        self.scattered, self.sent = [], []
        self.to_partner, self.along, self.onward, self.got = {}, {}, {}, []

    @staticmethod
    def scatter_semaphores(n):
        dma = pltpu.SemaphoreType.DMA
        return [dma((n,)), dma((n,))]

    @staticmethod
    def spread_semaphores(n, nf):
        dma = pltpu.SemaphoreType.DMA
        return [dma((n,))] * 2 + [dma((n, max(1, nf // 2 - 1)))] * 4

    def block(self, g, q):
        start = pl.multiple_of((g * self.place.n + q) * self.rows, self.rows)
        return self.w.at[pl.ds(start, self.rows)]

    def chip(self, q):
        place = self.place
        return {"fsdp": place.f_hi * 2 + q // place.h, "ctx": place.c_hi * place.h + q % place.h}

    def partner(self):
        place = self.place
        return {"ctx": (1 - place.c_hi) * place.h + place.c_lo}

    def line(self, e):
        return {"fsdp": flip(self.place.f_hi, e) * 2 + self.place.f_lo}

    def scatter(self, blocks, send, recv):
        q = self.place.q
        own = self.block(self.g, q)
        copy = pltpu.make_async_copy(blocks.at[q], own, recv.at[0])
        copy.start()
        self.scattered.append(copy)
        for d in range(1, self.place.n):
            to = flip(q, d)
            self.scattered.append(remote(blocks.at[to], own, send.at[d], recv.at[d], self.chip(to)))

    def arrived(self, d):
        if d:
            self.scattered[d].wait_recv()
        else:
            self.scattered[0].wait()

    def scatter_sent(self):
        for copy in self.scattered[1:]:
            copy.wait_send()

    def use(self, *sems):
        self.sems = sems

    def spread(self, d):
        send_z, recv_z, send_y, recv_y = self.sems[:4]
        at = self.block(self.g, flip(self.place.q, d))
        self.to_partner[d] = remote(at, at, send_z.at[d], recv_z.at[d], self.partner())
        for e in self.links:
            self.along[d, e] = remote(at, at, send_y.at[d, e - 1], recv_y.at[d, e - 1], self.line(e))

    def landed(self, d):
        if d in self.to_partner and d not in self.got:
            self.to_partner[d].wait_recv()
            self.got.append(d)

    def forward(self, d):
        send, recv = self.sems[4:]
        self.landed(d)
        at = self.block(flip(self.g, 1), flip(self.place.q, d))
        for e in self.links:
            self.onward[d, e] = remote(at, at, send.at[d, e - 1], recv.at[d, e - 1], self.line(e))

    def complete(self):
        for d in list(self.to_partner):
            self.landed(d)
        for copy in list(self.along.values()) + list(self.onward.values()):
            copy.wait_recv()

    def sent_all(self):
        for copies in (self.to_partner, self.along, self.onward):
            for copy in copies.values():
                copy.wait_send()


def enter(place, nf=0, scatters=False, home=False, ring=True, trees=0):
    bar = pltpu.get_barrier_semaphore()
    devices = [{"tp": 1 - place.t}]
    guide = Spread(place, nf, None, 0)
    if scatters:
        devices += [guide.chip(flip(place.q, d)) for d in range(1, place.n)]
    elif ring:
        devices += [place.ring(1)[1], place.ring(-1)[1]]
    if nf:
        devices += [guide.partner()] + [guide.line(e) for e in guide.links]
    devices += [{"fsdp": flip(place.f, e)} for e in range(1, trees)]
    for device in devices:
        pl.semaphore_signal(bar, inc=1, device_id=device, device_id_type=MESH)
    count = len(devices)
    if home:

        @pl.when(place.away == 1)
        def greet():
            pl.semaphore_signal(bar, inc=1, device_id=place.home, device_id_type=MESH)

        count = count + place.away
    pl.semaphore_wait(bar, count)


class Home:
    def __init__(self, place, out, send, recv):
        self.place, self.out = place, out
        self.send, self.recv = send, recv

    @staticmethod
    def semaphores():
        dma = pltpu.SemaphoreType.DMA
        return [dma((2,)), dma((2,))]

    def start(self, rows):
        place, slot = self.place, self.out.at[self.place.t]
        far = pltpu.make_async_remote_copy(
            src_ref=rows, dst_ref=slot, send_sem=self.send.at[0], recv_sem=self.recv.at[0],
            device_id=place.home, device_id_type=MESH,
        )
        near = pltpu.make_async_copy(rows, slot, self.recv.at[0])
        self.far = far
        pl.when(place.away == 1)(far.start)
        pl.when(place.away == 0)(near.start)
        self.near = near

    def land(self, share=True):
        pl.when(self.place.away == 1)(self.far.wait)
        pl.when(self.place.away == 0)(self.near.wait)
        if share:
            slot = self.out.at[self.place.t]
            self.across = remote(slot, slot, self.send.at[1], self.recv.at[1], {"tp": 1 - self.place.t})

    def finish(self):
        self.across.wait()


class TreeMove(Home):
    def __init__(self, place, rows, out, send, recv):
        super().__init__(place, out, send, recv)
        self.rows = rows
        self.slot = out.at[place.f]

    def start(self):
        place = self.place
        target = self.out.at[place.f_hi * 2 + place.c_hi]
        self.far = pltpu.make_async_remote_copy(
            src_ref=self.rows, dst_ref=target, send_sem=self.send.at[0], recv_sem=self.recv.at[0],
            device_id=place.home, device_id_type=MESH,
        )
        self.near = pltpu.make_async_copy(self.rows, target, self.recv.at[0])
        pl.when(place.away == 1)(self.far.start)
        pl.when(place.away == 0)(self.near.start)

    def land(self):
        super().land(False)


class Work:
    def __init__(self, place, nf, rows, scatters, spreads, schedule):
        self.n, self.schedule = place.n, schedule
        self.scatters, self.spreads = [], []
        for blocks, w, sems in scatters:
            self.scatters.append((Spread(place, nf, w, rows), blocks, sems))
        for w, sems in spreads:
            piece = Spread(place, nf, w, rows)
            piece.use(*sems)
            self.spreads.append(piece)

    def at(self, point):
        for what, i, *d in self.schedule[point] if point < len(self.schedule) else ():
            if what == "scatter":
                piece, blocks, sems = self.scatters[i]
                piece.scatter(blocks, *sems)
            elif what == "spread":
                self.spreads[i].spread(*d)
            else:
                self.spreads[i].forward(*d)

    def complete(self, i):
        self.spreads[i].complete()

    def settle(self, done=()):
        for i, piece in enumerate(self.spreads):
            if i not in done:
                piece.complete()
            piece.sent_all()
        for piece, _, _ in self.scatters:
            for d in range(self.n):
                piece.arrived(d)
            piece.scatter_sent()


def parts(n, first, last):
    return range(first * n // 4, last * n // 4)


def moves(what, piece, places):
    return [(what, piece, d) for d in places]


def weights_kernel(
    n, nf, units, share, layers,
    qkv, output, gate_up, down, *refs,
):
    place = Place(n)
    rows, hidden = down.shape[1:]
    w_a, w_g, w_d = refs[:3]
    later = refs[3 : 3 * layers]
    a_first, g_first, d_first, raw_g, raw_d, cut_sems, raw_sems = refs[3 * layers : 3 * layers + 7]
    sems = refs[3 * layers + 7 :]
    a_blocks = [a_first] + list(later[: layers - 1])
    g_blocks = [g_first] + list(later[layers - 1 : 2 * layers - 2])
    d_blocks = [d_first] + list(later[2 * layers - 2 :])
    cuts = []
    for l in range(layers):
        for q in range(n):
            columns = pl.ds(q // share * VD, VD)
            for i in range(4):
                source = qkv.at[l, i, :, columns] if i < 3 else output.at[l, :, columns]
                target = a_blocks[l].at[q, :, pl.ds(i * VD, VD)]
                cuts.append(pltpu.make_async_copy(source, target, cut_sems.at[l, q, i]))
    for copy in cuts[: 4 * n]:
        copy.start()
    raws = []
    for l in range(layers):
        raws.append(pltpu.make_async_copy(gate_up.at[l], raw_g.at[l], raw_sems.at[l, 0]))
        raws.append(pltpu.make_async_copy(down.at[l], raw_d.at[l], raw_sems.at[l, 1]))
    for copy in raws:
        copy.start()
    attention, forward, back = (Spread(place, nf, w, rows) for w in (w_a, w_g, w_d))
    attention.use(*sems[2:8])
    forward.use(*sems[10:16])
    enter(place, nf, True)
    for copy in cuts[: 4 * n]:
        copy.wait()
    attention.scatter(a_first, *sems[:2])
    for copy in cuts[4 * n :]:
        copy.start()

    def fill(target, j, at, value):
        width = min(units, hidden - j * units)
        target[j, :, at : at + width] = value(pl.ds(j * units, width))
        if width < units:
            target[j, :, at + width : at + units] = jnp.zeros((rows, units - width), BF)

    def cut_gate_up(l):
        raws[2 * l].wait()
        for i in range(2):
            for j in range(n):
                fill(g_blocks[l], j, i * units, lambda at, i=i: raw_g[l, :, i, at])

    def cut_down(l):
        raws[2 * l + 1].wait()
        for j in range(n):
            fill(d_blocks[l], j, 0, lambda at: raw_d[l, :, at])

    cut_gate_up(0)
    for d in range(n):
        attention.arrived(d)
        attention.spread(d)
    forward.scatter(g_first, *sems[8:10])
    cut_down(0)
    back.scatter(d_first, *sems[16:18])
    for d in parts(n, 0, 1):
        attention.forward(d)
    for l in range(1, layers):
        cut_gate_up(l)
        cut_down(l)
    for copy in cuts[4 * n :]:
        copy.wait()
    for d in parts(n, 1, 3):
        attention.forward(d)
    for d in range(n):
        forward.arrived(d)
    for d in parts(n, 0, 1):
        forward.spread(d)
    for d in parts(n, 3, 4):
        attention.forward(d)
    attention.complete()
    forward.complete()
    attention.scatter_sent()
    attention.sent_all()
    forward.scatter_sent()
    forward.sent_all()
    for d in range(n):
        back.arrived(d)
    back.scatter_sent()


class Gather:
    def __init__(self, place, x, send_r, recv_r, send_l, recv_l, core_send, core_recv):
        self.place, self.x = place, x
        self.sems = (send_r, recv_r, send_l, recv_l, core_send, core_recv)
        self.to_right, self.to_left, self.across = [], [], []

    @staticmethod
    def semaphores(n):
        dma = pltpu.SemaphoreType.DMA
        return [dma((n // 2,))] * 4 + [dma((n,))] * 2

    def _pass_on(self, s):
        place, x = self.place, self.x
        send_r, recv_r, send_l, recv_l = self.sems[:4]
        rows, half, t = x.shape[2], place.n // 2, place.t
        top = rows // 2
        part_r = pl.ds(0, top) if s == half - 1 else pl.ds(0, rows)
        part_l = pl.ds(top, top) if s == half - 1 else pl.ds(0, rows)
        right_at = x.at[place.ring(-s)[0], t, part_r]
        left_at = x.at[place.ring(s)[0], t, part_l]
        self.to_right.append(remote(right_at, right_at, send_r.at[s], recv_r.at[s], place.ring(1)[1]))
        self.to_left.append(remote(left_at, left_at, send_l.at[s], recv_l.at[s], place.ring(-1)[1]))

    def _cross(self, q):
        core_send, core_recv = self.sems[4:]
        slot, at = len(self.across), self.x.at[q, self.place.t]
        other = {"tp": 1 - self.place.t}
        self.across.append(remote(at, at, core_send.at[slot], core_recv.at[slot], other))

    def begin(self):
        self._pass_on(0)
        self._cross(self.place.q)

    def chunks(self):
        place, half = self.place, self.place.n // 2
        self.across[0].wait_recv()
        yield place.q
        for s in range(half):
            self.to_right[s].wait_recv()
            self.to_left[s].wait_recv()
            arrived = [place.ring(half)[0]] if s == half - 1 else [place.ring(-s - 1)[0], place.ring(s + 1)[0]]
            if s < half - 1:
                self._pass_on(s + 1)
            first = len(self.across)
            for q in arrived:
                self._cross(q)
            for i, q in enumerate(arrived):
                self.across[first + i].wait_recv()
                yield q

    def finish(self):
        for copy in self.to_right + self.to_left + self.across:
            copy.wait_send()


def by_rows(count, body, step=16):
    def one(i, carry):
        body(pl.ds(pl.multiple_of(i * step, step), step))
        return carry

    lax.fori_loop(0, count // step, one, 0)


class Reduce:
    def __init__(self, place, p, from_core, in_r, in_l, send_r, recv_r, send_l, recv_l, core_send, core_recv):
        self.place, self.p, self.from_core, self.in_r, self.in_l = place, p, from_core, in_r, in_l
        self.sems = (send_r, recv_r, send_l, recv_l, core_send, core_recv)
        half = place.n // 2
        self.order = [half] + [k for j in range(half - 1, 0, -1) for k in (j, -j)] + [0]
        self.chips = {k: place.ring(k)[0] for k in self.order}
        self.across, self.to_right, self.to_left = {}, [], []

    @staticmethod
    def scratch(n, rows, width):
        dma = pltpu.SemaphoreType.DMA
        wide = [pltpu.VMEM((n, rows, width), BF)] + [pltpu.VMEM((n // 2, rows, width), BF)] * 2
        return wide + [dma((n // 2,))] * 4 + [dma((n,))] * 2

    def offer(self, k):
        core_send, core_recv = self.sems[4:]
        slot, q, t = len(self.across), self.chips[k], self.place.t
        self.across[k] = remote(
            self.p.at[q, 1 - t], self.from_core.at[q], core_send.at[slot], core_recv.at[slot], {"tp": 1 - t}
        )

    def _local(self, k, at):
        q = self.chips[k]
        return self.p[q, self.place.t, at].astype(F32) + self.from_core[q, at].astype(F32)

    def _add(self, k, start, count, extra=None):
        def body(at):
            whole = pl.ds(pl.multiple_of(start + at.start, 16), at.size)
            total = self._local(k, whole)
            if extra is not None:
                total = total + extra[whole].astype(F32)
            self.from_core[self.chips[k], whole] = total.astype(BF)

        by_rows(count, body)

    def far(self):
        send_r, recv_r, send_l, recv_l = self.sems[:4]
        place, half = self.place, self.place.n // 2
        rows = self.p.shape[2]
        top = rows // 2
        self.across[half].wait_recv()
        self._add(half, 0, rows)
        low, high = pl.ds(0, top), pl.ds(top, top)
        sums = self.from_core.at[self.chips[half]]
        right, left = place.ring(1)[1], place.ring(-1)[1]
        self.to_right.append(remote(sums.at[low], self.in_r.at[0, low], send_r.at[0], recv_r.at[0], right))
        self.to_left.append(remote(sums.at[high], self.in_l.at[0, high], send_l.at[0], recv_l.at[0], left))

    def near(self, s):
        send_r, recv_r, send_l, recv_l = self.sems[:4]
        place, k = self.place, self.place.n // 2 - s
        rows = self.p.shape[2]
        top = rows // 2
        self.across[k].wait_recv()
        self.across[-k].wait_recv()
        if s == 1:
            self._add(k, top, top)
            self._add(-k, 0, top)
        start = 0 if s == 1 else None
        self.to_right[-1].wait_recv()
        self._add(k, 0, top if s == 1 else rows, self.in_r.at[s - 1])
        self.to_right.append(
            remote(self.from_core.at[self.chips[k]], self.in_r.at[s], send_r.at[s], recv_r.at[s], place.ring(1)[1])
        )
        self.to_left[-1].wait_recv()
        self._add(-k, top if s == 1 else 0, top if s == 1 else rows, self.in_l.at[s - 1])
        self.to_left.append(
            remote(self.from_core.at[self.chips[-k]], self.in_l.at[s], send_l.at[s], recv_l.at[s], place.ring(-1)[1])
        )

    def end(self, use):
        half = self.place.n // 2
        self.across[0].wait_recv()
        self.to_right[-1].wait_recv()
        self.to_left[-1].wait_recv()

        def body(at):
            use(at, self._local(0, at) + self.in_r[half - 1, at].astype(F32) + self.in_l[half - 1, at].astype(F32))

        by_rows(self.p.shape[2], body)

    def finish(self):
        for copy in self.to_right + self.to_left + list(self.across.values()):
            copy.wait_send()

    def run(self, use, before=None):
        for k in self.order:
            self.offer(k)
        self.far()
        for s in range(1, self.place.n // 2):
            self.near(s)
        if before is not None:
            before()
        self.end(use)


def mm(a, b):
    return jnp.dot(a, b, preferred_element_type=F32)


def mm_t(a, b):
    return lax.dot_general(a, b, (((1,), (1,)), ((), ())), preferred_element_type=F32)


def t_mm(a, b):
    return lax.dot_general(a, b, (((0,), (0,)), ((), ())), preferred_element_type=F32)


def rms_scale(values):
    return lax.rsqrt(jnp.mean(values * values, axis=-1, keepdims=True) + EPSILON)


def norm_back(grad_normed, inputs, scale_rows, gain):
    unit = inputs * scale_rows
    scaled = grad_normed * gain
    return scale_rows * (scaled - unit * jnp.mean(scaled * unit, axis=-1, keepdims=True))


def tiles(count, width, body):
    def one(j, carry):
        body(pl.ds(pl.multiple_of(j * width, width), width))
        return carry

    lax.fori_loop(0, count // width, one, 0)


def tile_of(count):
    return 256 if count % 256 == 0 else 128


def turn(v, cosine, sine):
    return v * cosine + pltpu.roll(v, HD // 2, 1) * sine


def block_diagonal(out, parts, rank, width):
    out[...] = jnp.zeros(out.shape, out.dtype)
    for i in range(parts[1]):
        out[i * rank : (i + 1) * rank, i * width : (i + 1) * width] = parts[0][i * rank : (i + 1) * rank, :]


def write_norm(x_rows, source, gain):
    def body(at):
        v = source[at]
        x_rows[at] = (v * rms_scale(v) * gain[...]).astype(BF)

    by_rows(source.shape[0], body)


ROW_BLOCK = 128
KEY_STEP = 256


def row_blocks(tree, body):
    for j in range(tree // KEY_STEP):

        def one(i, carry, j=j):
            body(pl.ds(pl.multiple_of(j * KEY_STEP + i * ROW_BLOCK, ROW_BLOCK), ROW_BLOCK), (j + 1) * KEY_STEP)
            return carry

        lax.fori_loop(0, KEY_STEP // ROW_BLOCK, one, 0)


def seen(rows, keys, query_bits, key_bits):
    shared = (query_bits[rows] & key_bits[:, :keys]) != 0
    i = rows.start + lax.broadcasted_iota(jnp.int32, (ROW_BLOCK, keys), 0)
    j = lax.broadcasted_iota(jnp.int32, (ROW_BLOCK, keys), 1)
    return shared & (j <= i)


def attention_forward(
    n, nf, layer, part, rank, plan,
    residual, gain, w_hbm, a_model, a_head, cosine, sine, query_bits, key_bits, lam, *refs,
):
    jobs, refs = plan.split(refs)
    (middle, x_hbm, queries, keys, values, small, log_total, mixed, headed, side,
     x, p, w, raised, copy_sems, *sems) = refs
    place = Place(n)
    chip_rows, width = 2 * x_hbm.shape[2], x_hbm.shape[3]
    tree = n * chip_rows
    load = pltpu.make_async_copy(w_hbm, w, copy_sems.at[0])
    load.start()
    gather, reduce = Gather(place, x, *sems[:6]), Reduce(place, p, *sems[6:])
    write_norm(x.at[place.q, place.t], residual, gain)
    block_diagonal(raised, (a_head[rank : 4 * rank], 3), rank, VD)
    work = plan.work(place, nf, jobs)
    enter(place, nf, bool(plan.scatters))
    gather.begin()
    work.at(0)
    load.wait()

    def project(q):
        rows = pl.ds(pl.multiple_of(q * chip_rows, chip_rows), chip_rows)
        v = x[q].reshape(chip_rows, width)
        low = mm_t(v, a_model[: 3 * rank]).astype(BF)
        small[rows] = low
        for i, out in enumerate((queries, keys, values)):
            at = slice(i * VD, (i + 1) * VD)
            made = mm(v, w[:, at]) + ADAPTER_SCALE * mm(low, raised[:, at])
            if i < 2:
                for c in range(2):
                    half = slice(c * HD, (c + 1) * HD)
                    out[rows, half] = turn(made[:, half], cosine[rows], sine[rows]).astype(BF)
            else:
                out[rows] = made.astype(BF)

    for q in gather.chunks():
        project(q)
    work.at(1)
    keep = pltpu.make_async_copy(x, x_hbm, copy_sems.at[1])
    keep.start()
    score_scale = HD ** (-0.5)
    weight = lam[...]

    def attend(rows, count):
        visible = seen(rows, count, query_bits, key_bits)
        both = []
        for c in range(2):
            at = slice(c * HD, (c + 1) * HD)
            scores = mm_t(queries[rows, at], keys[:count, at]) * score_scale
            scores = jnp.where(visible, scores, NEGATIVE_BIG)
            top = jnp.max(scores, axis=-1, keepdims=True)
            raw = jnp.exp(scores - top)
            total = jnp.sum(raw, axis=-1, keepdims=True)
            log_total[rows, c : c + 1] = top + jnp.log(total)
            both.append(raw * (1.0 / total))
        mix = mm((both[0] - weight * both[1]).astype(BF), values[:count])
        mixed[rows] = mix.astype(BF)
        head = (mix * rms_scale(mix) * keep_factor(layer)).astype(BF)
        headed[rows] = head
        side[rows] = mm_t(head, a_head[:rank]).astype(BF)

    row_blocks(tree, attend)
    work.at(2)

    for k in reduce.order:
        q = reduce.chips[k]
        rows = pl.ds(pl.multiple_of(q * chip_rows, chip_rows), chip_rows)
        head, low = headed[rows], side[rows]

        def out_tile(at):
            made = mm_t(head, w[at, 3 * VD :]) + ADAPTER_SCALE * mm(low, a_model[9 * rank : 10 * rank, at])
            p[q, :, :, at] = (made * part).astype(BF).reshape(2, chip_rows // 2, at.size)

        tiles(width, 512, out_tile)
        reduce.offer(k)
        if k == reduce.order[2]:
            reduce.far()
    work.at(3)
    for s in range(1, n // 2):
        reduce.near(s)
    work.at(4)

    def use(at, total):
        middle[at] = residual[at] + total

    reduce.end(use)
    work.at(5)
    keep.wait()
    gather.finish()
    reduce.finish()
    work.settle()


def ffn_forward(
    n, nf, units, rank, plan,
    residual, gain, w_hbm, a_model, e_model, *refs,
):
    jobs, refs = plan.split(refs)
    (following, x_hbm, gates, ups, hidden, small, side,
     x, p, w, raised, copy_sems, *sems) = refs
    place = Place(n)
    chip_rows, width = 2 * x_hbm.shape[2], x_hbm.shape[3]
    tree = n * chip_rows
    load = pltpu.make_async_copy(w_hbm, w.at[:, pl.ds(0, 2 * units)], copy_sems.at[0])
    load.start()
    gather, reduce = Gather(place, x, *sems[:6]), Reduce(place, p, *sems[6:])
    write_norm(x.at[place.q, place.t], residual, gain)
    block_diagonal(raised, (e_model, 2), rank, units)
    work = plan.work(place, nf, jobs)
    enter(place, nf, bool(plan.scatters))
    gather.begin()
    work.at(0)
    load.wait()
    step = tile_of(units)

    for number, q in enumerate(gather.chunks()):
        if number == n - 1:
            work.at(1)
        rows = pl.ds(pl.multiple_of(q * chip_rows, chip_rows), chip_rows)
        v = x[q].reshape(chip_rows, width)
        low = mm_t(v, a_model[4 * rank : 6 * rank]).astype(BF)
        small[rows] = low

        def unit_tile(at):
            up_at = pl.ds(pl.multiple_of(units + at.start, step), step)
            gate = mm(v, w[:, at]) + ADAPTER_SCALE * mm(low, raised[:, at])
            up = mm(v, w[:, up_at]) + ADAPTER_SCALE * mm(low, raised[:, up_at])
            gates[rows, at] = gate.astype(BF)
            ups[rows, at] = up.astype(BF)
            hidden[rows, at] = (gate / (1.0 + jnp.exp(-gate)) * up).astype(BF)

        tiles(units, step, unit_tile)

    work.at(2)
    keep = pltpu.make_async_copy(x, x_hbm, copy_sems.at[1])
    keep.start()

    work.complete(0)
    load = pltpu.make_async_copy(plan.late(jobs), w.at[:, pl.ds(2 * units, units)], copy_sems.at[0])
    load.start()
    load.wait()
    for k in reduce.order:
        q = reduce.chips[k]
        rows = pl.ds(pl.multiple_of(q * chip_rows, chip_rows), chip_rows)
        made_hidden = hidden[rows]
        low = mm_t(made_hidden, e_model[2 * rank : 3 * rank]).astype(BF)
        side[rows] = low

        def out_tile(at):
            made = mm_t(made_hidden, w[at, 2 * units :])
            made = made + ADAPTER_SCALE * mm(low, a_model[10 * rank : 11 * rank, at])
            p[q, :, :, at] = made.astype(BF).reshape(2, chip_rows // 2, at.size)

        tiles(width, 512, out_tile)
        reduce.offer(k)
        if k == reduce.order[2]:
            reduce.far()
    work.at(3)
    for s in range(1, n // 2):
        reduce.near(s)
    work.at(4)

    def use(at, total):
        following[at] = residual[at] + total

    reduce.end(use)
    work.at(5)
    keep.wait()
    gather.finish()
    reduce.finish()
    work.settle((0,))


def ffn_backward(
    n, units, rank, carry,
    grad, middle, gain, w_hbm, w_down_hbm, a_model, e_model, x_hbm, gates, ups, hidden, small, side, *refs,
):
    if carry:
        final, final_out, *refs = refs
        *refs, final_rows, home_send, home_recv = refs
    (grad_out, grad_up_down, grad_in, grad_units,
     x, p, w, kept, dgu, dsmall, dside, raised, copy_sems, *sems) = refs
    place = Place(n)
    chip_rows, width = 2 * x_hbm.shape[2], x_hbm.shape[3]
    tree = n * chip_rows
    load = pltpu.make_async_copy(w_hbm, w.at[:, pl.ds(0, 2 * units)], copy_sems.at[0])
    load.start()
    load_down = pltpu.make_async_copy(w_down_hbm, w.at[:, pl.ds(2 * units, units)], copy_sems.at[2])
    load_down.start()
    fetch = pltpu.make_async_copy(x_hbm, kept, copy_sems.at[1])
    fetch.start()
    gather, reduce = Gather(place, x, *sems[:6]), Reduce(place, p, *sems[6:])

    def own(at):
        x[place.q, place.t, at] = grad[at].astype(BF)

    by_rows(grad.shape[0], own)
    block_diagonal(raised, (e_model, 2), rank, units)
    if carry:

        def last_rows(at):
            final_rows[at] = final[at].astype(BF)

        by_rows(final.shape[0], last_rows)
    enter(place, home=carry)
    gather.begin()
    if carry:
        home = Home(place, final_out, home_send, home_recv)
        home.start(final_rows)
    load.wait()
    load_down.wait()
    step = tile_of(units)

    for q in gather.chunks():
        rows = pl.ds(pl.multiple_of(q * chip_rows, chip_rows), chip_rows)
        v = x[q].reshape(chip_rows, width)
        low = (ADAPTER_SCALE * mm_t(v, a_model[10 * rank : 11 * rank])).astype(BF)
        dside[rows] = low

        def unit_tile(at):
            up_at = pl.ds(pl.multiple_of(units + at.start, step), step)
            down_at = pl.ds(pl.multiple_of(2 * units + at.start, step), step)
            dhidden = mm(v, w[:, down_at]) + mm(low, e_model[2 * rank : 3 * rank, at])
            gate, up = gates[rows, at].astype(F32), ups[rows, at].astype(F32)
            sig = 1.0 / (1.0 + jnp.exp(-gate))
            dgu[rows, at] = (dhidden * up * sig * (1.0 + gate * (1.0 - sig))).astype(BF)
            dgu[rows, up_at] = (dhidden * gate * sig).astype(BF)

        tiles(units, step, unit_tile)
        back = dgu[rows]
        low_back = (ADAPTER_SCALE * mm_t(back, raised[...])).astype(BF)
        dsmall[rows] = low_back

        def out_tile(at):
            made = mm_t(back, w[at, : 2 * units]) + mm(low_back, a_model[4 * rank : 6 * rank, at])
            p[q, :, :, at] = made.astype(BF).reshape(2, chip_rows // 2, at.size)

        tiles(width, 512, out_tile)

    def use(at, total):
        inputs = middle[at]
        grad_out[at] = grad[at] + norm_back(total, inputs, rms_scale(inputs), gain[...])

    def adapters():
        fetch.wait()

        def model_tile(at):
            flat = x[:, :, :, at].reshape(tree, at.size)
            grad_up_down[:, at] = (ADAPTER_SCALE * t_mm(side[...], flat)).astype(BF)
            flat = kept[:, :, :, at].reshape(tree, at.size)
            grad_in[:, at] = t_mm(dsmall[...], flat).astype(BF)

        tiles(width, 256, model_tile)

        def unit_tile(at):
            up_at = pl.ds(pl.multiple_of(units + at.start, step), step)
            grad_units[:rank, at] = (ADAPTER_SCALE * t_mm(small[...], dgu[:, at])[:rank]).astype(BF)
            grad_units[rank : 2 * rank, at] = (ADAPTER_SCALE * t_mm(small[...], dgu[:, up_at])[rank:]).astype(BF)
            grad_units[2 * rank : 3 * rank, at] = t_mm(dside[...], hidden[:, at]).astype(BF)
            grad_units[3 * rank :, at] = jnp.zeros((rank, at.size), BF)

        tiles(units, step, unit_tile)

    reduce.run(use, adapters)
    gather.finish()
    reduce.finish()
    if carry:
        home.land()
        home.finish()


def attention_backward(
    n, layer, share, heads_tp, rank,
    grad, residual, gain, w_hbm, a_model, a_head, cosine, sine, query_bits, key_bits, lam,
    x_hbm, queries, keys, values, small, log_total, mixed, headed, side,
    grad_up_down, grad_ffn_in, grad_units,
    grad_out, own_sum, all_units,
    x, p, w, dmixed, dq, dk, dv, dprojected, dsmall, dside, raised, grad_a9, p_own, copy_sems, *sems,
):
    place = Place(n)
    part = 1.0 / share
    chip_rows, width = 2 * x_hbm.shape[2], x_hbm.shape[3]
    tree = n * chip_rows
    load = pltpu.make_async_copy(w_hbm, w, copy_sems.at[0])
    load.start()
    gather, reduce = Gather(place, x, *sems[:6]), Reduce(place, p, *sems[6:15])
    gather_units, reduce_own = Gather(place, all_units, *sems[15:21]), Reduce(place, p_own, *sems[21:])

    def own(at):
        x[place.q, place.t, at] = grad[at].astype(BF)

    by_rows(grad.shape[0], own)
    block_diagonal(raised, (a_head[rank : 4 * rank], 3), rank, VD)
    all_units[place.q, place.t] = grad_units[...]
    enter(place)
    gather.begin()
    gather_units.begin()
    dk[...] = jnp.zeros(dk.shape, F32)
    dv[...] = jnp.zeros(dv.shape, F32)
    load.wait()

    for q in gather.chunks():
        rows = pl.ds(pl.multiple_of(q * chip_rows, chip_rows), chip_rows)
        v = x[q].reshape(chip_rows, width)
        low = (ADAPTER_SCALE * mm_t(v, a_model[9 * rank : 10 * rank])).astype(BF)
        dside[rows] = low
        dheaded = mm(v, w[:, 3 * VD :]) + mm(low, a_head[:rank])
        inputs = mixed[rows].astype(F32)
        dmixed[rows] = norm_back(dheaded, inputs, rms_scale(inputs), keep_factor(layer)).astype(BF)

    def out_gradient(at):
        flat = x[:, :, :, at].reshape(tree, at.size)
        grad_a9[:, at] = (ADAPTER_SCALE * part * t_mm(side[...], flat)).astype(BF)

    tiles(width, 256, out_gradient)
    gather.finish()
    fetch = pltpu.make_async_copy(x_hbm, x, copy_sems.at[1])
    fetch.start()
    score_scale = HD ** (-0.5)
    weight = lam[...]

    def attend(rows, count):
        visible = seen(rows, count, query_bits, key_bits)
        dmix = dmixed[rows]
        dweights = mm_t(dmix, values[:count])
        both = []
        for c in range(2):
            at = slice(c * HD, (c + 1) * HD)
            scores = mm_t(queries[rows, at], keys[:count, at]) * score_scale
            probability = jnp.exp(jnp.where(visible, scores - log_total[rows, c : c + 1], NEGATIVE_BIG))
            both.append(probability)
            weighted = probability * dweights
            dscores = weighted - probability * jnp.sum(weighted, axis=-1, keepdims=True)
            dscores = (dscores * -weight if c else dscores).astype(BF)
            dq[rows, at] = mm(dscores, keys[:count, at])
            dk[:count, at] += t_mm(dscores, queries[rows, at])
        dv[:count] += t_mm((both[0] - weight * both[1]).astype(BF), dmix)

    row_blocks(tree, attend)

    fetch.wait()
    for _ in gather_units.chunks():
        pass

    def project(i, carry):
        rows = pl.ds(pl.multiple_of(i * chip_rows, chip_rows), chip_rows)
        for j, source in enumerate((dq, dk)):
            for c in range(2):
                half = slice(c * HD, (c + 1) * HD)
                turned = turn(source[rows, half] * score_scale, cosine[rows], -sine[rows])
                dprojected[rows, j * VD + c * HD : j * VD + (c + 1) * HD] = turned.astype(BF)
        dprojected[rows, 2 * VD :] = dv[rows].astype(BF)
        dsmall[rows] = (ADAPTER_SCALE * mm_t(dprojected[rows], raised[...])).astype(BF)
        return carry

    lax.fori_loop(0, n, project, 0)

    def send_part(k):
        q = reduce.chips[k]
        rows = pl.ds(pl.multiple_of(q * chip_rows, chip_rows), chip_rows)
        back, low_back = dprojected[rows], dsmall[rows]

        def out_tile(at):
            made = mm_t(back, w[at, : 3 * VD]) + mm(low_back, a_model[: 3 * rank, at])
            p[q, :, :, at] = (made * part).astype(BF).reshape(2, chip_rows // 2, at.size)

        tiles(width, 512, out_tile)
        reduce.offer(k)

    for k in reduce.order[:3]:
        send_part(k)
    reduce.far()

    block = width // (2 * n)

    def full_tile(jp, carry):
        at = pl.ds(pl.multiple_of(jp * block, block), block)
        j = jp // 4 * 4 + jp % 2 * 2 + jp // 2 % 2
        q, t = j // 2, j % 2
        flat = x[:, :, :, at].reshape(tree, block)
        p_own[q, t, : 3 * rank] = (part * t_mm(dsmall[...], flat)).astype(BF)
        p_own[q, t, 4 * rank : 6 * rank] = grad_ffn_in[:, at]
        p_own[q, t, 9 * rank : 10 * rank] = grad_a9[:, at]
        p_own[q, t, 10 * rank : 11 * rank] = grad_up_down[:, at]
        p_own[q, t, 11 * rank :] = jnp.zeros((rank, block), BF)
        return carry

    lax.fori_loop(0, 2 * n, full_tile, 0)
    of_head = [part * t_mm(dside[...], headed[...])]
    for i in range(3):
        made = t_mm(small[...], dprojected[:, i * VD : (i + 1) * VD])[i * rank : (i + 1) * rank]
        of_head.append(ADAPTER_SCALE * part * made)
    head = place.t * heads_tp + place.q // share
    for j in range(2 * n):
        start = j * block % VD
        own = (head == j * block // VD).astype(F32)
        for i, k in enumerate((3, 6, 7, 8)):
            made = of_head[i][:, start : start + block] * own
            p_own[j // 2, j % 2, k * rank : (k + 1) * rank] = made.astype(BF)

    for k in reduce.order[3:]:
        send_part(k)
    for k in reduce.order:
        reduce_own.offer(k)
    reduce_own.far()
    for s in range(1, n // 2):
        reduce.near(s)
        reduce_own.near(s)

    def use_own(at, total):
        own_sum[at] = total.astype(BF)

    def use(at, total):
        inputs = residual[at]
        grad_out[at] = grad[at] + norm_back(total, inputs, rms_scale(inputs), gain[...])

    reduce.end(use)
    reduce_own.end(use_own)
    gather_units.finish()
    reduce.finish()
    reduce_own.finish()


def finish_kernel(
    n, nf, layers, rank,
    grad, own_sums, own_units, slot,
    tokens_grad, model_grad, hidden_grad,
    rows_out, landed, sent_sums, all_sums, all_units, home_send, home_recv, tree_send, tree_recv,
):
    place = Place(n)
    own = model_grad.shape[2]
    tall = own_sums.shape[0]

    def cut(at):
        rows_out[at] = grad[at].astype(BF)

    by_rows(grad.shape[0], cut)
    sent_sums[...] = own_sums[...]
    sent_sums[tall - rank :] = jnp.broadcast_to(slot[...], (rank, own_sums.shape[1])).astype(BF)
    enter(place, home=True, ring=False, trees=nf)
    moves = [Home(place, landed, home_send.at[0], home_recv.at[0])]
    moves[0].start(rows_out)
    away = {}
    for i, (source, target) in enumerate(((sent_sums, all_sums), (own_units, all_units))):
        away[i] = TreeMove(place, source, target, home_send.at[i + 1], home_recv.at[i + 1])
        away[i].start()
    copies = []
    for i in range(2):
        away[i].land()
        slot_of = away[i].slot
        for e in range(1, nf):
            copies.append(
                remote(slot_of, slot_of, tree_send.at[i, e], tree_recv.at[i, e], {"fsdp": flip(place.f, e)})
            )
    moves[0].land()
    for copy in copies:
        copy.wait_recv()
    block, units = all_sums.shape[2], all_units.shape[2]
    per_layer = tall // layers
    for b in range(own):
        number = (place.f * own + b).astype(F32)
        keeps = [
            (all_sums[f, tall - rank : tall - rank + 1, :1].astype(F32) == number).astype(F32) for f in range(nf)
        ]
        for l in range(layers):
            for k in range(11):
                at = slice(l * per_layer + k * rank, l * per_layer + (k + 1) * rank)
                model_grad[l, k, b] = sum(keeps[f] * all_sums[f, at].astype(F32) for f in range(nf))
            for k in range(3):
                at = slice((l * 3 + k) * rank, (l * 3 + k + 1) * rank)
                hidden_grad[l, k, b] = sum(keeps[f] * all_units[f, at].astype(F32) for f in range(nf))
    moves[0].finish()
    for core in range(2):

        def widen(at, core=core):
            rows = landed.shape[1]
            tokens_grad[pl.ds(pl.multiple_of(core * rows + at.start, 16), at.size)] = landed[core, at].astype(F32)

        by_rows(landed.shape[1], widen)
    for copy in copies:
        copy.wait_send()


class Plan:
    def __init__(self, n, nf, rows, scatters, spreads, schedule):
        self.n, self.nf, self.rows, self.schedule = n, nf, rows, schedule
        self.scatters, self.spreads = scatters, spreads

    def ins(self):
        return [(blocks, True) for blocks, _ in self.scatters] + [(w, True) for w in self.spreads]

    def outs(self):
        made = [(shape, BF, True) for _, shape in self.scatters]
        return made + [(w.shape, BF, True) for w in self.spreads]

    def semaphores(self):
        made = Spread.scatter_semaphores(self.n) * len(self.scatters)
        return made + Spread.spread_semaphores(self.n, self.nf) * len(self.spreads)

    def split(self, refs):
        a, b = len(self.scatters), len(self.spreads)
        count = 2 * a + 6 * b
        refs = list(refs)
        taken = refs[: a + b], refs[a + b : 2 * (a + b)], refs[len(refs) - count :]
        return taken, refs[2 * (a + b) : len(refs) - count]

    def work(self, place, nf, jobs):
        a, b = len(self.scatters), len(self.spreads)
        ins, outs, sems = jobs
        scatters = [(ins[i], outs[i], sems[2 * i : 2 * i + 2]) for i in range(a)]
        spreads = [(outs[a + i], sems[2 * a + 6 * i : 2 * a + 6 * i + 6]) for i in range(b)]
        return Work(place, nf, self.rows, scatters, spreads, self.schedule)

    def late(self, jobs):
        return jobs[1][len(self.scatters)]


def call(kernel, collective, ins, outs, scratch, plan=None):
    spec = lambda hbm: pl.BlockSpec(memory_space=pl.ANY if hbm else pltpu.VMEM)
    aliases = {}
    if plan is not None:
        first_in, count = len(ins), len(plan.scatters)
        aliases = {first_in + count + i: count + i for i in range(len(plan.spreads))}
        ins, outs, scratch = ins + plan.ins(), plan.outs() + outs, scratch + plan.semaphores()
    made = pl.pallas_call(
        kernel,
        out_shape=[jax.ShapeDtypeStruct(shape, kind) for shape, kind, _ in outs],
        in_specs=[spec(hbm) for _, hbm in ins],
        out_specs=[spec(hbm) for _, _, hbm in outs],
        scratch_shapes=scratch,
        input_output_aliases=aliases,
        compiler_params=pltpu.CompilerParams(
            collective_id=collective, has_side_effects=True, vmem_limit_bytes=62 << 20
        ),
    )(*[array for array, _ in ins])
    return list(made)


def line_bits(parent_row, seg):
    number = jnp.arange(NSEG)
    one = lambda x: lax.shift_left(jnp.ones_like(x), x)
    grand = jnp.sum(jnp.where(parent_row[:, None] == number[None, :], parent_row[None, :], 0), axis=1)
    line = one(number) | one(parent_row) | one(grand)
    mine = jnp.sum(jnp.where(seg[:, None] == number[None, :], line[None, :], 0), axis=1)
    return mine, one(seg)


def keep_factor(layer):
    return 0.2 + 0.6 * math.exp(-0.3 * layer)


def chips_of(nf, nc):
    h = nc // 2
    for f in range(nf):
        for c in range(nc):
            yield f * nc + c, (f // 2, f % 2, c // h, c % h)


def permute(x, nf, nc, target):
    h = nc // 2
    pairs = []
    for source, spot in chips_of(nf, nc):
        f_hi, f_lo, c_hi, c_lo = target(*spot)
        pairs.append((source, (f_hi * 2 + f_lo) * nc + c_hi * h + c_lo))
    return lax.ppermute(x, ("fsdp", "ctx"), pairs)


def swap_trees(x, nf, nc):
    return permute(x, nf, nc, lambda f_hi, f_lo, c_hi, c_lo: (f_hi, c_hi, f_lo, c_lo))


def shards(
    nf,
    nc,
    tokens,
    cotangent,
    segments,
    depths,
    parents,
    tree_adapter_index,
    layer_norm_gains,
    difference_lambda,
    query_key_value_weight,
    output_weight,
    gate_up_weight,
    down_weight,
    adapter_model_factors,
    adapter_hidden_factors,
):
    n = nc
    place = Place(n)
    q, t = place.q, place.t
    tokens_dev, width = tokens.shape
    rows = tokens_dev // 2
    tree = tokens_dev * n
    layers, weight_rows = query_key_value_weight.shape[:2]
    heads_tp = difference_lambda.shape[1]
    share = max(1, n // heads_tp)
    head = q // share
    hidden_tp = down_weight.shape[2]
    units = (hidden_tp + n * 128 - 1) // (n * 128) * 128
    rank, adapters = adapter_model_factors.shape[3], adapter_model_factors.shape[2]
    h = n // 2

    def swap_columns(x):
        lead = x.shape[:-1]
        cut = x.reshape(lead + (nf // 2, 2, 2, h * weight_rows))
        return jnp.swapaxes(cut, -3, -2).reshape(lead + (width,))

    of_tree = lax.all_gather(jnp.stack([segments, depths]), "ctx", axis=1, tiled=True)
    notes = jnp.concatenate([of_tree[0], of_tree[1], parents[0], tree_adapter_index])
    notes = swap_trees(notes, nf, nc)
    seg, dep = notes[:tree], notes[tree : 2 * tree]
    parent_row, slot = notes[2 * tree : 2 * tree + NSEG], notes[2 * tree + NSEG]
    own_tokens = lax.dynamic_slice_in_dim(tokens, t * rows, rows, 0)
    own_cotangent = lax.dynamic_slice_in_dim(cotangent, t * rows, rows, 0)
    residual = swap_columns(swap_trees(own_tokens, nf, nc)).astype(F32)
    own_cotangent = swap_columns(swap_trees(own_cotangent, nf, nc))

    query_bits, key_bits = line_bits(parent_row, seg)
    query_bits, key_bits = query_bits[:, None], key_bits[None, :]
    frequency = 10000.0 ** (-jnp.arange(HD // 2).astype(F32) / (HD // 2))
    angles = dep.astype(F32)[:, None] * frequency[None, :]
    cosine, sine = jnp.cos(angles), jnp.sin(angles)
    cosine = jnp.concatenate([cosine, cosine], axis=1)
    sine = jnp.concatenate([-sine, sine], axis=1)
    gains = swap_columns(layer_norm_gains)

    a_all = lax.dynamic_index_in_dim(adapter_model_factors, slot, 2, keepdims=False)
    e_all = lax.dynamic_index_in_dim(adapter_hidden_factors, slot, 2, keepdims=False)
    a_model = swap_columns(a_all).reshape(layers, 11 * rank, width)
    e_all = e_all.reshape(layers, 3 * rank, -1)
    head_at = (t * heads_tp + head) * VD

    heads_of = lax.dynamic_slice_in_dim(a_all, head_at, VD, 3)
    a_head = jnp.concatenate([heads_of[:, 3:4], heads_of[:, 6:9]], axis=1).reshape(layers, 4 * rank, VD)

    def unit_columns(x):
        x = lax.dynamic_slice_in_dim(x, t * hidden_tp, hidden_tp, x.ndim - 1)
        x = jnp.pad(x, ((0, 0),) * (x.ndim - 1) + ((0, n * units - hidden_tp),))
        return lax.dynamic_slice_in_dim(x, q * units, units, x.ndim - 1)

    e_model = unit_columns(e_all)

    part = 1.0 / share
    vmem = lambda *spec: pltpu.VMEM(*spec)
    calls = [0]
    whole_x = ((n, 2, rows, width), BF)
    sems = Gather.semaphores(n) + Reduce.scratch(n, rows, width)
    pair = pltpu.SemaphoreType.DMA((3,))
    big = [vmem(*whole_x), vmem(*whole_x)]

    def run(kernel, ins, outs, scratch, plan=None):
        calls[0] += 1
        return call(kernel, calls[0], ins, outs, scratch, plan)

    near = lambda *arrays: [(array, False) for array in arrays]
    far = lambda *arrays: [(array, True) for array in arrays]
    out = lambda shape, kind, hbm=False: (shape, kind, hbm)

    dma = pltpu.SemaphoreType.DMA
    c_a, c_g, c_d = 4 * VD, 2 * units, units
    tall = nf * n * weight_rows
    cut = lambda columns: out((n, weight_rows, columns), BF)
    calls[0] += 1
    made = call(
        functools.partial(weights_kernel, n, nf, units, share, layers),
        calls[0],
        far(jnp.transpose(query_key_value_weight, (0, 2, 1, 3)), output_weight, gate_up_weight, down_weight),
        [out((tall, c_a), BF, True), out((tall, c_g), BF, True), out((tall, c_d), BF, True)]
        + ([cut(c_a)] + [cut(c_g)] + [cut(c_d)]) * (layers - 1),
        [
            vmem((n, weight_rows, c_a), BF),
            vmem((n, weight_rows, c_g), BF),
            vmem((n, weight_rows, c_d), BF),
            vmem((layers, weight_rows, 2, hidden_tp), BF),
            vmem((layers, weight_rows, hidden_tp), BF),
            dma((layers, n, 4)),
            dma((layers, 2)),
        ]
        + (Spread.scatter_semaphores(n) + Spread.spread_semaphores(n, nf)) * 2
        + Spread.scatter_semaphores(n),
    )
    w_a, w_g, w_d = [made[0]], [made[1]], [made[2]]
    a_blocks = [None] + made[3 : 2 + layers]
    g_blocks = [None] + made[2 + layers : 1 + 2 * layers]
    d_blocks = [None] + made[1 + 2 * layers :]

    def plan_of(scatters, spreads, *schedule):
        return Plan(n, nf, weight_rows, scatters, spreads, schedule)

    saved = []
    for l in range(layers):
        last = l == layers - 1
        w_attention = w_a[l]
        lam = lax.dynamic_slice_in_dim(difference_lambda[l], head, 1).reshape(1, 1)
        gain_a, gain_f = gains[l, 0:1], gains[l, 1:2]
        shared = (a_model[l], a_head[l], cosine, sine, query_bits, key_bits, lam)
        plan = plan_of(
            [] if last else [(a_blocks[l + 1], (tall, c_a)), (g_blocks[l + 1], (tall, c_g))],
            [w_g[l], w_d[l]],
            moves("forward", 0, parts(n, 0, 1)) + moves("spread", 0, parts(n, 1, 4)),
            moves("forward", 0, parts(n, 1, 2)) + ([] if last else [("scatter", 0)]),
            moves("spread", 1, parts(n, 0, 2)) + moves("forward", 0, parts(n, 2, 3)),
            moves("forward", 0, parts(n, 3, 4)) + ([] if last else [("scatter", 1)]),
        )
        got = run(
            functools.partial(attention_forward, n, nf, l, part, rank, plan),
            near(residual, gain_a) + far(w_attention) + near(*shared),
            [
                out((rows, width), F32),
                out(*whole_x, True),
                out((tree, VD), BF),
                out((tree, VD), BF),
                out((tree, VD), BF),
                out((tree, 3 * rank), BF),
                out((tree, 2), F32),
                out((tree, VD), BF),
                out((tree, VD), BF),
                out((tree, rank), BF),
            ],
            big + [vmem((width, 4 * VD), BF), vmem((3 * rank, 3 * VD), BF), pair] + sems,
            plan,
        )
        if not last:
            w_a.append(got[0])
            w_g.append(got[1])
            got = got[2:]
        w_g[l], w_d[l], middle, *kept = got
        plan = plan_of(
            [] if last else [(d_blocks[l + 1], (tall, c_d))],
            [w_d[l]] + ([] if last else [w_a[l + 1], w_g[l + 1]]),
            moves("forward", 0, parts(n, 0, 2)) + moves("spread", 0, parts(n, 2, 4)),
            moves("forward", 0, parts(n, 2, 3)),
            moves("forward", 0, parts(n, 3, 4)) + ([] if last else moves("spread", 1, parts(n, 0, 4)) + [("scatter", 0)]),
            [] if last else moves("forward", 1, parts(n, 0, 1)),
            [] if last else moves("forward", 1, parts(n, 1, 2)) + moves("spread", 2, parts(n, 0, 1)),
            [] if last else moves("forward", 1, parts(n, 2, 4)),
        )
        ffn = run(
            functools.partial(ffn_forward, n, nf, units, rank, plan),
            near(middle, gain_f) + far(w_g[l]) + near(a_model[l], e_model[l]),
            [
                out((rows, width), F32),
                out(*whole_x, True),
                out((tree, units), BF),
                out((tree, units), BF),
                out((tree, units), BF),
                out((tree, 2 * rank), BF),
                out((tree, rank), BF),
            ],
            big + [vmem((width, 3 * units), BF), vmem((2 * rank, 2 * units), BF), pair] + sems,
            plan,
        )
        if not last:
            w_d.append(ffn[0])
            w_d[l], w_a[l + 1], w_g[l + 1], *ffn = ffn[1:]
        else:
            w_d[l], *ffn = ffn
        saved.append((residual, middle, gain_a, gain_f, shared, kept, ffn[1:]))
        residual = ffn[0]

    grad = own_cotangent.astype(F32)
    units_here, sums_here, block = [], [], width // (2 * n)
    for l in reversed(range(layers)):
        residual_in, middle, gain_a, gain_f, shared, kept, ffn = saved[l]
        carry = l == layers - 1
        made = run(
            functools.partial(ffn_backward, n, units, rank, carry),
            near(grad, middle, gain_f) + far(w_g[l], w_d[l]) + near(a_model[l], e_model[l]) + far(ffn[0]) + near(*ffn[1:])
            + (near(residual) if carry else []),
            ([out((2, rows, width), BF)] if carry else [])
            + [
                out((rows, width), F32),
                out((rank, width), BF),
                out((2 * rank, width), BF),
                out((4 * rank, units), BF),
            ],
            big
            + [
                vmem((width, 3 * units), BF),
                vmem(*whole_x),
                vmem((tree, 2 * units), BF),
                vmem((tree, 2 * rank), BF),
                vmem((tree, rank), BF),
                vmem((2 * rank, 2 * units), BF),
                pair,
            ]
            + sems
            + ([vmem((rows, width), BF)] + Home.semaphores() if carry else []),
        )
        if carry:
            outputs, *made = made
        grad, *ffn_grads = made
        grad, own_sum, all_units = run(
            functools.partial(attention_backward, n, l, share, heads_tp, rank),
            near(grad, residual_in, gain_a) + far(w_a[l]) + near(*shared) + far(kept[0]) + near(*kept[1:], *ffn_grads),
            [
                out((rows, width), F32),
                out((12 * rank, block), BF),
                out((n, 2, 4 * rank, units), BF),
            ],
            big
            + [
                vmem((width, 4 * VD), BF),
                vmem((tree, VD), BF),
                vmem((tree, VD), F32),
                vmem((tree, VD), F32),
                vmem((tree, VD), F32),
                vmem((tree, 3 * VD), BF),
                vmem((tree, 3 * rank), BF),
                vmem((tree, rank), BF),
                vmem((3 * rank, 3 * VD), BF),
                vmem((rank, width), BF),
                vmem((n, 2, 12 * rank, block), BF),
                pair,
            ]
            + sems
            + Gather.semaphores(n)
            + Reduce.scratch(n, 12 * rank, block),
        )

        number = (q * 2 + t) * (hidden_tp // n)
        half = lax.dynamic_index_in_dim(all_units, number // hidden_tp, 1, keepdims=False)
        flat = half[:, : 3 * rank].transpose(1, 0, 2).reshape(3 * rank, n * units)
        units_here.insert(0, lax.dynamic_slice_in_dim(flat, number % hidden_tp, hidden_tp // n, 1))
        sums_here.insert(0, own_sum)

    own = adapters // nf
    dma = pltpu.SemaphoreType.DMA
    wide = hidden_tp // n
    tokens_grad, grad_model, grad_hidden = run(
        functools.partial(finish_kernel, n, nf, layers, rank),
        near(grad, jnp.concatenate(sums_here), jnp.concatenate(units_here), slot.astype(F32).reshape(1, 1)),
        [
            out((2 * rows, width), F32),
            out((layers, 11, own, rank, block), F32),
            out((layers, 3, own, rank, wide), F32),
        ],
        [
            vmem((rows, width), BF),
            vmem((2, rows, width), BF),
            vmem((layers * 12 * rank, block), BF),
            vmem((nf, layers * 12 * rank, block), BF),
            vmem((nf, layers * 3 * rank, wide), BF),
            dma((3, 2)),
            dma((3, 2)),
            dma((2, nf)),
            dma((2, nf)),
        ],
    )
    return (
        swap_columns(outputs.reshape(2 * rows, width)),
        swap_columns(tokens_grad),
        grad_model,
        grad_hidden,
    )


def solution(mesh):
    in_specs = (
        P(("fsdp", "ctx"), None),
        P(("fsdp", "ctx"), None),
        P(("fsdp", "ctx")),
        P(("fsdp", "ctx")),
        P("fsdp", None),
        P("fsdp"),
        P(),
        P(None, "tp"),
        P(None, ("fsdp", "ctx"), None, "tp"),
        P(None, ("fsdp", "ctx"), "tp"),
        P(None, ("fsdp", "ctx"), None, "tp"),
        P(None, ("fsdp", "ctx"), "tp"),
        P(),
        P(),
    )
    out_specs = (
        P(("fsdp", "ctx"), None),
        P(("fsdp", "ctx"), None),
        P(None, None, "fsdp", None, ("ctx", "tp")),
        P(None, None, "fsdp", None, ("ctx", "tp")),
    )
    body = functools.partial(shards, mesh.shape["fsdp"], mesh.shape["ctx"])
    return jax.shard_map(body, mesh=mesh, in_specs=in_specs, out_specs=out_specs, check_vma=False)
```

```python
import functools
import math

import jax
import jax.numpy as jnp
from jax import lax
from jax.experimental import pallas as pl
from jax.experimental.pallas import tpu as pltpu
from jax.sharding import PartitionSpec as P

HD = 128
VD = 256
NSEG = 13
EPSILON = 1e-05
ADAPTER_SCALE = 0.5
NEGATIVE_BIG = -1e30
MESH = pl.DeviceIdType.MESH
BF = jnp.bfloat16
F32 = jnp.float32


class Place:
    def __init__(self, n):
        self.n, self.h = n, n // 2
        self.f, self.c, self.t = lax.axis_index("fsdp"), lax.axis_index("ctx"), lax.axis_index("tp")
        self.f_hi, self.f_lo = self.f // 2, self.f % 2
        self.c_hi, self.c_lo = self.c // self.h, self.c % self.h
        self.q = self.f_lo * self.h + self.c_lo
        self.away = self.f_lo + self.c_hi - 2 * self.f_lo * self.c_hi
        self.home = {"fsdp": self.f_hi * 2 + self.c_hi, "ctx": self.f_lo * self.h + self.c_lo}
        self.pos = self.f_lo * (n - 1) + (1 - 2 * self.f_lo) * self.c_lo

    def ring(self, k):
        n, h = self.n, self.h
        p = lax.rem(self.pos + k + 2 * n, n)
        low = p // h
        column = (1 - low) * p + low * (n - 1 - p)
        device = {"fsdp": self.f_hi * 2 + low, "ctx": self.c_hi * h + column}
        return low * h + column, device


def remote(src, dst, send, recv, device):
    copy = pltpu.make_async_remote_copy(
        src_ref=src, dst_ref=dst, send_sem=send, recv_sem=recv, device_id=device, device_id_type=MESH
    )
    copy.start()
    return copy


def when_even(place, body):
    even = place.pos % 2 == 0
    pl.when(even)(lambda: body(True))
    pl.when(jnp.logical_not(even))(lambda: body(False))


def flip(number, bits):
    b = 1
    while b <= bits:
        if bits & b:
            number = number + b * (1 - 2 * ((number // b) % 2))
        b *= 2
    return number


class Spread:
    def __init__(self, place, nf, w, rows):
        self.place, self.nf, self.w, self.rows = place, nf, w, rows
        self.g = place.f_hi * 2 + place.c_hi
        self.links = range(1, nf // 2)
        self.scattered, self.sent = [], []
        self.to_partner, self.along, self.onward, self.got = {}, {}, {}, []

    @staticmethod
    def scatter_semaphores(n):
        dma = pltpu.SemaphoreType.DMA
        return [dma((n,)), dma((n,))]

    @staticmethod
    def spread_semaphores(n, nf):
        dma = pltpu.SemaphoreType.DMA
        return [dma((n,))] * 2 + [dma((n, max(1, nf // 2 - 1)))] * 4

    def block(self, g, q):
        n, h = self.place.n, self.place.h
        source = (g // 2 * 2 + q // h) * n + g % 2 * h + q % h
        start = pl.multiple_of(source * self.rows, self.rows)
        return self.w.at[pl.ds(start, self.rows)]

    def chip(self, q):
        place = self.place
        return {"fsdp": place.f_hi * 2 + q // place.h, "ctx": place.c_hi * place.h + q % place.h}

    def partner(self):
        place = self.place
        return {"ctx": (1 - place.c_hi) * place.h + place.c_lo}

    def line(self, e):
        return {"fsdp": flip(self.place.f_hi, e) * 2 + self.place.f_lo}

    def scatter(self, blocks, send, recv):
        q = self.place.q
        own = self.block(self.g, q)
        copy = pltpu.make_async_copy(blocks.at[q], own, recv.at[0])
        copy.start()
        self.scattered.append(copy)
        for d in range(1, self.place.n):
            to = flip(q, d)
            self.scattered.append(remote(blocks.at[to], own, send.at[d], recv.at[d], self.chip(to)))

    def arrived(self, d):
        if d:
            self.scattered[d].wait_recv()
        else:
            self.scattered[0].wait()

    def scatter_sent(self):
        for copy in self.scattered[1:]:
            copy.wait_send()

    def use(self, *sems):
        self.sems = sems

    def spread(self, d):
        send_z, recv_z, send_y, recv_y = self.sems[:4]
        at = self.block(self.g, flip(self.place.q, d))
        self.to_partner[d] = remote(at, at, send_z.at[d], recv_z.at[d], self.partner())
        for e in self.links:
            self.along[d, e] = remote(at, at, send_y.at[d, e - 1], recv_y.at[d, e - 1], self.line(e))

    def landed(self, d):
        if d in self.to_partner and d not in self.got:
            self.to_partner[d].wait_recv()
            self.got.append(d)

    def forward(self, d):
        send, recv = self.sems[4:]
        self.landed(d)
        at = self.block(flip(self.g, 1), flip(self.place.q, d))
        for e in self.links:
            self.onward[d, e] = remote(at, at, send.at[d, e - 1], recv.at[d, e - 1], self.line(e))

    def complete(self):
        for d in list(self.to_partner):
            self.landed(d)
        for copy in list(self.along.values()) + list(self.onward.values()):
            copy.wait_recv()

    def sent_all(self):
        for copies in (self.to_partner, self.along, self.onward):
            for copy in copies.values():
                copy.wait_send()


def enter(place, nf=0, scatters=False, home=False, ring=True, trees=0):
    bar = pltpu.get_barrier_semaphore()
    devices = [{"tp": 1 - place.t}]
    guide = Spread(place, nf, None, 0)
    if scatters:
        devices += [guide.chip(flip(place.q, d)) for d in range(1, place.n)]
    elif ring:
        devices += [place.ring(1)[1], place.ring(-1)[1]]
    if nf:
        devices += [guide.partner()] + [guide.line(e) for e in guide.links]
    devices += [{"fsdp": flip(place.f, e)} for e in range(1, trees)]
    for device in devices:
        pl.semaphore_signal(bar, inc=1, device_id=device, device_id_type=MESH)
    count = len(devices)
    if home:

        @pl.when(place.away == 1)
        def greet():
            pl.semaphore_signal(bar, inc=1, device_id=place.home, device_id_type=MESH)

        count = count + place.away
    pl.semaphore_wait(bar, count)


class Home:
    def __init__(self, place, out, send, recv):
        self.place, self.out = place, out
        self.send, self.recv = send, recv

    @staticmethod
    def semaphores():
        dma = pltpu.SemaphoreType.DMA
        return [dma((2,)), dma((2,))]

    def start(self, rows):
        place, slot = self.place, self.out.at[self.place.t]
        far = pltpu.make_async_remote_copy(
            src_ref=rows, dst_ref=slot, send_sem=self.send.at[0], recv_sem=self.recv.at[0],
            device_id=place.home, device_id_type=MESH,
        )
        near = pltpu.make_async_copy(rows, slot, self.recv.at[0])
        self.far = far
        pl.when(place.away == 1)(far.start)
        pl.when(place.away == 0)(near.start)
        self.near = near

    def land(self, share=True):
        pl.when(self.place.away == 1)(self.far.wait)
        pl.when(self.place.away == 0)(self.near.wait)
        if share:
            slot = self.out.at[self.place.t]
            self.across = remote(slot, slot, self.send.at[1], self.recv.at[1], {"tp": 1 - self.place.t})

    def finish(self):
        self.across.wait()


class TreeMove(Home):
    def __init__(self, place, rows, out, send, recv):
        super().__init__(place, out, send, recv)
        self.rows = rows
        self.slot = out.at[place.f]

    def start(self):
        place = self.place
        target = self.out.at[place.f_hi * 2 + place.c_hi]
        self.far = pltpu.make_async_remote_copy(
            src_ref=self.rows, dst_ref=target, send_sem=self.send.at[0], recv_sem=self.recv.at[0],
            device_id=place.home, device_id_type=MESH,
        )
        self.near = pltpu.make_async_copy(self.rows, target, self.recv.at[0])
        pl.when(place.away == 1)(self.far.start)
        pl.when(place.away == 0)(self.near.start)

    def land(self):
        super().land(False)


class Work:
    def __init__(self, place, nf, rows, scatters, spreads, schedule):
        self.n, self.schedule = place.n, schedule
        self.scatters, self.spreads = [], []
        for blocks, w, sems in scatters:
            self.scatters.append((Spread(place, nf, w, rows), blocks, sems))
        for w, sems in spreads:
            piece = Spread(place, nf, w, rows)
            piece.use(*sems)
            self.spreads.append(piece)

    def at(self, point):
        for what, i, *d in self.schedule[point] if point < len(self.schedule) else ():
            if what == "scatter":
                piece, blocks, sems = self.scatters[i]
                piece.scatter(blocks, *sems)
            elif what == "spread":
                self.spreads[i].spread(*d)
            else:
                self.spreads[i].forward(*d)

    def complete(self, i):
        self.spreads[i].complete()

    def settle(self, done=()):
        for i, piece in enumerate(self.spreads):
            if i not in done:
                piece.complete()
            piece.sent_all()
        for piece, _, _ in self.scatters:
            for d in range(self.n):
                piece.arrived(d)
            piece.scatter_sent()


def parts(n, first, last):
    return range(first * n // 4, last * n // 4)


def moves(what, piece, places):
    return [(what, piece, d) for d in places]


def weights_kernel(
    n, nf, units, share, layers,
    qkv, output, gate_up, down, *refs,
):
    place = Place(n)
    rows, hidden = down.shape[1:]
    w_a, w_g, w_d = refs[:3]
    later = refs[3 : 3 * layers]
    a_first, g_first, d_first, raw_g, raw_d, cut_sems, raw_sems = refs[3 * layers : 3 * layers + 7]
    sems = refs[3 * layers + 7 :]
    a_blocks = [a_first] + list(later[: layers - 1])
    g_blocks = [g_first] + list(later[layers - 1 : 2 * layers - 2])
    d_blocks = [d_first] + list(later[2 * layers - 2 :])
    cuts = []
    for l in range(layers):
        for q in range(n):
            columns = pl.ds(q // share * VD, VD)
            for i in range(4):
                source = qkv.at[l, i, :, columns] if i < 3 else output.at[l, :, columns]
                target = a_blocks[l].at[q, :, pl.ds(i * VD, VD)]
                cuts.append(pltpu.make_async_copy(source, target, cut_sems.at[l, q, i]))
    for copy in cuts[: 4 * n]:
        copy.start()
    raws = []
    for l in range(layers):
        raws.append(pltpu.make_async_copy(gate_up.at[l], raw_g.at[l], raw_sems.at[l, 0]))
        raws.append(pltpu.make_async_copy(down.at[l], raw_d.at[l], raw_sems.at[l, 1]))
    for copy in raws:
        copy.start()
    attention, forward, back = (Spread(place, nf, w, rows) for w in (w_a, w_g, w_d))
    attention.use(*sems[2:8])
    forward.use(*sems[10:16])
    enter(place, nf, True)
    for copy in cuts[: 4 * n]:
        copy.wait()
    attention.scatter(a_first, *sems[:2])
    for copy in cuts[4 * n :]:
        copy.start()

    def fill(target, j, at, value):
        width = min(units, hidden - j * units)
        target[j, :, at : at + width] = value(pl.ds(j * units, width))
        if width < units:
            target[j, :, at + width : at + units] = jnp.zeros((rows, units - width), BF)

    def cut_gate_up(l):
        raws[2 * l].wait()
        for i in range(2):
            for j in range(n):
                fill(g_blocks[l], j, i * units, lambda at, i=i: raw_g[l, :, i, at])

    def cut_down(l):
        raws[2 * l + 1].wait()
        for j in range(n):
            fill(d_blocks[l], j, 0, lambda at: raw_d[l, :, at])

    cut_gate_up(0)
    for d in range(n):
        attention.arrived(d)
        attention.spread(d)
    forward.scatter(g_first, *sems[8:10])
    cut_down(0)
    back.scatter(d_first, *sems[16:18])
    for d in parts(n, 0, 1):
        attention.forward(d)
    for l in range(1, layers):
        cut_gate_up(l)
        cut_down(l)
    for copy in cuts[4 * n :]:
        copy.wait()
    for d in parts(n, 1, 3):
        attention.forward(d)
    for d in range(n):
        forward.arrived(d)
    for d in parts(n, 0, 1):
        forward.spread(d)
    for d in parts(n, 3, 4):
        attention.forward(d)
    attention.complete()
    forward.complete()
    attention.scatter_sent()
    attention.sent_all()
    forward.scatter_sent()
    forward.sent_all()
    for d in range(n):
        back.arrived(d)
    back.scatter_sent()


class Gather:
    def __init__(self, place, x, send_r, recv_r, send_l, recv_l, core_send, core_recv, lean=False):
        self.place, self.x = place, x
        self.sems = (send_r, recv_r, send_l, recv_l, core_send, core_recv)
        self.lean = lean and place.n == 4
        self.right, self.left, self.across = {}, {}, []

    @staticmethod
    def semaphores(n):
        dma = pltpu.SemaphoreType.DMA
        return [dma((n,))] * 4 + [dma((n,))] * 2

    def _make(self, s):
        place, x = self.place, self.x
        send_r, recv_r, send_l, recv_l = self.sems[:4]
        top = x.shape[2] // 2
        last = s == place.n // 2 - 1
        for i in range(1 if last and not self.lean else 2):
            for made, sign, send, recv in ((self.right, 1, send_r, recv_r), (self.left, -1, send_l, recv_l)):
                piece = i if sign > 0 else 1 - i
                at = x.at[place.ring(-sign * s)[0], place.t, pl.ds(piece * top, top)]
                made[s, i] = pltpu.make_async_remote_copy(
                    src_ref=at, dst_ref=at, send_sem=send.at[2 * s + i], recv_sem=recv.at[2 * s + i],
                    device_id=place.ring(sign)[1], device_id_type=MESH,
                )

    def _cross(self, q):
        core_send, core_recv = self.sems[4:]
        slot, at = len(self.across), self.x.at[q, self.place.t]
        other = {"tp": 1 - self.place.t}
        self.across.append(remote(at, at, core_send.at[slot], core_recv.at[slot], other))

    def begin(self):
        for s in range(self.place.n // 2):
            self._make(s)
        for i in range(2):
            self.right[0, i].start()
            self.left[0, i].start()
        self._cross(self.place.q)

    def _hop(self, s):
        last = self.place.n // 2 - 1
        if not self.lean:
            for i in range(1 if s == last else 2):
                for stream in (self.right, self.left):
                    stream[s, i].wait_recv()
                    if s < last - 1 or (s == last - 1 and i == 0):
                        stream[s + 1, i].start()
            return

        def body(even):
            along_ctx, along_fsdp = (self.left, self.right) if even else (self.right, self.left)
            for i in range(2):
                if s == 0:
                    along_ctx[0, i].wait_recv()
                    along_ctx[1, i].start()
                    along_fsdp[0, i].wait_recv()
                else:
                    along_fsdp[1, i].wait_recv()

        when_even(self.place, body)

    def chunks(self):
        place, half = self.place, self.place.n // 2
        self.across[0].wait_recv()
        yield place.q
        for s in range(half):
            self._hop(s)
            arrived = [place.ring(half)[0]] if s == half - 1 else [place.ring(-s - 1)[0], place.ring(s + 1)[0]]
            first = len(self.across)
            for q in arrived:
                self._cross(q)
            for i, q in enumerate(arrived):
                self.across[first + i].wait_recv()
                yield q

    def finish(self):
        last = self.place.n // 2 - 1
        for s in range(last + 1):
            for i in range(2):
                if s < last:
                    self.right[s, i].wait_send()
                    self.left[s, i].wait_send()
                elif not self.lean and i == 0:
                    self.right[s, 0].wait_send()
                    self.left[s, 0].wait_send()
        if self.lean:

            def body(even):
                for i in range(2):
                    (self.left if even else self.right)[1, i].wait_send()

            when_even(self.place, body)
        for copy in self.across:
            copy.wait_send()


def by_rows(count, body, step=16):
    def one(i, carry):
        body(pl.ds(pl.multiple_of(i * step, step), step))
        return carry

    lax.fori_loop(0, count // step, one, 0)


class Reduce:
    def __init__(self, place, p, from_core, in_r, in_l, send_r, recv_r, send_l, recv_l, core_send, core_recv, lean=False):
        self.place, self.p, self.from_core, self.in_r, self.in_l = place, p, from_core, in_r, in_l
        self.sems = (send_r, recv_r, send_l, recv_l, core_send, core_recv)
        self.lean = lean and place.n == 4
        half = place.n // 2
        self.order = [half] + [k for j in range(half - 1, 0, -1) for k in (j, -j)] + [0]
        self.chips = {k: place.ring(k)[0] for k in self.order}
        self.across, self.copies = {}, {}
        for sign in (1, -1):
            for s in range(half):
                for piece in range(2):
                    if s or self.lean or piece == (sign < 0):
                        self._copy(sign, s, piece)

    @staticmethod
    def scratch(n, rows, width):
        dma = pltpu.SemaphoreType.DMA
        wide = [pltpu.VMEM((n, rows, width), BF)] + [pltpu.VMEM((n // 2, rows, width), BF)] * 2
        return wide + [dma((n // 2, 2))] * 4 + [dma((n,))] * 2

    def offer(self, k):
        core_send, core_recv = self.sems[4:]
        slot, q, t = len(self.across), self.chips[k], self.place.t
        self.across[k] = remote(
            self.p.at[q, 1 - t], self.from_core.at[q], core_send.at[slot], core_recv.at[slot], {"tp": 1 - t}
        )

    def _local(self, k, at):
        q = self.chips[k]
        return self.p[q, self.place.t, at].astype(F32) + self.from_core[q, at].astype(F32)

    def _add(self, k, piece, extra=None):
        top = self.p.shape[2] // 2

        def body(at):
            whole = pl.ds(pl.multiple_of(piece * top + at.start, 16), at.size)
            total = self._local(k, whole)
            if extra is not None:
                total = total + extra[whole].astype(F32)
            self.from_core[self.chips[k], whole] = total.astype(BF)

        by_rows(top, body)

    def _copy(self, sign, s, piece):
        if (sign, s, piece) not in self.copies:
            place, top = self.place, self.p.shape[2] // 2
            send, recv = self.sems[:2] if sign > 0 else self.sems[2:4]
            target = self.in_r if sign > 0 else self.in_l
            k = place.n // 2 - s
            rows = pl.ds(piece * top, top)
            self.copies[sign, s, piece] = pltpu.make_async_remote_copy(
                src_ref=self.from_core.at[self.chips[sign * k if s else k], rows], dst_ref=target.at[s, rows],
                send_sem=send.at[s, piece], recv_sem=recv.at[s, piece],
                device_id=place.ring(sign)[1], device_id_type=MESH,
            )
        return self.copies[sign, s, piece]

    def far(self):
        half = self.place.n // 2
        self.across[half].wait_recv()
        self._add(half, 0)
        self._add(half, 1)
        if self.lean:
            self.across[1].wait_recv()
            self.across[-1].wait_recv()

            def body(even):
                sign = -1 if even else 1
                for piece in range(2):
                    self._copy(sign, 0, piece).start()
                for piece in range(2):
                    self._add(sign, piece)
                    self._copy(sign, 1, piece).start()

            when_even(self.place, body)
            return
        self._copy(1, 0, 0).start()
        self._copy(-1, 0, 1).start()
        if half > 1:
            k = half - 1
            for sign, piece in ((1, 1), (-1, 0)):
                self.across[sign * k].wait_recv()
                self._add(sign * k, piece)
                self._copy(sign, 1, piece).start()

    def near(self, s):
        half = self.place.n // 2
        k = half - s
        if self.lean:

            def body(even):
                sign = 1 if even else -1
                for piece in range(2):
                    self._copy(sign, 0, piece).wait_recv()
                    self._add(sign, piece, (self.in_r if even else self.in_l).at[0])
                    self._copy(sign, 1, piece).start()

            when_even(self.place, body)
            return
        if s > 1:
            self.across[k].wait_recv()
            self.across[-k].wait_recv()
        for sign, first, held in ((1, 0, self.in_r), (-1, 1, self.in_l)):
            for piece in (first,) if s == 1 else (first, 1 - first):
                self._copy(sign, s - 1, piece).wait_recv()
                self._add(sign * k, piece, held.at[s - 1])
                self._copy(sign, s, piece).start()

    def end(self, use):
        half = self.place.n // 2
        self.across[0].wait_recv()
        for sign in (1, -1):
            for piece in range(2):
                self._copy(sign, half - 1, piece).wait_recv()

        def body(at):
            use(at, self._local(0, at) + self.in_r[half - 1, at].astype(F32) + self.in_l[half - 1, at].astype(F32))

        by_rows(self.p.shape[2], body)

    def finish(self):
        half = self.place.n // 2
        if self.lean:

            def body(even):
                for piece in range(2):
                    self._copy(-1 if even else 1, 0, piece).wait_send()

            when_even(self.place, body)
        else:
            self._copy(1, 0, 0).wait_send()
            self._copy(-1, 0, 1).wait_send()
        for s in range(1, half):
            for sign in (1, -1):
                for piece in range(2):
                    self._copy(sign, s, piece).wait_send()
        for copy in self.across.values():
            copy.wait_send()

    def run(self, use, before=None):
        for k in self.order:
            self.offer(k)
        self.far()
        for s in range(1, self.place.n // 2):
            self.near(s)
        if before is not None:
            before()
        self.end(use)


def mm(a, b):
    return jnp.dot(a, b, preferred_element_type=F32)


def mm_t(a, b):
    return lax.dot_general(a, b, (((1,), (1,)), ((), ())), preferred_element_type=F32)


def t_mm(a, b):
    return lax.dot_general(a, b, (((0,), (0,)), ((), ())), preferred_element_type=F32)


def rms_scale(values):
    return lax.rsqrt(jnp.mean(values * values, axis=-1, keepdims=True) + EPSILON)


def norm_back(grad_normed, inputs, scale_rows, gain):
    unit = inputs * scale_rows
    scaled = grad_normed * gain
    return scale_rows * (scaled - unit * jnp.mean(scaled * unit, axis=-1, keepdims=True))


def tiles(count, width, body):
    def one(j, carry):
        body(pl.ds(pl.multiple_of(j * width, width), width))
        return carry

    lax.fori_loop(0, count // width, one, 0)


def tile_of(count):
    return 256 if count % 256 == 0 else 128


def turn(v, cosine, sine):
    return v * cosine + pltpu.roll(v, HD // 2, 1) * sine


def block_diagonal(out, parts, rank, width):
    out[...] = jnp.zeros(out.shape, out.dtype)
    for i in range(parts[1]):
        out[i * rank : (i + 1) * rank, i * width : (i + 1) * width] = parts[0][i * rank : (i + 1) * rank, :]


def write_norm(x_rows, source, gain):
    def body(at):
        v = source[at].astype(F32)
        x_rows[at] = (v * rms_scale(v) * gain[...]).astype(BF)

    by_rows(source.shape[0], body)


ROW_BLOCK = 128
KEY_STEP = 256


def row_blocks(tree, body):
    for j in range(tree // KEY_STEP):

        def one(i, carry, j=j):
            body(pl.ds(pl.multiple_of(j * KEY_STEP + i * ROW_BLOCK, ROW_BLOCK), ROW_BLOCK), (j + 1) * KEY_STEP)
            return carry

        lax.fori_loop(0, KEY_STEP // ROW_BLOCK, one, 0)


def seen(rows, keys, query_bits, key_bits):
    shared = (query_bits[rows] & key_bits[:, :keys]) != 0
    i = rows.start + lax.broadcasted_iota(jnp.int32, (ROW_BLOCK, keys), 0)
    j = lax.broadcasted_iota(jnp.int32, (ROW_BLOCK, keys), 1)
    return shared & (j <= i)


def attention_forward(
    n, nf, layer, part, rank, lean, plan,
    residual, gain, w_hbm, a_model, a_head, cosine, sine, query_bits, key_bits, lam, *refs,
):
    jobs, refs = plan.split(refs)
    (middle, x_hbm, queries, keys, values, small, log_total, mixed, headed, side,
     x, p, w, raised, copy_sems, *sems) = refs
    place = Place(n)
    chip_rows, width = 2 * x_hbm.shape[2], x_hbm.shape[3]
    tree = n * chip_rows
    load = pltpu.make_async_copy(w_hbm, w, copy_sems.at[0])
    load.start()
    gather, reduce = Gather(place, x, *sems[:6], lean=lean), Reduce(place, p, *sems[6:], lean=lean)
    write_norm(x.at[place.q, place.t], residual, gain)
    block_diagonal(raised, (a_head[rank : 4 * rank], 3), rank, VD)
    work = plan.work(place, nf, jobs)
    enter(place, nf, bool(plan.scatters))
    gather.begin()
    work.at(0)
    load.wait()

    def project(q):
        rows = pl.ds(pl.multiple_of(q * chip_rows, chip_rows), chip_rows)
        v = x[q].reshape(chip_rows, width)
        low = mm_t(v, a_model[: 3 * rank]).astype(BF)
        small[rows] = low
        for i, out in enumerate((queries, keys, values)):
            at = slice(i * VD, (i + 1) * VD)
            made = mm(v, w[:, at]) + ADAPTER_SCALE * mm(low, raised[:, at])
            if i < 2:
                for c in range(2):
                    half = slice(c * HD, (c + 1) * HD)
                    out[rows, half] = turn(made[:, half], cosine[rows], sine[rows]).astype(BF)
            else:
                out[rows] = made.astype(BF)

    for q in gather.chunks():
        project(q)
    work.at(1)
    keep = pltpu.make_async_copy(x, x_hbm, copy_sems.at[1])
    keep.start()
    score_scale = HD ** (-0.5)
    weight = lam[...]

    def attend(rows, count):
        visible = seen(rows, count, query_bits, key_bits)
        both = []
        for c in range(2):
            at = slice(c * HD, (c + 1) * HD)
            scores = mm_t(queries[rows, at], keys[:count, at]) * score_scale
            scores = jnp.where(visible, scores, NEGATIVE_BIG)
            top = jnp.max(scores, axis=-1, keepdims=True)
            raw = jnp.exp(scores - top)
            total = jnp.sum(raw, axis=-1, keepdims=True)
            log_total[rows, c : c + 1] = top + jnp.log(total)
            both.append(raw * (1.0 / total))
        mix = mm((both[0] - weight * both[1]).astype(BF), values[:count])
        mixed[rows] = mix.astype(BF)
        head = (mix * rms_scale(mix) * keep_factor(layer)).astype(BF)
        headed[rows] = head
        side[rows] = mm_t(head, a_head[:rank]).astype(BF)

    row_blocks(tree, attend)
    work.at(2)

    for k in reduce.order:
        q = reduce.chips[k]
        rows = pl.ds(pl.multiple_of(q * chip_rows, chip_rows), chip_rows)
        head, low = headed[rows], side[rows]

        def out_tile(at):
            made = mm_t(head, w[at, 3 * VD :]) + ADAPTER_SCALE * mm(low, a_model[9 * rank : 10 * rank, at])
            p[q, :, :, at] = (made * part).astype(BF).reshape(2, chip_rows // 2, at.size)

        tiles(width, 512, out_tile)
        reduce.offer(k)
        if k == reduce.order[2]:
            reduce.far()
    work.at(3)
    for s in range(1, n // 2):
        reduce.near(s)
    work.at(4)

    def use(at, total):
        middle[at] = residual[at].astype(F32) + total

    reduce.end(use)
    work.at(5)
    keep.wait()
    gather.finish()
    reduce.finish()
    work.settle()


def ffn_forward(
    n, nf, units, rank, lean, plan,
    residual, gain, w_hbm, a_model, e_model, *refs,
):
    jobs, refs = plan.split(refs)
    (following, x_hbm, gates, ups, hidden, small, side,
     x, p, w, raised, copy_sems, *sems) = refs
    place = Place(n)
    chip_rows, width = 2 * x_hbm.shape[2], x_hbm.shape[3]
    tree = n * chip_rows
    load = pltpu.make_async_copy(w_hbm, w.at[:, pl.ds(0, 2 * units)], copy_sems.at[0])
    load.start()
    gather, reduce = Gather(place, x, *sems[:6], lean=lean), Reduce(place, p, *sems[6:], lean=lean)
    write_norm(x.at[place.q, place.t], residual, gain)
    block_diagonal(raised, (e_model, 2), rank, units)
    work = plan.work(place, nf, jobs)
    enter(place, nf, bool(plan.scatters))
    gather.begin()
    work.at(0)
    load.wait()
    step = tile_of(units)

    for number, q in enumerate(gather.chunks()):
        if number == n - 1:
            work.at(1)
        rows = pl.ds(pl.multiple_of(q * chip_rows, chip_rows), chip_rows)
        v = x[q].reshape(chip_rows, width)
        low = mm_t(v, a_model[4 * rank : 6 * rank]).astype(BF)
        small[rows] = low

        def unit_tile(at):
            up_at = pl.ds(pl.multiple_of(units + at.start, step), step)
            gate = mm(v, w[:, at]) + ADAPTER_SCALE * mm(low, raised[:, at])
            up = mm(v, w[:, up_at]) + ADAPTER_SCALE * mm(low, raised[:, up_at])
            gates[rows, at] = gate.astype(BF)
            ups[rows, at] = up.astype(BF)
            hidden[rows, at] = (gate / (1.0 + jnp.exp(-gate)) * up).astype(BF)

        tiles(units, step, unit_tile)

    work.at(2)
    keep = pltpu.make_async_copy(x, x_hbm, copy_sems.at[1])
    keep.start()

    work.complete(0)
    load = pltpu.make_async_copy(plan.late(jobs), w.at[:, pl.ds(2 * units, units)], copy_sems.at[0])
    load.start()
    load.wait()
    for k in reduce.order:
        q = reduce.chips[k]
        rows = pl.ds(pl.multiple_of(q * chip_rows, chip_rows), chip_rows)
        made_hidden = hidden[rows]
        low = mm_t(made_hidden, e_model[2 * rank : 3 * rank]).astype(BF)
        side[rows] = low

        def out_tile(at):
            made = mm_t(made_hidden, w[at, 2 * units :])
            made = made + ADAPTER_SCALE * mm(low, a_model[10 * rank : 11 * rank, at])
            p[q, :, :, at] = made.astype(BF).reshape(2, chip_rows // 2, at.size)

        tiles(width, 512, out_tile)
        reduce.offer(k)
        if k == reduce.order[2]:
            reduce.far()
    work.at(3)
    for s in range(1, n // 2):
        reduce.near(s)
    work.at(4)

    def use(at, total):
        following[at] = residual[at] + total

    reduce.end(use)
    work.at(5)
    keep.wait()
    gather.finish()
    reduce.finish()
    work.settle((0,))


def ffn_backward(
    n, units, rank, carry,
    grad, middle, gain, w_hbm, w_down_hbm, a_model, e_model, x_hbm, gates, ups, hidden, small, side, *refs,
):
    if carry:
        final, final_out, *refs = refs
        *refs, final_rows, home_send, home_recv = refs
    (grad_out, grad_up_down, grad_in, grad_units,
     x, p, w, kept, dgu, dsmall, dside, raised, copy_sems, *sems) = refs
    place = Place(n)
    chip_rows, width = 2 * x_hbm.shape[2], x_hbm.shape[3]
    tree = n * chip_rows
    load = pltpu.make_async_copy(w_hbm, w.at[:, pl.ds(0, 2 * units)], copy_sems.at[0])
    load.start()
    load_down = pltpu.make_async_copy(w_down_hbm, w.at[:, pl.ds(2 * units, units)], copy_sems.at[2])
    load_down.start()
    fetch = pltpu.make_async_copy(x_hbm, kept, copy_sems.at[1])
    fetch.start()
    gather, reduce = Gather(place, x, *sems[:6]), Reduce(place, p, *sems[6:])

    def own(at):
        x[place.q, place.t, at] = grad[at].astype(BF)

    by_rows(grad.shape[0], own)
    block_diagonal(raised, (e_model, 2), rank, units)
    if carry:

        def last_rows(at):
            final_rows[at] = final[at].astype(BF)

        by_rows(final.shape[0], last_rows)
    enter(place, home=carry)
    gather.begin()
    if carry:
        home = Home(place, final_out, home_send, home_recv)
        home.start(final_rows)
    load.wait()
    load_down.wait()
    step = tile_of(units)

    for q in gather.chunks():
        rows = pl.ds(pl.multiple_of(q * chip_rows, chip_rows), chip_rows)
        v = x[q].reshape(chip_rows, width)
        low = (ADAPTER_SCALE * mm_t(v, a_model[10 * rank : 11 * rank])).astype(BF)
        dside[rows] = low

        def unit_tile(at):
            up_at = pl.ds(pl.multiple_of(units + at.start, step), step)
            down_at = pl.ds(pl.multiple_of(2 * units + at.start, step), step)
            dhidden = mm(v, w[:, down_at]) + mm(low, e_model[2 * rank : 3 * rank, at])
            gate, up = gates[rows, at].astype(F32), ups[rows, at].astype(F32)
            sig = 1.0 / (1.0 + jnp.exp(-gate))
            dgu[rows, at] = (dhidden * up * sig * (1.0 + gate * (1.0 - sig))).astype(BF)
            dgu[rows, up_at] = (dhidden * gate * sig).astype(BF)

        tiles(units, step, unit_tile)
        back = dgu[rows]
        low_back = (ADAPTER_SCALE * mm_t(back, raised[...])).astype(BF)
        dsmall[rows] = low_back

        def out_tile(at):
            made = mm_t(back, w[at, : 2 * units]) + mm(low_back, a_model[4 * rank : 6 * rank, at])
            p[q, :, :, at] = made.astype(BF).reshape(2, chip_rows // 2, at.size)

        tiles(width, 512, out_tile)

    def use(at, total):
        inputs = middle[at]
        grad_out[at] = grad[at].astype(F32) + norm_back(total, inputs, rms_scale(inputs), gain[...])

    def adapters():
        fetch.wait()

        def model_tile(at):
            flat = x[:, :, :, at].reshape(tree, at.size)
            grad_up_down[:, at] = (ADAPTER_SCALE * t_mm(side[...], flat)).astype(BF)
            flat = kept[:, :, :, at].reshape(tree, at.size)
            grad_in[:, at] = t_mm(dsmall[...], flat).astype(BF)

        tiles(width, 256, model_tile)

        def unit_tile(at):
            up_at = pl.ds(pl.multiple_of(units + at.start, step), step)
            grad_units[:rank, at] = (ADAPTER_SCALE * t_mm(small[...], dgu[:, at])[:rank]).astype(BF)
            grad_units[rank : 2 * rank, at] = (ADAPTER_SCALE * t_mm(small[...], dgu[:, up_at])[rank:]).astype(BF)
            grad_units[2 * rank : 3 * rank, at] = t_mm(dside[...], hidden[:, at]).astype(BF)
            grad_units[3 * rank :, at] = jnp.zeros((rank, at.size), BF)

        tiles(units, step, unit_tile)

    reduce.run(use, adapters)
    gather.finish()
    reduce.finish()
    if carry:
        home.land()
        home.finish()


def attention_backward(
    n, layer, share, heads_tp, rank,
    grad, residual, gain, w_hbm, a_model, a_head, cosine, sine, query_bits, key_bits, lam,
    x_hbm, queries, keys, values, small, log_total, mixed, headed, side,
    grad_up_down, grad_ffn_in, grad_units,
    grad_out, own_sum, all_units,
    x, p, w, dmixed, dq, dk, dv, dprojected, dsmall, dside, raised, grad_a9, p_own, copy_sems, *sems,
):
    place = Place(n)
    part = 1.0 / share
    chip_rows, width = 2 * x_hbm.shape[2], x_hbm.shape[3]
    tree = n * chip_rows
    load = pltpu.make_async_copy(w_hbm, w, copy_sems.at[0])
    load.start()
    gather, reduce = Gather(place, x, *sems[:6]), Reduce(place, p, *sems[6:15])
    gather_units, reduce_own = Gather(place, all_units, *sems[15:21]), Reduce(place, p_own, *sems[21:])

    def own(at):
        x[place.q, place.t, at] = grad[at].astype(BF)

    by_rows(grad.shape[0], own)
    block_diagonal(raised, (a_head[rank : 4 * rank], 3), rank, VD)
    all_units[place.q, place.t] = grad_units[...]
    enter(place)
    gather.begin()
    gather_units.begin()
    dk[...] = jnp.zeros(dk.shape, F32)
    dv[...] = jnp.zeros(dv.shape, F32)
    load.wait()

    for q in gather.chunks():
        rows = pl.ds(pl.multiple_of(q * chip_rows, chip_rows), chip_rows)
        v = x[q].reshape(chip_rows, width)
        low = (ADAPTER_SCALE * mm_t(v, a_model[9 * rank : 10 * rank])).astype(BF)
        dside[rows] = low
        dheaded = mm(v, w[:, 3 * VD :]) + mm(low, a_head[:rank])
        inputs = mixed[rows].astype(F32)
        dmixed[rows] = norm_back(dheaded, inputs, rms_scale(inputs), keep_factor(layer)).astype(BF)

    def out_gradient(at):
        flat = x[:, :, :, at].reshape(tree, at.size)
        grad_a9[:, at] = (ADAPTER_SCALE * part * t_mm(side[...], flat)).astype(BF)

    tiles(width, 256, out_gradient)
    gather.finish()
    fetch = pltpu.make_async_copy(x_hbm, x, copy_sems.at[1])
    fetch.start()
    score_scale = HD ** (-0.5)
    weight = lam[...]

    def attend(rows, count):
        visible = seen(rows, count, query_bits, key_bits)
        dmix = dmixed[rows]
        dweights = mm_t(dmix, values[:count])
        both = []
        for c in range(2):
            at = slice(c * HD, (c + 1) * HD)
            scores = mm_t(queries[rows, at], keys[:count, at]) * score_scale
            probability = jnp.exp(jnp.where(visible, scores - log_total[rows, c : c + 1], NEGATIVE_BIG))
            both.append(probability)
            weighted = probability * dweights
            dscores = weighted - probability * jnp.sum(weighted, axis=-1, keepdims=True)
            dscores = (dscores * -weight if c else dscores).astype(BF)
            dq[rows, at] = mm(dscores, keys[:count, at])
            dk[:count, at] += t_mm(dscores, queries[rows, at])
        dv[:count] += t_mm((both[0] - weight * both[1]).astype(BF), dmix)

    row_blocks(tree, attend)

    fetch.wait()
    for _ in gather_units.chunks():
        pass

    def project(i, carry):
        rows = pl.ds(pl.multiple_of(i * chip_rows, chip_rows), chip_rows)
        for j, source in enumerate((dq, dk)):
            for c in range(2):
                half = slice(c * HD, (c + 1) * HD)
                turned = turn(source[rows, half] * score_scale, cosine[rows], -sine[rows])
                dprojected[rows, j * VD + c * HD : j * VD + (c + 1) * HD] = turned.astype(BF)
        dprojected[rows, 2 * VD :] = dv[rows].astype(BF)
        dsmall[rows] = (ADAPTER_SCALE * mm_t(dprojected[rows], raised[...])).astype(BF)
        return carry

    lax.fori_loop(0, n, project, 0)

    def send_part(k):
        q = reduce.chips[k]
        rows = pl.ds(pl.multiple_of(q * chip_rows, chip_rows), chip_rows)
        back, low_back = dprojected[rows], dsmall[rows]

        def out_tile(at):
            made = mm_t(back, w[at, : 3 * VD]) + mm(low_back, a_model[: 3 * rank, at])
            p[q, :, :, at] = (made * part).astype(BF).reshape(2, chip_rows // 2, at.size)

        tiles(width, 512, out_tile)
        reduce.offer(k)

    for k in reduce.order[:3]:
        send_part(k)
    reduce.far()

    block = width // (2 * n)

    def full_tile(jp, carry):
        at = pl.ds(pl.multiple_of(jp * block, block), block)
        q, t = jp // 2, jp % 2
        flat = x[:, :, :, at].reshape(tree, block)
        p_own[q, t, : 3 * rank] = (part * t_mm(dsmall[...], flat)).astype(BF)
        p_own[q, t, 4 * rank : 6 * rank] = grad_ffn_in[:, at]
        p_own[q, t, 9 * rank : 10 * rank] = grad_a9[:, at]
        p_own[q, t, 10 * rank : 11 * rank] = grad_up_down[:, at]
        p_own[q, t, 11 * rank :] = jnp.zeros((rank, block), BF)
        return carry

    lax.fori_loop(0, 2 * n, full_tile, 0)
    of_head = [part * t_mm(dside[...], headed[...])]
    for i in range(3):
        made = t_mm(small[...], dprojected[:, i * VD : (i + 1) * VD])[i * rank : (i + 1) * rank]
        of_head.append(ADAPTER_SCALE * part * made)
    head = place.t * heads_tp + place.q // share
    for j in range(2 * n):
        start = j * block % VD
        own = (head == j * block // VD).astype(F32)
        for i, k in enumerate((3, 6, 7, 8)):
            made = of_head[i][:, start : start + block] * own
            p_own[j // 2, j % 2, k * rank : (k + 1) * rank] = made.astype(BF)

    for k in reduce.order[3:]:
        send_part(k)
    for k in reduce.order:
        reduce_own.offer(k)
    reduce_own.far()
    for s in range(1, n // 2):
        reduce.near(s)
        reduce_own.near(s)

    def use_own(at, total):
        own_sum[at] = total.astype(BF)

    def use(at, total):
        inputs = residual[at].astype(F32)
        grad_out[at] = grad[at].astype(F32) + norm_back(total, inputs, rms_scale(inputs), gain[...])

    reduce.end(use)
    reduce_own.end(use_own)
    gather_units.finish()
    reduce.finish()
    reduce_own.finish()


def finish_kernel(
    n, nf, layers, rank,
    grad, own_sums, own_units, slot,
    tokens_grad, model_grad, hidden_grad,
    rows_out, landed, sent_sums, all_sums, all_units, home_send, home_recv, tree_send, tree_recv,
):
    place = Place(n)
    own = model_grad.shape[2]
    tall = own_sums.shape[0]

    def cut(at):
        rows_out[at] = grad[at].astype(BF)

    by_rows(grad.shape[0], cut)
    sent_sums[...] = own_sums[...]
    sent_sums[tall - rank :] = jnp.broadcast_to(slot[...], (rank, own_sums.shape[1])).astype(BF)
    enter(place, home=True, ring=False, trees=nf)
    moves = [Home(place, landed, home_send.at[0], home_recv.at[0])]
    moves[0].start(rows_out)
    away = {}
    for i, (source, target) in enumerate(((sent_sums, all_sums), (own_units, all_units))):
        away[i] = TreeMove(place, source, target, home_send.at[i + 1], home_recv.at[i + 1])
        away[i].start()
    copies = []
    for i in range(2):
        away[i].land()
        slot_of = away[i].slot
        for e in range(1, nf):
            copies.append(
                remote(slot_of, slot_of, tree_send.at[i, e], tree_recv.at[i, e], {"fsdp": flip(place.f, e)})
            )
    moves[0].land()
    for copy in copies:
        copy.wait_recv()
    block, units = all_sums.shape[2], all_units.shape[2]
    per_layer = tall // layers
    for b in range(own):
        number = (place.f * own + b).astype(F32)
        keeps = [
            (all_sums[f, tall - rank : tall - rank + 1, :1].astype(F32) == number).astype(F32) for f in range(nf)
        ]
        for l in range(layers):
            for k in range(11):
                at = slice(l * per_layer + k * rank, l * per_layer + (k + 1) * rank)
                model_grad[l, k, b] = sum(keeps[f] * all_sums[f, at].astype(F32) for f in range(nf))
            for k in range(3):
                at = slice((l * 3 + k) * rank, (l * 3 + k + 1) * rank)
                hidden_grad[l, k, b] = sum(keeps[f] * all_units[f, at].astype(F32) for f in range(nf))
    moves[0].finish()
    for core in range(2):

        def widen(at, core=core):
            rows = landed.shape[1]
            tokens_grad[pl.ds(pl.multiple_of(core * rows + at.start, 16), at.size)] = landed[core, at].astype(F32)

        by_rows(landed.shape[1], widen)
    for copy in copies:
        copy.wait_send()


class Plan:
    def __init__(self, n, nf, rows, scatters, spreads, schedule):
        self.n, self.nf, self.rows, self.schedule = n, nf, rows, schedule
        self.scatters, self.spreads = scatters, spreads

    def ins(self):
        return [(blocks, True) for blocks, _ in self.scatters] + [(w, True) for w in self.spreads]

    def outs(self):
        made = [(shape, BF, True) for _, shape in self.scatters]
        return made + [(w.shape, BF, True) for w in self.spreads]

    def semaphores(self):
        made = Spread.scatter_semaphores(self.n) * len(self.scatters)
        return made + Spread.spread_semaphores(self.n, self.nf) * len(self.spreads)

    def split(self, refs):
        a, b = len(self.scatters), len(self.spreads)
        count = 2 * a + 6 * b
        refs = list(refs)
        taken = refs[: a + b], refs[a + b : 2 * (a + b)], refs[len(refs) - count :]
        return taken, refs[2 * (a + b) : len(refs) - count]

    def work(self, place, nf, jobs):
        a, b = len(self.scatters), len(self.spreads)
        ins, outs, sems = jobs
        scatters = [(ins[i], outs[i], sems[2 * i : 2 * i + 2]) for i in range(a)]
        spreads = [(outs[a + i], sems[2 * a + 6 * i : 2 * a + 6 * i + 6]) for i in range(b)]
        return Work(place, nf, self.rows, scatters, spreads, self.schedule)

    def late(self, jobs):
        return jobs[1][len(self.scatters)]


def call(kernel, collective, ins, outs, scratch, plan=None):
    spec = lambda hbm: pl.BlockSpec(memory_space=pl.ANY if hbm else pltpu.VMEM)
    aliases = {}
    if plan is not None:
        first_in, count = len(ins), len(plan.scatters)
        aliases = {first_in + count + i: count + i for i in range(len(plan.spreads))}
        ins, outs, scratch = ins + plan.ins(), plan.outs() + outs, scratch + plan.semaphores()
    made = pl.pallas_call(
        kernel,
        out_shape=[jax.ShapeDtypeStruct(shape, kind) for shape, kind, _ in outs],
        in_specs=[spec(hbm) for _, hbm in ins],
        out_specs=[spec(hbm) for _, _, hbm in outs],
        scratch_shapes=scratch,
        input_output_aliases=aliases,
        compiler_params=pltpu.CompilerParams(
            collective_id=collective, has_side_effects=True, vmem_limit_bytes=62 << 20
        ),
    )(*[array for array, _ in ins])
    return list(made)


def line_bits(parent_row, seg):
    number = jnp.arange(NSEG)
    one = lambda x: lax.shift_left(jnp.ones_like(x), x)
    grand = jnp.sum(jnp.where(parent_row[:, None] == number[None, :], parent_row[None, :], 0), axis=1)
    line = one(number) | one(parent_row) | one(grand)
    mine = jnp.sum(jnp.where(seg[:, None] == number[None, :], line[None, :], 0), axis=1)
    return mine, one(seg)


def keep_factor(layer):
    return 0.2 + 0.6 * math.exp(-0.3 * layer)


def chips_of(nf, nc):
    h = nc // 2
    for f in range(nf):
        for c in range(nc):
            yield f * nc + c, (f // 2, f % 2, c // h, c % h)


def permute(x, nf, nc, target):
    h = nc // 2
    pairs = []
    for source, spot in chips_of(nf, nc):
        f_hi, f_lo, c_hi, c_lo = target(*spot)
        pairs.append((source, (f_hi * 2 + f_lo) * nc + c_hi * h + c_lo))
    return lax.ppermute(x, ("fsdp", "ctx"), pairs)


def swap_trees(x, nf, nc):
    return permute(x, nf, nc, lambda f_hi, f_lo, c_hi, c_lo: (f_hi, c_hi, f_lo, c_lo))


def shards(
    nf,
    nc,
    tokens,
    cotangent,
    segments,
    depths,
    parents,
    tree_adapter_index,
    layer_norm_gains,
    difference_lambda,
    query_key_value_weight,
    output_weight,
    gate_up_weight,
    down_weight,
    adapter_model_factors,
    adapter_hidden_factors,
):
    n = nc
    place = Place(n)
    q, t = place.q, place.t
    tokens_dev, width = tokens.shape
    rows = tokens_dev // 2
    tree = tokens_dev * n
    layers, weight_rows = query_key_value_weight.shape[:2]
    heads_tp = difference_lambda.shape[1]
    share = max(1, n // heads_tp)
    head = q // share
    hidden_tp = down_weight.shape[2]
    units = (hidden_tp + n * 128 - 1) // (n * 128) * 128
    rank, adapters = adapter_model_factors.shape[3], adapter_model_factors.shape[2]
    h = n // 2

    notes = jnp.concatenate([segments, depths, parents[0], tree_adapter_index])
    order = jnp.arange(n)
    of_tree = jnp.zeros((n, notes.shape[0]), jnp.int32)
    for d in range(n):

        def hand_out(f_hi, f_lo, c_hi, c_lo, d=d):
            to = (c_hi * (n // 2) + c_lo) ^ d
            return f_hi, to // (n // 2), f_lo, to % (n // 2)

        part_of_tree = permute(notes, nf, nc, hand_out)
        of_tree = of_tree + jnp.where(order[:, None] == flip(q, d), part_of_tree[None], 0)
    seg, dep = of_tree[:, :tokens_dev].reshape(tree), of_tree[:, tokens_dev : 2 * tokens_dev].reshape(tree)
    parent_row, slot = of_tree[0, 2 * tokens_dev : 2 * tokens_dev + NSEG], of_tree[0, 2 * tokens_dev + NSEG]
    own_tokens = lax.dynamic_slice_in_dim(tokens, t * rows, rows, 0)
    own_cotangent = lax.dynamic_slice_in_dim(cotangent, t * rows, rows, 0)
    residual = swap_trees(own_tokens, nf, nc)
    own_cotangent = swap_trees(own_cotangent, nf, nc)

    query_bits, key_bits = line_bits(parent_row, seg)
    query_bits, key_bits = query_bits[:, None], key_bits[None, :]
    frequency = 10000.0 ** (-jnp.arange(HD // 2).astype(F32) / (HD // 2))
    angles = dep.astype(F32)[:, None] * frequency[None, :]
    cosine, sine = jnp.cos(angles), jnp.sin(angles)
    cosine = jnp.concatenate([cosine, cosine], axis=1)
    sine = jnp.concatenate([-sine, sine], axis=1)
    gains = layer_norm_gains

    a_all = lax.dynamic_index_in_dim(adapter_model_factors, slot, 2, keepdims=False)
    e_all = lax.dynamic_index_in_dim(adapter_hidden_factors, slot, 2, keepdims=False)
    a_model = a_all.reshape(layers, 11 * rank, width)
    e_all = e_all.reshape(layers, 3 * rank, -1)
    head_at = (t * heads_tp + head) * VD

    heads_of = lax.dynamic_slice_in_dim(a_all, head_at, VD, 3)
    a_head = jnp.concatenate([heads_of[:, 3:4], heads_of[:, 6:9]], axis=1).reshape(layers, 4 * rank, VD)

    def unit_columns(x):
        x = lax.dynamic_slice_in_dim(x, t * hidden_tp, hidden_tp, x.ndim - 1)
        x = jnp.pad(x, ((0, 0),) * (x.ndim - 1) + ((0, n * units - hidden_tp),))
        return lax.dynamic_slice_in_dim(x, q * units, units, x.ndim - 1)

    e_model = unit_columns(e_all)

    part = 1.0 / share
    vmem = lambda *spec: pltpu.VMEM(*spec)
    calls = [0]
    whole_x = ((n, 2, rows, width), BF)
    sems = Gather.semaphores(n) + Reduce.scratch(n, rows, width)
    pair = pltpu.SemaphoreType.DMA((3,))
    big = [vmem(*whole_x), vmem(*whole_x)]

    def run(kernel, ins, outs, scratch, plan=None):
        calls[0] += 1
        return call(kernel, calls[0], ins, outs, scratch, plan)

    near = lambda *arrays: [(array, False) for array in arrays]
    far = lambda *arrays: [(array, True) for array in arrays]
    out = lambda shape, kind, hbm=False: (shape, kind, hbm)

    dma = pltpu.SemaphoreType.DMA
    c_a, c_g, c_d = 4 * VD, 2 * units, units
    tall = nf * n * weight_rows
    cut = lambda columns: out((n, weight_rows, columns), BF)
    calls[0] += 1
    made = call(
        functools.partial(weights_kernel, n, nf, units, share, layers),
        calls[0],
        far(jnp.transpose(query_key_value_weight, (0, 2, 1, 3)), output_weight, gate_up_weight, down_weight),
        [out((tall, c_a), BF, True), out((tall, c_g), BF, True), out((tall, c_d), BF, True)]
        + ([cut(c_a)] + [cut(c_g)] + [cut(c_d)]) * (layers - 1),
        [
            vmem((n, weight_rows, c_a), BF),
            vmem((n, weight_rows, c_g), BF),
            vmem((n, weight_rows, c_d), BF),
            vmem((layers, weight_rows, 2, hidden_tp), BF),
            vmem((layers, weight_rows, hidden_tp), BF),
            dma((layers, n, 4)),
            dma((layers, 2)),
        ]
        + (Spread.scatter_semaphores(n) + Spread.spread_semaphores(n, nf)) * 2
        + Spread.scatter_semaphores(n),
    )
    w_a, w_g, w_d = [made[0]], [made[1]], [made[2]]
    a_blocks = [None] + made[3 : 2 + layers]
    g_blocks = [None] + made[2 + layers : 1 + 2 * layers]
    d_blocks = [None] + made[1 + 2 * layers :]

    def plan_of(scatters, spreads, *schedule):
        return Plan(n, nf, weight_rows, scatters, spreads, schedule)

    saved = []
    for l in range(layers):
        last = l == layers - 1
        w_attention = w_a[l]
        lam = lax.dynamic_slice_in_dim(difference_lambda[l], head, 1).reshape(1, 1)
        gain_a, gain_f = gains[l, 0:1], gains[l, 1:2]
        shared = (a_model[l], a_head[l], cosine, sine, query_bits, key_bits, lam)
        plan = plan_of(
            [] if last else [(a_blocks[l + 1], (tall, c_a)), (g_blocks[l + 1], (tall, c_g))],
            [w_g[l], w_d[l]],
            moves("forward", 0, parts(n, 0, 1)) + moves("spread", 0, parts(n, 1, 4)),
            moves("forward", 0, parts(n, 1, 2)) + ([] if last else [("scatter", 0)]),
            moves("spread", 1, parts(n, 0, 2)) + moves("forward", 0, parts(n, 2, 3)),
            moves("forward", 0, parts(n, 3, 4)) + ([] if last else [("scatter", 1)]),
        )
        got = run(
            functools.partial(attention_forward, n, nf, l, part, rank, not last, plan),
            near(residual, gain_a) + far(w_attention) + near(*shared),
            [
                out((rows, width), F32),
                out(*whole_x, True),
                out((tree, VD), BF),
                out((tree, VD), BF),
                out((tree, VD), BF),
                out((tree, 3 * rank), BF),
                out((tree, 2), F32),
                out((tree, VD), BF),
                out((tree, VD), BF),
                out((tree, rank), BF),
            ],
            big + [vmem((width, 4 * VD), BF), vmem((3 * rank, 3 * VD), BF), pair] + sems,
            plan,
        )
        if not last:
            w_a.append(got[0])
            w_g.append(got[1])
            got = got[2:]
        w_g[l], w_d[l], middle, *kept = got
        plan = plan_of(
            [] if last else [(d_blocks[l + 1], (tall, c_d))],
            [w_d[l]] + ([] if last else [w_a[l + 1], w_g[l + 1]]),
            moves("forward", 0, parts(n, 0, 2)) + moves("spread", 0, parts(n, 2, 4)),
            moves("forward", 0, parts(n, 2, 3)),
            moves("forward", 0, parts(n, 3, 4)) + ([] if last else moves("spread", 1, parts(n, 0, 4)) + [("scatter", 0)]),
            [] if last else moves("forward", 1, parts(n, 0, 1)),
            [] if last else moves("forward", 1, parts(n, 1, 2)) + moves("spread", 2, parts(n, 0, 1)),
            [] if last else moves("forward", 1, parts(n, 2, 4)),
        )
        ffn = run(
            functools.partial(ffn_forward, n, nf, units, rank, not last, plan),
            near(middle, gain_f) + far(w_g[l]) + near(a_model[l], e_model[l]),
            [
                out((rows, width), F32),
                out(*whole_x, True),
                out((tree, units), BF),
                out((tree, units), BF),
                out((tree, units), BF),
                out((tree, 2 * rank), BF),
                out((tree, rank), BF),
            ],
            big + [vmem((width, 3 * units), BF), vmem((2 * rank, 2 * units), BF), pair] + sems,
            plan,
        )
        if not last:
            w_d.append(ffn[0])
            w_d[l], w_a[l + 1], w_g[l + 1], *ffn = ffn[1:]
        else:
            w_d[l], *ffn = ffn
        saved.append((residual, middle, gain_a, gain_f, shared, kept, ffn[1:]))
        residual = ffn[0]

    grad = own_cotangent
    units_here, sums_here, block = [], [], width // (2 * n)
    for l in reversed(range(layers)):
        residual_in, middle, gain_a, gain_f, shared, kept, ffn = saved[l]
        carry = l == layers - 1
        made = run(
            functools.partial(ffn_backward, n, units, rank, carry),
            near(grad, middle, gain_f) + far(w_g[l], w_d[l]) + near(a_model[l], e_model[l]) + far(ffn[0]) + near(*ffn[1:])
            + (near(residual) if carry else []),
            ([out((2, rows, width), BF)] if carry else [])
            + [
                out((rows, width), F32),
                out((rank, width), BF),
                out((2 * rank, width), BF),
                out((4 * rank, units), BF),
            ],
            big
            + [
                vmem((width, 3 * units), BF),
                vmem(*whole_x),
                vmem((tree, 2 * units), BF),
                vmem((tree, 2 * rank), BF),
                vmem((tree, rank), BF),
                vmem((2 * rank, 2 * units), BF),
                pair,
            ]
            + sems
            + ([vmem((rows, width), BF)] + Home.semaphores() if carry else []),
        )
        if carry:
            outputs, *made = made
        grad, *ffn_grads = made
        grad, own_sum, all_units = run(
            functools.partial(attention_backward, n, l, share, heads_tp, rank),
            near(grad, residual_in, gain_a) + far(w_a[l]) + near(*shared) + far(kept[0]) + near(*kept[1:], *ffn_grads),
            [
                out((rows, width), F32),
                out((12 * rank, block), BF),
                out((n, 2, 4 * rank, units), BF),
            ],
            big
            + [
                vmem((width, 4 * VD), BF),
                vmem((tree, VD), BF),
                vmem((tree, VD), F32),
                vmem((tree, VD), F32),
                vmem((tree, VD), F32),
                vmem((tree, 3 * VD), BF),
                vmem((tree, 3 * rank), BF),
                vmem((tree, rank), BF),
                vmem((3 * rank, 3 * VD), BF),
                vmem((rank, width), BF),
                vmem((n, 2, 12 * rank, block), BF),
                pair,
            ]
            + sems
            + Gather.semaphores(n)
            + Reduce.scratch(n, 12 * rank, block),
        )

        number = (q * 2 + t) * (hidden_tp // n)
        half = lax.dynamic_index_in_dim(all_units, number // hidden_tp, 1, keepdims=False)
        flat = half[:, : 3 * rank].transpose(1, 0, 2).reshape(3 * rank, n * units)
        units_here.insert(0, lax.dynamic_slice_in_dim(flat, number % hidden_tp, hidden_tp // n, 1))
        sums_here.insert(0, own_sum)

    own = adapters // nf
    dma = pltpu.SemaphoreType.DMA
    wide = hidden_tp // n
    tokens_grad, grad_model, grad_hidden = run(
        functools.partial(finish_kernel, n, nf, layers, rank),
        near(grad, jnp.concatenate(sums_here), jnp.concatenate(units_here), slot.astype(F32).reshape(1, 1)),
        [
            out((2 * rows, width), F32),
            out((layers, 11, own, rank, block), F32),
            out((layers, 3, own, rank, wide), F32),
        ],
        [
            vmem((rows, width), BF),
            vmem((2, rows, width), BF),
            vmem((layers * 12 * rank, block), BF),
            vmem((nf, layers * 12 * rank, block), BF),
            vmem((nf, layers * 3 * rank, wide), BF),
            dma((3, 2)),
            dma((3, 2)),
            dma((2, nf)),
            dma((2, nf)),
        ],
    )
    return (
        outputs.reshape(2 * rows, width),
        tokens_grad,
        grad_model,
        grad_hidden,
    )


def solution(mesh):
    in_specs = (
        P(("fsdp", "ctx"), None),
        P(("fsdp", "ctx"), None),
        P(("fsdp", "ctx")),
        P(("fsdp", "ctx")),
        P("fsdp", None),
        P("fsdp"),
        P(),
        P(None, "tp"),
        P(None, ("fsdp", "ctx"), None, "tp"),
        P(None, ("fsdp", "ctx"), "tp"),
        P(None, ("fsdp", "ctx"), None, "tp"),
        P(None, ("fsdp", "ctx"), "tp"),
        P(),
        P(),
    )
    out_specs = (
        P(("fsdp", "ctx"), None),
        P(("fsdp", "ctx"), None),
        P(None, None, "fsdp", None, ("ctx", "tp")),
        P(None, None, "fsdp", None, ("ctx", "tp")),
    )
    body = functools.partial(shards, mesh.shape["fsdp"], mesh.shape["ctx"])
    return jax.shard_map(body, mesh=mesh, in_specs=in_specs, out_specs=out_specs, check_vma=False)
```

```python
import functools
import math

import jax
import jax.numpy as jnp
from jax import lax
from jax.experimental import pallas as pl
from jax.experimental.pallas import tpu as pltpu
from jax.sharding import PartitionSpec as P

HD = 128
VD = 256
NSEG = 13
EPSILON = 1e-05
ADAPTER_SCALE = 0.5
NEGATIVE_BIG = -1e30
MESH = pl.DeviceIdType.MESH
BF = jnp.bfloat16
F32 = jnp.float32


class Place:
    def __init__(self, n):
        self.n, self.h = n, n // 2
        self.f, self.c, self.t = lax.axis_index("fsdp"), lax.axis_index("ctx"), lax.axis_index("tp")
        self.f_hi, self.f_lo = self.f // 2, self.f % 2
        self.c_hi, self.c_lo = self.c // self.h, self.c % self.h
        self.q = self.f_lo * self.h + self.c_lo
        self.away = self.f_lo + self.c_hi - 2 * self.f_lo * self.c_hi
        self.home = {"fsdp": self.f_hi * 2 + self.c_hi, "ctx": self.f_lo * self.h + self.c_lo}
        self.pos = self.f_lo * (n - 1) + (1 - 2 * self.f_lo) * self.c_lo

    def ring(self, k):
        n, h = self.n, self.h
        p = lax.rem(self.pos + k + 2 * n, n)
        low = p // h
        column = (1 - low) * p + low * (n - 1 - p)
        device = {"fsdp": self.f_hi * 2 + low, "ctx": self.c_hi * h + column}
        return low * h + column, device


def remote(src, dst, send, recv, device):
    copy = pltpu.make_async_remote_copy(
        src_ref=src, dst_ref=dst, send_sem=send, recv_sem=recv, device_id=device, device_id_type=MESH
    )
    copy.start()
    return copy


def when_even(place, body):
    even = place.pos % 2 == 0
    pl.when(even)(lambda: body(True))
    pl.when(jnp.logical_not(even))(lambda: body(False))


def flip(number, bits):
    b = 1
    while b <= bits:
        if bits & b:
            number = number + b * (1 - 2 * ((number // b) % 2))
        b *= 2
    return number


class Spread:
    def __init__(self, place, nf, w, rows):
        self.place, self.nf, self.w, self.rows = place, nf, w, rows
        self.g = place.f_hi * 2 + place.c_hi
        self.links = range(1, nf // 2)
        self.scattered, self.sent = [], []
        self.to_partner, self.along, self.onward, self.got = {}, {}, {}, []

    @staticmethod
    def scatter_semaphores(n):
        dma = pltpu.SemaphoreType.DMA
        return [dma((n,)), dma((n,))]

    @staticmethod
    def spread_semaphores(n, nf):
        dma = pltpu.SemaphoreType.DMA
        return [dma((n,))] * 2 + [dma((n, max(1, nf // 2 - 1)))] * 4

    def block(self, g, q):
        n, h = self.place.n, self.place.h
        source = (g // 2 * 2 + q // h) * n + g % 2 * h + q % h
        start = pl.multiple_of(source * self.rows, self.rows)
        return self.w.at[pl.ds(start, self.rows)]

    def chip(self, q):
        place = self.place
        return {"fsdp": place.f_hi * 2 + q // place.h, "ctx": place.c_hi * place.h + q % place.h}

    def partner(self):
        place = self.place
        return {"ctx": (1 - place.c_hi) * place.h + place.c_lo}

    def line(self, e):
        return {"fsdp": flip(self.place.f_hi, e) * 2 + self.place.f_lo}

    def scatter(self, blocks, send, recv):
        q = self.place.q
        own = self.block(self.g, q)
        copy = pltpu.make_async_copy(blocks.at[q], own, recv.at[0])
        copy.start()
        self.scattered.append(copy)
        for d in range(1, self.place.n):
            to = flip(q, d)
            self.scattered.append(remote(blocks.at[to], own, send.at[d], recv.at[d], self.chip(to)))

    def arrived(self, d):
        if d:
            self.scattered[d].wait_recv()
        else:
            self.scattered[0].wait()

    def scatter_sent(self):
        for copy in self.scattered[1:]:
            copy.wait_send()

    def use(self, *sems):
        self.sems = sems

    def spread(self, d):
        send_z, recv_z, send_y, recv_y = self.sems[:4]
        at = self.block(self.g, flip(self.place.q, d))
        self.to_partner[d] = remote(at, at, send_z.at[d], recv_z.at[d], self.partner())
        for e in self.links:
            self.along[d, e] = remote(at, at, send_y.at[d, e - 1], recv_y.at[d, e - 1], self.line(e))

    def landed(self, d):
        if d in self.to_partner and d not in self.got:
            self.to_partner[d].wait_recv()
            self.got.append(d)

    def forward(self, d):
        send, recv = self.sems[4:]
        self.landed(d)
        at = self.block(flip(self.g, 1), flip(self.place.q, d))
        for e in self.links:
            self.onward[d, e] = remote(at, at, send.at[d, e - 1], recv.at[d, e - 1], self.line(e))

    def complete(self):
        for d in list(self.to_partner):
            self.landed(d)
        for copy in list(self.along.values()) + list(self.onward.values()):
            copy.wait_recv()

    def sent_all(self):
        for copies in (self.to_partner, self.along, self.onward):
            for copy in copies.values():
                copy.wait_send()


def enter(place, nf=0, scatters=False, home=False, ring=True, trees=0):
    bar = pltpu.get_barrier_semaphore()
    devices = [{"tp": 1 - place.t}]
    guide = Spread(place, nf, None, 0)
    if scatters:
        devices += [guide.chip(flip(place.q, d)) for d in range(1, place.n)]
    elif ring:
        devices += [place.ring(1)[1], place.ring(-1)[1]]
    if nf:
        devices += [guide.partner()] + [guide.line(e) for e in guide.links]
    devices += [{"fsdp": flip(place.f, e)} for e in range(1, trees)]
    for device in devices:
        pl.semaphore_signal(bar, inc=1, device_id=device, device_id_type=MESH)
    count = len(devices)
    if home:

        @pl.when(place.away == 1)
        def greet():
            pl.semaphore_signal(bar, inc=1, device_id=place.home, device_id_type=MESH)

        count = count + place.away
    pl.semaphore_wait(bar, count)


class Home:
    def __init__(self, place, out, send, recv):
        self.place, self.out = place, out
        self.send, self.recv = send, recv

    @staticmethod
    def semaphores():
        dma = pltpu.SemaphoreType.DMA
        return [dma((2,)), dma((2,))]

    def start(self, rows):
        place, slot = self.place, self.out.at[self.place.t]
        far = pltpu.make_async_remote_copy(
            src_ref=rows, dst_ref=slot, send_sem=self.send.at[0], recv_sem=self.recv.at[0],
            device_id=place.home, device_id_type=MESH,
        )
        near = pltpu.make_async_copy(rows, slot, self.recv.at[0])
        self.far = far
        pl.when(place.away == 1)(far.start)
        pl.when(place.away == 0)(near.start)
        self.near = near

    def land(self, share=True):
        pl.when(self.place.away == 1)(self.far.wait)
        pl.when(self.place.away == 0)(self.near.wait)
        if share:
            slot = self.out.at[self.place.t]
            self.across = remote(slot, slot, self.send.at[1], self.recv.at[1], {"tp": 1 - self.place.t})

    def finish(self):
        self.across.wait()


class TreeMove(Home):
    def __init__(self, place, rows, out, send, recv):
        super().__init__(place, out, send, recv)
        self.rows = rows
        self.slot = out.at[place.f]

    def start(self):
        place = self.place
        target = self.out.at[place.f_hi * 2 + place.c_hi]
        self.far = pltpu.make_async_remote_copy(
            src_ref=self.rows, dst_ref=target, send_sem=self.send.at[0], recv_sem=self.recv.at[0],
            device_id=place.home, device_id_type=MESH,
        )
        self.near = pltpu.make_async_copy(self.rows, target, self.recv.at[0])
        pl.when(place.away == 1)(self.far.start)
        pl.when(place.away == 0)(self.near.start)

    def land(self):
        super().land(False)


class Work:
    def __init__(self, place, nf, rows, scatters, spreads, schedule):
        self.n, self.schedule = place.n, schedule
        self.scatters, self.spreads = [], []
        for blocks, w, sems in scatters:
            self.scatters.append((Spread(place, nf, w, rows), blocks, sems))
        for w, sems in spreads:
            piece = Spread(place, nf, w, rows)
            piece.use(*sems)
            self.spreads.append(piece)

    def at(self, point):
        for what, i, *d in self.schedule[point] if point < len(self.schedule) else ():
            if what == "scatter":
                piece, blocks, sems = self.scatters[i]
                piece.scatter(blocks, *sems)
            elif what == "spread":
                self.spreads[i].spread(*d)
            else:
                self.spreads[i].forward(*d)

    def complete(self, i):
        self.spreads[i].complete()

    def settle(self, done=()):
        for i, piece in enumerate(self.spreads):
            if i not in done:
                piece.complete()
            piece.sent_all()
        for piece, _, _ in self.scatters:
            for d in range(self.n):
                piece.arrived(d)
            piece.scatter_sent()


def parts(n, first, last):
    return range(first * n // 4, last * n // 4)


def moves(what, piece, places):
    return [(what, piece, d) for d in places]


def weights_kernel(
    n, nf, units, share, layers,
    qkv, output, gate_up, down, *refs,
):
    place = Place(n)
    rows, hidden = down.shape[1:]
    w_a, w_g, w_d = refs[:3]
    later = refs[3 : 3 * layers]
    a_first, g_first, d_first, raw_g, raw_d, cut_sems, raw_sems = refs[3 * layers : 3 * layers + 7]
    sems = refs[3 * layers + 7 :]
    a_blocks = [a_first] + list(later[: layers - 1])
    g_blocks = [g_first] + list(later[layers - 1 : 2 * layers - 2])
    d_blocks = [d_first] + list(later[2 * layers - 2 :])
    cuts = []
    for l in range(layers):
        for q in range(n):
            columns = pl.ds(q // share * VD, VD)
            for i in range(4):
                source = qkv.at[l, i, :, columns] if i < 3 else output.at[l, :, columns]
                target = a_blocks[l].at[q, :, pl.ds(i * VD, VD)]
                cuts.append(pltpu.make_async_copy(source, target, cut_sems.at[l, q, i]))
    for copy in cuts[: 4 * n]:
        copy.start()
    raws = []
    for l in range(layers):
        raws.append(pltpu.make_async_copy(gate_up.at[l], raw_g.at[l], raw_sems.at[l, 0]))
        raws.append(pltpu.make_async_copy(down.at[l], raw_d.at[l], raw_sems.at[l, 1]))
    for copy in raws:
        copy.start()
    attention, forward, back = (Spread(place, nf, w, rows) for w in (w_a, w_g, w_d))
    attention.use(*sems[2:8])
    forward.use(*sems[10:16])
    enter(place, nf, True)
    for copy in cuts[: 4 * n]:
        copy.wait()
    attention.scatter(a_first, *sems[:2])
    for copy in cuts[4 * n :]:
        copy.start()

    def fill(target, j, at, value):
        width = min(units, hidden - j * units)
        target[j, :, at : at + width] = value(pl.ds(j * units, width))
        if width < units:
            target[j, :, at + width : at + units] = jnp.zeros((rows, units - width), BF)

    def cut_gate_up(l):
        raws[2 * l].wait()
        for i in range(2):
            for j in range(n):
                fill(g_blocks[l], j, i * units, lambda at, i=i: raw_g[l, :, i, at])

    def cut_down(l):
        raws[2 * l + 1].wait()
        for j in range(n):
            fill(d_blocks[l], j, 0, lambda at: raw_d[l, :, at])

    cut_gate_up(0)
    for d in range(n):
        attention.arrived(d)
        attention.spread(d)
    forward.scatter(g_first, *sems[8:10])
    cut_down(0)
    back.scatter(d_first, *sems[16:18])
    for d in parts(n, 0, 1):
        attention.forward(d)
    for l in range(1, layers):
        cut_gate_up(l)
        cut_down(l)
    for copy in cuts[4 * n :]:
        copy.wait()
    for d in parts(n, 1, 3):
        attention.forward(d)
    for d in range(n):
        forward.arrived(d)
    for d in parts(n, 0, 1):
        forward.spread(d)
    for d in parts(n, 3, 4):
        attention.forward(d)
    attention.complete()
    forward.complete()
    attention.scatter_sent()
    attention.sent_all()
    forward.scatter_sent()
    forward.sent_all()
    for d in range(n):
        back.arrived(d)
    back.scatter_sent()


class Gather:
    def __init__(self, place, x, send_r, recv_r, send_l, recv_l, core_send, core_recv, lean=False):
        self.place, self.x = place, x
        self.sems = (send_r, recv_r, send_l, recv_l, core_send, core_recv)
        self.lean = lean and place.n == 4
        self.right, self.left, self.across = {}, {}, []

    @staticmethod
    def semaphores(n):
        dma = pltpu.SemaphoreType.DMA
        return [dma((n,))] * 4 + [dma((n,))] * 2

    def _make(self, s):
        place, x = self.place, self.x
        send_r, recv_r, send_l, recv_l = self.sems[:4]
        top = x.shape[2] // 2
        last = s == place.n // 2 - 1
        for i in range(1 if last and not self.lean else 2):
            for made, sign, send, recv in ((self.right, 1, send_r, recv_r), (self.left, -1, send_l, recv_l)):
                piece = i if sign > 0 else 1 - i
                at = x.at[place.ring(-sign * s)[0], place.t, pl.ds(piece * top, top)]
                made[s, i] = pltpu.make_async_remote_copy(
                    src_ref=at, dst_ref=at, send_sem=send.at[2 * s + i], recv_sem=recv.at[2 * s + i],
                    device_id=place.ring(sign)[1], device_id_type=MESH,
                )

    def _cross(self, q):
        core_send, core_recv = self.sems[4:]
        slot, at = len(self.across), self.x.at[q, self.place.t]
        other = {"tp": 1 - self.place.t}
        self.across.append(remote(at, at, core_send.at[slot], core_recv.at[slot], other))

    def begin(self):
        for s in range(self.place.n // 2):
            self._make(s)
        for i in range(2):
            self.right[0, i].start()
            self.left[0, i].start()
        self._cross(self.place.q)

    def _hop(self, s):
        last = self.place.n // 2 - 1
        if not self.lean:
            for i in range(1 if s == last else 2):
                for stream in (self.right, self.left):
                    stream[s, i].wait_recv()
                    if s < last - 1 or (s == last - 1 and i == 0):
                        stream[s + 1, i].start()
            return

        def body(even):
            along_ctx, along_fsdp = (self.left, self.right) if even else (self.right, self.left)
            for i in range(2):
                if s == 0:
                    along_ctx[0, i].wait_recv()
                    along_ctx[1, i].start()
                    along_fsdp[0, i].wait_recv()
                else:
                    along_fsdp[1, i].wait_recv()

        when_even(self.place, body)

    def chunks(self):
        place, half = self.place, self.place.n // 2
        self.across[0].wait_recv()
        yield place.q
        for s in range(half):
            self._hop(s)
            arrived = [place.ring(half)[0]] if s == half - 1 else [place.ring(-s - 1)[0], place.ring(s + 1)[0]]
            first = len(self.across)
            for q in arrived:
                self._cross(q)
            for i, q in enumerate(arrived):
                self.across[first + i].wait_recv()
                yield q

    def finish(self):
        last = self.place.n // 2 - 1
        for s in range(last + 1):
            for i in range(2):
                if s < last:
                    self.right[s, i].wait_send()
                    self.left[s, i].wait_send()
                elif not self.lean and i == 0:
                    self.right[s, 0].wait_send()
                    self.left[s, 0].wait_send()
        if self.lean:

            def body(even):
                for i in range(2):
                    (self.left if even else self.right)[1, i].wait_send()

            when_even(self.place, body)
        for copy in self.across:
            copy.wait_send()


def by_rows(count, body, step=16):
    def one(i, carry):
        body(pl.ds(pl.multiple_of(i * step, step), step))
        return carry

    lax.fori_loop(0, count // step, one, 0)


class Reduce:
    def __init__(self, place, p, from_core, in_r, in_l, send_r, recv_r, send_l, recv_l, core_send, core_recv, lean=False):
        self.place, self.p, self.from_core, self.in_r, self.in_l = place, p, from_core, in_r, in_l
        self.sems = (send_r, recv_r, send_l, recv_l, core_send, core_recv)
        self.lean = lean and place.n == 4
        half = place.n // 2
        self.order = [half] + [k for j in range(half - 1, 0, -1) for k in (j, -j)] + [0]
        self.chips = {k: place.ring(k)[0] for k in self.order}
        self.across, self.copies = {}, {}
        for sign in (1, -1):
            for s in range(half):
                for piece in range(2):
                    if s or self.lean or piece == (sign < 0):
                        self._copy(sign, s, piece)

    @staticmethod
    def scratch(n, rows, width):
        dma = pltpu.SemaphoreType.DMA
        wide = [pltpu.VMEM((n, rows, width), BF)] + [pltpu.VMEM((n // 2, rows, width), BF)] * 2
        return wide + [dma((n // 2, 2))] * 4 + [dma((n,))] * 2

    def offer(self, k):
        core_send, core_recv = self.sems[4:]
        slot, q, t = len(self.across), self.chips[k], self.place.t
        self.across[k] = remote(
            self.p.at[q, 1 - t], self.from_core.at[q], core_send.at[slot], core_recv.at[slot], {"tp": 1 - t}
        )

    def _local(self, k, at):
        q = self.chips[k]
        return self.p[q, self.place.t, at].astype(F32) + self.from_core[q, at].astype(F32)

    def _add(self, k, piece, extra=None):
        top = self.p.shape[2] // 2

        def body(at):
            whole = pl.ds(pl.multiple_of(piece * top + at.start, 16), at.size)
            total = self._local(k, whole)
            if extra is not None:
                total = total + extra[whole].astype(F32)
            self.from_core[self.chips[k], whole] = total.astype(BF)

        by_rows(top, body)

    def _copy(self, sign, s, piece):
        if (sign, s, piece) not in self.copies:
            place, top = self.place, self.p.shape[2] // 2
            send, recv = self.sems[:2] if sign > 0 else self.sems[2:4]
            target = self.in_r if sign > 0 else self.in_l
            k = place.n // 2 - s
            rows = pl.ds(piece * top, top)
            self.copies[sign, s, piece] = pltpu.make_async_remote_copy(
                src_ref=self.from_core.at[self.chips[sign * k if s else k], rows], dst_ref=target.at[s, rows],
                send_sem=send.at[s, piece], recv_sem=recv.at[s, piece],
                device_id=place.ring(sign)[1], device_id_type=MESH,
            )
        return self.copies[sign, s, piece]

    def far(self):
        half = self.place.n // 2
        self.across[half].wait_recv()
        self._add(half, 0)
        self._add(half, 1)
        if self.lean:
            self.across[1].wait_recv()
            self.across[-1].wait_recv()

            def body(even):
                sign = -1 if even else 1
                for piece in range(2):
                    self._copy(sign, 0, piece).start()
                for piece in range(2):
                    self._add(sign, piece)
                    self._copy(sign, 1, piece).start()

            when_even(self.place, body)
            return
        self._copy(1, 0, 0).start()
        self._copy(-1, 0, 1).start()
        if half > 1:
            k = half - 1
            for sign, piece in ((1, 1), (-1, 0)):
                self.across[sign * k].wait_recv()
                self._add(sign * k, piece)
                self._copy(sign, 1, piece).start()

    def near(self, s):
        half = self.place.n // 2
        k = half - s
        if self.lean:

            def body(even):
                sign = 1 if even else -1
                for piece in range(2):
                    self._copy(sign, 0, piece).wait_recv()
                    self._add(sign, piece, (self.in_r if even else self.in_l).at[0])
                    self._copy(sign, 1, piece).start()

            when_even(self.place, body)
            return
        if s > 1:
            self.across[k].wait_recv()
            self.across[-k].wait_recv()
        for sign, first, held in ((1, 0, self.in_r), (-1, 1, self.in_l)):
            for piece in (first,) if s == 1 else (first, 1 - first):
                self._copy(sign, s - 1, piece).wait_recv()
                self._add(sign * k, piece, held.at[s - 1])
                self._copy(sign, s, piece).start()

    def end(self, use):
        half = self.place.n // 2
        self.across[0].wait_recv()
        for sign in (1, -1):
            for piece in range(2):
                self._copy(sign, half - 1, piece).wait_recv()

        def body(at):
            use(at, self._local(0, at) + self.in_r[half - 1, at].astype(F32) + self.in_l[half - 1, at].astype(F32))

        by_rows(self.p.shape[2], body)

    def finish(self):
        half = self.place.n // 2
        if self.lean:

            def body(even):
                for piece in range(2):
                    self._copy(-1 if even else 1, 0, piece).wait_send()

            when_even(self.place, body)
        else:
            self._copy(1, 0, 0).wait_send()
            self._copy(-1, 0, 1).wait_send()
        for s in range(1, half):
            for sign in (1, -1):
                for piece in range(2):
                    self._copy(sign, s, piece).wait_send()
        for copy in self.across.values():
            copy.wait_send()

    def run(self, use, before=None, offered=False):
        if not offered:
            for k in self.order:
                self.offer(k)
            self.far()
        for s in range(1, self.place.n // 2):
            self.near(s)
        if before is not None:
            before()
        self.end(use)


def mm(a, b):
    return jnp.dot(a, b, preferred_element_type=F32)


def mm_t(a, b):
    return lax.dot_general(a, b, (((1,), (1,)), ((), ())), preferred_element_type=F32)


def t_mm(a, b):
    return lax.dot_general(a, b, (((0,), (0,)), ((), ())), preferred_element_type=F32)


def rms_scale(values):
    return lax.rsqrt(jnp.mean(values * values, axis=-1, keepdims=True) + EPSILON)


def norm_back(grad_normed, inputs, scale_rows, gain):
    unit = inputs * scale_rows
    scaled = grad_normed * gain
    return scale_rows * (scaled - unit * jnp.mean(scaled * unit, axis=-1, keepdims=True))


def tiles(count, width, body):
    def one(j, carry):
        body(pl.ds(pl.multiple_of(j * width, width), width))
        return carry

    lax.fori_loop(0, count // width, one, 0)


def tile_of(count):
    return 256 if count % 256 == 0 else 128


def turn(v, cosine, sine):
    return v * cosine + pltpu.roll(v, HD // 2, 1) * sine


def block_diagonal(out, parts, rank, width):
    out[...] = jnp.zeros(out.shape, out.dtype)
    for i in range(parts[1]):
        out[i * rank : (i + 1) * rank, i * width : (i + 1) * width] = parts[0][i * rank : (i + 1) * rank, :]


def write_norm(x_rows, source, gain):
    def body(at):
        v = source[at].astype(F32)
        x_rows[at] = (v * rms_scale(v) * gain[...]).astype(BF)

    by_rows(source.shape[0], body)


ROW_BLOCK = 128
KEY_STEP = 256


def row_blocks(tree, body):
    for j in range(tree // KEY_STEP):

        def one(i, carry, j=j):
            body(pl.ds(pl.multiple_of(j * KEY_STEP + i * ROW_BLOCK, ROW_BLOCK), ROW_BLOCK), (j + 1) * KEY_STEP)
            return carry

        lax.fori_loop(0, KEY_STEP // ROW_BLOCK, one, 0)


def seen(rows, keys, query_bits, key_bits):
    shared = (query_bits[rows] & key_bits[:, :keys]) != 0
    i = rows.start + lax.broadcasted_iota(jnp.int32, (ROW_BLOCK, keys), 0)
    j = lax.broadcasted_iota(jnp.int32, (ROW_BLOCK, keys), 1)
    return shared & (j <= i)


def attention_forward(
    n, nf, layer, part, rank, lean, plan,
    residual, gain, w_hbm, a_model, a_head, cosine, sine, query_bits, key_bits, lam, *refs, pace,
):
    jobs, refs = plan.split(refs)
    (middle, x_hbm, queries, keys, values, small, log_total, mixed, headed, side,
     x, p, w, raised, copy_sems, *sems) = refs
    place = Place(n)
    chip_rows, width = 2 * x_hbm.shape[2], x_hbm.shape[3]
    tree = n * chip_rows
    load = pltpu.make_async_copy(w_hbm, w, copy_sems.at[0])
    load.start()
    gather, reduce = Gather(place, x, *sems[:6], lean=lean), Reduce(place, p, *sems[6:], lean=lean)
    write_norm(x.at[place.q, place.t], residual, gain)
    block_diagonal(raised, (a_head[rank : 4 * rank], 3), rank, VD)
    work = plan.work(place, nf, jobs)
    enter(place, nf, bool(plan.scatters))
    gather.begin()
    work.at(0)
    pace.ready()
    load.wait()

    def project(q):
        rows = pl.ds(pl.multiple_of(q * chip_rows, chip_rows), chip_rows)
        v = x[q].reshape(chip_rows, width)
        low = mm_t(v, a_model[: 3 * rank]).astype(BF)
        small[rows] = low
        for i, out in enumerate((queries, keys, values)):
            at = slice(i * VD, (i + 1) * VD)
            made = mm(v, w[:, at]) + ADAPTER_SCALE * mm(low, raised[:, at])
            if i < 2:
                for c in range(2):
                    half = slice(c * HD, (c + 1) * HD)
                    out[rows, half] = turn(made[:, half], cosine[rows], sine[rows]).astype(BF)
            else:
                out[rows] = made.astype(BF)

    for q in gather.chunks():
        project(q)
    work.at(1)
    keep = pltpu.make_async_copy(x, x_hbm, copy_sems.at[1])
    keep.start()
    score_scale = HD ** (-0.5)
    weight = lam[...]

    def attend(rows, count):
        visible = seen(rows, count, query_bits, key_bits)
        both = []
        for c in range(2):
            at = slice(c * HD, (c + 1) * HD)
            scores = mm_t(queries[rows, at], keys[:count, at]) * score_scale
            scores = jnp.where(visible, scores, NEGATIVE_BIG)
            top = jnp.max(scores, axis=-1, keepdims=True)
            raw = jnp.exp(scores - top)
            total = jnp.sum(raw, axis=-1, keepdims=True)
            log_total[rows, c : c + 1] = top + jnp.log(total)
            both.append(raw * (1.0 / total))
        mix = mm((both[0] - weight * both[1]).astype(BF), values[:count])
        mixed[rows] = mix.astype(BF)
        head = (mix * rms_scale(mix) * keep_factor(layer)).astype(BF)
        headed[rows] = head
        side[rows] = mm_t(head, a_head[:rank]).astype(BF)

    row_blocks(tree, attend)
    pace.flush()
    work.at(2)

    for k in reduce.order:
        q = reduce.chips[k]
        rows = pl.ds(pl.multiple_of(q * chip_rows, chip_rows), chip_rows)
        head, low = headed[rows], side[rows]

        def out_tile(at):
            made = mm_t(head, w[at, 3 * VD :]) + ADAPTER_SCALE * mm(low, a_model[9 * rank : 10 * rank, at])
            p[q, :, :, at] = (made * part).astype(BF).reshape(2, chip_rows // 2, at.size)

        tiles(width, 512, out_tile)
        reduce.offer(k)
        if k == reduce.order[2]:
            reduce.far()
    work.at(3)
    for s in range(1, n // 2):
        reduce.near(s)
    work.at(4)

    def use(at, total):
        middle[at] = residual[at].astype(F32) + total

    reduce.end(use)
    work.at(5)
    keep.wait()
    gather.finish()
    reduce.finish()
    work.settle()


def ffn_forward(
    n, nf, units, rank, last, plan,
    residual, gain, w_hbm, a_model, e_model, *refs, pace,
):
    place = Place(n)
    if last:
        cotangent, *refs = refs
    jobs, refs = plan.split(refs)
    if last:
        all_refs = refs
        next_hbm, *refs, next_x = refs[:-6]
        next_gather = Gather(place, next_x, *all_refs[-6:])
    (following, x_hbm, gates, ups, hidden, small, side,
     x, p, w, raised, copy_sems, *sems) = refs
    chip_rows, width = 2 * x_hbm.shape[2], x_hbm.shape[3]
    tree = n * chip_rows
    load = pltpu.make_async_copy(w_hbm, w.at[:, pl.ds(0, 2 * units)], copy_sems.at[0])
    load.start()
    gather, reduce = Gather(place, x, *sems[:6], lean=not last), Reduce(place, p, *sems[6:], lean=not last)
    write_norm(x.at[place.q, place.t], residual, gain)
    block_diagonal(raised, (e_model, 2), rank, units)
    work = plan.work(place, nf, jobs)
    enter(place, nf, bool(plan.scatters))
    gather.begin()
    work.at(0)
    pace.ready()
    load.wait()
    step = tile_of(units)

    for number, q in enumerate(gather.chunks()):
        if number == n - 1:
            work.at(1)
        rows = pl.ds(pl.multiple_of(q * chip_rows, chip_rows), chip_rows)
        v = x[q].reshape(chip_rows, width)
        low = mm_t(v, a_model[4 * rank : 6 * rank]).astype(BF)
        small[rows] = low

        def unit_tile(at):
            up_at = pl.ds(pl.multiple_of(units + at.start, step), step)
            gate = mm(v, w[:, at]) + ADAPTER_SCALE * mm(low, raised[:, at])
            up = mm(v, w[:, up_at]) + ADAPTER_SCALE * mm(low, raised[:, up_at])
            gates[rows, at] = gate.astype(BF)
            ups[rows, at] = up.astype(BF)
            hidden[rows, at] = (gate / (1.0 + jnp.exp(-gate)) * up).astype(BF)

        tiles(units, step, unit_tile)

    pace.flush()
    if last:
        next_x[place.q, place.t] = cotangent[...]
        next_gather.begin()
    work.at(2)
    keep = pltpu.make_async_copy(x, x_hbm, copy_sems.at[1])
    keep.start()

    if last:
        for _ in next_gather.chunks():
            pass
        keep_next = pltpu.make_async_copy(next_x, next_hbm, copy_sems.at[2])
        keep_next.start()
    work.complete(0)
    load = pltpu.make_async_copy(plan.late(jobs), w.at[:, pl.ds(2 * units, units)], copy_sems.at[0])
    load.start()
    load.wait()
    for k in reduce.order:
        q = reduce.chips[k]
        rows = pl.ds(pl.multiple_of(q * chip_rows, chip_rows), chip_rows)
        made_hidden = hidden[rows]
        low = mm_t(made_hidden, e_model[2 * rank : 3 * rank]).astype(BF)
        side[rows] = low

        def out_tile(at):
            made = mm_t(made_hidden, w[at, 2 * units :])
            made = made + ADAPTER_SCALE * mm(low, a_model[10 * rank : 11 * rank, at])
            p[q, :, :, at] = made.astype(BF).reshape(2, chip_rows // 2, at.size)

        tiles(width, 512, out_tile)
        reduce.offer(k)
        if k == reduce.order[2]:
            reduce.far()
    work.at(3)
    for s in range(1, n // 2):
        reduce.near(s)
    work.at(4)

    def use(at, total):
        following[at] = residual[at] + total

    reduce.end(use)
    work.at(5)
    keep.wait()
    if last:
        keep_next.wait()
        next_gather.finish()
    gather.finish()
    reduce.finish()
    work.settle((0,))


def ffn_backward(
    n, units, rank, carry,
    grad, middle, gain, w_hbm, w_down_hbm, a_model, e_model, x_hbm, gates, ups, hidden, small, side, *refs, pace,
):
    if carry:
        final, gathered, final_out, *refs = refs
        *refs, final_rows, home_send, home_recv = refs
    (grad_out, grad_up_down, grad_in, grad_units,
     x, p, w, kept, dgu, dsmall, dside, raised, copy_sems, *sems) = refs
    place = Place(n)
    chip_rows, width = 2 * x_hbm.shape[2], x_hbm.shape[3]
    tree = n * chip_rows
    load = pltpu.make_async_copy(w_hbm, w.at[:, pl.ds(0, 2 * units)], copy_sems.at[0])
    load.start()
    load_down = pltpu.make_async_copy(w_down_hbm, w.at[:, pl.ds(2 * units, units)], copy_sems.at[2])
    load_down.start()
    fetch = pltpu.make_async_copy(x_hbm, kept, copy_sems.at[1])
    fetch.start()
    gather, reduce = Gather(place, x, *sems[:6]), Reduce(place, p, *sems[6:])

    if carry:
        come = pltpu.make_async_copy(gathered, x, copy_sems.at[3])
        come.start()
    else:

        def own(at):
            x[place.q, place.t, at] = grad[at].astype(BF)

        by_rows(grad.shape[0], own)
    block_diagonal(raised, (e_model, 2), rank, units)
    if carry:

        def last_rows(at):
            final_rows[at] = final[at].astype(BF)

        by_rows(final.shape[0], last_rows)
    enter(place, home=carry)
    if not carry:
        gather.begin()
    else:
        home = Home(place, final_out, home_send, home_recv)
        home.start(final_rows)
    pace.ready()
    load.wait()
    load_down.wait()
    step = tile_of(units)

    if carry:
        come.wait()
    for q in list(reduce.chips.values()) if carry else gather.chunks():
        rows = pl.ds(pl.multiple_of(q * chip_rows, chip_rows), chip_rows)
        v = x[q].reshape(chip_rows, width)
        low = (ADAPTER_SCALE * mm_t(v, a_model[10 * rank : 11 * rank])).astype(BF)
        dside[rows] = low

        def unit_tile(at):
            up_at = pl.ds(pl.multiple_of(units + at.start, step), step)
            down_at = pl.ds(pl.multiple_of(2 * units + at.start, step), step)
            dhidden = mm(v, w[:, down_at]) + mm(low, e_model[2 * rank : 3 * rank, at])
            gate, up = gates[rows, at].astype(F32), ups[rows, at].astype(F32)
            sig = 1.0 / (1.0 + jnp.exp(-gate))
            dgu[rows, at] = (dhidden * up * sig * (1.0 + gate * (1.0 - sig))).astype(BF)
            dgu[rows, up_at] = (dhidden * gate * sig).astype(BF)

        tiles(units, step, unit_tile)
        back = dgu[rows]
        low_back = (ADAPTER_SCALE * mm_t(back, raised[...])).astype(BF)
        dsmall[rows] = low_back

        def out_tile(at):
            made = mm_t(back, w[at, : 2 * units]) + mm(low_back, a_model[4 * rank : 6 * rank, at])
            p[q, :, :, at] = made.astype(BF).reshape(2, chip_rows // 2, at.size)

        tiles(width, 512, out_tile)
        if carry:
            k = reduce.order[len(reduce.across)]
            reduce.offer(k)
            if k == reduce.order[2]:
                reduce.far()

    def use(at, total):
        inputs = middle[at]
        grad_out[at] = grad[at].astype(F32) + norm_back(total, inputs, rms_scale(inputs), gain[...])

    def adapters():
        fetch.wait()

        def model_tile(at):
            flat = x[:, :, :, at].reshape(tree, at.size)
            grad_up_down[:, at] = (ADAPTER_SCALE * t_mm(side[...], flat)).astype(BF)
            flat = kept[:, :, :, at].reshape(tree, at.size)
            grad_in[:, at] = t_mm(dsmall[...], flat).astype(BF)

        tiles(width, 256, model_tile)

        def unit_tile(at):
            up_at = pl.ds(pl.multiple_of(units + at.start, step), step)
            grad_units[:rank, at] = (ADAPTER_SCALE * t_mm(small[...], dgu[:, at])[:rank]).astype(BF)
            grad_units[rank : 2 * rank, at] = (ADAPTER_SCALE * t_mm(small[...], dgu[:, up_at])[rank:]).astype(BF)
            grad_units[2 * rank : 3 * rank, at] = t_mm(dside[...], hidden[:, at]).astype(BF)
            grad_units[3 * rank :, at] = jnp.zeros((rank, at.size), BF)

        tiles(units, step, unit_tile)

    reduce.run(use, adapters, carry)
    if not carry:
        gather.finish()
    reduce.finish()
    if carry:
        home.land()
        home.finish()


def attention_backward(
    n, layer, share, heads_tp, rank,
    grad, residual, gain, w_hbm, a_model, a_head, cosine, sine, query_bits, key_bits, lam,
    x_hbm, queries, keys, values, small, log_total, mixed, headed, side,
    grad_up_down, grad_ffn_in, grad_units,
    grad_out, own_sum, all_units,
    x, p, w, dmixed, dq, dk, dv, dprojected, dsmall, dside, raised, grad_a9, p_own, copy_sems, *sems, pace,
):
    place = Place(n)
    part = 1.0 / share
    chip_rows, width = 2 * x_hbm.shape[2], x_hbm.shape[3]
    tree = n * chip_rows
    load = pltpu.make_async_copy(w_hbm, w, copy_sems.at[0])
    load.start()
    gather, reduce = Gather(place, x, *sems[:6]), Reduce(place, p, *sems[6:15])
    gather_units, reduce_own = Gather(place, all_units, *sems[15:21]), Reduce(place, p_own, *sems[21:])

    def own(at):
        x[place.q, place.t, at] = grad[at].astype(BF)

    by_rows(grad.shape[0], own)
    block_diagonal(raised, (a_head[rank : 4 * rank], 3), rank, VD)
    all_units[place.q, place.t] = grad_units[...]
    enter(place)
    gather.begin()
    gather_units.begin()
    dk[...] = jnp.zeros(dk.shape, F32)
    dv[...] = jnp.zeros(dv.shape, F32)
    pace.ready()
    load.wait()

    score_scale = HD ** (-0.5)
    weight = lam[...]

    def attend(rows, count):
        visible = seen(rows, count, query_bits, key_bits)
        dmix = dmixed[rows]
        dweights = mm_t(dmix, values[:count])
        both = []
        for c in range(2):
            at = slice(c * HD, (c + 1) * HD)
            scores = mm_t(queries[rows, at], keys[:count, at]) * score_scale
            probability = jnp.exp(jnp.where(visible, scores - log_total[rows, c : c + 1], NEGATIVE_BIG))
            both.append(probability)
            weighted = probability * dweights
            dscores = weighted - probability * jnp.sum(weighted, axis=-1, keepdims=True)
            dscores = (dscores * -weight if c else dscores).astype(BF)
            dq[rows, at] = mm(dscores, keys[:count, at])
            dk[:count, at] += t_mm(dscores, queries[rows, at])
        dv[:count] += t_mm((both[0] - weight * both[1]).astype(BF), dmix)

    for q in gather.chunks():
        rows = pl.ds(pl.multiple_of(q * chip_rows, chip_rows), chip_rows)
        v = x[q].reshape(chip_rows, width)
        low = (ADAPTER_SCALE * mm_t(v, a_model[9 * rank : 10 * rank])).astype(BF)
        dside[rows] = low
        dheaded = mm(v, w[:, 3 * VD :]) + mm(low, a_head[:rank])
        inputs = mixed[rows].astype(F32)
        dmixed[rows] = norm_back(dheaded, inputs, rms_scale(inputs), keep_factor(layer)).astype(BF)

        def block(i, carry, q=q):
            attend(pl.ds(pl.multiple_of(q * chip_rows + i * ROW_BLOCK, ROW_BLOCK), ROW_BLOCK), tree)
            return carry

        lax.fori_loop(0, chip_rows // ROW_BLOCK, block, 0)

    def out_gradient(at):
        flat = x[:, :, :, at].reshape(tree, at.size)
        grad_a9[:, at] = (ADAPTER_SCALE * part * t_mm(side[...], flat)).astype(BF)

    tiles(width, 256, out_gradient)
    gather.finish()
    fetch = pltpu.make_async_copy(x_hbm, x, copy_sems.at[1])
    fetch.start()

    fetch.wait()
    for _ in gather_units.chunks():
        pass

    def project(i, carry):
        rows = pl.ds(pl.multiple_of(i * chip_rows, chip_rows), chip_rows)
        for j, source in enumerate((dq, dk)):
            for c in range(2):
                half = slice(c * HD, (c + 1) * HD)
                turned = turn(source[rows, half] * score_scale, cosine[rows], -sine[rows])
                dprojected[rows, j * VD + c * HD : j * VD + (c + 1) * HD] = turned.astype(BF)
        dprojected[rows, 2 * VD :] = dv[rows].astype(BF)
        dsmall[rows] = (ADAPTER_SCALE * mm_t(dprojected[rows], raised[...])).astype(BF)
        return carry

    lax.fori_loop(0, n, project, 0)

    def send_part(k):
        q = reduce.chips[k]
        rows = pl.ds(pl.multiple_of(q * chip_rows, chip_rows), chip_rows)
        back, low_back = dprojected[rows], dsmall[rows]

        def out_tile(at):
            made = mm_t(back, w[at, : 3 * VD]) + mm(low_back, a_model[: 3 * rank, at])
            p[q, :, :, at] = (made * part).astype(BF).reshape(2, chip_rows // 2, at.size)

        tiles(width, 512, out_tile)
        reduce.offer(k)

    for k in reduce.order[:3]:
        send_part(k)
    reduce.far()

    block = width // (2 * n)

    def full_tile(jp, carry):
        at = pl.ds(pl.multiple_of(jp * block, block), block)
        q, t = jp // 2, jp % 2
        flat = x[:, :, :, at].reshape(tree, block)
        p_own[q, t, : 3 * rank] = (part * t_mm(dsmall[...], flat)).astype(BF)
        p_own[q, t, 4 * rank : 6 * rank] = grad_ffn_in[:, at]
        p_own[q, t, 9 * rank : 10 * rank] = grad_a9[:, at]
        p_own[q, t, 10 * rank : 11 * rank] = grad_up_down[:, at]
        p_own[q, t, 11 * rank :] = jnp.zeros((rank, block), BF)
        return carry

    lax.fori_loop(0, 2 * n, full_tile, 0)
    of_head = [part * t_mm(dside[...], headed[...])]
    for i in range(3):
        made = t_mm(small[...], dprojected[:, i * VD : (i + 1) * VD])[i * rank : (i + 1) * rank]
        of_head.append(ADAPTER_SCALE * part * made)
    head = place.t * heads_tp + place.q // share
    for j in range(2 * n):
        start = j * block % VD
        own = (head == j * block // VD).astype(F32)
        for i, k in enumerate((3, 6, 7, 8)):
            made = of_head[i][:, start : start + block] * own
            p_own[j // 2, j % 2, k * rank : (k + 1) * rank] = made.astype(BF)

    for k in reduce.order[3:]:
        send_part(k)
    for k in reduce.order:
        reduce_own.offer(k)
    reduce_own.far()
    for s in range(1, n // 2):
        reduce.near(s)
        reduce_own.near(s)

    def use_own(at, total):
        own_sum[at] = total.astype(BF)

    def use(at, total):
        inputs = residual[at].astype(F32)
        grad_out[at] = grad[at].astype(F32) + norm_back(total, inputs, rms_scale(inputs), gain[...])

    reduce.end(use)
    reduce_own.end(use_own)
    gather_units.finish()
    reduce.finish()
    reduce_own.finish()


def finish_kernel(
    n, nf, layers, rank,
    grad, own_sums, own_units, slot,
    tokens_grad, model_grad, hidden_grad,
    rows_out, landed, sent_sums, all_sums, all_units, home_send, home_recv, tree_send, tree_recv,
):
    place = Place(n)
    own = model_grad.shape[2]
    tall = own_sums.shape[0]

    def cut(at):
        rows_out[at] = grad[at].astype(BF)

    by_rows(grad.shape[0], cut)
    sent_sums[...] = own_sums[...]
    sent_sums[tall - rank :] = jnp.broadcast_to(slot[...], (rank, own_sums.shape[1])).astype(BF)
    enter(place, home=True, ring=False, trees=nf)
    moves = [Home(place, landed, home_send.at[0], home_recv.at[0])]
    away = {}
    for i, (source, target) in enumerate(((sent_sums, all_sums), (own_units, all_units))):
        away[i] = TreeMove(place, source, target, home_send.at[i + 1], home_recv.at[i + 1])
        away[i].start()
    copies = []
    for i in range(2):
        away[i].land()
        if i == 1:
            moves[0].start(rows_out)
        slot_of = away[i].slot
        for e in range(1, nf):
            copies.append(
                remote(slot_of, slot_of, tree_send.at[i, e], tree_recv.at[i, e], {"fsdp": flip(place.f, e)})
            )
    moves[0].land()
    for copy in copies:
        copy.wait_recv()
    block, units = all_sums.shape[2], all_units.shape[2]
    per_layer = tall // layers
    for b in range(own):
        number = (place.f * own + b).astype(F32)
        keeps = [
            (all_sums[f, tall - rank : tall - rank + 1, :1].astype(F32) == number).astype(F32) for f in range(nf)
        ]
        for l in range(layers):
            for k in range(11):
                at = slice(l * per_layer + k * rank, l * per_layer + (k + 1) * rank)
                model_grad[l, k, b] = sum(keeps[f] * all_sums[f, at].astype(F32) for f in range(nf))
            for k in range(3):
                at = slice((l * 3 + k) * rank, (l * 3 + k + 1) * rank)
                hidden_grad[l, k, b] = sum(keeps[f] * all_units[f, at].astype(F32) for f in range(nf))
    moves[0].finish()
    for core in range(2):

        def widen(at, core=core):
            rows = landed.shape[1]
            tokens_grad[pl.ds(pl.multiple_of(core * rows + at.start, 16), at.size)] = landed[core, at].astype(F32)

        by_rows(landed.shape[1], widen)
    for copy in copies:
        copy.wait_send()


class Plan:
    def __init__(self, n, nf, rows, scatters, spreads, schedule):
        self.n, self.nf, self.rows, self.schedule = n, nf, rows, schedule
        self.scatters, self.spreads = scatters, spreads

    def ins(self):
        return [(blocks, True) for blocks, _ in self.scatters] + [(w, True) for w in self.spreads]

    def outs(self):
        made = [(shape, BF, True) for _, shape in self.scatters]
        return made + [(w.shape, BF, True) for w in self.spreads]

    def semaphores(self):
        made = Spread.scatter_semaphores(self.n) * len(self.scatters)
        return made + Spread.spread_semaphores(self.n, self.nf) * len(self.spreads)

    def split(self, refs):
        a, b = len(self.scatters), len(self.spreads)
        count = 2 * a + 6 * b
        refs = list(refs)
        taken = refs[: a + b], refs[a + b : 2 * (a + b)], refs[len(refs) - count :]
        return taken, refs[2 * (a + b) : len(refs) - count]

    def work(self, place, nf, jobs):
        a, b = len(self.scatters), len(self.spreads)
        ins, outs, sems = jobs
        scatters = [(ins[i], outs[i], sems[2 * i : 2 * i + 2]) for i in range(a)]
        spreads = [(outs[a + i], sems[2 * a + 6 * i : 2 * a + 6 * i + 6]) for i in range(b)]
        return Work(place, nf, self.rows, scatters, spreads, self.schedule)

    def late(self, jobs):
        return jobs[1][len(self.scatters)]


class Pace:
    def __init__(self, loads, stores):
        self.loads, self.stores = loads, stores
        for copy in loads:
            copy.start()

    def ready(self):
        for copy in self.loads:
            copy.wait()

    def flush(self):
        for copy in self.stores:
            copy.start()

    def end(self):
        for copy in self.stores:
            copy.wait()


def call(kernel, collective, ins, outs, scratch, plan=None):
    spec = lambda hbm: pl.BlockSpec(memory_space=pl.ANY if hbm else pltpu.VMEM)
    aliases = {}
    if plan is not None:
        first_in, count = len(ins), len(plan.scatters)
        aliases = {first_in + count + i: count + i for i in range(len(plan.spreads))}
        ins, outs, scratch = ins + plan.ins(), plan.outs() + outs, scratch + plan.semaphores()
    late_in = [i for i, (_, hbm) in enumerate(ins) if hbm == "paced"]
    late_out = [i for i, (_, _, hbm) in enumerate(outs) if hbm == "paced"]
    extra = [pltpu.VMEM(ins[i][0].shape, ins[i][0].dtype) for i in late_in]
    extra += [pltpu.VMEM(outs[i][0], outs[i][1]) for i in late_out]
    if late_in or late_out:
        extra.append(pltpu.SemaphoreType.DMA((len(late_in) + len(late_out),)))

        def paced(*refs):
            refs, held = list(refs[: -len(extra)]), refs[-len(extra) :]
            loads, stores = [], []
            for slot, i in enumerate(late_in):
                loads.append(pltpu.make_async_copy(refs[i], held[slot], held[-1].at[slot]))
                refs[i] = held[slot]
            for slot, i in enumerate(late_out, len(late_in)):
                stores.append(pltpu.make_async_copy(held[slot], refs[len(ins) + i], held[-1].at[slot]))
                refs[len(ins) + i] = held[slot]
            pace = Pace(loads, stores)
            kernel(*refs, pace=pace)
            pace.end()

        body = paced
    else:
        body = kernel
    made = pl.pallas_call(
        body,
        out_shape=[jax.ShapeDtypeStruct(shape, kind) for shape, kind, _ in outs],
        in_specs=[spec(hbm) for _, hbm in ins],
        out_specs=[spec(hbm) for _, _, hbm in outs],
        scratch_shapes=scratch + extra,
        input_output_aliases=aliases,
        compiler_params=pltpu.CompilerParams(
            collective_id=collective, has_side_effects=True, vmem_limit_bytes=62 << 20
        ),
    )(*[array for array, _ in ins])
    return list(made)


def line_bits(parent_row, seg):
    number = jnp.arange(NSEG)
    one = lambda x: lax.shift_left(jnp.ones_like(x), x)
    grand = jnp.sum(jnp.where(parent_row[:, None] == number[None, :], parent_row[None, :], 0), axis=1)
    line = one(number) | one(parent_row) | one(grand)
    mine = jnp.sum(jnp.where(seg[:, None] == number[None, :], line[None, :], 0), axis=1)
    return mine, one(seg)


def keep_factor(layer):
    return 0.2 + 0.6 * math.exp(-0.3 * layer)


def chips_of(nf, nc):
    h = nc // 2
    for f in range(nf):
        for c in range(nc):
            yield f * nc + c, (f // 2, f % 2, c // h, c % h)


def permute(x, nf, nc, target):
    h = nc // 2
    pairs = []
    for source, spot in chips_of(nf, nc):
        f_hi, f_lo, c_hi, c_lo = target(*spot)
        pairs.append((source, (f_hi * 2 + f_lo) * nc + c_hi * h + c_lo))
    return lax.ppermute(x, ("fsdp", "ctx"), pairs)


def swap_trees(x, nf, nc):
    return permute(x, nf, nc, lambda f_hi, f_lo, c_hi, c_lo: (f_hi, c_hi, f_lo, c_lo))


def shards(
    nf,
    nc,
    tokens,
    cotangent,
    segments,
    depths,
    parents,
    tree_adapter_index,
    layer_norm_gains,
    difference_lambda,
    query_key_value_weight,
    output_weight,
    gate_up_weight,
    down_weight,
    adapter_model_factors,
    adapter_hidden_factors,
):
    n = nc
    place = Place(n)
    q, t = place.q, place.t
    tokens_dev, width = tokens.shape
    rows = tokens_dev // 2
    tree = tokens_dev * n
    layers, weight_rows = query_key_value_weight.shape[:2]
    heads_tp = difference_lambda.shape[1]
    share = max(1, n // heads_tp)
    head = q // share
    hidden_tp = down_weight.shape[2]
    units = (hidden_tp + n * 128 - 1) // (n * 128) * 128
    rank, adapters = adapter_model_factors.shape[3], adapter_model_factors.shape[2]
    h = n // 2

    notes = jnp.concatenate([segments, depths, parents[0], tree_adapter_index])
    order = jnp.arange(n)
    of_tree = jnp.zeros((n, notes.shape[0]), jnp.int32)
    for d in range(n):

        def hand_out(f_hi, f_lo, c_hi, c_lo, d=d):
            to = (c_hi * (n // 2) + c_lo) ^ d
            return f_hi, to // (n // 2), f_lo, to % (n // 2)

        part_of_tree = permute(notes, nf, nc, hand_out)
        of_tree = of_tree + jnp.where(order[:, None] == flip(q, d), part_of_tree[None], 0)
    seg, dep = of_tree[:, :tokens_dev].reshape(tree), of_tree[:, tokens_dev : 2 * tokens_dev].reshape(tree)
    parent_row, slot = of_tree[0, 2 * tokens_dev : 2 * tokens_dev + NSEG], of_tree[0, 2 * tokens_dev + NSEG]
    own_tokens = lax.dynamic_slice_in_dim(tokens, t * rows, rows, 0)
    own_cotangent = lax.dynamic_slice_in_dim(cotangent, t * rows, rows, 0)
    residual = swap_trees(own_tokens, nf, nc)
    own_cotangent = swap_trees(own_cotangent, nf, nc)

    query_bits, key_bits = line_bits(parent_row, seg)
    query_bits, key_bits = query_bits[:, None], key_bits[None, :]
    frequency = 10000.0 ** (-jnp.arange(HD // 2).astype(F32) / (HD // 2))
    angles = dep.astype(F32)[:, None] * frequency[None, :]
    cosine, sine = jnp.cos(angles), jnp.sin(angles)
    cosine = jnp.concatenate([cosine, cosine], axis=1)
    sine = jnp.concatenate([-sine, sine], axis=1)
    gains = layer_norm_gains

    a_all = lax.dynamic_index_in_dim(adapter_model_factors, slot, 2, keepdims=False)
    e_all = lax.dynamic_index_in_dim(adapter_hidden_factors, slot, 2, keepdims=False)
    a_model = a_all.reshape(layers, 11 * rank, width)
    e_all = e_all.reshape(layers, 3 * rank, -1)
    head_at = (t * heads_tp + head) * VD

    heads_of = lax.dynamic_slice_in_dim(a_all, head_at, VD, 3)
    a_head = jnp.concatenate([heads_of[:, 3:4], heads_of[:, 6:9]], axis=1).reshape(layers, 4 * rank, VD)

    def unit_columns(x):
        x = lax.dynamic_slice_in_dim(x, t * hidden_tp, hidden_tp, x.ndim - 1)
        x = jnp.pad(x, ((0, 0),) * (x.ndim - 1) + ((0, n * units - hidden_tp),))
        return lax.dynamic_slice_in_dim(x, q * units, units, x.ndim - 1)

    e_model = unit_columns(e_all)

    part = 1.0 / share
    vmem = lambda *spec: pltpu.VMEM(*spec)
    calls = [0]
    whole_x = ((n, 2, rows, width), BF)
    sems = Gather.semaphores(n) + Reduce.scratch(n, rows, width)
    pair = pltpu.SemaphoreType.DMA((4,))
    big = [vmem(*whole_x), vmem(*whole_x)]

    def run(kernel, ins, outs, scratch, plan=None):
        calls[0] += 1
        return call(kernel, calls[0], ins, outs, scratch, plan)

    near = lambda *arrays: [(array, False) for array in arrays]
    far = lambda *arrays: [(array, True) for array in arrays]
    paced = lambda *arrays: [(array, "paced") for array in arrays]
    out = lambda shape, kind, hbm=False: (shape, kind, hbm)

    dma = pltpu.SemaphoreType.DMA
    c_a, c_g, c_d = 4 * VD, 2 * units, units
    tall = nf * n * weight_rows
    cut = lambda columns: out((n, weight_rows, columns), BF)
    calls[0] += 1
    made = call(
        functools.partial(weights_kernel, n, nf, units, share, layers),
        calls[0],
        far(jnp.transpose(query_key_value_weight, (0, 2, 1, 3)), output_weight, gate_up_weight, down_weight),
        [out((tall, c_a), BF, True), out((tall, c_g), BF, True), out((tall, c_d), BF, True)]
        + ([cut(c_a)] + [cut(c_g)] + [cut(c_d)]) * (layers - 1),
        [
            vmem((n, weight_rows, c_a), BF),
            vmem((n, weight_rows, c_g), BF),
            vmem((n, weight_rows, c_d), BF),
            vmem((layers, weight_rows, 2, hidden_tp), BF),
            vmem((layers, weight_rows, hidden_tp), BF),
            dma((layers, n, 4)),
            dma((layers, 2)),
        ]
        + (Spread.scatter_semaphores(n) + Spread.spread_semaphores(n, nf)) * 2
        + Spread.scatter_semaphores(n),
    )
    w_a, w_g, w_d = [made[0]], [made[1]], [made[2]]
    a_blocks = [None] + made[3 : 2 + layers]
    g_blocks = [None] + made[2 + layers : 1 + 2 * layers]
    d_blocks = [None] + made[1 + 2 * layers :]

    def plan_of(scatters, spreads, *schedule):
        return Plan(n, nf, weight_rows, scatters, spreads, schedule)

    saved = []
    for l in range(layers):
        last = l == layers - 1
        w_attention = w_a[l]
        lam = lax.dynamic_slice_in_dim(difference_lambda[l], head, 1).reshape(1, 1)
        gain_a, gain_f = gains[l, 0:1], gains[l, 1:2]
        shared = paced(a_model[l]) + near(a_head[l]) + paced(cosine, sine, query_bits) + near(key_bits, lam)
        plan = plan_of(
            [] if last else [(a_blocks[l + 1], (tall, c_a)), (g_blocks[l + 1], (tall, c_g))],
            [w_g[l], w_d[l]],
            moves("forward", 0, parts(n, 0, 1)) + moves("spread", 0, parts(n, 1, 4)),
            moves("forward", 0, parts(n, 1, 2)) + ([] if last else [("scatter", 0)]),
            moves("spread", 1, parts(n, 0, 2)) + moves("forward", 0, parts(n, 2, 3)),
            moves("forward", 0, parts(n, 3, 4)) + ([] if last else [("scatter", 1)]),
        )
        got = run(
            functools.partial(attention_forward, n, nf, l, part, rank, True, plan),
            near(residual, gain_a) + far(w_attention) + shared,
            [
                out((rows, width), F32),
                out(*whole_x, True),
                out((tree, VD), BF, "paced"),
                out((tree, VD), BF, "paced"),
                out((tree, VD), BF, "paced"),
                out((tree, 3 * rank), BF, "paced"),
                out((tree, 2), F32, "paced"),
                out((tree, VD), BF, "paced"),
                out((tree, VD), BF, "paced"),
                out((tree, rank), BF, "paced"),
            ],
            big + [vmem((width, 4 * VD), BF), vmem((3 * rank, 3 * VD), BF), pair] + sems,
            plan,
        )
        if not last:
            w_a.append(got[0])
            w_g.append(got[1])
            got = got[2:]
        w_g[l], w_d[l], middle, *kept = got
        plan = plan_of(
            [] if last else [(d_blocks[l + 1], (tall, c_d))],
            [w_d[l]] + ([] if last else [w_a[l + 1], w_g[l + 1]]),
            moves("forward", 0, parts(n, 0, 2)) + moves("spread", 0, parts(n, 2, 4)),
            moves("forward", 0, parts(n, 2, 3)),
            moves("forward", 0, parts(n, 3, 4)) + ([] if last else moves("spread", 1, parts(n, 0, 4)) + [("scatter", 0)]),
            [] if last else moves("forward", 1, parts(n, 0, 1)),
            [] if last else moves("forward", 1, parts(n, 1, 2)) + moves("spread", 2, parts(n, 0, 1)),
            [] if last else moves("forward", 1, parts(n, 2, 4)),
        )
        ffn = run(
            functools.partial(ffn_forward, n, nf, units, rank, last, plan),
            near(middle, gain_f) + far(w_g[l]) + paced(a_model[l]) + near(e_model[l])
            + (near(own_cotangent) if last else []),
            ([out(*whole_x, True)] if last else [])
            + [
                out((rows, width), F32),
                out(*whole_x, True),
                out((tree, units), BF, "paced"),
                out((tree, units), BF, "paced"),
                out((tree, units), BF, "paced"),
                out((tree, 2 * rank), BF, "paced"),
                out((tree, rank), BF),
            ],
            big + [vmem((width, 3 * units), BF), vmem((2 * rank, 2 * units), BF), pair] + sems
            + ([vmem(*whole_x)] + Gather.semaphores(n) if last else []),
            plan,
        )
        if not last:
            w_d.append(ffn[0])
            w_d[l], w_a[l + 1], w_g[l + 1], *ffn = ffn[1:]
        else:
            w_d[l], gathered, *ffn = ffn
        saved.append((residual, middle, gain_a, gain_f, shared, kept, ffn[1:]))
        residual = ffn[0]

    grad = own_cotangent
    units_here, sums_here, block = [], [], width // (2 * n)
    for l in reversed(range(layers)):
        residual_in, middle, gain_a, gain_f, shared, kept, ffn = saved[l]
        carry = l == layers - 1
        made = run(
            functools.partial(ffn_backward, n, units, rank, carry),
            near(grad) + paced(middle) + near(gain_f) + far(w_g[l], w_d[l]) + paced(a_model[l]) + near(e_model[l])
            + far(ffn[0]) + paced(*ffn[1:])
            + (near(residual) + far(gathered) if carry else []),
            ([out((2, rows, width), BF)] if carry else [])
            + [
                out((rows, width), F32),
                out((rank, width), BF),
                out((2 * rank, width), BF),
                out((4 * rank, units), BF),
            ],
            big
            + [
                vmem((width, 3 * units), BF),
                vmem(*whole_x),
                vmem((tree, 2 * units), BF),
                vmem((tree, 2 * rank), BF),
                vmem((tree, rank), BF),
                vmem((2 * rank, 2 * units), BF),
                pair,
            ]
            + sems
            + ([vmem((rows, width), BF)] + Home.semaphores() if carry else []),
        )
        if carry:
            outputs, *made = made
        grad, *ffn_grads = made
        grad, own_sum, all_units = run(
            functools.partial(attention_backward, n, l, share, heads_tp, rank),
            near(grad) + paced(residual_in) + near(gain_a) + far(w_a[l]) + shared + far(kept[0])
            + paced(*kept[1:]) + near(*ffn_grads),
            [
                out((rows, width), F32),
                out((12 * rank, block), BF),
                out((n, 2, 4 * rank, units), BF),
            ],
            big
            + [
                vmem((width, 4 * VD), BF),
                vmem((tree, VD), BF),
                vmem((tree, VD), F32),
                vmem((tree, VD), F32),
                vmem((tree, VD), F32),
                vmem((tree, 3 * VD), BF),
                vmem((tree, 3 * rank), BF),
                vmem((tree, rank), BF),
                vmem((3 * rank, 3 * VD), BF),
                vmem((rank, width), BF),
                vmem((n, 2, 12 * rank, block), BF),
                pair,
            ]
            + sems
            + Gather.semaphores(n)
            + Reduce.scratch(n, 12 * rank, block),
        )

        number = (q * 2 + t) * (hidden_tp // n)
        half = lax.dynamic_index_in_dim(all_units, number // hidden_tp, 1, keepdims=False)
        flat = half[:, : 3 * rank].transpose(1, 0, 2).reshape(3 * rank, n * units)
        units_here.insert(0, lax.dynamic_slice_in_dim(flat, number % hidden_tp, hidden_tp // n, 1))
        sums_here.insert(0, own_sum)

    own = adapters // nf
    dma = pltpu.SemaphoreType.DMA
    wide = hidden_tp // n
    tokens_grad, grad_model, grad_hidden = run(
        functools.partial(finish_kernel, n, nf, layers, rank),
        near(grad, jnp.concatenate(sums_here), jnp.concatenate(units_here), slot.astype(F32).reshape(1, 1)),
        [
            out((2 * rows, width), F32),
            out((layers, 11, own, rank, block), F32),
            out((layers, 3, own, rank, wide), F32),
        ],
        [
            vmem((rows, width), BF),
            vmem((2, rows, width), BF),
            vmem((layers * 12 * rank, block), BF),
            vmem((nf, layers * 12 * rank, block), BF),
            vmem((nf, layers * 3 * rank, wide), BF),
            dma((3, 2)),
            dma((3, 2)),
            dma((2, nf)),
            dma((2, nf)),
        ],
    )
    return (
        outputs.reshape(2 * rows, width),
        tokens_grad,
        grad_model,
        grad_hidden,
    )


def solution(mesh):
    in_specs = (
        P(("fsdp", "ctx"), None),
        P(("fsdp", "ctx"), None),
        P(("fsdp", "ctx")),
        P(("fsdp", "ctx")),
        P("fsdp", None),
        P("fsdp"),
        P(),
        P(None, "tp"),
        P(None, ("fsdp", "ctx"), None, "tp"),
        P(None, ("fsdp", "ctx"), "tp"),
        P(None, ("fsdp", "ctx"), None, "tp"),
        P(None, ("fsdp", "ctx"), "tp"),
        P(),
        P(),
    )
    out_specs = (
        P(("fsdp", "ctx"), None),
        P(("fsdp", "ctx"), None),
        P(None, None, "fsdp", None, ("ctx", "tp")),
        P(None, None, "fsdp", None, ("ctx", "tp")),
    )
    body = functools.partial(shards, mesh.shape["fsdp"], mesh.shape["ctx"])
    return jax.shard_map(body, mesh=mesh, in_specs=in_specs, out_specs=out_specs, check_vma=False)
```

```python
import functools
import math

import jax
import jax.numpy as jnp
from jax import lax
from jax.experimental import pallas as pl
from jax.experimental.pallas import tpu as pltpu
from jax.sharding import PartitionSpec as P

HD = 128
VD = 256
NSEG = 13
EPSILON = 1e-05
ADAPTER_SCALE = 0.5
NEGATIVE_BIG = -1e30
MESH = pl.DeviceIdType.MESH
BF = jnp.bfloat16
F32 = jnp.float32


class Place:
    def __init__(self, n):
        self.n, self.h = n, n // 2
        self.f, self.c, self.t = lax.axis_index("fsdp"), lax.axis_index("ctx"), lax.axis_index("tp")
        self.f_hi, self.f_lo = self.f // 2, self.f % 2
        self.c_hi, self.c_lo = self.c // self.h, self.c % self.h
        self.q = self.f_lo * self.h + self.c_lo
        self.away = self.f_lo + self.c_hi - 2 * self.f_lo * self.c_hi
        self.home = {"fsdp": self.f_hi * 2 + self.c_hi, "ctx": self.f_lo * self.h + self.c_lo}
        self.pos = self.f_lo * (n - 1) + (1 - 2 * self.f_lo) * self.c_lo

    def ring(self, k):
        n, h = self.n, self.h
        p = lax.rem(self.pos + k + 2 * n, n)
        low = p // h
        column = (1 - low) * p + low * (n - 1 - p)
        device = {"fsdp": self.f_hi * 2 + low, "ctx": self.c_hi * h + column}
        return low * h + column, device


def remote(src, dst, send, recv, device):
    copy = pltpu.make_async_remote_copy(
        src_ref=src, dst_ref=dst, send_sem=send, recv_sem=recv, device_id=device, device_id_type=MESH
    )
    copy.start()
    return copy


def when_even(place, body):
    even = place.pos % 2 == 0
    pl.when(even)(lambda: body(True))
    pl.when(jnp.logical_not(even))(lambda: body(False))


def flip(number, bits):
    b = 1
    while b <= bits:
        if bits & b:
            number = number + b * (1 - 2 * ((number // b) % 2))
        b *= 2
    return number


class Spread:
    def __init__(self, place, nf, w, rows):
        self.place, self.nf, self.w, self.rows = place, nf, w, rows
        self.g = place.f_hi * 2 + place.c_hi
        self.links = range(1, nf // 2)
        self.scattered, self.sent = [], []
        self.to_partner, self.along, self.onward, self.got = {}, {}, {}, []

    @staticmethod
    def scatter_semaphores(n):
        dma = pltpu.SemaphoreType.DMA
        return [dma((n,)), dma((n,))]

    @staticmethod
    def spread_semaphores(n, nf):
        dma = pltpu.SemaphoreType.DMA
        return [dma((n,))] * 2 + [dma((n, max(1, nf // 2 - 1)))] * 4

    def block(self, g, q):
        n, h = self.place.n, self.place.h
        source = (g // 2 * 2 + q // h) * n + g % 2 * h + q % h
        start = pl.multiple_of(source * self.rows, self.rows)
        return self.w.at[pl.ds(start, self.rows)]

    def chip(self, q):
        place = self.place
        return {"fsdp": place.f_hi * 2 + q // place.h, "ctx": place.c_hi * place.h + q % place.h}

    def partner(self):
        place = self.place
        return {"ctx": (1 - place.c_hi) * place.h + place.c_lo}

    def line(self, e):
        return {"fsdp": flip(self.place.f_hi, e) * 2 + self.place.f_lo}

    def scatter(self, blocks, send, recv):
        q = self.place.q
        own = self.block(self.g, q)
        copy = pltpu.make_async_copy(blocks.at[q], own, recv.at[0])
        copy.start()
        self.scattered.append(copy)
        for d in range(1, self.place.n):
            to = flip(q, d)
            self.scattered.append(remote(blocks.at[to], own, send.at[d], recv.at[d], self.chip(to)))

    def arrived(self, d):
        if d:
            self.scattered[d].wait_recv()
        else:
            self.scattered[0].wait()

    def scatter_sent(self):
        for copy in self.scattered[1:]:
            copy.wait_send()

    def use(self, *sems):
        self.sems = sems

    def spread(self, d):
        send_z, recv_z, send_y, recv_y = self.sems[:4]
        at = self.block(self.g, flip(self.place.q, d))
        self.to_partner[d] = remote(at, at, send_z.at[d], recv_z.at[d], self.partner())
        for e in self.links:
            self.along[d, e] = remote(at, at, send_y.at[d, e - 1], recv_y.at[d, e - 1], self.line(e))

    def landed(self, d):
        if d in self.to_partner and d not in self.got:
            self.to_partner[d].wait_recv()
            self.got.append(d)

    def forward(self, d):
        send, recv = self.sems[4:]
        self.landed(d)
        at = self.block(flip(self.g, 1), flip(self.place.q, d))
        for e in self.links:
            self.onward[d, e] = remote(at, at, send.at[d, e - 1], recv.at[d, e - 1], self.line(e))

    def complete(self):
        for d in list(self.to_partner):
            self.landed(d)
        for copy in list(self.along.values()) + list(self.onward.values()):
            copy.wait_recv()

    def sent_all(self):
        for copies in (self.to_partner, self.along, self.onward):
            for copy in copies.values():
                copy.wait_send()


def enter(place, nf=0, scatters=False, home=False, ring=True, trees=0):
    bar = pltpu.get_barrier_semaphore()
    devices = [{"tp": 1 - place.t}]
    guide = Spread(place, nf, None, 0)
    if scatters:
        devices += [guide.chip(flip(place.q, d)) for d in range(1, place.n)]
    elif ring:
        devices += [place.ring(1)[1], place.ring(-1)[1]]
    if nf:
        devices += [guide.partner()] + [guide.line(e) for e in guide.links]
    devices += [{"fsdp": flip(place.f, e)} for e in range(1, trees)]
    for device in devices:
        pl.semaphore_signal(bar, inc=1, device_id=device, device_id_type=MESH)
    count = len(devices)
    if home:

        @pl.when(place.away == 1)
        def greet():
            pl.semaphore_signal(bar, inc=1, device_id=place.home, device_id_type=MESH)

        count = count + place.away
    pl.semaphore_wait(bar, count)


class Home:
    def __init__(self, place, out, send, recv):
        self.place, self.out = place, out
        self.send, self.recv = send, recv

    @staticmethod
    def semaphores():
        dma = pltpu.SemaphoreType.DMA
        return [dma((2,)), dma((2,))]

    def start(self, rows):
        place, slot = self.place, self.out.at[self.place.t]
        far = pltpu.make_async_remote_copy(
            src_ref=rows, dst_ref=slot, send_sem=self.send.at[0], recv_sem=self.recv.at[0],
            device_id=place.home, device_id_type=MESH,
        )
        near = pltpu.make_async_copy(rows, slot, self.recv.at[0])
        self.far = far
        pl.when(place.away == 1)(far.start)
        pl.when(place.away == 0)(near.start)
        self.near = near

    def land(self, share=True):
        pl.when(self.place.away == 1)(self.far.wait)
        pl.when(self.place.away == 0)(self.near.wait)
        if share:
            slot = self.out.at[self.place.t]
            self.across = remote(slot, slot, self.send.at[1], self.recv.at[1], {"tp": 1 - self.place.t})

    def finish(self):
        self.across.wait()


class TreeMove(Home):
    def __init__(self, place, rows, out, send, recv):
        super().__init__(place, out, send, recv)
        self.rows = rows
        self.slot = out.at[place.f]

    def start(self):
        place = self.place
        target = self.out.at[place.f_hi * 2 + place.c_hi]
        self.far = pltpu.make_async_remote_copy(
            src_ref=self.rows, dst_ref=target, send_sem=self.send.at[0], recv_sem=self.recv.at[0],
            device_id=place.home, device_id_type=MESH,
        )
        self.near = pltpu.make_async_copy(self.rows, target, self.recv.at[0])
        pl.when(place.away == 1)(self.far.start)
        pl.when(place.away == 0)(self.near.start)

    def land(self):
        super().land(False)


class Work:
    def __init__(self, place, nf, rows, scatters, spreads, schedule):
        self.n, self.schedule = place.n, schedule
        self.scatters, self.spreads = [], []
        for blocks, w, sems in scatters:
            self.scatters.append((Spread(place, nf, w, rows), blocks, sems))
        for w, sems in spreads:
            piece = Spread(place, nf, w, rows)
            piece.use(*sems)
            self.spreads.append(piece)

    def at(self, point):
        for what, i, *d in self.schedule[point] if point < len(self.schedule) else ():
            if what == "scatter":
                piece, blocks, sems = self.scatters[i]
                piece.scatter(blocks, *sems)
            elif what == "spread":
                self.spreads[i].spread(*d)
            else:
                self.spreads[i].forward(*d)

    def complete(self, i):
        self.spreads[i].complete()

    def settle(self, done=()):
        for i, piece in enumerate(self.spreads):
            if i not in done:
                piece.complete()
            piece.sent_all()
        for piece, _, _ in self.scatters:
            for d in range(self.n):
                piece.arrived(d)
            piece.scatter_sent()


def parts(n, first, last):
    return range(first * n // 4, last * n // 4)


def moves(what, piece, places):
    return [(what, piece, d) for d in places]


def weights_kernel(
    n, nf, units, share, layers,
    qkv, output, gate_up, down, *refs,
):
    place = Place(n)
    rows, hidden = down.shape[1:]
    w_a, w_g, w_d = refs[:3]
    later = refs[3 : 3 * layers]
    a_first, g_first, d_first, raw_g, raw_d, cut_sems, raw_sems = refs[3 * layers : 3 * layers + 7]
    sems = refs[3 * layers + 7 :]
    a_blocks = [a_first] + list(later[: layers - 1])
    g_blocks = [g_first] + list(later[layers - 1 : 2 * layers - 2])
    d_blocks = [d_first] + list(later[2 * layers - 2 :])
    cuts = []
    for l in range(layers):
        for q in range(n):
            columns = pl.ds(q // share * VD, VD)
            for i in range(4):
                source = qkv.at[l, i, :, columns] if i < 3 else output.at[l, :, columns]
                target = a_blocks[l].at[q, :, pl.ds(i * VD, VD)]
                cuts.append(pltpu.make_async_copy(source, target, cut_sems.at[l, q, i]))
    for copy in cuts[: 4 * n]:
        copy.start()
    raws = []
    for l in range(layers):
        raws.append(pltpu.make_async_copy(gate_up.at[l], raw_g.at[l], raw_sems.at[l, 0]))
        raws.append(pltpu.make_async_copy(down.at[l], raw_d.at[l], raw_sems.at[l, 1]))
    for copy in raws:
        copy.start()
    attention, forward, back = (Spread(place, nf, w, rows) for w in (w_a, w_g, w_d))
    attention.use(*sems[2:8])
    forward.use(*sems[10:16])
    enter(place, nf, True)
    for copy in cuts[: 4 * n]:
        copy.wait()
    attention.scatter(a_first, *sems[:2])
    for copy in cuts[4 * n :]:
        copy.start()

    def fill(target, j, at, value):
        width = min(units, hidden - j * units)
        target[j, :, at : at + width] = value(pl.ds(j * units, width))
        if width < units:
            target[j, :, at + width : at + units] = jnp.zeros((rows, units - width), BF)

    def cut_gate_up(l):
        raws[2 * l].wait()
        for i in range(2):
            for j in range(n):
                fill(g_blocks[l], j, i * units, lambda at, i=i: raw_g[l, :, i, at])

    def cut_down(l):
        raws[2 * l + 1].wait()
        for j in range(n):
            fill(d_blocks[l], j, 0, lambda at: raw_d[l, :, at])

    cut_gate_up(0)
    for d in range(n):
        attention.arrived(d)
        attention.spread(d)
    forward.scatter(g_first, *sems[8:10])
    cut_down(0)
    back.scatter(d_first, *sems[16:18])
    for d in parts(n, 0, 1):
        attention.forward(d)
    for l in range(1, layers):
        cut_gate_up(l)
        cut_down(l)
    for copy in cuts[4 * n :]:
        copy.wait()
    for d in parts(n, 1, 3):
        attention.forward(d)
    for d in range(n):
        forward.arrived(d)
    for d in parts(n, 0, 1):
        forward.spread(d)
    for d in parts(n, 3, 4):
        attention.forward(d)
    attention.complete()
    forward.complete()
    attention.scatter_sent()
    attention.sent_all()
    forward.scatter_sent()
    forward.sent_all()
    for d in range(n):
        back.arrived(d)
    back.scatter_sent()


class Gather:
    def __init__(self, place, x, send_r, recv_r, send_l, recv_l, core_send, core_recv, lean=False):
        self.place, self.x = place, x
        self.sems = (send_r, recv_r, send_l, recv_l, core_send, core_recv)
        self.lean = lean and place.n == 4
        self.right, self.left, self.across = {}, {}, []

    @staticmethod
    def semaphores(n):
        dma = pltpu.SemaphoreType.DMA
        return [dma((n,))] * 4 + [dma((n,))] * 2

    def _make(self, s):
        place, x = self.place, self.x
        send_r, recv_r, send_l, recv_l = self.sems[:4]
        top = x.shape[2] // 2
        last = s == place.n // 2 - 1
        for i in range(1 if last and not self.lean else 2):
            for made, sign, send, recv in ((self.right, 1, send_r, recv_r), (self.left, -1, send_l, recv_l)):
                piece = i if sign > 0 else 1 - i
                at = x.at[place.ring(-sign * s)[0], place.t, pl.ds(piece * top, top)]
                made[s, i] = pltpu.make_async_remote_copy(
                    src_ref=at, dst_ref=at, send_sem=send.at[2 * s + i], recv_sem=recv.at[2 * s + i],
                    device_id=place.ring(sign)[1], device_id_type=MESH,
                )

    def _cross(self, q):
        core_send, core_recv = self.sems[4:]
        slot, at = len(self.across), self.x.at[q, self.place.t]
        other = {"tp": 1 - self.place.t}
        self.across.append(remote(at, at, core_send.at[slot], core_recv.at[slot], other))

    def begin(self):
        for s in range(self.place.n // 2):
            self._make(s)
        for i in range(2):
            self.right[0, i].start()
            self.left[0, i].start()
        self._cross(self.place.q)

    def _hop(self, s):
        last = self.place.n // 2 - 1
        if not self.lean:
            for i in range(1 if s == last else 2):
                for stream in (self.right, self.left):
                    stream[s, i].wait_recv()
                    if s < last - 1 or (s == last - 1 and i == 0):
                        stream[s + 1, i].start()
            return

        def body(even):
            along_ctx, along_fsdp = (self.left, self.right) if even else (self.right, self.left)
            for i in range(2):
                if s == 0:
                    along_ctx[0, i].wait_recv()
                    along_ctx[1, i].start()
                    along_fsdp[0, i].wait_recv()
                else:
                    along_fsdp[1, i].wait_recv()

        when_even(self.place, body)

    def chunks(self):
        place, half = self.place, self.place.n // 2
        self.across[0].wait_recv()
        yield place.q
        for s in range(half):
            self._hop(s)
            arrived = [place.ring(half)[0]] if s == half - 1 else [place.ring(-s - 1)[0], place.ring(s + 1)[0]]
            first = len(self.across)
            for q in arrived:
                self._cross(q)
            for i, q in enumerate(arrived):
                self.across[first + i].wait_recv()
                yield q

    def finish(self):
        last = self.place.n // 2 - 1
        for s in range(last + 1):
            for i in range(2):
                if s < last:
                    self.right[s, i].wait_send()
                    self.left[s, i].wait_send()
                elif not self.lean and i == 0:
                    self.right[s, 0].wait_send()
                    self.left[s, 0].wait_send()
        if self.lean:

            def body(even):
                for i in range(2):
                    (self.left if even else self.right)[1, i].wait_send()

            when_even(self.place, body)
        for copy in self.across:
            copy.wait_send()


def by_rows(count, body, step=16):
    def one(i, carry):
        body(pl.ds(pl.multiple_of(i * step, step), step))
        return carry

    lax.fori_loop(0, count // step, one, 0)


class Reduce:
    def __init__(self, place, p, from_core, in_r, in_l, send_r, recv_r, send_l, recv_l, core_send, core_recv, lean=False):
        self.place, self.p, self.from_core, self.in_r, self.in_l = place, p, from_core, in_r, in_l
        self.sems = (send_r, recv_r, send_l, recv_l, core_send, core_recv)
        self.lean = lean and place.n == 4
        half = place.n // 2
        self.order = [half] + [k for j in range(half - 1, 0, -1) for k in (j, -j)] + [0]
        self.chips = {k: place.ring(k)[0] for k in self.order}
        self.across, self.copies = {}, {}
        for sign in (1, -1):
            for s in range(half):
                for piece in range(2):
                    if s or self.lean or piece == (sign < 0):
                        self._copy(sign, s, piece)

    @staticmethod
    def scratch(n, rows, width):
        dma = pltpu.SemaphoreType.DMA
        wide = [pltpu.VMEM((n, rows, width), BF)] + [pltpu.VMEM((n // 2, rows, width), BF)] * 2
        return wide + [dma((n // 2, 2))] * 4 + [dma((n,))] * 2

    def offer(self, k):
        core_send, core_recv = self.sems[4:]
        slot, q, t = len(self.across), self.chips[k], self.place.t
        self.across[k] = remote(
            self.p.at[q, 1 - t], self.from_core.at[q], core_send.at[slot], core_recv.at[slot], {"tp": 1 - t}
        )

    def _local(self, k, at):
        q = self.chips[k]
        return self.p[q, self.place.t, at].astype(F32) + self.from_core[q, at].astype(F32)

    def _add(self, k, piece, extra=None):
        top = self.p.shape[2] // 2

        def body(at):
            whole = pl.ds(pl.multiple_of(piece * top + at.start, 16), at.size)
            total = self._local(k, whole)
            if extra is not None:
                total = total + extra[whole].astype(F32)
            self.from_core[self.chips[k], whole] = total.astype(BF)

        by_rows(top, body)

    def _copy(self, sign, s, piece):
        if (sign, s, piece) not in self.copies:
            place, top = self.place, self.p.shape[2] // 2
            send, recv = self.sems[:2] if sign > 0 else self.sems[2:4]
            target = self.in_r if sign > 0 else self.in_l
            k = place.n // 2 - s
            rows = pl.ds(piece * top, top)
            self.copies[sign, s, piece] = pltpu.make_async_remote_copy(
                src_ref=self.from_core.at[self.chips[sign * k if s else k], rows], dst_ref=target.at[s, rows],
                send_sem=send.at[s, piece], recv_sem=recv.at[s, piece],
                device_id=place.ring(sign)[1], device_id_type=MESH,
            )
        return self.copies[sign, s, piece]

    def far(self):
        half = self.place.n // 2
        self.across[half].wait_recv()
        self._add(half, 0)
        self._add(half, 1)
        if self.lean:
            self.across[1].wait_recv()
            self.across[-1].wait_recv()

            def body(even):
                sign = -1 if even else 1
                for piece in range(2):
                    self._copy(sign, 0, piece).start()
                for piece in range(2):
                    self._add(sign, piece)
                    self._copy(sign, 1, piece).start()

            when_even(self.place, body)
            return
        self._copy(1, 0, 0).start()
        self._copy(-1, 0, 1).start()
        if half > 1:
            k = half - 1
            for sign, piece in ((1, 1), (-1, 0)):
                self.across[sign * k].wait_recv()
                self._add(sign * k, piece)
                self._copy(sign, 1, piece).start()

    def near(self, s):
        half = self.place.n // 2
        k = half - s
        if self.lean:

            def body(even):
                sign = 1 if even else -1
                for piece in range(2):
                    self._copy(sign, 0, piece).wait_recv()
                    self._add(sign, piece, (self.in_r if even else self.in_l).at[0])
                    self._copy(sign, 1, piece).start()

            when_even(self.place, body)
            return
        if s > 1:
            self.across[k].wait_recv()
            self.across[-k].wait_recv()
        for sign, first, held in ((1, 0, self.in_r), (-1, 1, self.in_l)):
            for piece in (first,) if s == 1 else (first, 1 - first):
                self._copy(sign, s - 1, piece).wait_recv()
                self._add(sign * k, piece, held.at[s - 1])
                self._copy(sign, s, piece).start()

    def end(self, use):
        half = self.place.n // 2
        self.across[0].wait_recv()
        for sign in (1, -1):
            for piece in range(2):
                self._copy(sign, half - 1, piece).wait_recv()

        def body(at):
            use(at, self._local(0, at) + self.in_r[half - 1, at].astype(F32) + self.in_l[half - 1, at].astype(F32))

        by_rows(self.p.shape[2], body)

    def finish(self):
        half = self.place.n // 2
        if self.lean:

            def body(even):
                for piece in range(2):
                    self._copy(-1 if even else 1, 0, piece).wait_send()

            when_even(self.place, body)
        else:
            self._copy(1, 0, 0).wait_send()
            self._copy(-1, 0, 1).wait_send()
        for s in range(1, half):
            for sign in (1, -1):
                for piece in range(2):
                    self._copy(sign, s, piece).wait_send()
        for copy in self.across.values():
            copy.wait_send()

    def run(self, use, before=None, offered=False):
        if not offered:
            for k in self.order:
                self.offer(k)
            self.far()
        for s in range(1, self.place.n // 2):
            self.near(s)
        if before is not None:
            before()
        self.end(use)


def mm(a, b):
    return jnp.dot(a, b, preferred_element_type=F32)


def mm_t(a, b):
    return lax.dot_general(a, b, (((1,), (1,)), ((), ())), preferred_element_type=F32)


def t_mm(a, b):
    return lax.dot_general(a, b, (((0,), (0,)), ((), ())), preferred_element_type=F32)


def rms_scale(values):
    return lax.rsqrt(jnp.mean(values * values, axis=-1, keepdims=True) + EPSILON)


def norm_back(grad_normed, inputs, scale_rows, gain):
    unit = inputs * scale_rows
    scaled = grad_normed * gain
    return scale_rows * (scaled - unit * jnp.mean(scaled * unit, axis=-1, keepdims=True))


def tiles(count, width, body):
    def one(j, carry):
        body(pl.ds(pl.multiple_of(j * width, width), width))
        return carry

    lax.fori_loop(0, count // width, one, 0)


def tile_of(count):
    return 256 if count % 256 == 0 else 128


def turn(v, cosine, sine):
    return v * cosine + pltpu.roll(v, HD // 2, 1) * sine


def block_diagonal(out, parts, rank, width):
    out[...] = jnp.zeros(out.shape, out.dtype)
    for i in range(parts[1]):
        out[i * rank : (i + 1) * rank, i * width : (i + 1) * width] = parts[0][i * rank : (i + 1) * rank, :]


def write_norm(x_rows, source, gain):
    def body(at):
        v = source[at].astype(F32)
        x_rows[at] = (v * rms_scale(v) * gain[...]).astype(BF)

    by_rows(source.shape[0], body)


ROW_BLOCK = 128
KEY_STEP = 256


def row_blocks(tree, body):
    for j in range(tree // KEY_STEP):

        def one(i, carry, j=j):
            body(pl.ds(pl.multiple_of(j * KEY_STEP + i * ROW_BLOCK, ROW_BLOCK), ROW_BLOCK), (j + 1) * KEY_STEP)
            return carry

        lax.fori_loop(0, KEY_STEP // ROW_BLOCK, one, 0)


def seen(rows, keys, query_bits, key_bits):
    shared = (query_bits[rows] & key_bits[:, :keys]) != 0
    i = rows.start + lax.broadcasted_iota(jnp.int32, (ROW_BLOCK, keys), 0)
    j = lax.broadcasted_iota(jnp.int32, (ROW_BLOCK, keys), 1)
    return shared & (j <= i)


def attention_forward(
    n, nf, layer, part, rank, lean, plan,
    residual, gain, w_hbm, a_model, a_head, cosine, sine, query_bits, key_bits, lam, *refs, pace,
):
    jobs, refs = plan.split(refs)
    (middle, x_hbm, queries, keys, values, small, log_total, mixed, headed, side,
     x, p, w, raised, copy_sems, *sems) = refs
    place = Place(n)
    chip_rows, width = 2 * x_hbm.shape[2], x_hbm.shape[3]
    tree = n * chip_rows
    load = pltpu.make_async_copy(w_hbm, w, copy_sems.at[0])
    load.start()
    gather, reduce = Gather(place, x, *sems[:6], lean=lean), Reduce(place, p, *sems[6:], lean=lean)
    write_norm(x.at[place.q, place.t], residual, gain)
    block_diagonal(raised, (a_head[rank : 4 * rank], 3), rank, VD)
    work = plan.work(place, nf, jobs)
    enter(place, nf, bool(plan.scatters))
    gather.begin()
    work.at(0)
    pace.ready()
    load.wait()

    def project(q):
        rows = pl.ds(pl.multiple_of(q * chip_rows, chip_rows), chip_rows)
        v = x[q].reshape(chip_rows, width)
        low = mm_t(v, a_model[: 3 * rank]).astype(BF)
        small[rows] = low
        for i, out in enumerate((queries, keys, values)):
            at = slice(i * VD, (i + 1) * VD)
            made = mm(v, w[:, at]) + ADAPTER_SCALE * mm(low, raised[:, at])
            if i < 2:
                for c in range(2):
                    half = slice(c * HD, (c + 1) * HD)
                    out[rows, half] = turn(made[:, half], cosine[rows], sine[rows]).astype(BF)
            else:
                out[rows] = made.astype(BF)

    for q in gather.chunks():
        project(q)
    work.at(1)
    keep = pltpu.make_async_copy(x, x_hbm, copy_sems.at[1])
    keep.start()
    score_scale = HD ** (-0.5)
    weight = lam[...]

    def attend(rows, count):
        visible = seen(rows, count, query_bits, key_bits)
        both = []
        for c in range(2):
            at = slice(c * HD, (c + 1) * HD)
            scores = mm_t(queries[rows, at], keys[:count, at]) * score_scale
            scores = jnp.where(visible, scores, NEGATIVE_BIG)
            top = jnp.max(scores, axis=-1, keepdims=True)
            raw = jnp.exp(scores - top)
            total = jnp.sum(raw, axis=-1, keepdims=True)
            log_total[rows, c : c + 1] = top + jnp.log(total)
            both.append(raw * (1.0 / total))
        mix = mm((both[0] - weight * both[1]).astype(BF), values[:count])
        mixed[rows] = mix.astype(BF)
        head = (mix * rms_scale(mix) * keep_factor(layer)).astype(BF)
        headed[rows] = head
        side[rows] = mm_t(head, a_head[:rank]).astype(BF)

    row_blocks(tree, attend)
    pace.flush()
    work.at(2)

    for k in reduce.order:
        q = reduce.chips[k]
        rows = pl.ds(pl.multiple_of(q * chip_rows, chip_rows), chip_rows)
        head, low = headed[rows], side[rows]

        def out_tile(at):
            made = mm_t(head, w[at, 3 * VD :]) + ADAPTER_SCALE * mm(low, a_model[9 * rank : 10 * rank, at])
            p[q, :, :, at] = (made * part).astype(BF).reshape(2, chip_rows // 2, at.size)

        tiles(width, 512, out_tile)
        reduce.offer(k)
        if k == reduce.order[2]:
            reduce.far()
    work.at(3)
    for s in range(1, n // 2):
        reduce.near(s)
    work.at(4)

    def use(at, total):
        middle[at] = residual[at].astype(F32) + total

    reduce.end(use)
    work.at(5)
    keep.wait()
    gather.finish()
    reduce.finish()
    work.settle()


def ffn_forward(
    n, nf, units, rank, last, plan,
    residual, gain, w_hbm, a_model, e_model, *refs, pace,
):
    place = Place(n)
    if last:
        cotangent, *refs = refs
    jobs, refs = plan.split(refs)
    if last:
        all_refs = refs
        next_hbm, *refs, next_x = refs[:-6]
        next_gather = Gather(place, next_x, *all_refs[-6:])
    (following, x_hbm, gates, ups, hidden, small, side,
     x, p, w, raised, copy_sems, *sems) = refs
    chip_rows, width = 2 * x_hbm.shape[2], x_hbm.shape[3]
    tree = n * chip_rows
    load = pltpu.make_async_copy(w_hbm, w.at[:, pl.ds(0, 2 * units)], copy_sems.at[0])
    load.start()
    gather, reduce = Gather(place, x, *sems[:6], lean=not last), Reduce(place, p, *sems[6:], lean=not last)
    write_norm(x.at[place.q, place.t], residual, gain)
    block_diagonal(raised, (e_model, 2), rank, units)
    work = plan.work(place, nf, jobs)
    enter(place, nf, bool(plan.scatters))
    gather.begin()
    work.at(0)
    pace.ready()
    load.wait()
    step = tile_of(units)

    for number, q in enumerate(gather.chunks()):
        if number == n - 1:
            work.at(1)
        rows = pl.ds(pl.multiple_of(q * chip_rows, chip_rows), chip_rows)
        v = x[q].reshape(chip_rows, width)
        low = mm_t(v, a_model[4 * rank : 6 * rank]).astype(BF)
        small[rows] = low

        def unit_tile(at):
            up_at = pl.ds(pl.multiple_of(units + at.start, step), step)
            gate = mm(v, w[:, at]) + ADAPTER_SCALE * mm(low, raised[:, at])
            up = mm(v, w[:, up_at]) + ADAPTER_SCALE * mm(low, raised[:, up_at])
            gates[rows, at] = gate.astype(BF)
            ups[rows, at] = up.astype(BF)
            hidden[rows, at] = (gate / (1.0 + jnp.exp(-gate)) * up).astype(BF)

        tiles(units, step, unit_tile)

    pace.flush()
    if last:
        next_x[place.q, place.t] = cotangent[...]
        next_gather.begin()
    work.at(2)
    keep = pltpu.make_async_copy(x, x_hbm, copy_sems.at[1])
    keep.start()

    work.complete(0)
    load = pltpu.make_async_copy(plan.late(jobs), w.at[:, pl.ds(2 * units, units)], copy_sems.at[0])
    load.start()
    load.wait()
    for k in reduce.order:
        q = reduce.chips[k]
        rows = pl.ds(pl.multiple_of(q * chip_rows, chip_rows), chip_rows)
        made_hidden = hidden[rows]
        low = mm_t(made_hidden, e_model[2 * rank : 3 * rank]).astype(BF)
        side[rows] = low

        def out_tile(at):
            made = mm_t(made_hidden, w[at, 2 * units :])
            made = made + ADAPTER_SCALE * mm(low, a_model[10 * rank : 11 * rank, at])
            p[q, :, :, at] = made.astype(BF).reshape(2, chip_rows // 2, at.size)

        tiles(width, 512, out_tile)
        reduce.offer(k)
        if k == reduce.order[2]:
            reduce.far()
    if last:
        coming = next_gather.chunks()
        for _ in range(n - 1):
            next(coming)
    work.at(3)
    for s in range(1, n // 2):
        reduce.near(s)
    work.at(4)

    def use(at, total):
        following[at] = residual[at] + total

    reduce.end(use)
    if last:
        for _ in coming:
            pass
        keep_next = pltpu.make_async_copy(next_x, next_hbm, copy_sems.at[2])
        keep_next.start()
    work.at(5)
    keep.wait()
    if last:
        keep_next.wait()
        next_gather.finish()
    gather.finish()
    reduce.finish()
    work.settle((0,))


def ffn_backward(
    n, units, rank, carry,
    grad, middle, gain, w_hbm, w_down_hbm, a_model, e_model, x_hbm, gates, ups, hidden, small, side, *refs, pace,
):
    if carry:
        final, gathered, final_out, *refs = refs
        *refs, final_rows, home_send, home_recv = refs
    else:
        sums, here, sums_out, here_out, *refs = refs
        *refs, home_send, home_recv = refs
    (grad_out, grad_up_down, grad_in, grad_units,
     x, p, w, kept, dgu, dsmall, dside, raised, copy_sems, *sems) = refs
    place = Place(n)
    chip_rows, width = 2 * x_hbm.shape[2], x_hbm.shape[3]
    tree = n * chip_rows
    load = pltpu.make_async_copy(w_hbm, w.at[:, pl.ds(0, 2 * units)], copy_sems.at[0])
    load.start()
    load_down = pltpu.make_async_copy(w_down_hbm, w.at[:, pl.ds(2 * units, units)], copy_sems.at[2])
    load_down.start()
    fetch = pltpu.make_async_copy(x_hbm, kept, copy_sems.at[1])
    gather, reduce = Gather(place, x, *sems[:6]), Reduce(place, p, *sems[6:])

    if carry:
        come = pltpu.make_async_copy(gathered, x, copy_sems.at[3])
        come.start()
    else:

        def own(at):
            x[place.q, place.t, at] = grad[at].astype(BF)

        by_rows(grad.shape[0], own)
    block_diagonal(raised, (e_model, 2), rank, units)
    if carry:

        def last_rows(at):
            final_rows[at] = final[at].astype(BF)

        by_rows(final.shape[0], last_rows)
    enter(place, home=True)
    if not carry:
        gather.begin()
        going = [
            TreeMove(place, source, target, home_send.at[i], home_recv.at[i])
            for i, (source, target) in enumerate(((sums, sums_out), (here, here_out)))
        ]
    else:
        home = Home(place, final_out, home_send, home_recv)
        home.start(final_rows)
    pace.ready()
    load.wait()
    load_down.wait()
    step = tile_of(units)

    if carry:
        come.wait()
    coming = [0] + [k for s in range(1, n // 2) for k in (-s, s)] + [n // 2]
    for q in list(reduce.chips.values()) if carry else gather.chunks():
        rows = pl.ds(pl.multiple_of(q * chip_rows, chip_rows), chip_rows)
        v = x[q].reshape(chip_rows, width)
        low = (ADAPTER_SCALE * mm_t(v, a_model[10 * rank : 11 * rank])).astype(BF)
        dside[rows] = low

        def unit_tile(at):
            up_at = pl.ds(pl.multiple_of(units + at.start, step), step)
            down_at = pl.ds(pl.multiple_of(2 * units + at.start, step), step)
            dhidden = mm(v, w[:, down_at]) + mm(low, e_model[2 * rank : 3 * rank, at])
            gate, up = gates[rows, at].astype(F32), ups[rows, at].astype(F32)
            sig = 1.0 / (1.0 + jnp.exp(-gate))
            dgu[rows, at] = (dhidden * up * sig * (1.0 + gate * (1.0 - sig))).astype(BF)
            dgu[rows, up_at] = (dhidden * gate * sig).astype(BF)

        tiles(units, step, unit_tile)
        back = dgu[rows]
        low_back = (ADAPTER_SCALE * mm_t(back, raised[...])).astype(BF)
        dsmall[rows] = low_back

        def out_tile(at):
            made = mm_t(back, w[at, : 2 * units]) + mm(low_back, a_model[4 * rank : 6 * rank, at])
            p[q, :, :, at] = made.astype(BF).reshape(2, chip_rows // 2, at.size)

        tiles(width, 512, out_tile)
        if carry:
            k = reduce.order[len(reduce.across)]
        else:
            k = coming.pop(0)
        reduce.offer(k)
        if k == (reduce.order[2] if carry else n // 2):
            reduce.far()

    fetch.start()
    if not carry:
        for move in going:
            move.start()

    def use(at, total):
        inputs = middle[at]
        grad_out[at] = grad[at].astype(F32) + norm_back(total, inputs, rms_scale(inputs), gain[...])

    def adapters():
        fetch.wait()

        def model_tile(at):
            flat = x[:, :, :, at].reshape(tree, at.size)
            grad_up_down[:, at] = (ADAPTER_SCALE * t_mm(side[...], flat)).astype(BF)
            flat = kept[:, :, :, at].reshape(tree, at.size)
            grad_in[:, at] = t_mm(dsmall[...], flat).astype(BF)

        tiles(width, 256, model_tile)

        def unit_tile(at):
            up_at = pl.ds(pl.multiple_of(units + at.start, step), step)
            grad_units[:rank, at] = (ADAPTER_SCALE * t_mm(small[...], dgu[:, at])[:rank]).astype(BF)
            grad_units[rank : 2 * rank, at] = (ADAPTER_SCALE * t_mm(small[...], dgu[:, up_at])[rank:]).astype(BF)
            grad_units[2 * rank : 3 * rank, at] = t_mm(dside[...], hidden[:, at]).astype(BF)
            grad_units[3 * rank :, at] = jnp.zeros((rank, at.size), BF)

        tiles(units, step, unit_tile)

    reduce.run(use, adapters, True)
    if not carry:
        gather.finish()
    reduce.finish()
    if carry:
        home.land()
        home.finish()
    else:
        for move in going:
            move.land()


def attention_backward(
    n, layer, share, heads_tp, rank,
    grad, residual, gain, w_hbm, a_model, a_head, cosine, sine, query_bits, key_bits, lam,
    x_hbm, queries, keys, values, small, log_total, mixed, headed, side,
    grad_up_down, grad_ffn_in, grad_units,
    grad_out, own_sum, all_units,
    x, p, w, dmixed, dq, dk, dv, dprojected, dsmall, dside, raised, grad_a9, p_own, copy_sems, *sems, pace,
):
    place = Place(n)
    part = 1.0 / share
    chip_rows, width = 2 * x_hbm.shape[2], x_hbm.shape[3]
    tree = n * chip_rows
    load = pltpu.make_async_copy(w_hbm, w, copy_sems.at[0])
    load.start()
    gather, reduce = Gather(place, x, *sems[:6]), Reduce(place, p, *sems[6:15])
    gather_units, reduce_own = Gather(place, all_units, *sems[15:21]), Reduce(place, p_own, *sems[21:])

    def own(at):
        x[place.q, place.t, at] = grad[at].astype(BF)

    by_rows(grad.shape[0], own)
    block_diagonal(raised, (a_head[rank : 4 * rank], 3), rank, VD)
    all_units[place.q, place.t] = grad_units[...]
    enter(place)
    gather.begin()
    dk[...] = jnp.zeros(dk.shape, F32)
    dv[...] = jnp.zeros(dv.shape, F32)
    pace.ready()
    load.wait()

    score_scale = HD ** (-0.5)
    weight = lam[...]

    def attend(rows, count):
        visible = seen(rows, count, query_bits, key_bits)
        dmix = dmixed[rows]
        dweights = mm_t(dmix, values[:count])
        both = []
        for c in range(2):
            at = slice(c * HD, (c + 1) * HD)
            scores = mm_t(queries[rows, at], keys[:count, at]) * score_scale
            probability = jnp.exp(jnp.where(visible, scores - log_total[rows, c : c + 1], NEGATIVE_BIG))
            both.append(probability)
            weighted = probability * dweights
            dscores = weighted - probability * jnp.sum(weighted, axis=-1, keepdims=True)
            dscores = (dscores * -weight if c else dscores).astype(BF)
            dq[rows, at] = mm(dscores, keys[:count, at])
            dk[:count, at] += t_mm(dscores, queries[rows, at])
        dv[:count] += t_mm((both[0] - weight * both[1]).astype(BF), dmix)

    for q in gather.chunks():
        rows = pl.ds(pl.multiple_of(q * chip_rows, chip_rows), chip_rows)
        v = x[q].reshape(chip_rows, width)
        low = (ADAPTER_SCALE * mm_t(v, a_model[9 * rank : 10 * rank])).astype(BF)
        dside[rows] = low
        dheaded = mm(v, w[:, 3 * VD :]) + mm(low, a_head[:rank])
        inputs = mixed[rows].astype(F32)
        dmixed[rows] = norm_back(dheaded, inputs, rms_scale(inputs), keep_factor(layer)).astype(BF)

        def block(i, carry, q=q):
            attend(pl.ds(pl.multiple_of(q * chip_rows + i * ROW_BLOCK, ROW_BLOCK), ROW_BLOCK), tree)
            return carry

        lax.fori_loop(0, chip_rows // ROW_BLOCK, block, 0)

    gather_units.begin()

    def send_part(k):
        q = reduce.chips[k]
        rows = pl.ds(pl.multiple_of(q * chip_rows, chip_rows), chip_rows)
        for j, source in enumerate((dq, dk)):
            for c in range(2):
                half = slice(c * HD, (c + 1) * HD)
                turned = turn(source[rows, half] * score_scale, cosine[rows], -sine[rows])
                dprojected[rows, j * VD + c * HD : j * VD + (c + 1) * HD] = turned.astype(BF)
        dprojected[rows, 2 * VD :] = dv[rows].astype(BF)
        back = dprojected[rows]
        low_back = (ADAPTER_SCALE * mm_t(back, raised[...])).astype(BF)
        dsmall[rows] = low_back

        def out_tile(at):
            made = mm_t(back, w[at, : 3 * VD]) + mm(low_back, a_model[: 3 * rank, at])
            p[q, :, :, at] = (made * part).astype(BF).reshape(2, chip_rows // 2, at.size)

        tiles(width, 512, out_tile)
        reduce.offer(k)

    for k in reduce.order[:3]:
        send_part(k)
    reduce.far()

    def out_gradient(at):
        flat = x[:, :, :, at].reshape(tree, at.size)
        grad_a9[:, at] = (ADAPTER_SCALE * part * t_mm(side[...], flat)).astype(BF)

    tiles(width, 256, out_gradient)
    gather.finish()
    fetch = pltpu.make_async_copy(x_hbm, x, copy_sems.at[1])
    fetch.start()
    for k in reduce.order[3:]:
        send_part(k)
    for _ in gather_units.chunks():
        pass
    fetch.wait()

    block = width // (2 * n)

    def full_tile(jp, carry):
        at = pl.ds(pl.multiple_of(jp * block, block), block)
        q, t = jp // 2, jp % 2
        flat = x[:, :, :, at].reshape(tree, block)
        p_own[q, t, : 3 * rank] = (part * t_mm(dsmall[...], flat)).astype(BF)
        p_own[q, t, 4 * rank : 6 * rank] = grad_ffn_in[:, at]
        p_own[q, t, 9 * rank : 10 * rank] = grad_a9[:, at]
        p_own[q, t, 10 * rank : 11 * rank] = grad_up_down[:, at]
        p_own[q, t, 11 * rank :] = jnp.zeros((rank, block), BF)
        return carry

    lax.fori_loop(0, 2 * n, full_tile, 0)
    of_head = [part * t_mm(dside[...], headed[...])]
    for i in range(3):
        made = t_mm(small[...], dprojected[:, i * VD : (i + 1) * VD])[i * rank : (i + 1) * rank]
        of_head.append(ADAPTER_SCALE * part * made)
    head = place.t * heads_tp + place.q // share
    for j in range(2 * n):
        start = j * block % VD
        own = (head == j * block // VD).astype(F32)
        for i, k in enumerate((3, 6, 7, 8)):
            made = of_head[i][:, start : start + block] * own
            p_own[j // 2, j % 2, k * rank : (k + 1) * rank] = made.astype(BF)

    for k in reduce.order:
        reduce_own.offer(k)
    reduce_own.far()
    for s in range(1, n // 2):
        reduce.near(s)
        reduce_own.near(s)

    def use_own(at, total):
        own_sum[at] = total.astype(BF)

    def use(at, total):
        inputs = residual[at].astype(F32)
        grad_out[at] = grad[at].astype(F32) + norm_back(total, inputs, rms_scale(inputs), gain[...])

    reduce.end(use)
    reduce_own.end(use_own)
    gather_units.finish()
    reduce.finish()
    reduce_own.finish()


def finish_kernel(
    n, nf, layers, rank,
    grad, own_sums, own_units, slot, *refs,
):
    earlier, refs = refs[: 2 * layers - 2], refs[2 * layers - 2 :]
    (tokens_grad, model_grad, hidden_grad,
     rows_out, landed, sent_sums, all_sums, all_units, home_send, home_recv, tree_send, tree_recv) = refs
    place = Place(n)
    own = model_grad.shape[2]
    tall = own_sums.shape[0]

    def cut(at):
        rows_out[at] = grad[at].astype(BF)

    by_rows(grad.shape[0], cut)
    sent_sums[...] = own_sums[...]
    sent_sums[tall - rank :] = jnp.broadcast_to(slot[...], (rank, own_sums.shape[1])).astype(BF)
    enter(place, home=True, ring=False, trees=nf)
    moves = [Home(place, landed, home_send.at[0], home_recv.at[0])]
    away = {}
    for i, (source, target) in enumerate(((sent_sums, all_sums), (own_units, all_units))):
        away[i] = TreeMove(place, source, target.at[:, 0], home_send.at[i + 1], home_recv.at[i + 1])
        away[i].start()
    copies = []

    def hand_round(source, target, l, i):
        to = target.at[place.f, l]
        for e in range(1, nf):
            sems = tree_send.at[l, i, e], tree_recv.at[l, i, e]
            copies.append(remote(source, to, *sems, {"fsdp": flip(place.f, e)}))

    for l in range(1, layers):
        for i, target in enumerate((all_sums, all_units)):
            source = earlier[2 * l - 2 + i].at[place.f]
            target[place.f, l] = earlier[2 * l - 2 + i][place.f]
            hand_round(source, target, l, i)
    for i, target in enumerate((all_sums, all_units)):
        away[i].land()
        if i == 1:
            moves[0].start(rows_out)
        hand_round(target.at[place.f, 0], target, 0, i)
    moves[0].land()
    for copy in copies:
        copy.wait_recv()
    for b in range(own):
        number = (place.f * own + b).astype(F32)
        keeps = [
            (all_sums[f, 0, tall - rank : tall - rank + 1, :1].astype(F32) == number).astype(F32) for f in range(nf)
        ]
        for l in range(layers):
            for k in range(11):
                at = slice(k * rank, (k + 1) * rank)
                model_grad[l, k, b] = sum(keeps[f] * all_sums[f, l, at].astype(F32) for f in range(nf))
            for k in range(3):
                at = slice(k * rank, (k + 1) * rank)
                hidden_grad[l, k, b] = sum(keeps[f] * all_units[f, l, at].astype(F32) for f in range(nf))
    moves[0].finish()
    for core in range(2):

        def widen(at, core=core):
            rows = landed.shape[1]
            tokens_grad[pl.ds(pl.multiple_of(core * rows + at.start, 16), at.size)] = landed[core, at].astype(F32)

        by_rows(landed.shape[1], widen)
    for copy in copies:
        copy.wait_send()


class Plan:
    def __init__(self, n, nf, rows, scatters, spreads, schedule):
        self.n, self.nf, self.rows, self.schedule = n, nf, rows, schedule
        self.scatters, self.spreads = scatters, spreads

    def ins(self):
        return [(blocks, True) for blocks, _ in self.scatters] + [(w, True) for w in self.spreads]

    def outs(self):
        made = [(shape, BF, True) for _, shape in self.scatters]
        return made + [(w.shape, BF, True) for w in self.spreads]

    def semaphores(self):
        made = Spread.scatter_semaphores(self.n) * len(self.scatters)
        return made + Spread.spread_semaphores(self.n, self.nf) * len(self.spreads)

    def split(self, refs):
        a, b = len(self.scatters), len(self.spreads)
        count = 2 * a + 6 * b
        refs = list(refs)
        taken = refs[: a + b], refs[a + b : 2 * (a + b)], refs[len(refs) - count :]
        return taken, refs[2 * (a + b) : len(refs) - count]

    def work(self, place, nf, jobs):
        a, b = len(self.scatters), len(self.spreads)
        ins, outs, sems = jobs
        scatters = [(ins[i], outs[i], sems[2 * i : 2 * i + 2]) for i in range(a)]
        spreads = [(outs[a + i], sems[2 * a + 6 * i : 2 * a + 6 * i + 6]) for i in range(b)]
        return Work(place, nf, self.rows, scatters, spreads, self.schedule)

    def late(self, jobs):
        return jobs[1][len(self.scatters)]


class Pace:
    def __init__(self, loads, stores):
        self.loads, self.stores = loads, stores
        for copy in loads:
            copy.start()

    def ready(self):
        for copy in self.loads:
            copy.wait()

    def flush(self):
        for copy in self.stores:
            copy.start()

    def end(self):
        for copy in self.stores:
            copy.wait()


def call(kernel, collective, ins, outs, scratch, plan=None):
    spec = lambda hbm: pl.BlockSpec(memory_space=pl.ANY if hbm else pltpu.VMEM)
    aliases = {}
    if plan is not None:
        first_in, count = len(ins), len(plan.scatters)
        aliases = {first_in + count + i: count + i for i in range(len(plan.spreads))}
        ins, outs, scratch = ins + plan.ins(), plan.outs() + outs, scratch + plan.semaphores()
    late_in = [i for i, (_, hbm) in enumerate(ins) if hbm == "paced"]
    late_out = [i for i, (_, _, hbm) in enumerate(outs) if hbm == "paced"]
    extra = [pltpu.VMEM(ins[i][0].shape, ins[i][0].dtype) for i in late_in]
    extra += [pltpu.VMEM(outs[i][0], outs[i][1]) for i in late_out]
    if late_in or late_out:
        extra.append(pltpu.SemaphoreType.DMA((len(late_in) + len(late_out),)))

        def paced(*refs):
            refs, held = list(refs[: -len(extra)]), refs[-len(extra) :]
            loads, stores = [], []
            for slot, i in enumerate(late_in):
                loads.append(pltpu.make_async_copy(refs[i], held[slot], held[-1].at[slot]))
                refs[i] = held[slot]
            for slot, i in enumerate(late_out, len(late_in)):
                stores.append(pltpu.make_async_copy(held[slot], refs[len(ins) + i], held[-1].at[slot]))
                refs[len(ins) + i] = held[slot]
            pace = Pace(loads, stores)
            kernel(*refs, pace=pace)
            pace.end()

        body = paced
    else:
        body = kernel
    made = pl.pallas_call(
        body,
        out_shape=[jax.ShapeDtypeStruct(shape, kind) for shape, kind, _ in outs],
        in_specs=[spec(hbm) for _, hbm in ins],
        out_specs=[spec(hbm) for _, _, hbm in outs],
        scratch_shapes=scratch + extra,
        input_output_aliases=aliases,
        compiler_params=pltpu.CompilerParams(
            collective_id=collective, has_side_effects=True, vmem_limit_bytes=62 << 20
        ),
    )(*[array for array, _ in ins])
    return list(made)


def line_bits(parent_row, seg):
    number = jnp.arange(NSEG)
    one = lambda x: lax.shift_left(jnp.ones_like(x), x)
    grand = jnp.sum(jnp.where(parent_row[:, None] == number[None, :], parent_row[None, :], 0), axis=1)
    line = one(number) | one(parent_row) | one(grand)
    mine = jnp.sum(jnp.where(seg[:, None] == number[None, :], line[None, :], 0), axis=1)
    return mine, one(seg)


def keep_factor(layer):
    return 0.2 + 0.6 * math.exp(-0.3 * layer)


def chips_of(nf, nc):
    h = nc // 2
    for f in range(nf):
        for c in range(nc):
            yield f * nc + c, (f // 2, f % 2, c // h, c % h)


def permute(x, nf, nc, target):
    h = nc // 2
    pairs = []
    for source, spot in chips_of(nf, nc):
        f_hi, f_lo, c_hi, c_lo = target(*spot)
        pairs.append((source, (f_hi * 2 + f_lo) * nc + c_hi * h + c_lo))
    return lax.ppermute(x, ("fsdp", "ctx"), pairs)


def swap_trees(x, nf, nc):
    return permute(x, nf, nc, lambda f_hi, f_lo, c_hi, c_lo: (f_hi, c_hi, f_lo, c_lo))


def shards(
    nf,
    nc,
    tokens,
    cotangent,
    segments,
    depths,
    parents,
    tree_adapter_index,
    layer_norm_gains,
    difference_lambda,
    query_key_value_weight,
    output_weight,
    gate_up_weight,
    down_weight,
    adapter_model_factors,
    adapter_hidden_factors,
):
    n = nc
    place = Place(n)
    q, t = place.q, place.t
    tokens_dev, width = tokens.shape
    rows = tokens_dev // 2
    tree = tokens_dev * n
    layers, weight_rows = query_key_value_weight.shape[:2]
    heads_tp = difference_lambda.shape[1]
    share = max(1, n // heads_tp)
    head = q // share
    hidden_tp = down_weight.shape[2]
    units = (hidden_tp + n * 128 - 1) // (n * 128) * 128
    rank, adapters = adapter_model_factors.shape[3], adapter_model_factors.shape[2]
    h = n // 2

    notes = jnp.concatenate([segments, depths, parents[0], tree_adapter_index])
    order = jnp.arange(n)
    of_tree = jnp.zeros((n, notes.shape[0]), jnp.int32)
    for d in range(n):

        def hand_out(f_hi, f_lo, c_hi, c_lo, d=d):
            to = (c_hi * (n // 2) + c_lo) ^ d
            return f_hi, to // (n // 2), f_lo, to % (n // 2)

        part_of_tree = permute(notes, nf, nc, hand_out)
        of_tree = of_tree + jnp.where(order[:, None] == flip(q, d), part_of_tree[None], 0)
    seg, dep = of_tree[:, :tokens_dev].reshape(tree), of_tree[:, tokens_dev : 2 * tokens_dev].reshape(tree)
    parent_row, slot = of_tree[0, 2 * tokens_dev : 2 * tokens_dev + NSEG], of_tree[0, 2 * tokens_dev + NSEG]
    own_tokens = lax.dynamic_slice_in_dim(tokens, t * rows, rows, 0)
    own_cotangent = lax.dynamic_slice_in_dim(cotangent, t * rows, rows, 0)
    residual = swap_trees(own_tokens, nf, nc)
    own_cotangent = swap_trees(own_cotangent, nf, nc)

    query_bits, key_bits = line_bits(parent_row, seg)
    query_bits, key_bits = query_bits[:, None], key_bits[None, :]
    frequency = 10000.0 ** (-jnp.arange(HD // 2).astype(F32) / (HD // 2))
    angles = dep.astype(F32)[:, None] * frequency[None, :]
    cosine, sine = jnp.cos(angles), jnp.sin(angles)
    cosine = jnp.concatenate([cosine, cosine], axis=1)
    sine = jnp.concatenate([-sine, sine], axis=1)
    gains = layer_norm_gains

    a_all = lax.dynamic_index_in_dim(adapter_model_factors, slot, 2, keepdims=False)
    e_all = lax.dynamic_index_in_dim(adapter_hidden_factors, slot, 2, keepdims=False)
    a_model = a_all.reshape(layers, 11 * rank, width)
    e_all = e_all.reshape(layers, 3 * rank, -1)
    head_at = (t * heads_tp + head) * VD

    heads_of = lax.dynamic_slice_in_dim(a_all, head_at, VD, 3)
    a_head = jnp.concatenate([heads_of[:, 3:4], heads_of[:, 6:9]], axis=1).reshape(layers, 4 * rank, VD)

    def unit_columns(x):
        x = lax.dynamic_slice_in_dim(x, t * hidden_tp, hidden_tp, x.ndim - 1)
        x = jnp.pad(x, ((0, 0),) * (x.ndim - 1) + ((0, n * units - hidden_tp),))
        return lax.dynamic_slice_in_dim(x, q * units, units, x.ndim - 1)

    e_model = unit_columns(e_all)

    part = 1.0 / share
    vmem = lambda *spec: pltpu.VMEM(*spec)
    calls = [0]
    whole_x = ((n, 2, rows, width), BF)
    sems = Gather.semaphores(n) + Reduce.scratch(n, rows, width)
    pair = pltpu.SemaphoreType.DMA((4,))
    big = [vmem(*whole_x), vmem(*whole_x)]

    def run(kernel, ins, outs, scratch, plan=None):
        calls[0] += 1
        return call(kernel, calls[0], ins, outs, scratch, plan)

    near = lambda *arrays: [(array, False) for array in arrays]
    far = lambda *arrays: [(array, True) for array in arrays]
    paced = lambda *arrays: [(array, "paced") for array in arrays]
    out = lambda shape, kind, hbm=False: (shape, kind, hbm)

    dma = pltpu.SemaphoreType.DMA
    c_a, c_g, c_d = 4 * VD, 2 * units, units
    tall = nf * n * weight_rows
    cut = lambda columns: out((n, weight_rows, columns), BF)
    calls[0] += 1
    made = call(
        functools.partial(weights_kernel, n, nf, units, share, layers),
        calls[0],
        far(jnp.transpose(query_key_value_weight, (0, 2, 1, 3)), output_weight, gate_up_weight, down_weight),
        [out((tall, c_a), BF, True), out((tall, c_g), BF, True), out((tall, c_d), BF, True)]
        + ([cut(c_a)] + [cut(c_g)] + [cut(c_d)]) * (layers - 1),
        [
            vmem((n, weight_rows, c_a), BF),
            vmem((n, weight_rows, c_g), BF),
            vmem((n, weight_rows, c_d), BF),
            vmem((layers, weight_rows, 2, hidden_tp), BF),
            vmem((layers, weight_rows, hidden_tp), BF),
            dma((layers, n, 4)),
            dma((layers, 2)),
        ]
        + (Spread.scatter_semaphores(n) + Spread.spread_semaphores(n, nf)) * 2
        + Spread.scatter_semaphores(n),
    )
    w_a, w_g, w_d = [made[0]], [made[1]], [made[2]]
    a_blocks = [None] + made[3 : 2 + layers]
    g_blocks = [None] + made[2 + layers : 1 + 2 * layers]
    d_blocks = [None] + made[1 + 2 * layers :]

    def plan_of(scatters, spreads, *schedule):
        return Plan(n, nf, weight_rows, scatters, spreads, schedule)

    saved = []
    for l in range(layers):
        last = l == layers - 1
        w_attention = w_a[l]
        lam = lax.dynamic_slice_in_dim(difference_lambda[l], head, 1).reshape(1, 1)
        gain_a, gain_f = gains[l, 0:1], gains[l, 1:2]
        shared = paced(a_model[l]) + near(a_head[l]) + paced(cosine, sine, query_bits) + near(key_bits, lam)
        plan = plan_of(
            [] if last else [(a_blocks[l + 1], (tall, c_a)), (g_blocks[l + 1], (tall, c_g))],
            [w_g[l], w_d[l]],
            moves("forward", 0, parts(n, 0, 1)) + moves("spread", 0, parts(n, 1, 4)),
            moves("forward", 0, parts(n, 1, 2)) + ([] if last else [("scatter", 0)]),
            moves("spread", 1, parts(n, 0, 2)) + moves("forward", 0, parts(n, 2, 3)),
            moves("forward", 0, parts(n, 3, 4)) + ([] if last else [("scatter", 1)]),
        )
        got = run(
            functools.partial(attention_forward, n, nf, l, part, rank, True, plan),
            near(residual, gain_a) + far(w_attention) + shared,
            [
                out((rows, width), F32),
                out(*whole_x, True),
                out((tree, VD), BF, "paced"),
                out((tree, VD), BF, "paced"),
                out((tree, VD), BF, "paced"),
                out((tree, 3 * rank), BF, "paced"),
                out((tree, 2), F32, "paced"),
                out((tree, VD), BF, "paced"),
                out((tree, VD), BF, "paced"),
                out((tree, rank), BF, "paced"),
            ],
            big + [vmem((width, 4 * VD), BF), vmem((3 * rank, 3 * VD), BF), pair] + sems,
            plan,
        )
        if not last:
            w_a.append(got[0])
            w_g.append(got[1])
            got = got[2:]
        w_g[l], w_d[l], middle, *kept = got
        plan = plan_of(
            [] if last else [(d_blocks[l + 1], (tall, c_d))],
            [w_d[l]] + ([] if last else [w_a[l + 1], w_g[l + 1]]),
            moves("forward", 0, parts(n, 0, 2)) + moves("spread", 0, parts(n, 2, 4)),
            moves("forward", 0, parts(n, 2, 3)),
            moves("forward", 0, parts(n, 3, 4)) + ([] if last else moves("spread", 1, parts(n, 0, 4)) + [("scatter", 0)]),
            [] if last else moves("forward", 1, parts(n, 0, 1)),
            [] if last else moves("forward", 1, parts(n, 1, 2)) + moves("spread", 2, parts(n, 0, 1)),
            [] if last else moves("forward", 1, parts(n, 2, 4)),
        )
        ffn = run(
            functools.partial(ffn_forward, n, nf, units, rank, last, plan),
            near(middle, gain_f) + far(w_g[l]) + paced(a_model[l]) + near(e_model[l])
            + (near(own_cotangent) if last else []),
            ([out(*whole_x, True)] if last else [])
            + [
                out((rows, width), F32),
                out(*whole_x, True),
                out((tree, units), BF, "paced"),
                out((tree, units), BF, "paced"),
                out((tree, units), BF, "paced"),
                out((tree, 2 * rank), BF, "paced"),
                out((tree, rank), BF),
            ],
            big + [vmem((width, 3 * units), BF), vmem((2 * rank, 2 * units), BF), pair] + sems
            + ([vmem(*whole_x)] + Gather.semaphores(n) if last else []),
            plan,
        )
        if not last:
            w_d.append(ffn[0])
            w_d[l], w_a[l + 1], w_g[l + 1], *ffn = ffn[1:]
        else:
            w_d[l], gathered, *ffn = ffn
        saved.append((residual, middle, gain_a, gain_f, shared, kept, ffn[1:]))
        residual = ffn[0]

    grad = own_cotangent
    units_here, sums_here, earlier, block = [], [], [], width // (2 * n)
    wide = hidden_tp // n
    for l in reversed(range(layers)):
        residual_in, middle, gain_a, gain_f, shared, kept, ffn = saved[l]
        carry = l == layers - 1
        made = run(
            functools.partial(ffn_backward, n, units, rank, carry),
            near(grad) + paced(middle) + near(gain_f) + far(w_g[l], w_d[l]) + paced(a_model[l]) + near(e_model[l])
            + far(ffn[0]) + paced(*ffn[1:])
            + (near(residual) + far(gathered) if carry else near(sums_here[0], units_here[0])),
            ([out((2, rows, width), BF)] if carry else [out((nf, 12 * rank, block), BF), out((nf, 3 * rank, wide), BF)])
            + [
                out((rows, width), F32),
                out((rank, width), BF),
                out((2 * rank, width), BF),
                out((4 * rank, units), BF),
            ],
            big
            + [
                vmem((width, 3 * units), BF),
                vmem(*whole_x),
                vmem((tree, 2 * units), BF),
                vmem((tree, 2 * rank), BF),
                vmem((tree, rank), BF),
                vmem((2 * rank, 2 * units), BF),
                pair,
            ]
            + sems
            + ([vmem((rows, width), BF)] + Home.semaphores() if carry else [dma((2, 2)), dma((2, 2))]),
        )
        if carry:
            outputs, *made = made
        else:
            earlier += made[:2]
            made = made[2:]
        grad, *ffn_grads = made
        grad, own_sum, all_units = run(
            functools.partial(attention_backward, n, l, share, heads_tp, rank),
            near(grad) + paced(residual_in) + near(gain_a) + far(w_a[l]) + shared + far(kept[0])
            + paced(*kept[1:]) + near(*ffn_grads),
            [
                out((rows, width), F32),
                out((12 * rank, block), BF),
                out((n, 2, 4 * rank, units), BF),
            ],
            big
            + [
                vmem((width, 4 * VD), BF),
                vmem((tree, VD), BF),
                vmem((tree, VD), F32),
                vmem((tree, VD), F32),
                vmem((tree, VD), F32),
                vmem((tree, 3 * VD), BF),
                vmem((tree, 3 * rank), BF),
                vmem((tree, rank), BF),
                vmem((3 * rank, 3 * VD), BF),
                vmem((rank, width), BF),
                vmem((n, 2, 12 * rank, block), BF),
                pair,
            ]
            + sems
            + Gather.semaphores(n)
            + Reduce.scratch(n, 12 * rank, block),
        )

        number = (q * 2 + t) * (hidden_tp // n)
        half = lax.dynamic_index_in_dim(all_units, number // hidden_tp, 1, keepdims=False)
        flat = half[:, : 3 * rank].transpose(1, 0, 2).reshape(3 * rank, n * units)
        units_here.insert(0, lax.dynamic_slice_in_dim(flat, number % hidden_tp, hidden_tp // n, 1))
        sums_here.insert(0, own_sum)

    own = adapters // nf
    dma = pltpu.SemaphoreType.DMA
    tokens_grad, grad_model, grad_hidden = run(
        functools.partial(finish_kernel, n, nf, layers, rank),
        near(grad, sums_here[0], units_here[0], slot.astype(F32).reshape(1, 1), *earlier),
        [
            out((2 * rows, width), F32),
            out((layers, 11, own, rank, block), F32),
            out((layers, 3, own, rank, wide), F32),
        ],
        [
            vmem((rows, width), BF),
            vmem((2, rows, width), BF),
            vmem((12 * rank, block), BF),
            vmem((nf, layers, 12 * rank, block), BF),
            vmem((nf, layers, 3 * rank, wide), BF),
            dma((3, 2)),
            dma((3, 2)),
            dma((layers, 2, nf)),
            dma((layers, 2, nf)),
        ],
    )
    return (
        outputs.reshape(2 * rows, width),
        tokens_grad,
        grad_model,
        grad_hidden,
    )


def solution(mesh):
    in_specs = (
        P(("fsdp", "ctx"), None),
        P(("fsdp", "ctx"), None),
        P(("fsdp", "ctx")),
        P(("fsdp", "ctx")),
        P("fsdp", None),
        P("fsdp"),
        P(),
        P(None, "tp"),
        P(None, ("fsdp", "ctx"), None, "tp"),
        P(None, ("fsdp", "ctx"), "tp"),
        P(None, ("fsdp", "ctx"), None, "tp"),
        P(None, ("fsdp", "ctx"), "tp"),
        P(),
        P(),
    )
    out_specs = (
        P(("fsdp", "ctx"), None),
        P(("fsdp", "ctx"), None),
        P(None, None, "fsdp", None, ("ctx", "tp")),
        P(None, None, "fsdp", None, ("ctx", "tp")),
    )
    body = functools.partial(shards, mesh.shape["fsdp"], mesh.shape["ctx"])
    return jax.shard_map(body, mesh=mesh, in_specs=in_specs, out_specs=out_specs, check_vma=False)
```

```python
import functools
import math

import jax
import jax.numpy as jnp
from jax import lax
from jax.experimental import pallas as pl
from jax.experimental.pallas import tpu as pltpu
from jax.sharding import PartitionSpec as P

HD = 128
VD = 256
NSEG = 13
EPSILON = 1e-05
ADAPTER_SCALE = 0.5
NEGATIVE_BIG = -1e30
MESH = pl.DeviceIdType.MESH
BF = jnp.bfloat16
F32 = jnp.float32


class Place:
    def __init__(self, n):
        self.n, self.h = n, n // 2
        self.f, self.c, self.t = lax.axis_index("fsdp"), lax.axis_index("ctx"), lax.axis_index("tp")
        self.f_hi, self.f_lo = self.f // 2, self.f % 2
        self.c_hi, self.c_lo = self.c // self.h, self.c % self.h
        self.q = self.f_lo * self.h + self.c_lo
        self.away = self.f_lo + self.c_hi - 2 * self.f_lo * self.c_hi
        self.home = {"fsdp": self.f_hi * 2 + self.c_hi, "ctx": self.f_lo * self.h + self.c_lo}
        self.pos = self.f_lo * (n - 1) + (1 - 2 * self.f_lo) * self.c_lo

    def ring(self, k):
        n, h = self.n, self.h
        p = lax.rem(self.pos + k + 2 * n, n)
        low = p // h
        column = (1 - low) * p + low * (n - 1 - p)
        device = {"fsdp": self.f_hi * 2 + low, "ctx": self.c_hi * h + column}
        return low * h + column, device


def remote(src, dst, send, recv, device):
    copy = pltpu.make_async_remote_copy(
        src_ref=src, dst_ref=dst, send_sem=send, recv_sem=recv, device_id=device, device_id_type=MESH
    )
    copy.start()
    return copy


def when_even(place, body):
    even = place.pos % 2 == 0
    pl.when(even)(lambda: body(True))
    pl.when(jnp.logical_not(even))(lambda: body(False))


def flip(number, bits):
    b = 1
    while b <= bits:
        if bits & b:
            number = number + b * (1 - 2 * ((number // b) % 2))
        b *= 2
    return number


class Spread:
    def __init__(self, place, nf, w, rows):
        self.place, self.nf, self.w, self.rows = place, nf, w, rows
        self.g = place.f_hi * 2 + place.c_hi
        self.links = range(1, nf // 2)
        self.scattered, self.sent = [], []
        self.to_partner, self.along, self.onward, self.got = {}, {}, {}, []

    @staticmethod
    def scatter_semaphores(n):
        dma = pltpu.SemaphoreType.DMA
        return [dma((n,)), dma((n,))]

    @staticmethod
    def spread_semaphores(n, nf):
        dma = pltpu.SemaphoreType.DMA
        return [dma((n,))] * 2 + [dma((n, max(1, nf // 2 - 1)))] * 4

    def block(self, g, q):
        n, h = self.place.n, self.place.h
        source = (g // 2 * 2 + q // h) * n + g % 2 * h + q % h
        start = pl.multiple_of(source * self.rows, self.rows)
        return self.w.at[pl.ds(start, self.rows)]

    def chip(self, q):
        place = self.place
        return {"fsdp": place.f_hi * 2 + q // place.h, "ctx": place.c_hi * place.h + q % place.h}

    def partner(self):
        place = self.place
        return {"ctx": (1 - place.c_hi) * place.h + place.c_lo}

    def line(self, e):
        return {"fsdp": flip(self.place.f_hi, e) * 2 + self.place.f_lo}

    def scatter(self, blocks, send, recv):
        q = self.place.q
        own = self.block(self.g, q)
        copy = pltpu.make_async_copy(blocks.at[q], own, recv.at[0])
        copy.start()
        self.scattered.append(copy)
        for d in range(1, self.place.n):
            to = flip(q, d)
            self.scattered.append(remote(blocks.at[to], own, send.at[d], recv.at[d], self.chip(to)))

    def arrived(self, d):
        if d:
            self.scattered[d].wait_recv()
        else:
            self.scattered[0].wait()

    def scatter_sent(self):
        for copy in self.scattered[1:]:
            copy.wait_send()

    def use(self, *sems):
        self.sems = sems

    def spread(self, d):
        send_z, recv_z, send_y, recv_y = self.sems[:4]
        at = self.block(self.g, flip(self.place.q, d))
        self.to_partner[d] = remote(at, at, send_z.at[d], recv_z.at[d], self.partner())
        for e in self.links:
            self.along[d, e] = remote(at, at, send_y.at[d, e - 1], recv_y.at[d, e - 1], self.line(e))

    def landed(self, d):
        if d in self.to_partner and d not in self.got:
            self.to_partner[d].wait_recv()
            self.got.append(d)

    def forward(self, d):
        send, recv = self.sems[4:]
        self.landed(d)
        at = self.block(flip(self.g, 1), flip(self.place.q, d))
        for e in self.links:
            self.onward[d, e] = remote(at, at, send.at[d, e - 1], recv.at[d, e - 1], self.line(e))

    def complete(self):
        for d in list(self.to_partner):
            self.landed(d)
        for copy in list(self.along.values()) + list(self.onward.values()):
            copy.wait_recv()

    def sent_all(self):
        for copies in (self.to_partner, self.along, self.onward):
            for copy in copies.values():
                copy.wait_send()


def enter(place, nf=0, scatters=False, home=False, ring=True, trees=0):
    bar = pltpu.get_barrier_semaphore()
    devices = [{"tp": 1 - place.t}]
    guide = Spread(place, nf, None, 0)
    if scatters:
        devices += [guide.chip(flip(place.q, d)) for d in range(1, place.n)]
    elif ring:
        devices += [place.ring(1)[1], place.ring(-1)[1]]
    if nf:
        devices += [guide.partner()] + [guide.line(e) for e in guide.links]
    devices += [{"fsdp": flip(place.f, e)} for e in range(1, trees)]
    for device in devices:
        pl.semaphore_signal(bar, inc=1, device_id=device, device_id_type=MESH)
    count = len(devices)
    if home:

        @pl.when(place.away == 1)
        def greet():
            pl.semaphore_signal(bar, inc=1, device_id=place.home, device_id_type=MESH)

        count = count + place.away
    pl.semaphore_wait(bar, count)


class Home:
    def __init__(self, place, out, send, recv):
        self.place, self.out = place, out
        self.send, self.recv = send, recv

    @staticmethod
    def semaphores():
        dma = pltpu.SemaphoreType.DMA
        return [dma((2,)), dma((2,))]

    def start(self, rows):
        place, slot = self.place, self.out.at[self.place.t]
        far = pltpu.make_async_remote_copy(
            src_ref=rows, dst_ref=slot, send_sem=self.send.at[0], recv_sem=self.recv.at[0],
            device_id=place.home, device_id_type=MESH,
        )
        near = pltpu.make_async_copy(rows, slot, self.recv.at[0])
        self.far = far
        pl.when(place.away == 1)(far.start)
        pl.when(place.away == 0)(near.start)
        self.near = near

    def land(self, share=True):
        pl.when(self.place.away == 1)(self.far.wait)
        pl.when(self.place.away == 0)(self.near.wait)
        if share:
            slot = self.out.at[self.place.t]
            self.across = remote(slot, slot, self.send.at[1], self.recv.at[1], {"tp": 1 - self.place.t})

    def finish(self):
        self.across.wait()


class TreeMove(Home):
    def __init__(self, place, rows, out, send, recv):
        super().__init__(place, out, send, recv)
        self.rows = rows
        self.slot = out.at[place.f]

    def start(self):
        place = self.place
        target = self.out.at[place.f_hi * 2 + place.c_hi]
        self.far = pltpu.make_async_remote_copy(
            src_ref=self.rows, dst_ref=target, send_sem=self.send.at[0], recv_sem=self.recv.at[0],
            device_id=place.home, device_id_type=MESH,
        )
        self.near = pltpu.make_async_copy(self.rows, target, self.recv.at[0])
        pl.when(place.away == 1)(self.far.start)
        pl.when(place.away == 0)(self.near.start)

    def land(self):
        super().land(False)


class Work:
    def __init__(self, place, nf, rows, scatters, spreads, schedule):
        self.n, self.schedule = place.n, schedule
        self.scatters, self.spreads = [], []
        for blocks, w, sems in scatters:
            self.scatters.append((Spread(place, nf, w, rows), blocks, sems))
        for w, sems in spreads:
            piece = Spread(place, nf, w, rows)
            piece.use(*sems)
            self.spreads.append(piece)

    def at(self, point):
        for what, i, *d in self.schedule[point] if point < len(self.schedule) else ():
            if what == "scatter":
                piece, blocks, sems = self.scatters[i]
                piece.scatter(blocks, *sems)
            elif what == "spread":
                self.spreads[i].spread(*d)
            else:
                self.spreads[i].forward(*d)

    def complete(self, i):
        self.spreads[i].complete()

    def settle(self, done=()):
        for i, piece in enumerate(self.spreads):
            if i not in done:
                piece.complete()
            piece.sent_all()
        for piece, _, _ in self.scatters:
            for d in range(self.n):
                piece.arrived(d)
            piece.scatter_sent()


def parts(n, first, last):
    return range(first * n // 4, last * n // 4)


def moves(what, piece, places):
    return [(what, piece, d) for d in places]


def weights_kernel(
    n, nf, units, share, layers,
    qkv, output, gate_up, down, *refs,
):
    place = Place(n)
    rows, hidden = down.shape[1:]
    w_a, w_g, w_d = refs[:3]
    later = refs[3 : 3 * layers]
    a_first, g_first, d_first, raw_g, raw_d, cut_sems, raw_sems = refs[3 * layers : 3 * layers + 7]
    sems = refs[3 * layers + 7 :]
    a_blocks = [a_first] + list(later[: layers - 1])
    g_blocks = [g_first] + list(later[layers - 1 : 2 * layers - 2])
    d_blocks = [d_first] + list(later[2 * layers - 2 :])
    cuts = []
    for l in range(layers):
        for q in range(n):
            columns = pl.ds(q // share * VD, VD)
            for i in range(4):
                source = qkv.at[l, i, :, columns] if i < 3 else output.at[l, :, columns]
                target = a_blocks[l].at[q, :, pl.ds(i * VD, VD)]
                cuts.append(pltpu.make_async_copy(source, target, cut_sems.at[l, q, i]))
    for copy in cuts[: 4 * n]:
        copy.start()
    raws = []
    for l in range(layers):
        raws.append(pltpu.make_async_copy(gate_up.at[l], raw_g.at[l], raw_sems.at[l, 0]))
        raws.append(pltpu.make_async_copy(down.at[l], raw_d.at[l], raw_sems.at[l, 1]))
    for copy in raws:
        copy.start()
    attention, forward, back = (Spread(place, nf, w, rows) for w in (w_a, w_g, w_d))
    attention.use(*sems[2:8])
    forward.use(*sems[10:16])
    enter(place, nf, True)
    for copy in cuts[: 4 * n]:
        copy.wait()
    attention.scatter(a_first, *sems[:2])
    for copy in cuts[4 * n :]:
        copy.start()

    def fill(target, j, at, value):
        width = min(units, hidden - j * units)
        target[j, :, at : at + width] = value(pl.ds(j * units, width))
        if width < units:
            target[j, :, at + width : at + units] = jnp.zeros((rows, units - width), BF)

    def cut_gate_up(l):
        raws[2 * l].wait()
        for i in range(2):
            for j in range(n):
                fill(g_blocks[l], j, i * units, lambda at, i=i: raw_g[l, :, i, at])

    def cut_down(l):
        raws[2 * l + 1].wait()
        for j in range(n):
            fill(d_blocks[l], j, 0, lambda at: raw_d[l, :, at])

    cut_gate_up(0)
    for d in range(n):
        attention.arrived(d)
        attention.spread(d)
    forward.scatter(g_first, *sems[8:10])
    cut_down(0)
    back.scatter(d_first, *sems[16:18])
    for d in parts(n, 0, 1):
        attention.forward(d)
    for l in range(1, layers):
        cut_gate_up(l)
        cut_down(l)
    for copy in cuts[4 * n :]:
        copy.wait()
    for d in parts(n, 1, 3):
        attention.forward(d)
    for d in range(n):
        forward.arrived(d)
    for d in parts(n, 0, 1):
        forward.spread(d)
    for d in parts(n, 3, 4):
        attention.forward(d)
    attention.complete()
    forward.complete()
    attention.scatter_sent()
    attention.sent_all()
    forward.scatter_sent()
    forward.sent_all()
    for d in range(n):
        back.arrived(d)
    back.scatter_sent()


class Gather:
    def __init__(self, place, x, send_r, recv_r, send_l, recv_l, core_send, core_recv, lean=False):
        self.place, self.x = place, x
        self.sems = (send_r, recv_r, send_l, recv_l, core_send, core_recv)
        self.lean = lean and place.n == 4
        self.right, self.left, self.across = {}, {}, []

    @staticmethod
    def semaphores(n):
        dma = pltpu.SemaphoreType.DMA
        return [dma((n,))] * 4 + [dma((n,))] * 2

    def _make(self, s):
        place, x = self.place, self.x
        send_r, recv_r, send_l, recv_l = self.sems[:4]
        top = x.shape[2] // 2
        last = s == place.n // 2 - 1
        for i in range(1 if last and not self.lean else 2):
            for made, sign, send, recv in ((self.right, 1, send_r, recv_r), (self.left, -1, send_l, recv_l)):
                piece = i if sign > 0 else 1 - i
                at = x.at[place.ring(-sign * s)[0], place.t, pl.ds(piece * top, top)]
                made[s, i] = pltpu.make_async_remote_copy(
                    src_ref=at, dst_ref=at, send_sem=send.at[2 * s + i], recv_sem=recv.at[2 * s + i],
                    device_id=place.ring(sign)[1], device_id_type=MESH,
                )

    def _cross(self, q):
        core_send, core_recv = self.sems[4:]
        slot, at = len(self.across), self.x.at[q, self.place.t]
        other = {"tp": 1 - self.place.t}
        self.across.append(remote(at, at, core_send.at[slot], core_recv.at[slot], other))

    def begin(self):
        for s in range(self.place.n // 2):
            self._make(s)
        for i in range(2):
            self.right[0, i].start()
            self.left[0, i].start()
        self._cross(self.place.q)

    def _hop(self, s):
        last = self.place.n // 2 - 1
        if not self.lean:
            for i in range(1 if s == last else 2):
                for stream in (self.right, self.left):
                    stream[s, i].wait_recv()
                    if s < last - 1 or (s == last - 1 and i == 0):
                        stream[s + 1, i].start()
            return

        def body(even):
            along_ctx, along_fsdp = (self.left, self.right) if even else (self.right, self.left)
            for i in range(2):
                if s == 0:
                    along_ctx[0, i].wait_recv()
                    along_ctx[1, i].start()
                    along_fsdp[0, i].wait_recv()
                else:
                    along_fsdp[1, i].wait_recv()

        when_even(self.place, body)

    def chunks(self):
        place, half = self.place, self.place.n // 2
        self.across[0].wait_recv()
        yield place.q
        for s in range(half):
            self._hop(s)
            arrived = [place.ring(half)[0]] if s == half - 1 else [place.ring(-s - 1)[0], place.ring(s + 1)[0]]
            first = len(self.across)
            for q in arrived:
                self._cross(q)
            for i, q in enumerate(arrived):
                self.across[first + i].wait_recv()
                yield q

    def finish(self):
        last = self.place.n // 2 - 1
        for s in range(last + 1):
            for i in range(2):
                if s < last:
                    self.right[s, i].wait_send()
                    self.left[s, i].wait_send()
                elif not self.lean and i == 0:
                    self.right[s, 0].wait_send()
                    self.left[s, 0].wait_send()
        if self.lean:

            def body(even):
                for i in range(2):
                    (self.left if even else self.right)[1, i].wait_send()

            when_even(self.place, body)
        for copy in self.across:
            copy.wait_send()


def by_rows(count, body, step=16):
    def one(i, carry):
        body(pl.ds(pl.multiple_of(i * step, step), step))
        return carry

    lax.fori_loop(0, count // step, one, 0)


class Reduce:
    def __init__(self, place, p, from_core, in_r, in_l, send_r, recv_r, send_l, recv_l, core_send, core_recv, lean=False):
        self.place, self.p, self.from_core, self.in_r, self.in_l = place, p, from_core, in_r, in_l
        self.sems = (send_r, recv_r, send_l, recv_l, core_send, core_recv)
        self.lean = lean and place.n == 4
        half = place.n // 2
        self.order = [half] + [k for j in range(half - 1, 0, -1) for k in (j, -j)] + [0]
        self.chips = {k: place.ring(k)[0] for k in self.order}
        self.across, self.copies = {}, {}
        for sign in (1, -1):
            for s in range(half):
                for piece in range(2):
                    if s or self.lean or piece == (sign < 0):
                        self._copy(sign, s, piece)

    @staticmethod
    def scratch(n, rows, width):
        dma = pltpu.SemaphoreType.DMA
        wide = [pltpu.VMEM((n, rows, width), BF)] + [pltpu.VMEM((n // 2, rows, width), BF)] * 2
        return wide + [dma((n // 2, 2))] * 4 + [dma((n,))] * 2

    def offer(self, k):
        core_send, core_recv = self.sems[4:]
        slot, q, t = len(self.across), self.chips[k], self.place.t
        self.across[k] = remote(
            self.p.at[q, 1 - t], self.from_core.at[q], core_send.at[slot], core_recv.at[slot], {"tp": 1 - t}
        )

    def _local(self, k, at):
        q = self.chips[k]
        return self.p[q, self.place.t, at].astype(F32) + self.from_core[q, at].astype(F32)

    def _add(self, k, piece, extra=None):
        top = self.p.shape[2] // 2

        def body(at):
            whole = pl.ds(pl.multiple_of(piece * top + at.start, 16), at.size)
            total = self._local(k, whole)
            if extra is not None:
                total = total + extra[whole].astype(F32)
            self.from_core[self.chips[k], whole] = total.astype(BF)

        by_rows(top, body)

    def _copy(self, sign, s, piece):
        if (sign, s, piece) not in self.copies:
            place, top = self.place, self.p.shape[2] // 2
            send, recv = self.sems[:2] if sign > 0 else self.sems[2:4]
            target = self.in_r if sign > 0 else self.in_l
            k = place.n // 2 - s
            rows = pl.ds(piece * top, top)
            self.copies[sign, s, piece] = pltpu.make_async_remote_copy(
                src_ref=self.from_core.at[self.chips[sign * k if s else k], rows], dst_ref=target.at[s, rows],
                send_sem=send.at[s, piece], recv_sem=recv.at[s, piece],
                device_id=place.ring(sign)[1], device_id_type=MESH,
            )
        return self.copies[sign, s, piece]

    def far(self):
        half = self.place.n // 2
        self.across[half].wait_recv()
        self._add(half, 0)
        self._add(half, 1)
        if self.lean:

            def body(even):
                for piece in range(2):
                    self._copy(-1 if even else 1, 0, piece).start()

            when_even(self.place, body)
        else:
            self._copy(1, 0, 0).start()
            self._copy(-1, 0, 1).start()

    def free(self):
        k = self.place.n // 2 - 1
        if self.lean:
            self.across[1].wait_recv()
            self.across[-1].wait_recv()

            def body(even):
                sign = -1 if even else 1
                for piece in range(2):
                    self._add(sign, piece)
                    self._copy(sign, 1, piece).start()

            when_even(self.place, body)
        elif k:
            for sign, piece in ((1, 1), (-1, 0)):
                self.across[sign * k].wait_recv()
                self._add(sign * k, piece)
                self._copy(sign, 1, piece).start()

    def near(self, s):
        half = self.place.n // 2
        k = half - s
        if self.lean:

            def body(even):
                sign = 1 if even else -1
                for piece in range(2):
                    self._copy(sign, 0, piece).wait_recv()
                    self._add(sign, piece, (self.in_r if even else self.in_l).at[0])
                    self._copy(sign, 1, piece).start()

            when_even(self.place, body)
            return
        if s > 1:
            self.across[k].wait_recv()
            self.across[-k].wait_recv()
        for sign, first, held in ((1, 0, self.in_r), (-1, 1, self.in_l)):
            for piece in (first,) if s == 1 else (first, 1 - first):
                self._copy(sign, s - 1, piece).wait_recv()
                self._add(sign * k, piece, held.at[s - 1])
                self._copy(sign, s, piece).start()

    def end(self, use):
        half = self.place.n // 2
        self.across[0].wait_recv()
        for sign in (1, -1):
            for piece in range(2):
                self._copy(sign, half - 1, piece).wait_recv()

        def body(at):
            use(at, self._local(0, at) + self.in_r[half - 1, at].astype(F32) + self.in_l[half - 1, at].astype(F32))

        by_rows(self.p.shape[2], body)

    def finish(self):
        half = self.place.n // 2
        if self.lean:

            def body(even):
                for piece in range(2):
                    self._copy(-1 if even else 1, 0, piece).wait_send()

            when_even(self.place, body)
        else:
            self._copy(1, 0, 0).wait_send()
            self._copy(-1, 0, 1).wait_send()
        for s in range(1, half):
            for sign in (1, -1):
                for piece in range(2):
                    self._copy(sign, s, piece).wait_send()
        for copy in self.across.values():
            copy.wait_send()

    def run(self, use, before=None, offered=False):
        if not offered:
            for k in self.order:
                self.offer(k)
            self.far()
            self.free()
        for s in range(1, self.place.n // 2):
            self.near(s)
        if before is not None:
            before()
        self.end(use)


def mm(a, b):
    return jnp.dot(a, b, preferred_element_type=F32)


def mm_t(a, b):
    return lax.dot_general(a, b, (((1,), (1,)), ((), ())), preferred_element_type=F32)


def t_mm(a, b):
    return lax.dot_general(a, b, (((0,), (0,)), ((), ())), preferred_element_type=F32)


def rms_scale(values):
    return lax.rsqrt(jnp.mean(values * values, axis=-1, keepdims=True) + EPSILON)


def norm_back(grad_normed, inputs, scale_rows, gain):
    unit = inputs * scale_rows
    scaled = grad_normed * gain
    return scale_rows * (scaled - unit * jnp.mean(scaled * unit, axis=-1, keepdims=True))


def tiles(count, width, body):
    def one(j, carry):
        body(pl.ds(pl.multiple_of(j * width, width), width))
        return carry

    lax.fori_loop(0, count // width, one, 0)


def tile_of(count):
    return 256 if count % 256 == 0 else 128


def turn(v, cosine, sine):
    return v * cosine + pltpu.roll(v, HD // 2, 1) * sine


def block_diagonal(out, parts, rank, width):
    out[...] = jnp.zeros(out.shape, out.dtype)
    for i in range(parts[1]):
        out[i * rank : (i + 1) * rank, i * width : (i + 1) * width] = parts[0][i * rank : (i + 1) * rank, :]


def write_norm(x_rows, source, gain):
    def body(at):
        v = source[at].astype(F32)
        x_rows[at] = (v * rms_scale(v) * gain[...]).astype(BF)

    by_rows(source.shape[0], body)


ROW_BLOCK = 128
KEY_STEP = 256


def row_blocks(tree, body):
    for j in range(tree // KEY_STEP):

        def one(i, carry, j=j):
            body(pl.ds(pl.multiple_of(j * KEY_STEP + i * ROW_BLOCK, ROW_BLOCK), ROW_BLOCK), (j + 1) * KEY_STEP)
            return carry

        lax.fori_loop(0, KEY_STEP // ROW_BLOCK, one, 0)


def seen(rows, keys, query_bits, key_bits):
    shared = (query_bits[rows] & key_bits[:, :keys]) != 0
    i = rows.start + lax.broadcasted_iota(jnp.int32, (ROW_BLOCK, keys), 0)
    j = lax.broadcasted_iota(jnp.int32, (ROW_BLOCK, keys), 1)
    return shared & (j <= i)


def attention_forward(
    n, nf, layer, part, rank, lean, plan,
    residual, gain, w_hbm, a_model, a_head, cosine, sine, query_bits, key_bits, lam, *refs, pace,
):
    jobs, refs = plan.split(refs)
    (middle, x_hbm, queries, keys, values, small, log_total, mixed, headed, side,
     x, p, w, raised, copy_sems, *sems) = refs
    place = Place(n)
    chip_rows, width = 2 * x_hbm.shape[2], x_hbm.shape[3]
    tree = n * chip_rows
    load = pltpu.make_async_copy(w_hbm, w, copy_sems.at[0])
    load.start()
    gather, reduce = Gather(place, x, *sems[:6], lean=lean), Reduce(place, p, *sems[6:], lean=lean)
    write_norm(x.at[place.q, place.t], residual, gain)
    block_diagonal(raised, (a_head[rank : 4 * rank], 3), rank, VD)
    work = plan.work(place, nf, jobs)
    enter(place, nf, bool(plan.scatters))
    gather.begin()
    work.at(0)
    pace.ready()
    load.wait()

    def project(q):
        rows = pl.ds(pl.multiple_of(q * chip_rows, chip_rows), chip_rows)
        v = x[q].reshape(chip_rows, width)
        low = mm_t(v, a_model[: 3 * rank]).astype(BF)
        small[rows] = low
        for i, out in enumerate((queries, keys, values)):
            at = slice(i * VD, (i + 1) * VD)
            made = mm(v, w[:, at]) + ADAPTER_SCALE * mm(low, raised[:, at])
            if i < 2:
                for c in range(2):
                    half = slice(c * HD, (c + 1) * HD)
                    out[rows, half] = turn(made[:, half], cosine[rows], sine[rows]).astype(BF)
            else:
                out[rows] = made.astype(BF)

    for q in gather.chunks():
        project(q)
    work.at(1)
    keep = pltpu.make_async_copy(x, x_hbm, copy_sems.at[1])
    keep.start()
    score_scale = HD ** (-0.5)
    weight = lam[...]

    def attend(rows, count):
        visible = seen(rows, count, query_bits, key_bits)
        both = []
        for c in range(2):
            at = slice(c * HD, (c + 1) * HD)
            scores = mm_t(queries[rows, at], keys[:count, at]) * score_scale
            scores = jnp.where(visible, scores, NEGATIVE_BIG)
            top = jnp.max(scores, axis=-1, keepdims=True)
            raw = jnp.exp(scores - top)
            total = jnp.sum(raw, axis=-1, keepdims=True)
            log_total[rows, c : c + 1] = top + jnp.log(total)
            both.append(raw * (1.0 / total))
        mix = mm((both[0] - weight * both[1]).astype(BF), values[:count])
        mixed[rows] = mix.astype(BF)
        head = (mix * rms_scale(mix) * keep_factor(layer)).astype(BF)
        headed[rows] = head
        side[rows] = mm_t(head, a_head[:rank]).astype(BF)

    row_blocks(tree, attend)
    pace.flush()
    work.at(2)

    for k in reduce.order:
        q = reduce.chips[k]
        rows = pl.ds(pl.multiple_of(q * chip_rows, chip_rows), chip_rows)
        head, low = headed[rows], side[rows]

        def out_tile(at):
            made = mm_t(head, w[at, 3 * VD :]) + ADAPTER_SCALE * mm(low, a_model[9 * rank : 10 * rank, at])
            p[q, :, :, at] = (made * part).astype(BF).reshape(2, chip_rows // 2, at.size)

        tiles(width, 512, out_tile)
        reduce.offer(k)
        if k == reduce.order[0]:
            reduce.far()
        if k == reduce.order[2]:
            reduce.free()
    work.at(3)
    for s in range(1, n // 2):
        reduce.near(s)
    work.at(4)

    def use(at, total):
        middle[at] = residual[at].astype(F32) + total

    reduce.end(use)
    work.at(5)
    keep.wait()
    gather.finish()
    reduce.finish()
    work.settle()


def ffn_forward(
    n, nf, units, rank, last, plan,
    residual, gain, w_hbm, a_model, e_model, *refs, pace,
):
    place = Place(n)
    if last:
        cotangent, *refs = refs
    jobs, refs = plan.split(refs)
    if last:
        all_refs = refs
        next_hbm, *refs, next_x = refs[:-6]
        next_gather = Gather(place, next_x, *all_refs[-6:])
    (following, x_hbm, gates, ups, hidden, small, side,
     x, p, w, raised, copy_sems, *sems) = refs
    chip_rows, width = 2 * x_hbm.shape[2], x_hbm.shape[3]
    tree = n * chip_rows
    load = pltpu.make_async_copy(w_hbm, w.at[:, pl.ds(0, 2 * units)], copy_sems.at[0])
    load.start()
    gather, reduce = Gather(place, x, *sems[:6], lean=not last), Reduce(place, p, *sems[6:], lean=not last)
    write_norm(x.at[place.q, place.t], residual, gain)
    block_diagonal(raised, (e_model, 2), rank, units)
    work = plan.work(place, nf, jobs)
    enter(place, nf, bool(plan.scatters))
    gather.begin()
    work.at(0)
    pace.ready()
    load.wait()
    step = tile_of(units)

    for number, q in enumerate(gather.chunks()):
        if number == n - 1:
            work.at(1)
        rows = pl.ds(pl.multiple_of(q * chip_rows, chip_rows), chip_rows)
        v = x[q].reshape(chip_rows, width)
        low = mm_t(v, a_model[4 * rank : 6 * rank]).astype(BF)
        small[rows] = low

        def unit_tile(at):
            up_at = pl.ds(pl.multiple_of(units + at.start, step), step)
            gate = mm(v, w[:, at]) + ADAPTER_SCALE * mm(low, raised[:, at])
            up = mm(v, w[:, up_at]) + ADAPTER_SCALE * mm(low, raised[:, up_at])
            gates[rows, at] = gate.astype(BF)
            ups[rows, at] = up.astype(BF)
            hidden[rows, at] = (gate / (1.0 + jnp.exp(-gate)) * up).astype(BF)

        tiles(units, step, unit_tile)

    pace.flush()
    if last:
        next_x[place.q, place.t] = cotangent[...]
        next_gather.begin()
    work.at(2)
    keep = pltpu.make_async_copy(x, x_hbm, copy_sems.at[1])
    keep.start()

    work.complete(0)
    load = pltpu.make_async_copy(plan.late(jobs), w.at[:, pl.ds(2 * units, units)], copy_sems.at[0])
    load.start()
    load.wait()
    for k in reduce.order:
        q = reduce.chips[k]
        rows = pl.ds(pl.multiple_of(q * chip_rows, chip_rows), chip_rows)
        made_hidden = hidden[rows]
        low = mm_t(made_hidden, e_model[2 * rank : 3 * rank]).astype(BF)
        side[rows] = low

        def out_tile(at):
            made = mm_t(made_hidden, w[at, 2 * units :])
            made = made + ADAPTER_SCALE * mm(low, a_model[10 * rank : 11 * rank, at])
            p[q, :, :, at] = made.astype(BF).reshape(2, chip_rows // 2, at.size)

        tiles(width, 512, out_tile)
        reduce.offer(k)
        if k == reduce.order[0]:
            reduce.far()
        if k == reduce.order[2]:
            reduce.free()
    if last:
        coming = next_gather.chunks()
        for _ in range(n - 1):
            next(coming)
    work.at(3)
    for s in range(1, n // 2):
        reduce.near(s)
    work.at(4)

    def use(at, total):
        following[at] = residual[at] + total

    reduce.end(use)
    if last:
        for _ in coming:
            pass
        keep_next = pltpu.make_async_copy(next_x, next_hbm, copy_sems.at[2])
        keep_next.start()
    work.at(5)
    keep.wait()
    if last:
        keep_next.wait()
        next_gather.finish()
    gather.finish()
    reduce.finish()
    work.settle((0,))


def ffn_backward(
    n, units, rank, carry,
    grad, middle, gain, w_hbm, w_down_hbm, a_model, e_model, x_hbm, gates, ups, hidden, small, side, *refs, pace,
):
    if carry:
        final, gathered, final_out, *refs = refs
        *refs, final_rows, home_send, home_recv = refs
    else:
        sums, here, sums_out, here_out, *refs = refs
        *refs, home_send, home_recv = refs
    (grad_out, grad_up_down, grad_in, grad_units,
     x, p, w, kept, dgu, dsmall, dside, raised, copy_sems, *sems) = refs
    place = Place(n)
    chip_rows, width = 2 * x_hbm.shape[2], x_hbm.shape[3]
    tree = n * chip_rows
    load = pltpu.make_async_copy(w_hbm, w.at[:, pl.ds(0, 2 * units)], copy_sems.at[0])
    load.start()
    load_down = pltpu.make_async_copy(w_down_hbm, w.at[:, pl.ds(2 * units, units)], copy_sems.at[2])
    load_down.start()
    fetch = pltpu.make_async_copy(x_hbm, kept, copy_sems.at[1])
    gather, reduce = Gather(place, x, *sems[:6]), Reduce(place, p, *sems[6:])

    if carry:
        come = pltpu.make_async_copy(gathered, x, copy_sems.at[3])
        come.start()
    else:

        def own(at):
            x[place.q, place.t, at] = grad[at].astype(BF)

        by_rows(grad.shape[0], own)
    block_diagonal(raised, (e_model, 2), rank, units)
    if carry:

        def last_rows(at):
            final_rows[at] = final[at].astype(BF)

        by_rows(final.shape[0], last_rows)
    enter(place, home=True)
    if not carry:
        gather.begin()
        going = [
            TreeMove(place, source, target, home_send.at[i], home_recv.at[i])
            for i, (source, target) in enumerate(((sums, sums_out), (here, here_out)))
        ]
    else:
        home = Home(place, final_out, home_send, home_recv)
        home.start(final_rows)
    pace.ready()
    load.wait()
    load_down.wait()
    step = tile_of(units)

    if carry:
        come.wait()
    coming = [0] + [k for s in range(1, n // 2) for k in (-s, s)] + [n // 2]
    for q in list(reduce.chips.values()) if carry else gather.chunks():
        rows = pl.ds(pl.multiple_of(q * chip_rows, chip_rows), chip_rows)
        v = x[q].reshape(chip_rows, width)
        low = (ADAPTER_SCALE * mm_t(v, a_model[10 * rank : 11 * rank])).astype(BF)
        dside[rows] = low

        def unit_tile(at):
            up_at = pl.ds(pl.multiple_of(units + at.start, step), step)
            down_at = pl.ds(pl.multiple_of(2 * units + at.start, step), step)
            dhidden = mm(v, w[:, down_at]) + mm(low, e_model[2 * rank : 3 * rank, at])
            gate, up = gates[rows, at].astype(F32), ups[rows, at].astype(F32)
            sig = 1.0 / (1.0 + jnp.exp(-gate))
            dgu[rows, at] = (dhidden * up * sig * (1.0 + gate * (1.0 - sig))).astype(BF)
            dgu[rows, up_at] = (dhidden * gate * sig).astype(BF)

        tiles(units, step, unit_tile)
        back = dgu[rows]
        low_back = (ADAPTER_SCALE * mm_t(back, raised[...])).astype(BF)
        dsmall[rows] = low_back

        def out_tile(at):
            made = mm_t(back, w[at, : 2 * units]) + mm(low_back, a_model[4 * rank : 6 * rank, at])
            p[q, :, :, at] = made.astype(BF).reshape(2, chip_rows // 2, at.size)

        tiles(width, 512, out_tile)
        if carry:
            k = reduce.order[len(reduce.across)]
        else:
            k = coming.pop(0)
        reduce.offer(k)
        if k == n // 2:
            reduce.far()
        if k == (reduce.order[2] if carry else n // 2):
            reduce.free()

    fetch.start()
    if not carry:
        for move in going:
            move.start()

    def use(at, total):
        inputs = middle[at]
        grad_out[at] = grad[at].astype(F32) + norm_back(total, inputs, rms_scale(inputs), gain[...])

    def adapters():
        fetch.wait()

        def model_tile(at):
            flat = x[:, :, :, at].reshape(tree, at.size)
            grad_up_down[:, at] = (ADAPTER_SCALE * t_mm(side[...], flat)).astype(BF)
            flat = kept[:, :, :, at].reshape(tree, at.size)
            grad_in[:, at] = t_mm(dsmall[...], flat).astype(BF)

        tiles(width, 256, model_tile)

        def unit_tile(at):
            up_at = pl.ds(pl.multiple_of(units + at.start, step), step)
            grad_units[:rank, at] = (ADAPTER_SCALE * t_mm(small[...], dgu[:, at])[:rank]).astype(BF)
            grad_units[rank : 2 * rank, at] = (ADAPTER_SCALE * t_mm(small[...], dgu[:, up_at])[rank:]).astype(BF)
            grad_units[2 * rank : 3 * rank, at] = t_mm(dside[...], hidden[:, at]).astype(BF)
            grad_units[3 * rank :, at] = jnp.zeros((rank, at.size), BF)

        tiles(units, step, unit_tile)

    reduce.run(use, adapters, True)
    if not carry:
        gather.finish()
    reduce.finish()
    if carry:
        home.land()
        home.finish()
    else:
        for move in going:
            move.land()


def attention_backward(
    n, layer, share, heads_tp, rank,
    grad, residual, gain, w_hbm, a_model, a_head, cosine, sine, query_bits, key_bits, lam,
    x_hbm, queries, keys, values, small, log_total, mixed, headed, side,
    grad_up_down, grad_ffn_in, grad_units,
    grad_out, own_sum, all_units,
    x, p, w, dmixed, dq, dk, dv, dprojected, dsmall, dside, raised, grad_a9, p_own, copy_sems, *sems, pace,
):
    place = Place(n)
    part = 1.0 / share
    chip_rows, width = 2 * x_hbm.shape[2], x_hbm.shape[3]
    tree = n * chip_rows
    load = pltpu.make_async_copy(w_hbm, w, copy_sems.at[0])
    load.start()
    gather, reduce = Gather(place, x, *sems[:6]), Reduce(place, p, *sems[6:15])
    gather_units, reduce_own = Gather(place, all_units, *sems[15:21]), Reduce(place, p_own, *sems[21:])

    def own(at):
        x[place.q, place.t, at] = grad[at].astype(BF)

    by_rows(grad.shape[0], own)
    block_diagonal(raised, (a_head[rank : 4 * rank], 3), rank, VD)
    all_units[place.q, place.t] = grad_units[...]
    enter(place)
    gather.begin()
    dk[...] = jnp.zeros(dk.shape, F32)
    dv[...] = jnp.zeros(dv.shape, F32)
    pace.ready()
    load.wait()

    score_scale = HD ** (-0.5)
    weight = lam[...]

    def attend(rows, count):
        visible = seen(rows, count, query_bits, key_bits)
        dmix = dmixed[rows]
        dweights = mm_t(dmix, values[:count])
        both = []
        for c in range(2):
            at = slice(c * HD, (c + 1) * HD)
            scores = mm_t(queries[rows, at], keys[:count, at]) * score_scale
            probability = jnp.exp(jnp.where(visible, scores - log_total[rows, c : c + 1], NEGATIVE_BIG))
            both.append(probability)
            weighted = probability * dweights
            dscores = weighted - probability * jnp.sum(weighted, axis=-1, keepdims=True)
            dscores = (dscores * -weight if c else dscores).astype(BF)
            dq[rows, at] = mm(dscores, keys[:count, at])
            dk[:count, at] += t_mm(dscores, queries[rows, at])
        dv[:count] += t_mm((both[0] - weight * both[1]).astype(BF), dmix)

    for q in gather.chunks():
        rows = pl.ds(pl.multiple_of(q * chip_rows, chip_rows), chip_rows)
        v = x[q].reshape(chip_rows, width)
        low = (ADAPTER_SCALE * mm_t(v, a_model[9 * rank : 10 * rank])).astype(BF)
        dside[rows] = low
        dheaded = mm(v, w[:, 3 * VD :]) + mm(low, a_head[:rank])
        inputs = mixed[rows].astype(F32)
        dmixed[rows] = norm_back(dheaded, inputs, rms_scale(inputs), keep_factor(layer)).astype(BF)

        def block(i, carry, q=q):
            attend(pl.ds(pl.multiple_of(q * chip_rows + i * ROW_BLOCK, ROW_BLOCK), ROW_BLOCK), tree)
            return carry

        lax.fori_loop(0, chip_rows // ROW_BLOCK, block, 0)

    gather_units.begin()

    def send_part(k):
        q = reduce.chips[k]
        rows = pl.ds(pl.multiple_of(q * chip_rows, chip_rows), chip_rows)
        for j, source in enumerate((dq, dk)):
            for c in range(2):
                half = slice(c * HD, (c + 1) * HD)
                turned = turn(source[rows, half] * score_scale, cosine[rows], -sine[rows])
                dprojected[rows, j * VD + c * HD : j * VD + (c + 1) * HD] = turned.astype(BF)
        dprojected[rows, 2 * VD :] = dv[rows].astype(BF)
        back = dprojected[rows]
        low_back = (ADAPTER_SCALE * mm_t(back, raised[...])).astype(BF)
        dsmall[rows] = low_back

        def out_tile(at):
            made = mm_t(back, w[at, : 3 * VD]) + mm(low_back, a_model[: 3 * rank, at])
            p[q, :, :, at] = (made * part).astype(BF).reshape(2, chip_rows // 2, at.size)

        tiles(width, 512, out_tile)
        reduce.offer(k)

    for k in reduce.order[:3]:
        send_part(k)
        if k == n // 2:
            reduce.far()
    reduce.free()

    def out_gradient(at):
        flat = x[:, :, :, at].reshape(tree, at.size)
        grad_a9[:, at] = (ADAPTER_SCALE * part * t_mm(side[...], flat)).astype(BF)

    tiles(width, 256, out_gradient)
    gather.finish()
    fetch = pltpu.make_async_copy(x_hbm, x, copy_sems.at[1])
    fetch.start()
    for k in reduce.order[3:]:
        send_part(k)
    for _ in gather_units.chunks():
        pass
    fetch.wait()

    block = width // (2 * n)

    def full_tile(jp, carry):
        at = pl.ds(pl.multiple_of(jp * block, block), block)
        q, t = jp // 2, jp % 2
        flat = x[:, :, :, at].reshape(tree, block)
        p_own[q, t, : 3 * rank] = (part * t_mm(dsmall[...], flat)).astype(BF)
        p_own[q, t, 4 * rank : 6 * rank] = grad_ffn_in[:, at]
        p_own[q, t, 9 * rank : 10 * rank] = grad_a9[:, at]
        p_own[q, t, 10 * rank : 11 * rank] = grad_up_down[:, at]
        p_own[q, t, 11 * rank :] = jnp.zeros((rank, block), BF)
        return carry

    lax.fori_loop(0, 2 * n, full_tile, 0)
    of_head = [part * t_mm(dside[...], headed[...])]
    for i in range(3):
        made = t_mm(small[...], dprojected[:, i * VD : (i + 1) * VD])[i * rank : (i + 1) * rank]
        of_head.append(ADAPTER_SCALE * part * made)
    head = place.t * heads_tp + place.q // share
    for j in range(2 * n):
        start = j * block % VD
        own = (head == j * block // VD).astype(F32)
        for i, k in enumerate((3, 6, 7, 8)):
            made = of_head[i][:, start : start + block] * own
            p_own[j // 2, j % 2, k * rank : (k + 1) * rank] = made.astype(BF)

    for k in reduce.order:
        reduce_own.offer(k)
    reduce_own.far()
    reduce_own.free()
    for s in range(1, n // 2):
        reduce.near(s)
        reduce_own.near(s)

    def use_own(at, total):
        own_sum[at] = total.astype(BF)

    def use(at, total):
        inputs = residual[at].astype(F32)
        grad_out[at] = grad[at].astype(F32) + norm_back(total, inputs, rms_scale(inputs), gain[...])

    reduce.end(use)
    reduce_own.end(use_own)
    gather_units.finish()
    reduce.finish()
    reduce_own.finish()


def finish_kernel(
    n, nf, layers, rank,
    grad, own_sums, own_units, slot, *refs,
):
    earlier, refs = refs[: 2 * layers - 2], refs[2 * layers - 2 :]
    (tokens_grad, model_grad, hidden_grad,
     rows_out, landed, sent_sums, all_sums, all_units, home_send, home_recv, tree_send, tree_recv) = refs
    place = Place(n)
    own = model_grad.shape[2]
    tall = own_sums.shape[0]

    def cut(at):
        rows_out[at] = grad[at].astype(BF)

    by_rows(grad.shape[0], cut)
    sent_sums[...] = own_sums[...]
    sent_sums[tall - rank :] = jnp.broadcast_to(slot[...], (rank, own_sums.shape[1])).astype(BF)
    enter(place, home=True, ring=False, trees=nf)
    moves = [Home(place, landed, home_send.at[0], home_recv.at[0])]
    away = {}
    for i, (source, target) in enumerate(((sent_sums, all_sums), (own_units, all_units))):
        away[i] = TreeMove(place, source, target.at[:, 0], home_send.at[i + 1], home_recv.at[i + 1])
        away[i].start()
    copies = []

    def hand_round(source, target, l, i):
        to = target.at[place.f, l]
        for e in range(1, nf):
            sems = tree_send.at[l, i, e], tree_recv.at[l, i, e]
            copies.append(remote(source, to, *sems, {"fsdp": flip(place.f, e)}))

    for l in range(1, layers):
        for i, target in enumerate((all_sums, all_units)):
            source = earlier[2 * l - 2 + i].at[place.f]
            target[place.f, l] = earlier[2 * l - 2 + i][place.f]
            hand_round(source, target, l, i)
    for i, target in enumerate((all_sums, all_units)):
        away[i].land()
        if i == 1:
            moves[0].start(rows_out)
        hand_round(target.at[place.f, 0], target, 0, i)
    moves[0].land()
    for copy in copies:
        copy.wait_recv()
    for b in range(own):
        number = (place.f * own + b).astype(F32)
        keeps = [
            (all_sums[f, 0, tall - rank : tall - rank + 1, :1].astype(F32) == number).astype(F32) for f in range(nf)
        ]
        for l in range(layers):
            for k in range(11):
                at = slice(k * rank, (k + 1) * rank)
                model_grad[l, k, b] = sum(keeps[f] * all_sums[f, l, at].astype(F32) for f in range(nf))
            for k in range(3):
                at = slice(k * rank, (k + 1) * rank)
                hidden_grad[l, k, b] = sum(keeps[f] * all_units[f, l, at].astype(F32) for f in range(nf))
    moves[0].finish()
    for core in range(2):

        def widen(at, core=core):
            rows = landed.shape[1]
            tokens_grad[pl.ds(pl.multiple_of(core * rows + at.start, 16), at.size)] = landed[core, at].astype(F32)

        by_rows(landed.shape[1], widen)
    for copy in copies:
        copy.wait_send()


class Plan:
    def __init__(self, n, nf, rows, scatters, spreads, schedule):
        self.n, self.nf, self.rows, self.schedule = n, nf, rows, schedule
        self.scatters, self.spreads = scatters, spreads

    def ins(self):
        return [(blocks, True) for blocks, _ in self.scatters] + [(w, True) for w in self.spreads]

    def outs(self):
        made = [(shape, BF, True) for _, shape in self.scatters]
        return made + [(w.shape, BF, True) for w in self.spreads]

    def semaphores(self):
        made = Spread.scatter_semaphores(self.n) * len(self.scatters)
        return made + Spread.spread_semaphores(self.n, self.nf) * len(self.spreads)

    def split(self, refs):
        a, b = len(self.scatters), len(self.spreads)
        count = 2 * a + 6 * b
        refs = list(refs)
        taken = refs[: a + b], refs[a + b : 2 * (a + b)], refs[len(refs) - count :]
        return taken, refs[2 * (a + b) : len(refs) - count]

    def work(self, place, nf, jobs):
        a, b = len(self.scatters), len(self.spreads)
        ins, outs, sems = jobs
        scatters = [(ins[i], outs[i], sems[2 * i : 2 * i + 2]) for i in range(a)]
        spreads = [(outs[a + i], sems[2 * a + 6 * i : 2 * a + 6 * i + 6]) for i in range(b)]
        return Work(place, nf, self.rows, scatters, spreads, self.schedule)

    def late(self, jobs):
        return jobs[1][len(self.scatters)]


class Pace:
    def __init__(self, loads, stores):
        self.loads, self.stores = loads, stores
        for copy in loads:
            copy.start()

    def ready(self):
        for copy in self.loads:
            copy.wait()

    def flush(self):
        for copy in self.stores:
            copy.start()

    def end(self):
        for copy in self.stores:
            copy.wait()


def call(kernel, collective, ins, outs, scratch, plan=None):
    spec = lambda hbm: pl.BlockSpec(memory_space=pl.ANY if hbm else pltpu.VMEM)
    aliases = {}
    if plan is not None:
        first_in, count = len(ins), len(plan.scatters)
        aliases = {first_in + count + i: count + i for i in range(len(plan.spreads))}
        ins, outs, scratch = ins + plan.ins(), plan.outs() + outs, scratch + plan.semaphores()
    late_in = [i for i, (_, hbm) in enumerate(ins) if hbm == "paced"]
    late_out = [i for i, (_, _, hbm) in enumerate(outs) if hbm == "paced"]
    extra = [pltpu.VMEM(ins[i][0].shape, ins[i][0].dtype) for i in late_in]
    extra += [pltpu.VMEM(outs[i][0], outs[i][1]) for i in late_out]
    if late_in or late_out:
        extra.append(pltpu.SemaphoreType.DMA((len(late_in) + len(late_out),)))

        def paced(*refs):
            refs, held = list(refs[: -len(extra)]), refs[-len(extra) :]
            loads, stores = [], []
            for slot, i in enumerate(late_in):
                loads.append(pltpu.make_async_copy(refs[i], held[slot], held[-1].at[slot]))
                refs[i] = held[slot]
            for slot, i in enumerate(late_out, len(late_in)):
                stores.append(pltpu.make_async_copy(held[slot], refs[len(ins) + i], held[-1].at[slot]))
                refs[len(ins) + i] = held[slot]
            pace = Pace(loads, stores)
            kernel(*refs, pace=pace)
            pace.end()

        body = paced
    else:
        body = kernel
    made = pl.pallas_call(
        body,
        out_shape=[jax.ShapeDtypeStruct(shape, kind) for shape, kind, _ in outs],
        in_specs=[spec(hbm) for _, hbm in ins],
        out_specs=[spec(hbm) for _, _, hbm in outs],
        scratch_shapes=scratch + extra,
        input_output_aliases=aliases,
        compiler_params=pltpu.CompilerParams(
            collective_id=collective, has_side_effects=True, vmem_limit_bytes=62 << 20
        ),
    )(*[array for array, _ in ins])
    return list(made)


def line_bits(parent_row, seg):
    number = jnp.arange(NSEG)
    one = lambda x: lax.shift_left(jnp.ones_like(x), x)
    grand = jnp.sum(jnp.where(parent_row[:, None] == number[None, :], parent_row[None, :], 0), axis=1)
    line = one(number) | one(parent_row) | one(grand)
    mine = jnp.sum(jnp.where(seg[:, None] == number[None, :], line[None, :], 0), axis=1)
    return mine, one(seg)


def keep_factor(layer):
    return 0.2 + 0.6 * math.exp(-0.3 * layer)


def chips_of(nf, nc):
    h = nc // 2
    for f in range(nf):
        for c in range(nc):
            yield f * nc + c, (f // 2, f % 2, c // h, c % h)


def permute(x, nf, nc, target):
    h = nc // 2
    pairs = []
    for source, spot in chips_of(nf, nc):
        f_hi, f_lo, c_hi, c_lo = target(*spot)
        pairs.append((source, (f_hi * 2 + f_lo) * nc + c_hi * h + c_lo))
    return lax.ppermute(x, ("fsdp", "ctx"), pairs)


def swap_trees(x, nf, nc):
    return permute(x, nf, nc, lambda f_hi, f_lo, c_hi, c_lo: (f_hi, c_hi, f_lo, c_lo))


def shards(
    nf,
    nc,
    tokens,
    cotangent,
    segments,
    depths,
    parents,
    tree_adapter_index,
    layer_norm_gains,
    difference_lambda,
    query_key_value_weight,
    output_weight,
    gate_up_weight,
    down_weight,
    adapter_model_factors,
    adapter_hidden_factors,
):
    n = nc
    place = Place(n)
    q, t = place.q, place.t
    tokens_dev, width = tokens.shape
    rows = tokens_dev // 2
    tree = tokens_dev * n
    layers, weight_rows = query_key_value_weight.shape[:2]
    heads_tp = difference_lambda.shape[1]
    share = max(1, n // heads_tp)
    head = q // share
    hidden_tp = down_weight.shape[2]
    units = (hidden_tp + n * 128 - 1) // (n * 128) * 128
    rank, adapters = adapter_model_factors.shape[3], adapter_model_factors.shape[2]
    h = n // 2

    notes = jnp.concatenate([segments, depths, parents[0], tree_adapter_index])
    order = jnp.arange(n)
    of_tree = jnp.zeros((n, notes.shape[0]), jnp.int32)
    for d in range(n):

        def hand_out(f_hi, f_lo, c_hi, c_lo, d=d):
            to = (c_hi * (n // 2) + c_lo) ^ d
            return f_hi, to // (n // 2), f_lo, to % (n // 2)

        part_of_tree = permute(notes, nf, nc, hand_out)
        of_tree = of_tree + jnp.where(order[:, None] == flip(q, d), part_of_tree[None], 0)
    seg, dep = of_tree[:, :tokens_dev].reshape(tree), of_tree[:, tokens_dev : 2 * tokens_dev].reshape(tree)
    parent_row, slot = of_tree[0, 2 * tokens_dev : 2 * tokens_dev + NSEG], of_tree[0, 2 * tokens_dev + NSEG]
    own_tokens = lax.dynamic_slice_in_dim(tokens, t * rows, rows, 0)
    own_cotangent = lax.dynamic_slice_in_dim(cotangent, t * rows, rows, 0)
    residual = swap_trees(own_tokens, nf, nc)
    own_cotangent = swap_trees(own_cotangent, nf, nc)

    query_bits, key_bits = line_bits(parent_row, seg)
    query_bits, key_bits = query_bits[:, None], key_bits[None, :]
    frequency = 10000.0 ** (-jnp.arange(HD // 2).astype(F32) / (HD // 2))
    angles = dep.astype(F32)[:, None] * frequency[None, :]
    cosine, sine = jnp.cos(angles), jnp.sin(angles)
    cosine = jnp.concatenate([cosine, cosine], axis=1)
    sine = jnp.concatenate([-sine, sine], axis=1)
    gains = layer_norm_gains

    a_all = lax.dynamic_index_in_dim(adapter_model_factors, slot, 2, keepdims=False)
    e_all = lax.dynamic_index_in_dim(adapter_hidden_factors, slot, 2, keepdims=False)
    a_model = a_all.reshape(layers, 11 * rank, width)
    e_all = e_all.reshape(layers, 3 * rank, -1)
    head_at = (t * heads_tp + head) * VD

    heads_of = lax.dynamic_slice_in_dim(a_all, head_at, VD, 3)
    a_head = jnp.concatenate([heads_of[:, 3:4], heads_of[:, 6:9]], axis=1).reshape(layers, 4 * rank, VD)

    def unit_columns(x):
        x = lax.dynamic_slice_in_dim(x, t * hidden_tp, hidden_tp, x.ndim - 1)
        x = jnp.pad(x, ((0, 0),) * (x.ndim - 1) + ((0, n * units - hidden_tp),))
        return lax.dynamic_slice_in_dim(x, q * units, units, x.ndim - 1)

    e_model = unit_columns(e_all)

    part = 1.0 / share
    vmem = lambda *spec: pltpu.VMEM(*spec)
    calls = [0]
    whole_x = ((n, 2, rows, width), BF)
    sems = Gather.semaphores(n) + Reduce.scratch(n, rows, width)
    pair = pltpu.SemaphoreType.DMA((4,))
    big = [vmem(*whole_x), vmem(*whole_x)]

    def run(kernel, ins, outs, scratch, plan=None):
        calls[0] += 1
        return call(kernel, calls[0], ins, outs, scratch, plan)

    near = lambda *arrays: [(array, False) for array in arrays]
    far = lambda *arrays: [(array, True) for array in arrays]
    paced = lambda *arrays: [(array, "paced") for array in arrays]
    out = lambda shape, kind, hbm=False: (shape, kind, hbm)

    dma = pltpu.SemaphoreType.DMA
    c_a, c_g, c_d = 4 * VD, 2 * units, units
    tall = nf * n * weight_rows
    cut = lambda columns: out((n, weight_rows, columns), BF)
    calls[0] += 1
    made = call(
        functools.partial(weights_kernel, n, nf, units, share, layers),
        calls[0],
        far(jnp.transpose(query_key_value_weight, (0, 2, 1, 3)), output_weight, gate_up_weight, down_weight),
        [out((tall, c_a), BF, True), out((tall, c_g), BF, True), out((tall, c_d), BF, True)]
        + ([cut(c_a)] + [cut(c_g)] + [cut(c_d)]) * (layers - 1),
        [
            vmem((n, weight_rows, c_a), BF),
            vmem((n, weight_rows, c_g), BF),
            vmem((n, weight_rows, c_d), BF),
            vmem((layers, weight_rows, 2, hidden_tp), BF),
            vmem((layers, weight_rows, hidden_tp), BF),
            dma((layers, n, 4)),
            dma((layers, 2)),
        ]
        + (Spread.scatter_semaphores(n) + Spread.spread_semaphores(n, nf)) * 2
        + Spread.scatter_semaphores(n),
    )
    w_a, w_g, w_d = [made[0]], [made[1]], [made[2]]
    a_blocks = [None] + made[3 : 2 + layers]
    g_blocks = [None] + made[2 + layers : 1 + 2 * layers]
    d_blocks = [None] + made[1 + 2 * layers :]

    def plan_of(scatters, spreads, *schedule):
        return Plan(n, nf, weight_rows, scatters, spreads, schedule)

    saved = []
    for l in range(layers):
        last = l == layers - 1
        w_attention = w_a[l]
        lam = lax.dynamic_slice_in_dim(difference_lambda[l], head, 1).reshape(1, 1)
        gain_a, gain_f = gains[l, 0:1], gains[l, 1:2]
        shared = paced(a_model[l]) + near(a_head[l]) + paced(cosine, sine, query_bits) + near(key_bits, lam)
        come = 2 if l else 1
        plan = plan_of(
            [] if last else [(a_blocks[l + 1], (tall, c_a)), (g_blocks[l + 1], (tall, c_g))],
            [w_g[l], w_d[l]],
            moves("forward", 0, parts(n, 0, come)) + moves("spread", 0, parts(n, come, 4)),
            moves("forward", 0, parts(n, come, 2)) + ([] if last else [("scatter", 0)]),
            moves("spread", 1, parts(n, 0, 2)) + moves("forward", 0, parts(n, 2, 3)),
            moves("forward", 0, parts(n, 3, 4)) + ([] if last else [("scatter", 1)]),
        )
        got = run(
            functools.partial(attention_forward, n, nf, l, part, rank, True, plan),
            near(residual, gain_a) + far(w_attention) + shared,
            [
                out((rows, width), F32),
                out(*whole_x, True),
                out((tree, VD), BF, "paced"),
                out((tree, VD), BF, "paced"),
                out((tree, VD), BF, "paced"),
                out((tree, 3 * rank), BF, "paced"),
                out((tree, 2), F32, "paced"),
                out((tree, VD), BF, "paced"),
                out((tree, VD), BF, "paced"),
                out((tree, rank), BF, "paced"),
            ],
            big + [vmem((width, 4 * VD), BF), vmem((3 * rank, 3 * VD), BF), pair] + sems,
            plan,
        )
        if not last:
            w_a.append(got[0])
            w_g.append(got[1])
            got = got[2:]
        w_g[l], w_d[l], middle, *kept = got
        plan = plan_of(
            [] if last else [(d_blocks[l + 1], (tall, c_d))],
            [w_d[l]] + ([] if last else [w_a[l + 1], w_g[l + 1]]),
            moves("forward", 0, parts(n, 0, 2)) + moves("spread", 0, parts(n, 2, 4)),
            moves("forward", 0, parts(n, 2, 3)),
            moves("forward", 0, parts(n, 3, 4)) + ([] if last else moves("spread", 1, parts(n, 0, 4)) + [("scatter", 0)]),
            [] if last else moves("forward", 1, parts(n, 0, 1)),
            [] if last else moves("forward", 1, parts(n, 1, 2)) + moves("spread", 2, parts(n, 0, 2)),
            [] if last else moves("forward", 1, parts(n, 2, 4)),
        )
        ffn = run(
            functools.partial(ffn_forward, n, nf, units, rank, last, plan),
            near(middle, gain_f) + far(w_g[l]) + paced(a_model[l]) + near(e_model[l])
            + (near(own_cotangent) if last else []),
            ([out(*whole_x, True)] if last else [])
            + [
                out((rows, width), F32),
                out(*whole_x, True),
                out((tree, units), BF, "paced"),
                out((tree, units), BF, "paced"),
                out((tree, units), BF, "paced"),
                out((tree, 2 * rank), BF, "paced"),
                out((tree, rank), BF),
            ],
            big + [vmem((width, 3 * units), BF), vmem((2 * rank, 2 * units), BF), pair] + sems
            + ([vmem(*whole_x)] + Gather.semaphores(n) if last else []),
            plan,
        )
        if not last:
            w_d.append(ffn[0])
            w_d[l], w_a[l + 1], w_g[l + 1], *ffn = ffn[1:]
        else:
            w_d[l], gathered, *ffn = ffn
        saved.append((residual, middle, gain_a, gain_f, shared, kept, ffn[1:]))
        residual = ffn[0]

    grad = own_cotangent
    units_here, sums_here, earlier, block = [], [], [], width // (2 * n)
    wide = hidden_tp // n
    for l in reversed(range(layers)):
        residual_in, middle, gain_a, gain_f, shared, kept, ffn = saved[l]
        carry = l == layers - 1
        made = run(
            functools.partial(ffn_backward, n, units, rank, carry),
            near(grad) + paced(middle) + near(gain_f) + far(w_g[l], w_d[l]) + paced(a_model[l]) + near(e_model[l])
            + far(ffn[0]) + paced(*ffn[1:])
            + (near(residual) + far(gathered) if carry else near(sums_here[0], units_here[0])),
            ([out((2, rows, width), BF)] if carry else [out((nf, 12 * rank, block), BF), out((nf, 3 * rank, wide), BF)])
            + [
                out((rows, width), F32),
                out((rank, width), BF),
                out((2 * rank, width), BF),
                out((4 * rank, units), BF),
            ],
            big
            + [
                vmem((width, 3 * units), BF),
                vmem(*whole_x),
                vmem((tree, 2 * units), BF),
                vmem((tree, 2 * rank), BF),
                vmem((tree, rank), BF),
                vmem((2 * rank, 2 * units), BF),
                pair,
            ]
            + sems
            + ([vmem((rows, width), BF)] + Home.semaphores() if carry else [dma((2, 2)), dma((2, 2))]),
        )
        if carry:
            outputs, *made = made
        else:
            earlier += made[:2]
            made = made[2:]
        grad, *ffn_grads = made
        grad, own_sum, all_units = run(
            functools.partial(attention_backward, n, l, share, heads_tp, rank),
            near(grad) + paced(residual_in) + near(gain_a) + far(w_a[l]) + shared + far(kept[0])
            + paced(*kept[1:]) + near(*ffn_grads),
            [
                out((rows, width), F32),
                out((12 * rank, block), BF),
                out((n, 2, 4 * rank, units), BF),
            ],
            big
            + [
                vmem((width, 4 * VD), BF),
                vmem((tree, VD), BF),
                vmem((tree, VD), F32),
                vmem((tree, VD), F32),
                vmem((tree, VD), F32),
                vmem((tree, 3 * VD), BF),
                vmem((tree, 3 * rank), BF),
                vmem((tree, rank), BF),
                vmem((3 * rank, 3 * VD), BF),
                vmem((rank, width), BF),
                vmem((n, 2, 12 * rank, block), BF),
                pair,
            ]
            + sems
            + Gather.semaphores(n)
            + Reduce.scratch(n, 12 * rank, block),
        )

        number = (q * 2 + t) * (hidden_tp // n)
        half = lax.dynamic_index_in_dim(all_units, number // hidden_tp, 1, keepdims=False)
        flat = half[:, : 3 * rank].transpose(1, 0, 2).reshape(3 * rank, n * units)
        units_here.insert(0, lax.dynamic_slice_in_dim(flat, number % hidden_tp, hidden_tp // n, 1))
        sums_here.insert(0, own_sum)

    own = adapters // nf
    dma = pltpu.SemaphoreType.DMA
    tokens_grad, grad_model, grad_hidden = run(
        functools.partial(finish_kernel, n, nf, layers, rank),
        near(grad, sums_here[0], units_here[0], slot.astype(F32).reshape(1, 1), *earlier),
        [
            out((2 * rows, width), F32),
            out((layers, 11, own, rank, block), F32),
            out((layers, 3, own, rank, wide), F32),
        ],
        [
            vmem((rows, width), BF),
            vmem((2, rows, width), BF),
            vmem((12 * rank, block), BF),
            vmem((nf, layers, 12 * rank, block), BF),
            vmem((nf, layers, 3 * rank, wide), BF),
            dma((3, 2)),
            dma((3, 2)),
            dma((layers, 2, nf)),
            dma((layers, 2, nf)),
        ],
    )
    return (
        outputs.reshape(2 * rows, width),
        tokens_grad,
        grad_model,
        grad_hidden,
    )


def solution(mesh):
    in_specs = (
        P(("fsdp", "ctx"), None),
        P(("fsdp", "ctx"), None),
        P(("fsdp", "ctx")),
        P(("fsdp", "ctx")),
        P("fsdp", None),
        P("fsdp"),
        P(),
        P(None, "tp"),
        P(None, ("fsdp", "ctx"), None, "tp"),
        P(None, ("fsdp", "ctx"), "tp"),
        P(None, ("fsdp", "ctx"), None, "tp"),
        P(None, ("fsdp", "ctx"), "tp"),
        P(),
        P(),
    )
    out_specs = (
        P(("fsdp", "ctx"), None),
        P(("fsdp", "ctx"), None),
        P(None, None, "fsdp", None, ("ctx", "tp")),
        P(None, None, "fsdp", None, ("ctx", "tp")),
    )
    body = functools.partial(shards, mesh.shape["fsdp"], mesh.shape["ctx"])
    return jax.shard_map(body, mesh=mesh, in_specs=in_specs, out_specs=out_specs, check_vma=False)
```

```python
import functools
import math

import jax
import jax.numpy as jnp
from jax import lax
from jax.experimental import pallas as pl
from jax.experimental.pallas import tpu as pltpu
from jax.sharding import PartitionSpec as P

HD = 128
VD = 256
NSEG = 13
EPSILON = 1e-05
ADAPTER_SCALE = 0.5
NEGATIVE_BIG = -1e30
MESH = pl.DeviceIdType.MESH
BF = jnp.bfloat16
F32 = jnp.float32


class Place:
    def __init__(self, n):
        self.n, self.h = n, n // 2
        self.f, self.c, self.t = lax.axis_index("fsdp"), lax.axis_index("ctx"), lax.axis_index("tp")
        self.f_hi, self.f_lo = self.f // 2, self.f % 2
        self.c_hi, self.c_lo = self.c // self.h, self.c % self.h
        self.q = self.f_lo * self.h + self.c_lo
        self.away = self.f_lo + self.c_hi - 2 * self.f_lo * self.c_hi
        self.home = {"fsdp": self.f_hi * 2 + self.c_hi, "ctx": self.f_lo * self.h + self.c_lo}
        self.pos = self.f_lo * (n - 1) + (1 - 2 * self.f_lo) * self.c_lo

    def ring(self, k):
        n, h = self.n, self.h
        p = lax.rem(self.pos + k + 2 * n, n)
        low = p // h
        column = (1 - low) * p + low * (n - 1 - p)
        device = {"fsdp": self.f_hi * 2 + low, "ctx": self.c_hi * h + column}
        return low * h + column, device


def remote(src, dst, send, recv, device):
    copy = pltpu.make_async_remote_copy(
        src_ref=src, dst_ref=dst, send_sem=send, recv_sem=recv, device_id=device, device_id_type=MESH
    )
    copy.start()
    return copy


def when_even(place, body):
    even = place.pos % 2 == 0
    pl.when(even)(lambda: body(True))
    pl.when(jnp.logical_not(even))(lambda: body(False))


def flip(number, bits):
    b = 1
    while b <= bits:
        if bits & b:
            number = number + b * (1 - 2 * ((number // b) % 2))
        b *= 2
    return number


class Spread:
    def __init__(self, place, nf, w, rows):
        self.place, self.nf, self.w, self.rows = place, nf, w, rows
        self.g = place.f_hi * 2 + place.c_hi
        self.links = range(1, nf // 2)
        self.scattered, self.sent = [], []
        self.to_partner, self.along, self.onward, self.got = {}, {}, {}, []

    @staticmethod
    def scatter_semaphores(n):
        dma = pltpu.SemaphoreType.DMA
        return [dma((n,)), dma((n,))]

    @staticmethod
    def spread_semaphores(n, nf):
        dma = pltpu.SemaphoreType.DMA
        return [dma((n,))] * 2 + [dma((n, max(1, nf // 2 - 1)))] * 4

    def block(self, g, q):
        n, h = self.place.n, self.place.h
        source = (g // 2 * 2 + q // h) * n + g % 2 * h + q % h
        start = pl.multiple_of(source * self.rows, self.rows)
        return self.w.at[pl.ds(start, self.rows)]

    def chip(self, q):
        place = self.place
        return {"fsdp": place.f_hi * 2 + q // place.h, "ctx": place.c_hi * place.h + q % place.h}

    def partner(self):
        place = self.place
        return {"ctx": (1 - place.c_hi) * place.h + place.c_lo}

    def line(self, e):
        return {"fsdp": flip(self.place.f_hi, e) * 2 + self.place.f_lo}

    def scatter(self, blocks, send, recv):
        q = self.place.q
        own = self.block(self.g, q)
        copy = pltpu.make_async_copy(blocks.at[q], own, recv.at[0])
        copy.start()
        self.scattered.append(copy)
        for d in range(1, self.place.n):
            to = flip(q, d)
            self.scattered.append(remote(blocks.at[to], own, send.at[d], recv.at[d], self.chip(to)))

    def arrived(self, d):
        if d:
            self.scattered[d].wait_recv()
        else:
            self.scattered[0].wait()

    def scatter_sent(self):
        for copy in self.scattered[1:]:
            copy.wait_send()

    def use(self, *sems):
        self.sems = sems

    def spread(self, d):
        send_z, recv_z, send_y, recv_y = self.sems[:4]
        at = self.block(self.g, flip(self.place.q, d))
        self.to_partner[d] = remote(at, at, send_z.at[d], recv_z.at[d], self.partner())
        for e in self.links:
            self.along[d, e] = remote(at, at, send_y.at[d, e - 1], recv_y.at[d, e - 1], self.line(e))

    def landed(self, d):
        if d in self.to_partner and d not in self.got:
            self.to_partner[d].wait_recv()
            self.got.append(d)

    def forward(self, d):
        send, recv = self.sems[4:]
        self.landed(d)
        at = self.block(flip(self.g, 1), flip(self.place.q, d))
        for e in self.links:
            self.onward[d, e] = remote(at, at, send.at[d, e - 1], recv.at[d, e - 1], self.line(e))

    def complete(self):
        for d in list(self.to_partner):
            self.landed(d)
        for copy in list(self.along.values()) + list(self.onward.values()):
            copy.wait_recv()

    def sent_all(self):
        for copies in (self.to_partner, self.along, self.onward):
            for copy in copies.values():
                copy.wait_send()


def enter(place, nf=0, scatters=False, home=False, ring=True, trees=0, partner=False):
    bar = pltpu.get_barrier_semaphore()
    devices = [{"tp": 1 - place.t}]
    guide = Spread(place, nf, None, 0)
    if scatters:
        devices += [guide.chip(flip(place.q, d)) for d in range(1, place.n)]
    elif ring:
        devices += [place.ring(1)[1], place.ring(-1)[1]]
    if nf:
        devices += [guide.partner()] + [guide.line(e) for e in guide.links]
    devices += [{"fsdp": flip(place.f, e)} for e in range(1, trees)]
    if partner:
        devices.append(guide.partner())
    for device in devices:
        pl.semaphore_signal(bar, inc=1, device_id=device, device_id_type=MESH)
    count = len(devices)
    if home:

        @pl.when(place.away == 1)
        def greet():
            pl.semaphore_signal(bar, inc=1, device_id=place.home, device_id_type=MESH)

        count = count + place.away
    pl.semaphore_wait(bar, count)


class Home:
    def __init__(self, place, out, send, recv):
        self.place, self.out = place, out
        self.send, self.recv = send, recv

    @staticmethod
    def semaphores():
        dma = pltpu.SemaphoreType.DMA
        return [dma((2,)), dma((2,))]

    def start(self, rows):
        place, slot = self.place, self.out.at[self.place.t]
        far = pltpu.make_async_remote_copy(
            src_ref=rows, dst_ref=slot, send_sem=self.send.at[0], recv_sem=self.recv.at[0],
            device_id=place.home, device_id_type=MESH,
        )
        near = pltpu.make_async_copy(rows, slot, self.recv.at[0])
        self.far = far
        pl.when(place.away == 1)(far.start)
        pl.when(place.away == 0)(near.start)
        self.near = near

    def land(self, share=True):
        pl.when(self.place.away == 1)(self.far.wait)
        pl.when(self.place.away == 0)(self.near.wait)
        if share:
            slot = self.out.at[self.place.t]
            self.across = remote(slot, slot, self.send.at[1], self.recv.at[1], {"tp": 1 - self.place.t})

    def finish(self):
        self.across.wait()


class TreeMove(Home):
    def __init__(self, place, rows, out, send, recv):
        super().__init__(place, out, send, recv)
        self.rows = rows
        self.slot = out.at[place.f]

    def start(self):
        place = self.place
        target = self.out.at[place.f_hi * 2 + place.c_hi]
        self.far = pltpu.make_async_remote_copy(
            src_ref=self.rows, dst_ref=target, send_sem=self.send.at[0], recv_sem=self.recv.at[0],
            device_id=place.home, device_id_type=MESH,
        )
        self.near = pltpu.make_async_copy(self.rows, target, self.recv.at[0])
        pl.when(place.away == 1)(self.far.start)
        pl.when(place.away == 0)(self.near.start)

    def land(self):
        super().land(False)


class Work:
    def __init__(self, place, nf, rows, scatters, spreads, schedule):
        self.n, self.schedule = place.n, schedule
        self.scatters, self.spreads = [], []
        for blocks, w, sems in scatters:
            self.scatters.append((Spread(place, nf, w, rows), blocks, sems))
        for w, sems in spreads:
            piece = Spread(place, nf, w, rows)
            piece.use(*sems)
            self.spreads.append(piece)

    def at(self, point):
        for what, i, *d in self.schedule[point] if point < len(self.schedule) else ():
            if what == "scatter":
                piece, blocks, sems = self.scatters[i]
                piece.scatter(blocks, *sems)
            elif what == "spread":
                self.spreads[i].spread(*d)
            else:
                self.spreads[i].forward(*d)

    def complete(self, i):
        self.spreads[i].complete()

    def settle(self, done=()):
        for i, piece in enumerate(self.spreads):
            if i not in done:
                piece.complete()
            piece.sent_all()
        for piece, _, _ in self.scatters:
            for d in range(self.n):
                piece.arrived(d)
            piece.scatter_sent()


def parts(n, first, last):
    return range(first * n // 4, last * n // 4)


def moves(what, piece, places):
    return [(what, piece, d) for d in places]


def weights_kernel(
    n, nf, units, share, layers,
    qkv, output, gate_up, down, *refs,
):
    place = Place(n)
    rows, hidden = down.shape[1:]
    w_a, w_g, w_d = refs[:3]
    later = refs[3 : 3 * layers]
    a_first, g_first, d_first, raw_g, raw_d, cut_sems, raw_sems = refs[3 * layers : 3 * layers + 7]
    sems = refs[3 * layers + 7 :]
    a_blocks = [a_first] + list(later[: layers - 1])
    g_blocks = [g_first] + list(later[layers - 1 : 2 * layers - 2])
    d_blocks = [d_first] + list(later[2 * layers - 2 :])
    cuts = []
    for l in range(layers):
        for q in range(n):
            columns = pl.ds(q // share * VD, VD)
            for i in range(4):
                source = qkv.at[l, i, :, columns] if i < 3 else output.at[l, :, columns]
                target = a_blocks[l].at[q, :, pl.ds(i * VD, VD)]
                cuts.append(pltpu.make_async_copy(source, target, cut_sems.at[l, q, i]))
    for copy in cuts[: 4 * n]:
        copy.start()
    raws = []
    for l in range(layers):
        raws.append(pltpu.make_async_copy(gate_up.at[l], raw_g.at[l], raw_sems.at[l, 0]))
        raws.append(pltpu.make_async_copy(down.at[l], raw_d.at[l], raw_sems.at[l, 1]))
    for copy in raws:
        copy.start()
    attention, forward, back = (Spread(place, nf, w, rows) for w in (w_a, w_g, w_d))
    attention.use(*sems[2:8])
    forward.use(*sems[10:16])
    enter(place, nf, True)
    for copy in cuts[: 4 * n]:
        copy.wait()
    attention.scatter(a_first, *sems[:2])
    for copy in cuts[4 * n :]:
        copy.start()

    def fill(target, j, at, value):
        width = min(units, hidden - j * units)
        target[j, :, at : at + width] = value(pl.ds(j * units, width))
        if width < units:
            target[j, :, at + width : at + units] = jnp.zeros((rows, units - width), BF)

    def cut_gate_up(l):
        raws[2 * l].wait()
        for i in range(2):
            for j in range(n):
                fill(g_blocks[l], j, i * units, lambda at, i=i: raw_g[l, :, i, at])

    def cut_down(l):
        raws[2 * l + 1].wait()
        for j in range(n):
            fill(d_blocks[l], j, 0, lambda at: raw_d[l, :, at])

    cut_gate_up(0)
    for d in range(n):
        attention.arrived(d)
        attention.spread(d)
    forward.scatter(g_first, *sems[8:10])
    cut_down(0)
    back.scatter(d_first, *sems[16:18])
    for d in parts(n, 0, 1):
        attention.forward(d)
    for l in range(1, layers):
        cut_gate_up(l)
        cut_down(l)
    for copy in cuts[4 * n :]:
        copy.wait()
    for d in parts(n, 1, 3):
        attention.forward(d)
    for d in range(n):
        forward.arrived(d)
    for d in parts(n, 0, 1):
        forward.spread(d)
    for d in parts(n, 3, 4):
        attention.forward(d)
    attention.complete()
    forward.complete()
    attention.scatter_sent()
    attention.sent_all()
    forward.scatter_sent()
    forward.sent_all()
    for d in range(n):
        back.arrived(d)
    back.scatter_sent()


class Gather:
    def __init__(self, place, x, send_r, recv_r, send_l, recv_l, core_send, core_recv, lean=False):
        self.place, self.x = place, x
        self.sems = (send_r, recv_r, send_l, recv_l, core_send, core_recv)
        self.lean = lean and place.n == 4
        self.right, self.left, self.across = {}, {}, []

    @staticmethod
    def semaphores(n):
        dma = pltpu.SemaphoreType.DMA
        return [dma((n,))] * 4 + [dma((n,))] * 2

    def _make(self, s):
        place, x = self.place, self.x
        send_r, recv_r, send_l, recv_l = self.sems[:4]
        top = x.shape[2] // 2
        last = s == place.n // 2 - 1
        for i in range(1 if last and not self.lean else 2):
            for made, sign, send, recv in ((self.right, 1, send_r, recv_r), (self.left, -1, send_l, recv_l)):
                piece = i if sign > 0 else 1 - i
                at = x.at[place.ring(-sign * s)[0], place.t, pl.ds(piece * top, top)]
                made[s, i] = pltpu.make_async_remote_copy(
                    src_ref=at, dst_ref=at, send_sem=send.at[2 * s + i], recv_sem=recv.at[2 * s + i],
                    device_id=place.ring(sign)[1], device_id_type=MESH,
                )

    def _cross(self, q):
        core_send, core_recv = self.sems[4:]
        slot, at = len(self.across), self.x.at[q, self.place.t]
        other = {"tp": 1 - self.place.t}
        self.across.append(remote(at, at, core_send.at[slot], core_recv.at[slot], other))

    def begin(self):
        for s in range(self.place.n // 2):
            self._make(s)
        for i in range(2):
            self.right[0, i].start()
            self.left[0, i].start()
        self._cross(self.place.q)

    def _hop(self, s):
        last = self.place.n // 2 - 1
        if not self.lean:
            for i in range(1 if s == last else 2):
                for stream in (self.right, self.left):
                    stream[s, i].wait_recv()
                    if s < last - 1 or (s == last - 1 and i == 0):
                        stream[s + 1, i].start()
            return

        def body(even):
            along_ctx, along_fsdp = (self.left, self.right) if even else (self.right, self.left)
            for i in range(2):
                if s == 0:
                    along_ctx[0, i].wait_recv()
                    along_ctx[1, i].start()
                    along_fsdp[0, i].wait_recv()
                else:
                    along_fsdp[1, i].wait_recv()

        when_even(self.place, body)

    def chunks(self):
        place, half = self.place, self.place.n // 2
        self.across[0].wait_recv()
        yield place.q
        for s in range(half):
            self._hop(s)
            arrived = [place.ring(half)[0]] if s == half - 1 else [place.ring(-s - 1)[0], place.ring(s + 1)[0]]
            first = len(self.across)
            for q in arrived:
                self._cross(q)
            for i, q in enumerate(arrived):
                self.across[first + i].wait_recv()
                yield q

    def finish(self):
        last = self.place.n // 2 - 1
        for s in range(last + 1):
            for i in range(2):
                if s < last:
                    self.right[s, i].wait_send()
                    self.left[s, i].wait_send()
                elif not self.lean and i == 0:
                    self.right[s, 0].wait_send()
                    self.left[s, 0].wait_send()
        if self.lean:

            def body(even):
                for i in range(2):
                    (self.left if even else self.right)[1, i].wait_send()

            when_even(self.place, body)
        for copy in self.across:
            copy.wait_send()


def by_rows(count, body, step=16):
    def one(i, carry):
        body(pl.ds(pl.multiple_of(i * step, step), step))
        return carry

    lax.fori_loop(0, count // step, one, 0)


class Reduce:
    def __init__(self, place, p, from_core, in_r, in_l, send_r, recv_r, send_l, recv_l, core_send, core_recv, lean=False):
        self.place, self.p, self.from_core, self.in_r, self.in_l = place, p, from_core, in_r, in_l
        self.sems = (send_r, recv_r, send_l, recv_l, core_send, core_recv)
        self.lean = lean and place.n == 4
        half = place.n // 2
        self.order = [half] + [k for j in range(half - 1, 0, -1) for k in (j, -j)] + [0]
        self.chips = {k: place.ring(k)[0] for k in self.order}
        self.across, self.copies = {}, {}
        for sign in (1, -1):
            for s in range(half):
                for piece in range(2):
                    if s or self.lean or piece == (sign < 0):
                        self._copy(sign, s, piece)

    @staticmethod
    def scratch(n, rows, width):
        dma = pltpu.SemaphoreType.DMA
        wide = [pltpu.VMEM((n, rows, width), BF)] + [pltpu.VMEM((n // 2, rows, width), BF)] * 2
        return wide + [dma((n // 2, 2))] * 4 + [dma((n,))] * 2

    def offer(self, k):
        core_send, core_recv = self.sems[4:]
        slot, q, t = len(self.across), self.chips[k], self.place.t
        self.across[k] = remote(
            self.p.at[q, 1 - t], self.from_core.at[q], core_send.at[slot], core_recv.at[slot], {"tp": 1 - t}
        )

    def _local(self, k, at):
        q = self.chips[k]
        return self.p[q, self.place.t, at].astype(F32) + self.from_core[q, at].astype(F32)

    def _add(self, k, piece, extra=None):
        top = self.p.shape[2] // 2

        def body(at):
            whole = pl.ds(pl.multiple_of(piece * top + at.start, 16), at.size)
            total = self._local(k, whole)
            if extra is not None:
                total = total + extra[whole].astype(F32)
            self.from_core[self.chips[k], whole] = total.astype(BF)

        by_rows(top, body)

    def _copy(self, sign, s, piece):
        if (sign, s, piece) not in self.copies:
            place, top = self.place, self.p.shape[2] // 2
            send, recv = self.sems[:2] if sign > 0 else self.sems[2:4]
            target = self.in_r if sign > 0 else self.in_l
            k = place.n // 2 - s
            rows = pl.ds(piece * top, top)
            self.copies[sign, s, piece] = pltpu.make_async_remote_copy(
                src_ref=self.from_core.at[self.chips[sign * k if s else k], rows], dst_ref=target.at[s, rows],
                send_sem=send.at[s, piece], recv_sem=recv.at[s, piece],
                device_id=place.ring(sign)[1], device_id_type=MESH,
            )
        return self.copies[sign, s, piece]

    def far(self):
        half = self.place.n // 2
        self.across[half].wait_recv()
        self._add(half, 0)
        self._add(half, 1)
        if self.lean:

            def body(even):
                for piece in range(2):
                    self._copy(-1 if even else 1, 0, piece).start()

            when_even(self.place, body)
        else:
            self._copy(1, 0, 0).start()
            self._copy(-1, 0, 1).start()

    def free(self):
        k = self.place.n // 2 - 1
        if self.lean:
            self.across[1].wait_recv()
            self.across[-1].wait_recv()

            def body(even):
                sign = -1 if even else 1
                for piece in range(2):
                    self._add(sign, piece)
                    self._copy(sign, 1, piece).start()

            when_even(self.place, body)
        elif k:
            for sign, piece in ((1, 1), (-1, 0)):
                self.across[sign * k].wait_recv()
                self._add(sign * k, piece)
                self._copy(sign, 1, piece).start()

    def near(self, s):
        half = self.place.n // 2
        k = half - s
        if self.lean:

            def body(even):
                sign = 1 if even else -1
                for piece in range(2):
                    self._copy(sign, 0, piece).wait_recv()
                    self._add(sign, piece, (self.in_r if even else self.in_l).at[0])
                    self._copy(sign, 1, piece).start()

            when_even(self.place, body)
            return
        if s > 1:
            self.across[k].wait_recv()
            self.across[-k].wait_recv()
        for sign, first, held in ((1, 0, self.in_r), (-1, 1, self.in_l)):
            for piece in (first,) if s == 1 else (first, 1 - first):
                self._copy(sign, s - 1, piece).wait_recv()
                self._add(sign * k, piece, held.at[s - 1])
                self._copy(sign, s, piece).start()

    def end(self, use):
        half = self.place.n // 2
        self.across[0].wait_recv()
        for sign in (1, -1):
            for piece in range(2):
                self._copy(sign, half - 1, piece).wait_recv()

        def body(at):
            use(at, self._local(0, at) + self.in_r[half - 1, at].astype(F32) + self.in_l[half - 1, at].astype(F32))

        by_rows(self.p.shape[2], body)

    def finish(self):
        half = self.place.n // 2
        if self.lean:

            def body(even):
                for piece in range(2):
                    self._copy(-1 if even else 1, 0, piece).wait_send()

            when_even(self.place, body)
        else:
            self._copy(1, 0, 0).wait_send()
            self._copy(-1, 0, 1).wait_send()
        for s in range(1, half):
            for sign in (1, -1):
                for piece in range(2):
                    self._copy(sign, s, piece).wait_send()
        for copy in self.across.values():
            copy.wait_send()

    def run(self, use, before=None, offered=False):
        if not offered:
            for k in self.order:
                self.offer(k)
            self.far()
            self.free()
        for s in range(1, self.place.n // 2):
            self.near(s)
        if before is not None:
            before()
        self.end(use)


def mm(a, b):
    return jnp.dot(a, b, preferred_element_type=F32)


def mm_t(a, b):
    return lax.dot_general(a, b, (((1,), (1,)), ((), ())), preferred_element_type=F32)


def t_mm(a, b):
    return lax.dot_general(a, b, (((0,), (0,)), ((), ())), preferred_element_type=F32)


def rms_scale(values):
    return lax.rsqrt(jnp.mean(values * values, axis=-1, keepdims=True) + EPSILON)


def norm_back(grad_normed, inputs, scale_rows, gain):
    unit = inputs * scale_rows
    scaled = grad_normed * gain
    return scale_rows * (scaled - unit * jnp.mean(scaled * unit, axis=-1, keepdims=True))


def tiles(count, width, body):
    def one(j, carry):
        body(pl.ds(pl.multiple_of(j * width, width), width))
        return carry

    lax.fori_loop(0, count // width, one, 0)


def tile_of(count):
    return 256 if count % 256 == 0 else 128


def turn(v, cosine, sine):
    return v * cosine + pltpu.roll(v, HD // 2, 1) * sine


def block_diagonal(out, parts, rank, width):
    out[...] = jnp.zeros(out.shape, out.dtype)
    for i in range(parts[1]):
        out[i * rank : (i + 1) * rank, i * width : (i + 1) * width] = parts[0][i * rank : (i + 1) * rank, :]


def write_norm(x_rows, source, gain):
    def body(at):
        v = source[at].astype(F32)
        x_rows[at] = (v * rms_scale(v) * gain[...]).astype(BF)

    by_rows(source.shape[0], body)


ROW_BLOCK = 128
KEY_STEP = 256


def row_blocks(tree, body):
    for j in range(tree // KEY_STEP):

        def one(i, carry, j=j):
            body(pl.ds(pl.multiple_of(j * KEY_STEP + i * ROW_BLOCK, ROW_BLOCK), ROW_BLOCK), (j + 1) * KEY_STEP)
            return carry

        lax.fori_loop(0, KEY_STEP // ROW_BLOCK, one, 0)


def seen(rows, keys, query_bits, key_bits):
    shared = (query_bits[rows] & key_bits[:, :keys]) != 0
    i = rows.start + lax.broadcasted_iota(jnp.int32, (ROW_BLOCK, keys), 0)
    j = lax.broadcasted_iota(jnp.int32, (ROW_BLOCK, keys), 1)
    return shared & (j <= i)


def attention_forward(
    n, nf, layer, part, rank, lean, plan,
    residual, gain, w_hbm, a_model, a_head, cosine, sine, query_bits, key_bits, lam, *refs, pace,
):
    jobs, refs = plan.split(refs)
    (middle, x_hbm, queries, keys, values, small, log_total, mixed, headed, side,
     x, p, w, raised, copy_sems, *sems) = refs
    place = Place(n)
    chip_rows, width = 2 * x_hbm.shape[2], x_hbm.shape[3]
    tree = n * chip_rows
    load = pltpu.make_async_copy(w_hbm, w, copy_sems.at[0])
    load.start()
    gather, reduce = Gather(place, x, *sems[:6], lean=lean), Reduce(place, p, *sems[6:], lean=lean)
    write_norm(x.at[place.q, place.t], residual, gain)
    block_diagonal(raised, (a_head[rank : 4 * rank], 3), rank, VD)
    work = plan.work(place, nf, jobs)
    enter(place, nf, bool(plan.scatters))
    gather.begin()
    work.at(0)
    pace.ready()
    load.wait()

    def project(q):
        rows = pl.ds(pl.multiple_of(q * chip_rows, chip_rows), chip_rows)
        v = x[q].reshape(chip_rows, width)
        low = mm_t(v, a_model[: 3 * rank]).astype(BF)
        small[rows] = low
        for i, out in enumerate((queries, keys, values)):
            at = slice(i * VD, (i + 1) * VD)
            made = mm(v, w[:, at]) + ADAPTER_SCALE * mm(low, raised[:, at])
            if i < 2:
                for c in range(2):
                    half = slice(c * HD, (c + 1) * HD)
                    out[rows, half] = turn(made[:, half], cosine[rows], sine[rows]).astype(BF)
            else:
                out[rows] = made.astype(BF)

    for q in gather.chunks():
        project(q)
    work.at(1)
    keep = pltpu.make_async_copy(x, x_hbm, copy_sems.at[1])
    keep.start()
    score_scale = HD ** (-0.5)
    weight = lam[...]

    def attend(rows, count):
        visible = seen(rows, count, query_bits, key_bits)
        both = []
        for c in range(2):
            at = slice(c * HD, (c + 1) * HD)
            scores = mm_t(queries[rows, at], keys[:count, at]) * score_scale
            scores = jnp.where(visible, scores, NEGATIVE_BIG)
            top = jnp.max(scores, axis=-1, keepdims=True)
            raw = jnp.exp(scores - top)
            total = jnp.sum(raw, axis=-1, keepdims=True)
            log_total[rows, c : c + 1] = top + jnp.log(total)
            both.append(raw * (1.0 / total))
        mix = mm((both[0] - weight * both[1]).astype(BF), values[:count])
        mixed[rows] = mix.astype(BF)
        head = (mix * rms_scale(mix) * keep_factor(layer)).astype(BF)
        headed[rows] = head
        side[rows] = mm_t(head, a_head[:rank]).astype(BF)

    row_blocks(tree, attend)
    pace.flush()
    work.at(2)

    for k in reduce.order:
        q = reduce.chips[k]
        rows = pl.ds(pl.multiple_of(q * chip_rows, chip_rows), chip_rows)
        head, low = headed[rows], side[rows]

        def out_tile(at):
            made = mm_t(head, w[at, 3 * VD :]) + ADAPTER_SCALE * mm(low, a_model[9 * rank : 10 * rank, at])
            p[q, :, :, at] = (made * part).astype(BF).reshape(2, chip_rows // 2, at.size)

        tiles(width, 512, out_tile)
        reduce.offer(k)
        if k == reduce.order[0]:
            reduce.far()
        if k == reduce.order[2]:
            reduce.free()
    work.at(3)
    for s in range(1, n // 2):
        reduce.near(s)
    work.at(4)

    def use(at, total):
        middle[at] = residual[at].astype(F32) + total

    reduce.end(use)
    work.at(5)
    keep.wait()
    gather.finish()
    reduce.finish()
    work.settle()


def ffn_forward(
    n, nf, units, rank, last, plan,
    residual, gain, w_hbm, a_model, e_model, *refs, pace,
):
    place = Place(n)
    if last:
        cotangent, *refs = refs
    jobs, refs = plan.split(refs)
    if last:
        all_refs = refs
        next_hbm, *refs, next_x = refs[:-6]
        next_gather = Gather(place, next_x, *all_refs[-6:])
    (following, x_hbm, gates, ups, hidden, small, side,
     x, p, w, raised, copy_sems, *sems) = refs
    chip_rows, width = 2 * x_hbm.shape[2], x_hbm.shape[3]
    tree = n * chip_rows
    load = pltpu.make_async_copy(w_hbm, w.at[:, pl.ds(0, 2 * units)], copy_sems.at[0])
    load.start()
    gather, reduce = Gather(place, x, *sems[:6], lean=not last), Reduce(place, p, *sems[6:], lean=not last)
    write_norm(x.at[place.q, place.t], residual, gain)
    block_diagonal(raised, (e_model, 2), rank, units)
    work = plan.work(place, nf, jobs)
    enter(place, nf, bool(plan.scatters))
    gather.begin()
    work.at(0)
    pace.ready()
    load.wait()
    step = tile_of(units)

    for number, q in enumerate(gather.chunks()):
        if number == n - 1:
            work.at(1)
        rows = pl.ds(pl.multiple_of(q * chip_rows, chip_rows), chip_rows)
        v = x[q].reshape(chip_rows, width)
        low = mm_t(v, a_model[4 * rank : 6 * rank]).astype(BF)
        small[rows] = low

        def unit_tile(at):
            up_at = pl.ds(pl.multiple_of(units + at.start, step), step)
            gate = mm(v, w[:, at]) + ADAPTER_SCALE * mm(low, raised[:, at])
            up = mm(v, w[:, up_at]) + ADAPTER_SCALE * mm(low, raised[:, up_at])
            gates[rows, at] = gate.astype(BF)
            ups[rows, at] = up.astype(BF)
            hidden[rows, at] = (gate / (1.0 + jnp.exp(-gate)) * up).astype(BF)

        tiles(units, step, unit_tile)

    pace.flush()
    if last:
        next_x[place.q, place.t] = cotangent[...]
        next_gather.begin()
    work.at(2)
    keep = pltpu.make_async_copy(x, x_hbm, copy_sems.at[1])
    keep.start()

    work.complete(0)
    load = pltpu.make_async_copy(plan.late(jobs), w.at[:, pl.ds(2 * units, units)], copy_sems.at[0])
    load.start()
    load.wait()
    for k in reduce.order:
        q = reduce.chips[k]
        rows = pl.ds(pl.multiple_of(q * chip_rows, chip_rows), chip_rows)
        made_hidden = hidden[rows]
        low = mm_t(made_hidden, e_model[2 * rank : 3 * rank]).astype(BF)
        side[rows] = low

        def out_tile(at):
            made = mm_t(made_hidden, w[at, 2 * units :])
            made = made + ADAPTER_SCALE * mm(low, a_model[10 * rank : 11 * rank, at])
            p[q, :, :, at] = made.astype(BF).reshape(2, chip_rows // 2, at.size)

        tiles(width, 512, out_tile)
        reduce.offer(k)
        if k == reduce.order[0]:
            reduce.far()
        if k == reduce.order[2]:
            reduce.free()
    if last:
        coming = next_gather.chunks()
        for _ in range(n - 1):
            next(coming)
    work.at(3)
    for s in range(1, n // 2):
        reduce.near(s)
    work.at(4)

    def use(at, total):
        following[at] = residual[at] + total

    reduce.end(use)
    if last:
        for _ in coming:
            pass
        keep_next = pltpu.make_async_copy(next_x, next_hbm, copy_sems.at[2])
        keep_next.start()
    work.at(5)
    keep.wait()
    if last:
        keep_next.wait()
        next_gather.finish()
    gather.finish()
    reduce.finish()
    work.settle((0,))


def ffn_backward(
    n, units, rank, carry,
    grad, middle, gain, w_hbm, w_down_hbm, a_model, e_model, x_hbm, gates, ups, hidden, small, side, *refs, pace,
):
    if carry:
        final, gathered, final_out, *refs = refs
        *refs, final_rows, home_send, home_recv = refs
    else:
        sums, here, sums_out, here_out, *refs = refs
        *refs, home_send, home_recv = refs
    (grad_out, grad_up_down, grad_in, grad_units,
     x, p, w, kept, dgu, dsmall, dside, raised, copy_sems, *sems) = refs
    place = Place(n)
    chip_rows, width = 2 * x_hbm.shape[2], x_hbm.shape[3]
    tree = n * chip_rows
    load = pltpu.make_async_copy(w_hbm, w.at[:, pl.ds(0, 2 * units)], copy_sems.at[0])
    load.start()
    load_down = pltpu.make_async_copy(w_down_hbm, w.at[:, pl.ds(2 * units, units)], copy_sems.at[2])
    load_down.start()
    fetch = pltpu.make_async_copy(x_hbm, kept, copy_sems.at[1])
    gather, reduce = Gather(place, x, *sems[:6]), Reduce(place, p, *sems[6:])

    if carry:
        come = pltpu.make_async_copy(gathered, x, copy_sems.at[3])
        come.start()
    else:

        def own(at):
            x[place.q, place.t, at] = grad[at].astype(BF)

        by_rows(grad.shape[0], own)
    block_diagonal(raised, (e_model, 2), rank, units)
    if carry:

        def last_rows(at):
            final_rows[at] = final[at].astype(BF)

        by_rows(final.shape[0], last_rows)
    enter(place, home=True)
    if not carry:
        gather.begin()
        going = [
            TreeMove(place, source, target, home_send.at[i], home_recv.at[i])
            for i, (source, target) in enumerate(((sums, sums_out), (here, here_out)))
        ]
    else:
        home = Home(place, final_out, home_send, home_recv)
        home.start(final_rows)
    pace.ready()
    load.wait()
    load_down.wait()
    step = tile_of(units)

    if carry:
        come.wait()
    coming = [0] + [k for s in range(1, n // 2) for k in (-s, s)] + [n // 2]
    for q in list(reduce.chips.values()) if carry else gather.chunks():
        rows = pl.ds(pl.multiple_of(q * chip_rows, chip_rows), chip_rows)
        v = x[q].reshape(chip_rows, width)
        low = (ADAPTER_SCALE * mm_t(v, a_model[10 * rank : 11 * rank])).astype(BF)
        dside[rows] = low

        def unit_tile(at):
            up_at = pl.ds(pl.multiple_of(units + at.start, step), step)
            down_at = pl.ds(pl.multiple_of(2 * units + at.start, step), step)
            dhidden = mm(v, w[:, down_at]) + mm(low, e_model[2 * rank : 3 * rank, at])
            gate, up = gates[rows, at].astype(F32), ups[rows, at].astype(F32)
            sig = 1.0 / (1.0 + jnp.exp(-gate))
            dgu[rows, at] = (dhidden * up * sig * (1.0 + gate * (1.0 - sig))).astype(BF)
            dgu[rows, up_at] = (dhidden * gate * sig).astype(BF)

        tiles(units, step, unit_tile)
        back = dgu[rows]
        low_back = (ADAPTER_SCALE * mm_t(back, raised[...])).astype(BF)
        dsmall[rows] = low_back

        def out_tile(at):
            made = mm_t(back, w[at, : 2 * units]) + mm(low_back, a_model[4 * rank : 6 * rank, at])
            p[q, :, :, at] = made.astype(BF).reshape(2, chip_rows // 2, at.size)

        tiles(width, 512, out_tile)
        if carry:
            k = reduce.order[len(reduce.across)]
        else:
            k = coming.pop(0)
        reduce.offer(k)
        if k == n // 2:
            reduce.far()
        if k == (reduce.order[2] if carry else n // 2):
            reduce.free()

    fetch.start()
    if not carry:
        for move in going:
            move.start()

    def use(at, total):
        inputs = middle[at]
        grad_out[at] = grad[at].astype(F32) + norm_back(total, inputs, rms_scale(inputs), gain[...])

    def adapters():
        fetch.wait()

        def model_tile(at):
            flat = x[:, :, :, at].reshape(tree, at.size)
            grad_up_down[:, at] = (ADAPTER_SCALE * t_mm(side[...], flat)).astype(BF)
            flat = kept[:, :, :, at].reshape(tree, at.size)
            grad_in[:, at] = t_mm(dsmall[...], flat).astype(BF)

        tiles(width, 256, model_tile)

        def unit_tile(at):
            up_at = pl.ds(pl.multiple_of(units + at.start, step), step)
            grad_units[:rank, at] = (ADAPTER_SCALE * t_mm(small[...], dgu[:, at])[:rank]).astype(BF)
            grad_units[rank : 2 * rank, at] = (ADAPTER_SCALE * t_mm(small[...], dgu[:, up_at])[rank:]).astype(BF)
            grad_units[2 * rank : 3 * rank, at] = t_mm(dside[...], hidden[:, at]).astype(BF)
            grad_units[3 * rank :, at] = jnp.zeros((rank, at.size), BF)

        tiles(units, step, unit_tile)

    reduce.run(use, adapters, True)
    if not carry:
        gather.finish()
    reduce.finish()
    if carry:
        home.land()
        home.finish()
    else:
        for move in going:
            move.land()


def attention_backward(
    n, layer, share, heads_tp, rank,
    grad, residual, gain, w_hbm, a_model, a_head, cosine, sine, query_bits, key_bits, lam,
    x_hbm, queries, keys, values, small, log_total, mixed, headed, side,
    grad_up_down, grad_ffn_in, grad_units,
    grad_out, own_sum, all_units,
    x, p, w, dmixed, dq, dk, dv, dprojected, dsmall, dside, raised, grad_a9, p_own, copy_sems, *sems, pace,
):
    place = Place(n)
    part = 1.0 / share
    chip_rows, width = 2 * x_hbm.shape[2], x_hbm.shape[3]
    tree = n * chip_rows
    load = pltpu.make_async_copy(w_hbm, w, copy_sems.at[0])
    load.start()
    gather, reduce = Gather(place, x, *sems[:6]), Reduce(place, p, *sems[6:15])
    gather_units, reduce_own = Gather(place, all_units, *sems[15:21]), Reduce(place, p_own, *sems[21:])

    def own(at):
        x[place.q, place.t, at] = grad[at].astype(BF)

    by_rows(grad.shape[0], own)
    block_diagonal(raised, (a_head[rank : 4 * rank], 3), rank, VD)
    all_units[place.q, place.t] = grad_units[...]
    enter(place)
    gather.begin()
    dk[...] = jnp.zeros(dk.shape, F32)
    dv[...] = jnp.zeros(dv.shape, F32)
    pace.ready()
    load.wait()

    score_scale = HD ** (-0.5)
    weight = lam[...]

    def attend(rows, count):
        visible = seen(rows, count, query_bits, key_bits)
        dmix = dmixed[rows]
        dweights = mm_t(dmix, values[:count])
        both = []
        for c in range(2):
            at = slice(c * HD, (c + 1) * HD)
            scores = mm_t(queries[rows, at], keys[:count, at]) * score_scale
            probability = jnp.exp(jnp.where(visible, scores - log_total[rows, c : c + 1], NEGATIVE_BIG))
            both.append(probability)
            weighted = probability * dweights
            dscores = weighted - probability * jnp.sum(weighted, axis=-1, keepdims=True)
            dscores = (dscores * -weight if c else dscores).astype(BF)
            dq[rows, at] = mm(dscores, keys[:count, at])
            dk[:count, at] += t_mm(dscores, queries[rows, at])
        dv[:count] += t_mm((both[0] - weight * both[1]).astype(BF), dmix)

    for q in gather.chunks():
        rows = pl.ds(pl.multiple_of(q * chip_rows, chip_rows), chip_rows)
        v = x[q].reshape(chip_rows, width)
        low = (ADAPTER_SCALE * mm_t(v, a_model[9 * rank : 10 * rank])).astype(BF)
        dside[rows] = low
        dheaded = mm(v, w[:, 3 * VD :]) + mm(low, a_head[:rank])
        inputs = mixed[rows].astype(F32)
        dmixed[rows] = norm_back(dheaded, inputs, rms_scale(inputs), keep_factor(layer)).astype(BF)

        def block(i, carry, q=q):
            attend(pl.ds(pl.multiple_of(q * chip_rows + i * ROW_BLOCK, ROW_BLOCK), ROW_BLOCK), tree)
            return carry

        lax.fori_loop(0, chip_rows // ROW_BLOCK, block, 0)

    gather_units.begin()

    def send_part(k):
        q = reduce.chips[k]
        rows = pl.ds(pl.multiple_of(q * chip_rows, chip_rows), chip_rows)
        for j, source in enumerate((dq, dk)):
            for c in range(2):
                half = slice(c * HD, (c + 1) * HD)
                turned = turn(source[rows, half] * score_scale, cosine[rows], -sine[rows])
                dprojected[rows, j * VD + c * HD : j * VD + (c + 1) * HD] = turned.astype(BF)
        dprojected[rows, 2 * VD :] = dv[rows].astype(BF)
        back = dprojected[rows]
        low_back = (ADAPTER_SCALE * mm_t(back, raised[...])).astype(BF)
        dsmall[rows] = low_back

        def out_tile(at):
            made = mm_t(back, w[at, : 3 * VD]) + mm(low_back, a_model[: 3 * rank, at])
            p[q, :, :, at] = (made * part).astype(BF).reshape(2, chip_rows // 2, at.size)

        tiles(width, 512, out_tile)
        reduce.offer(k)

    for k in reduce.order[:3]:
        send_part(k)
        if k == n // 2:
            reduce.far()
    reduce.free()

    def out_gradient(at):
        flat = x[:, :, :, at].reshape(tree, at.size)
        grad_a9[:, at] = (ADAPTER_SCALE * part * t_mm(side[...], flat)).astype(BF)

    tiles(width, 256, out_gradient)
    gather.finish()
    fetch = pltpu.make_async_copy(x_hbm, x, copy_sems.at[1])
    fetch.start()
    for k in reduce.order[3:]:
        send_part(k)
    for _ in gather_units.chunks():
        pass
    fetch.wait()

    block = width // (2 * n)

    def full_tile(jp, carry):
        at = pl.ds(pl.multiple_of(jp * block, block), block)
        q, t = jp // 2, jp % 2
        flat = x[:, :, :, at].reshape(tree, block)
        p_own[q, t, : 3 * rank] = (part * t_mm(dsmall[...], flat)).astype(BF)
        p_own[q, t, 4 * rank : 6 * rank] = grad_ffn_in[:, at]
        p_own[q, t, 9 * rank : 10 * rank] = grad_a9[:, at]
        p_own[q, t, 10 * rank : 11 * rank] = grad_up_down[:, at]
        p_own[q, t, 11 * rank :] = jnp.zeros((rank, block), BF)
        return carry

    lax.fori_loop(0, 2 * n, full_tile, 0)
    of_head = [part * t_mm(dside[...], headed[...])]
    for i in range(3):
        made = t_mm(small[...], dprojected[:, i * VD : (i + 1) * VD])[i * rank : (i + 1) * rank]
        of_head.append(ADAPTER_SCALE * part * made)
    head = place.t * heads_tp + place.q // share
    for j in range(2 * n):
        start = j * block % VD
        own = (head == j * block // VD).astype(F32)
        for i, k in enumerate((3, 6, 7, 8)):
            made = of_head[i][:, start : start + block] * own
            p_own[j // 2, j % 2, k * rank : (k + 1) * rank] = made.astype(BF)

    for k in reduce.order:
        reduce_own.offer(k)
    reduce_own.far()
    reduce_own.free()
    for s in range(1, n // 2):
        reduce.near(s)
        reduce_own.near(s)

    def use_own(at, total):
        own_sum[at] = total.astype(BF)

    def use(at, total):
        inputs = residual[at].astype(F32)
        grad_out[at] = grad[at].astype(F32) + norm_back(total, inputs, rms_scale(inputs), gain[...])

    reduce.end(use)
    reduce_own.end(use_own)
    gather_units.finish()
    reduce.finish()
    reduce_own.finish()


def finish_kernel(
    n, nf, layers, rank,
    grad, own_sums, own_units, slot, *refs,
):
    earlier, refs = refs[: 2 * layers - 2], refs[2 * layers - 2 :]
    (landed, model_grad, hidden_grad,
     rows_out, passing, sent_sums, all_sums, all_units, home_send, home_recv, tree_send, tree_recv, relay_send, relay_recv) = refs
    place = Place(n)
    own = model_grad.shape[2]
    tall = own_sums.shape[0]

    def cut(at):
        rows_out[at] = grad[at].astype(BF)

    by_rows(grad.shape[0], cut)
    sent_sums[...] = own_sums[...]
    sent_sums[tall - rank :] = jnp.broadcast_to(slot[...], (rank, own_sums.shape[1])).astype(BF)
    enter(place, home=True, ring=False, trees=nf, partner=True)
    top = grad.shape[0] // 2
    low, high = pl.ds(0, top), pl.ds(top, top)
    slot_here = landed.at[place.t]
    partner = {"ctx": (1 - place.c_hi) * place.h + place.c_lo}
    beside = {"fsdp": place.f_hi * 2 + 1 - place.f_lo}

    def make(src, dst, i, device):
        return pltpu.make_async_remote_copy(
            src_ref=src, dst_ref=dst, send_sem=relay_send.at[i], recv_sem=relay_recv.at[i],
            device_id=device, device_id_type=MESH,
        )

    straight = make(rows_out.at[low], slot_here.at[low], 0, place.home)
    to_relay = make(rows_out.at[high], passing, 1, beside)
    from_relay = make(passing, slot_here.at[high], 2, partner)
    stay = pltpu.make_async_copy(rows_out, slot_here, relay_recv.at[3])
    cross = make(slot_here, slot_here, 4, {"tp": 1 - place.t})
    is_away, is_relay = place.away == 1, place.away == 0

    away = {}
    for i, (source, target) in enumerate(((sent_sums, all_sums), (own_units, all_units))):
        away[i] = TreeMove(place, source, target.at[:, 0], home_send.at[i + 1], home_recv.at[i + 1])
        away[i].start()
    copies = []

    def hand_round(source, target, l, i):
        to = target.at[place.f, l]
        for e in range(1, nf):
            sems = tree_send.at[l, i, e], tree_recv.at[l, i, e]
            copies.append(remote(source, to, *sems, {"fsdp": flip(place.f, e)}))

    for l in range(1, layers):
        for i, target in enumerate((all_sums, all_units)):
            source = earlier[2 * l - 2 + i].at[place.f]
            target[place.f, l] = earlier[2 * l - 2 + i][place.f]
            hand_round(source, target, l, i)
    for i, target in enumerate((all_sums, all_units)):
        away[i].land()
        if i == 1:

            @pl.when(is_away)
            def leave():
                straight.start()
                to_relay.start()

            pl.when(is_relay)(stay.start)
        hand_round(target.at[place.f, 0], target, 0, i)
    @pl.when(is_relay)
    def hand_on():
        to_relay.wait_recv()
        from_relay.start()

    for copy in copies:
        copy.wait_recv()
    for b in range(own):
        number = (place.f * own + b).astype(F32)
        keeps = [
            (all_sums[f, 0, tall - rank : tall - rank + 1, :1].astype(F32) == number).astype(F32) for f in range(nf)
        ]
        for l in range(layers):
            for k in range(11):
                at = slice(k * rank, (k + 1) * rank)
                model_grad[l, k, b] = sum(keeps[f] * all_sums[f, l, at].astype(F32) for f in range(nf))
            for k in range(3):
                at = slice(k * rank, (k + 1) * rank)
                hidden_grad[l, k, b] = sum(keeps[f] * all_units[f, l, at].astype(F32) for f in range(nf))

    @pl.when(is_relay)
    def rest():
        stay.wait()
        from_relay.wait_send()

    @pl.when(is_away)
    def arrive():
        straight.wait()
        to_relay.wait_send()
        from_relay.wait_recv()

    cross.start()
    cross.wait()
    for copy in copies:
        copy.wait_send()


class Plan:
    def __init__(self, n, nf, rows, scatters, spreads, schedule):
        self.n, self.nf, self.rows, self.schedule = n, nf, rows, schedule
        self.scatters, self.spreads = scatters, spreads

    def ins(self):
        return [(blocks, True) for blocks, _ in self.scatters] + [(w, True) for w in self.spreads]

    def outs(self):
        made = [(shape, BF, True) for _, shape in self.scatters]
        return made + [(w.shape, BF, True) for w in self.spreads]

    def semaphores(self):
        made = Spread.scatter_semaphores(self.n) * len(self.scatters)
        return made + Spread.spread_semaphores(self.n, self.nf) * len(self.spreads)

    def split(self, refs):
        a, b = len(self.scatters), len(self.spreads)
        count = 2 * a + 6 * b
        refs = list(refs)
        taken = refs[: a + b], refs[a + b : 2 * (a + b)], refs[len(refs) - count :]
        return taken, refs[2 * (a + b) : len(refs) - count]

    def work(self, place, nf, jobs):
        a, b = len(self.scatters), len(self.spreads)
        ins, outs, sems = jobs
        scatters = [(ins[i], outs[i], sems[2 * i : 2 * i + 2]) for i in range(a)]
        spreads = [(outs[a + i], sems[2 * a + 6 * i : 2 * a + 6 * i + 6]) for i in range(b)]
        return Work(place, nf, self.rows, scatters, spreads, self.schedule)

    def late(self, jobs):
        return jobs[1][len(self.scatters)]


class Pace:
    def __init__(self, loads, stores):
        self.loads, self.stores = loads, stores
        for copy in loads:
            copy.start()

    def ready(self):
        for copy in self.loads:
            copy.wait()

    def flush(self):
        for copy in self.stores:
            copy.start()

    def end(self):
        for copy in self.stores:
            copy.wait()


def call(kernel, collective, ins, outs, scratch, plan=None):
    spec = lambda hbm: pl.BlockSpec(memory_space=pl.ANY if hbm else pltpu.VMEM)
    aliases = {}
    if plan is not None:
        first_in, count = len(ins), len(plan.scatters)
        aliases = {first_in + count + i: count + i for i in range(len(plan.spreads))}
        ins, outs, scratch = ins + plan.ins(), plan.outs() + outs, scratch + plan.semaphores()
    late_in = [i for i, (_, hbm) in enumerate(ins) if hbm == "paced"]
    late_out = [i for i, (_, _, hbm) in enumerate(outs) if hbm == "paced"]
    extra = [pltpu.VMEM(ins[i][0].shape, ins[i][0].dtype) for i in late_in]
    extra += [pltpu.VMEM(outs[i][0], outs[i][1]) for i in late_out]
    if late_in or late_out:
        extra.append(pltpu.SemaphoreType.DMA((len(late_in) + len(late_out),)))

        def paced(*refs):
            refs, held = list(refs[: -len(extra)]), refs[-len(extra) :]
            loads, stores = [], []
            for slot, i in enumerate(late_in):
                loads.append(pltpu.make_async_copy(refs[i], held[slot], held[-1].at[slot]))
                refs[i] = held[slot]
            for slot, i in enumerate(late_out, len(late_in)):
                stores.append(pltpu.make_async_copy(held[slot], refs[len(ins) + i], held[-1].at[slot]))
                refs[len(ins) + i] = held[slot]
            pace = Pace(loads, stores)
            kernel(*refs, pace=pace)
            pace.end()

        body = paced
    else:
        body = kernel
    made = pl.pallas_call(
        body,
        out_shape=[jax.ShapeDtypeStruct(shape, kind) for shape, kind, _ in outs],
        in_specs=[spec(hbm) for _, hbm in ins],
        out_specs=[spec(hbm) for _, _, hbm in outs],
        scratch_shapes=scratch + extra,
        input_output_aliases=aliases,
        compiler_params=pltpu.CompilerParams(
            collective_id=collective, has_side_effects=True, vmem_limit_bytes=62 << 20
        ),
    )(*[array for array, _ in ins])
    return list(made)


def line_bits(parent_row, seg):
    number = jnp.arange(NSEG)
    one = lambda x: lax.shift_left(jnp.ones_like(x), x)
    grand = jnp.sum(jnp.where(parent_row[:, None] == number[None, :], parent_row[None, :], 0), axis=1)
    line = one(number) | one(parent_row) | one(grand)
    mine = jnp.sum(jnp.where(seg[:, None] == number[None, :], line[None, :], 0), axis=1)
    return mine, one(seg)


def keep_factor(layer):
    return 0.2 + 0.6 * math.exp(-0.3 * layer)


def chips_of(nf, nc):
    h = nc // 2
    for f in range(nf):
        for c in range(nc):
            yield f * nc + c, (f // 2, f % 2, c // h, c % h)


def permute(x, nf, nc, target):
    h = nc // 2
    pairs = []
    for source, spot in chips_of(nf, nc):
        f_hi, f_lo, c_hi, c_lo = target(*spot)
        pairs.append((source, (f_hi * 2 + f_lo) * nc + c_hi * h + c_lo))
    return lax.ppermute(x, ("fsdp", "ctx"), pairs)


def swap_trees(x, nf, nc):
    return permute(x, nf, nc, lambda f_hi, f_lo, c_hi, c_lo: (f_hi, c_hi, f_lo, c_lo))


def shards(
    nf,
    nc,
    tokens,
    cotangent,
    segments,
    depths,
    parents,
    tree_adapter_index,
    layer_norm_gains,
    difference_lambda,
    query_key_value_weight,
    output_weight,
    gate_up_weight,
    down_weight,
    adapter_model_factors,
    adapter_hidden_factors,
):
    n = nc
    place = Place(n)
    q, t = place.q, place.t
    tokens_dev, width = tokens.shape
    rows = tokens_dev // 2
    tree = tokens_dev * n
    layers, weight_rows = query_key_value_weight.shape[:2]
    heads_tp = difference_lambda.shape[1]
    share = max(1, n // heads_tp)
    head = q // share
    hidden_tp = down_weight.shape[2]
    units = (hidden_tp + n * 128 - 1) // (n * 128) * 128
    rank, adapters = adapter_model_factors.shape[3], adapter_model_factors.shape[2]
    h = n // 2

    notes = jnp.concatenate([segments, depths, parents[0], tree_adapter_index])
    order = jnp.arange(n)
    of_tree = jnp.zeros((n, notes.shape[0]), jnp.int32)
    for d in range(n):

        def hand_out(f_hi, f_lo, c_hi, c_lo, d=d):
            to = (c_hi * (n // 2) + c_lo) ^ d
            return f_hi, to // (n // 2), f_lo, to % (n // 2)

        part_of_tree = permute(notes, nf, nc, hand_out)
        of_tree = of_tree + jnp.where(order[:, None] == flip(q, d), part_of_tree[None], 0)
    seg, dep = of_tree[:, :tokens_dev].reshape(tree), of_tree[:, tokens_dev : 2 * tokens_dev].reshape(tree)
    parent_row, slot = of_tree[0, 2 * tokens_dev : 2 * tokens_dev + NSEG], of_tree[0, 2 * tokens_dev + NSEG]
    own_tokens = lax.dynamic_slice_in_dim(tokens, t * rows, rows, 0)
    own_cotangent = lax.dynamic_slice_in_dim(cotangent, t * rows, rows, 0)
    residual = swap_trees(own_tokens, nf, nc)
    own_cotangent = swap_trees(own_cotangent, nf, nc)

    query_bits, key_bits = line_bits(parent_row, seg)
    query_bits, key_bits = query_bits[:, None], key_bits[None, :]
    frequency = 10000.0 ** (-jnp.arange(HD // 2).astype(F32) / (HD // 2))
    angles = dep.astype(F32)[:, None] * frequency[None, :]
    cosine, sine = jnp.cos(angles), jnp.sin(angles)
    cosine = jnp.concatenate([cosine, cosine], axis=1)
    sine = jnp.concatenate([-sine, sine], axis=1)
    gains = layer_norm_gains

    a_all = lax.dynamic_index_in_dim(adapter_model_factors, slot, 2, keepdims=False)
    e_all = lax.dynamic_index_in_dim(adapter_hidden_factors, slot, 2, keepdims=False)
    a_model = a_all.reshape(layers, 11 * rank, width)
    e_all = e_all.reshape(layers, 3 * rank, -1)
    head_at = (t * heads_tp + head) * VD

    heads_of = lax.dynamic_slice_in_dim(a_all, head_at, VD, 3)
    a_head = jnp.concatenate([heads_of[:, 3:4], heads_of[:, 6:9]], axis=1).reshape(layers, 4 * rank, VD)

    def unit_columns(x):
        x = lax.dynamic_slice_in_dim(x, t * hidden_tp, hidden_tp, x.ndim - 1)
        x = jnp.pad(x, ((0, 0),) * (x.ndim - 1) + ((0, n * units - hidden_tp),))
        return lax.dynamic_slice_in_dim(x, q * units, units, x.ndim - 1)

    e_model = unit_columns(e_all)

    part = 1.0 / share
    vmem = lambda *spec: pltpu.VMEM(*spec)
    calls = [0]
    whole_x = ((n, 2, rows, width), BF)
    sems = Gather.semaphores(n) + Reduce.scratch(n, rows, width)
    pair = pltpu.SemaphoreType.DMA((4,))
    big = [vmem(*whole_x), vmem(*whole_x)]

    def run(kernel, ins, outs, scratch, plan=None):
        calls[0] += 1
        return call(kernel, calls[0], ins, outs, scratch, plan)

    near = lambda *arrays: [(array, False) for array in arrays]
    far = lambda *arrays: [(array, True) for array in arrays]
    paced = lambda *arrays: [(array, "paced") for array in arrays]
    out = lambda shape, kind, hbm=False: (shape, kind, hbm)

    dma = pltpu.SemaphoreType.DMA
    c_a, c_g, c_d = 4 * VD, 2 * units, units
    tall = nf * n * weight_rows
    cut = lambda columns: out((n, weight_rows, columns), BF)
    calls[0] += 1
    made = call(
        functools.partial(weights_kernel, n, nf, units, share, layers),
        calls[0],
        far(jnp.transpose(query_key_value_weight, (0, 2, 1, 3)), output_weight, gate_up_weight, down_weight),
        [out((tall, c_a), BF, True), out((tall, c_g), BF, True), out((tall, c_d), BF, True)]
        + ([cut(c_a)] + [cut(c_g)] + [cut(c_d)]) * (layers - 1),
        [
            vmem((n, weight_rows, c_a), BF),
            vmem((n, weight_rows, c_g), BF),
            vmem((n, weight_rows, c_d), BF),
            vmem((layers, weight_rows, 2, hidden_tp), BF),
            vmem((layers, weight_rows, hidden_tp), BF),
            dma((layers, n, 4)),
            dma((layers, 2)),
        ]
        + (Spread.scatter_semaphores(n) + Spread.spread_semaphores(n, nf)) * 2
        + Spread.scatter_semaphores(n),
    )
    w_a, w_g, w_d = [made[0]], [made[1]], [made[2]]
    a_blocks = [None] + made[3 : 2 + layers]
    g_blocks = [None] + made[2 + layers : 1 + 2 * layers]
    d_blocks = [None] + made[1 + 2 * layers :]

    def plan_of(scatters, spreads, *schedule):
        return Plan(n, nf, weight_rows, scatters, spreads, schedule)

    saved = []
    for l in range(layers):
        last = l == layers - 1
        w_attention = w_a[l]
        lam = lax.dynamic_slice_in_dim(difference_lambda[l], head, 1).reshape(1, 1)
        gain_a, gain_f = gains[l, 0:1], gains[l, 1:2]
        shared = paced(a_model[l]) + near(a_head[l]) + paced(cosine, sine, query_bits) + near(key_bits, lam)
        come = 2 if l else 1
        plan = plan_of(
            [] if last else [(a_blocks[l + 1], (tall, c_a)), (g_blocks[l + 1], (tall, c_g))],
            [w_g[l], w_d[l]],
            moves("forward", 0, parts(n, 0, come)) + moves("spread", 0, parts(n, come, 4)),
            moves("forward", 0, parts(n, come, 2)) + ([] if last else [("scatter", 0)]),
            moves("spread", 1, parts(n, 0, 2)) + moves("forward", 0, parts(n, 2, 3)),
            moves("forward", 0, parts(n, 3, 4)),
            [] if last else [("scatter", 1)],
        )
        got = run(
            functools.partial(attention_forward, n, nf, l, part, rank, True, plan),
            near(residual, gain_a) + far(w_attention) + shared,
            [
                out((rows, width), F32),
                out(*whole_x, True),
                out((tree, VD), BF, "paced"),
                out((tree, VD), BF, "paced"),
                out((tree, VD), BF, "paced"),
                out((tree, 3 * rank), BF, "paced"),
                out((tree, 2), F32, "paced"),
                out((tree, VD), BF, "paced"),
                out((tree, VD), BF, "paced"),
                out((tree, rank), BF, "paced"),
            ],
            big + [vmem((width, 4 * VD), BF), vmem((3 * rank, 3 * VD), BF), pair] + sems,
            plan,
        )
        if not last:
            w_a.append(got[0])
            w_g.append(got[1])
            got = got[2:]
        w_g[l], w_d[l], middle, *kept = got
        plan = plan_of(
            [] if last else [(d_blocks[l + 1], (tall, c_d))],
            [w_d[l]] + ([] if last else [w_a[l + 1], w_g[l + 1]]),
            moves("forward", 0, parts(n, 0, 2)) + moves("spread", 0, parts(n, 2, 4)),
            moves("forward", 0, parts(n, 2, 3)),
            moves("forward", 0, parts(n, 3, 4)) + ([] if last else moves("spread", 1, parts(n, 0, 4)) + [("scatter", 0)]),
            [] if last else moves("forward", 1, parts(n, 0, 1)),
            [] if last else moves("forward", 1, parts(n, 1, 2)) + moves("spread", 2, parts(n, 0, 2)),
            [] if last else moves("forward", 1, parts(n, 2, 4)),
        )
        ffn = run(
            functools.partial(ffn_forward, n, nf, units, rank, last, plan),
            near(middle, gain_f) + far(w_g[l]) + paced(a_model[l]) + near(e_model[l])
            + (near(own_cotangent) if last else []),
            ([out(*whole_x, True)] if last else [])
            + [
                out((rows, width), F32),
                out(*whole_x, True),
                out((tree, units), BF, "paced"),
                out((tree, units), BF, "paced"),
                out((tree, units), BF, "paced"),
                out((tree, 2 * rank), BF, "paced"),
                out((tree, rank), BF),
            ],
            big + [vmem((width, 3 * units), BF), vmem((2 * rank, 2 * units), BF), pair] + sems
            + ([vmem(*whole_x)] + Gather.semaphores(n) if last else []),
            plan,
        )
        if not last:
            w_d.append(ffn[0])
            w_d[l], w_a[l + 1], w_g[l + 1], *ffn = ffn[1:]
        else:
            w_d[l], gathered, *ffn = ffn
        saved.append((residual, middle, gain_a, gain_f, shared, kept, ffn[1:]))
        residual = ffn[0]

    grad = own_cotangent
    units_here, sums_here, earlier, block = [], [], [], width // (2 * n)
    wide = hidden_tp // n
    for l in reversed(range(layers)):
        residual_in, middle, gain_a, gain_f, shared, kept, ffn = saved[l]
        carry = l == layers - 1
        made = run(
            functools.partial(ffn_backward, n, units, rank, carry),
            near(grad) + paced(middle) + near(gain_f) + far(w_g[l], w_d[l]) + paced(a_model[l]) + near(e_model[l])
            + far(ffn[0]) + paced(*ffn[1:])
            + (near(residual) + far(gathered) if carry else near(sums_here[0], units_here[0])),
            ([out((2, rows, width), BF)] if carry else [out((nf, 12 * rank, block), BF), out((nf, 3 * rank, wide), BF)])
            + [
                out((rows, width), F32),
                out((rank, width), BF),
                out((2 * rank, width), BF),
                out((4 * rank, units), BF),
            ],
            big
            + [
                vmem((width, 3 * units), BF),
                vmem(*whole_x),
                vmem((tree, 2 * units), BF),
                vmem((tree, 2 * rank), BF),
                vmem((tree, rank), BF),
                vmem((2 * rank, 2 * units), BF),
                pair,
            ]
            + sems
            + ([vmem((rows, width), BF)] + Home.semaphores() if carry else [dma((2, 2)), dma((2, 2))]),
        )
        if carry:
            outputs, *made = made
        else:
            earlier += made[:2]
            made = made[2:]
        grad, *ffn_grads = made
        grad, own_sum, all_units = run(
            functools.partial(attention_backward, n, l, share, heads_tp, rank),
            near(grad) + paced(residual_in) + near(gain_a) + far(w_a[l]) + shared + far(kept[0])
            + paced(*kept[1:]) + near(*ffn_grads),
            [
                out((rows, width), F32),
                out((12 * rank, block), BF),
                out((n, 2, 4 * rank, units), BF),
            ],
            big
            + [
                vmem((width, 4 * VD), BF),
                vmem((tree, VD), BF),
                vmem((tree, VD), F32),
                vmem((tree, VD), F32),
                vmem((tree, VD), F32),
                vmem((tree, 3 * VD), BF),
                vmem((tree, 3 * rank), BF),
                vmem((tree, rank), BF),
                vmem((3 * rank, 3 * VD), BF),
                vmem((rank, width), BF),
                vmem((n, 2, 12 * rank, block), BF),
                pair,
            ]
            + sems
            + Gather.semaphores(n)
            + Reduce.scratch(n, 12 * rank, block),
        )

        number = (q * 2 + t) * (hidden_tp // n)
        half = lax.dynamic_index_in_dim(all_units, number // hidden_tp, 1, keepdims=False)
        flat = half[:, : 3 * rank].transpose(1, 0, 2).reshape(3 * rank, n * units)
        units_here.insert(0, lax.dynamic_slice_in_dim(flat, number % hidden_tp, hidden_tp // n, 1))
        sums_here.insert(0, own_sum)

    own = adapters // nf
    dma = pltpu.SemaphoreType.DMA
    tokens_grad, grad_model, grad_hidden = run(
        functools.partial(finish_kernel, n, nf, layers, rank),
        near(grad, sums_here[0], units_here[0], slot.astype(F32).reshape(1, 1), *earlier),
        [
            out((2, rows, width), BF),
            out((layers, 11, own, rank, block), F32),
            out((layers, 3, own, rank, wide), F32),
        ],
        [
            vmem((rows, width), BF),
            vmem((rows // 2, width), BF),
            vmem((12 * rank, block), BF),
            vmem((nf, layers, 12 * rank, block), BF),
            vmem((nf, layers, 3 * rank, wide), BF),
            dma((3, 2)),
            dma((3, 2)),
            dma((layers, 2, nf)),
            dma((layers, 2, nf)),
            dma((5,)),
            dma((5,)),
        ],
    )
    return (
        outputs.reshape(2 * rows, width),
        tokens_grad.reshape(2 * rows, width).astype(F32),
        grad_model,
        grad_hidden,
    )


def solution(mesh):
    in_specs = (
        P(("fsdp", "ctx"), None),
        P(("fsdp", "ctx"), None),
        P(("fsdp", "ctx")),
        P(("fsdp", "ctx")),
        P("fsdp", None),
        P("fsdp"),
        P(),
        P(None, "tp"),
        P(None, ("fsdp", "ctx"), None, "tp"),
        P(None, ("fsdp", "ctx"), "tp"),
        P(None, ("fsdp", "ctx"), None, "tp"),
        P(None, ("fsdp", "ctx"), "tp"),
        P(),
        P(),
    )
    out_specs = (
        P(("fsdp", "ctx"), None),
        P(("fsdp", "ctx"), None),
        P(None, None, "fsdp", None, ("ctx", "tp")),
        P(None, None, "fsdp", None, ("ctx", "tp")),
    )
    body = functools.partial(shards, mesh.shape["fsdp"], mesh.shape["ctx"])
    return jax.shard_map(body, mesh=mesh, in_specs=in_specs, out_specs=out_specs, check_vma=False)
```

```python
import functools
import math

import jax
import jax.numpy as jnp
from jax import lax
from jax.experimental import pallas as pl
from jax.experimental.pallas import tpu as pltpu
from jax.sharding import PartitionSpec as P

HD = 128
VD = 256
NSEG = 13
EPSILON = 1e-05
ADAPTER_SCALE = 0.5
NEGATIVE_BIG = -1e30
MESH = pl.DeviceIdType.MESH
BF = jnp.bfloat16
F32 = jnp.float32


class Place:
    def __init__(self, n):
        self.n, self.h = n, n // 2
        self.f, self.c, self.t = lax.axis_index("fsdp"), lax.axis_index("ctx"), lax.axis_index("tp")
        self.f_hi, self.f_lo = self.f // 2, self.f % 2
        self.c_hi, self.c_lo = self.c // self.h, self.c % self.h
        self.q = self.f_lo * self.h + self.c_lo
        self.away = self.f_lo + self.c_hi - 2 * self.f_lo * self.c_hi
        self.home = {"fsdp": self.f_hi * 2 + self.c_hi, "ctx": self.f_lo * self.h + self.c_lo}
        self.pos = self.f_lo * (n - 1) + (1 - 2 * self.f_lo) * self.c_lo

    def ring(self, k):
        n, h = self.n, self.h
        p = lax.rem(self.pos + k + 2 * n, n)
        low = p // h
        column = (1 - low) * p + low * (n - 1 - p)
        device = {"fsdp": self.f_hi * 2 + low, "ctx": self.c_hi * h + column}
        return low * h + column, device


def remote(src, dst, send, recv, device):
    copy = pltpu.make_async_remote_copy(
        src_ref=src, dst_ref=dst, send_sem=send, recv_sem=recv, device_id=device, device_id_type=MESH
    )
    copy.start()
    return copy


def when_even(place, body):
    even = place.pos % 2 == 0
    pl.when(even)(lambda: body(True))
    pl.when(jnp.logical_not(even))(lambda: body(False))


def flip(number, bits):
    b = 1
    while b <= bits:
        if bits & b:
            number = number + b * (1 - 2 * ((number // b) % 2))
        b *= 2
    return number


class Spread:
    def __init__(self, place, nf, w, rows):
        self.place, self.nf, self.w, self.rows = place, nf, w, rows
        self.g = place.f_hi * 2 + place.c_hi
        self.links = range(1, nf // 2)
        self.scattered, self.sent = [], []
        self.to_partner, self.along, self.onward, self.got = {}, {}, {}, []

    @staticmethod
    def scatter_semaphores(n):
        dma = pltpu.SemaphoreType.DMA
        return [dma((n,)), dma((n,))]

    @staticmethod
    def spread_semaphores(n, nf):
        dma = pltpu.SemaphoreType.DMA
        return [dma((n,))] * 2 + [dma((n, max(1, nf // 2 - 1)))] * 4

    def block(self, g, q):
        n, h = self.place.n, self.place.h
        source = (g // 2 * 2 + q // h) * n + g % 2 * h + q % h
        start = pl.multiple_of(source * self.rows, self.rows)
        return self.w.at[pl.ds(start, self.rows)]

    def chip(self, q):
        place = self.place
        return {"fsdp": place.f_hi * 2 + q // place.h, "ctx": place.c_hi * place.h + q % place.h}

    def partner(self):
        place = self.place
        return {"ctx": (1 - place.c_hi) * place.h + place.c_lo}

    def line(self, e):
        return {"fsdp": flip(self.place.f_hi, e) * 2 + self.place.f_lo}

    def scatter(self, blocks, send, recv):
        q = self.place.q
        own = self.block(self.g, q)
        copy = pltpu.make_async_copy(blocks.at[q], own, recv.at[0])
        copy.start()
        self.scattered.append(copy)
        for d in range(1, self.place.n):
            to = flip(q, d)
            self.scattered.append(remote(blocks.at[to], own, send.at[d], recv.at[d], self.chip(to)))

    def arrived(self, d):
        if d:
            self.scattered[d].wait_recv()
        else:
            self.scattered[0].wait()

    def scatter_sent(self):
        for copy in self.scattered[1:]:
            copy.wait_send()

    def use(self, *sems):
        self.sems = sems

    def spread(self, d):
        send_z, recv_z, send_y, recv_y = self.sems[:4]
        at = self.block(self.g, flip(self.place.q, d))
        self.to_partner[d] = remote(at, at, send_z.at[d], recv_z.at[d], self.partner())
        for e in self.links:
            self.along[d, e] = remote(at, at, send_y.at[d, e - 1], recv_y.at[d, e - 1], self.line(e))

    def landed(self, d):
        if d in self.to_partner and d not in self.got:
            self.to_partner[d].wait_recv()
            self.got.append(d)

    def forward(self, d):
        send, recv = self.sems[4:]
        self.landed(d)
        at = self.block(flip(self.g, 1), flip(self.place.q, d))
        for e in self.links:
            self.onward[d, e] = remote(at, at, send.at[d, e - 1], recv.at[d, e - 1], self.line(e))

    def complete(self):
        for d in list(self.to_partner):
            self.landed(d)
        for copy in list(self.along.values()) + list(self.onward.values()):
            copy.wait_recv()

    def sent_all(self):
        for copies in (self.to_partner, self.along, self.onward):
            for copy in copies.values():
                copy.wait_send()


def enter(place, nf=0, scatters=False, home=False, ring=True, trees=0, partner=False):
    bar = pltpu.get_barrier_semaphore()
    devices = [{"tp": 1 - place.t}]
    guide = Spread(place, nf, None, 0)
    if scatters:
        devices += [guide.chip(flip(place.q, d)) for d in range(1, place.n)]
    elif ring:
        devices += [place.ring(1)[1], place.ring(-1)[1]]
    if nf:
        devices += [guide.partner()] + [guide.line(e) for e in guide.links]
    devices += [{"fsdp": flip(place.f, e)} for e in range(1, trees)]
    if partner:
        devices.append(guide.partner())
    for device in devices:
        pl.semaphore_signal(bar, inc=1, device_id=device, device_id_type=MESH)
    count = len(devices)
    if home:

        @pl.when(place.away == 1)
        def greet():
            pl.semaphore_signal(bar, inc=1, device_id=place.home, device_id_type=MESH)

        count = count + place.away
    pl.semaphore_wait(bar, count)


class Home:
    def __init__(self, place, out, send, recv):
        self.place, self.out = place, out
        self.send, self.recv = send, recv

    @staticmethod
    def semaphores():
        dma = pltpu.SemaphoreType.DMA
        return [dma((2,)), dma((2,))]

    def start(self, rows):
        place, slot = self.place, self.out.at[self.place.t]
        far = pltpu.make_async_remote_copy(
            src_ref=rows, dst_ref=slot, send_sem=self.send.at[0], recv_sem=self.recv.at[0],
            device_id=place.home, device_id_type=MESH,
        )
        near = pltpu.make_async_copy(rows, slot, self.recv.at[0])
        self.far = far
        pl.when(place.away == 1)(far.start)
        pl.when(place.away == 0)(near.start)
        self.near = near

    def land(self, share=True):
        pl.when(self.place.away == 1)(self.far.wait)
        pl.when(self.place.away == 0)(self.near.wait)
        if share:
            slot = self.out.at[self.place.t]
            self.across = remote(slot, slot, self.send.at[1], self.recv.at[1], {"tp": 1 - self.place.t})

    def finish(self):
        self.across.wait()


class TreeMove(Home):
    def __init__(self, place, rows, out, send, recv):
        super().__init__(place, out, send, recv)
        self.rows = rows
        self.slot = out.at[place.f]

    def start(self):
        place = self.place
        target = self.out.at[place.f_hi * 2 + place.c_hi]
        self.far = pltpu.make_async_remote_copy(
            src_ref=self.rows, dst_ref=target, send_sem=self.send.at[0], recv_sem=self.recv.at[0],
            device_id=place.home, device_id_type=MESH,
        )
        self.near = pltpu.make_async_copy(self.rows, target, self.recv.at[0])
        pl.when(place.away == 1)(self.far.start)
        pl.when(place.away == 0)(self.near.start)

    def land(self):
        super().land(False)


class Work:
    def __init__(self, place, nf, rows, scatters, spreads, schedule):
        self.n, self.schedule = place.n, schedule
        self.scatters, self.spreads = [], []
        for blocks, w, sems in scatters:
            self.scatters.append((Spread(place, nf, w, rows), blocks, sems))
        for w, sems in spreads:
            piece = Spread(place, nf, w, rows)
            piece.use(*sems)
            self.spreads.append(piece)

    def at(self, point):
        for what, i, *d in self.schedule[point] if point < len(self.schedule) else ():
            if what == "scatter":
                piece, blocks, sems = self.scatters[i]
                piece.scatter(blocks, *sems)
            elif what == "spread":
                self.spreads[i].spread(*d)
            else:
                self.spreads[i].forward(*d)

    def complete(self, i):
        self.spreads[i].complete()

    def settle(self, done=()):
        for i, piece in enumerate(self.spreads):
            if i not in done:
                piece.complete()
            piece.sent_all()
        for piece, _, _ in self.scatters:
            for d in range(self.n):
                piece.arrived(d)
            piece.scatter_sent()


def parts(n, first, last):
    return range(first * n // 4, last * n // 4)


def moves(what, piece, places):
    return [(what, piece, d) for d in places]


def weights_kernel(
    n, nf, units, share, layers,
    qkv, output, gate_up, down, *refs,
):
    place = Place(n)
    rows, hidden = down.shape[1:]
    w_a, w_g, w_d = refs[:3]
    later = refs[3 : 3 * layers]
    a_first, g_first, d_first, raw_g, raw_d, cut_sems, raw_sems = refs[3 * layers : 3 * layers + 7]
    sems = refs[3 * layers + 7 :]
    a_blocks = [a_first] + list(later[: layers - 1])
    g_blocks = [g_first] + list(later[layers - 1 : 2 * layers - 2])
    d_blocks = [d_first] + list(later[2 * layers - 2 :])
    cuts = []
    for l in range(layers):
        for q in range(n):
            columns = pl.ds(q // share * VD, VD)
            for i in range(4):
                source = qkv.at[l, i, :, columns] if i < 3 else output.at[l, :, columns]
                target = a_blocks[l].at[q, :, pl.ds(i * VD, VD)]
                cuts.append(pltpu.make_async_copy(source, target, cut_sems.at[l, q, i]))
    for copy in cuts[: 4 * n]:
        copy.start()
    raws = []
    for l in range(layers):
        raws.append(pltpu.make_async_copy(gate_up.at[l], raw_g.at[l], raw_sems.at[l, 0]))
        raws.append(pltpu.make_async_copy(down.at[l], raw_d.at[l], raw_sems.at[l, 1]))
    for copy in raws:
        copy.start()
    attention, forward, back = (Spread(place, nf, w, rows) for w in (w_a, w_g, w_d))
    attention.use(*sems[2:8])
    forward.use(*sems[10:16])
    enter(place, nf, True)
    for copy in cuts[: 4 * n]:
        copy.wait()
    attention.scatter(a_first, *sems[:2])
    for copy in cuts[4 * n :]:
        copy.start()

    def fill(target, j, at, value):
        width = min(units, hidden - j * units)
        target[j, :, at : at + width] = value(pl.ds(j * units, width))
        if width < units:
            target[j, :, at + width : at + units] = jnp.zeros((rows, units - width), BF)

    def cut_gate_up(l):
        raws[2 * l].wait()
        for i in range(2):
            for j in range(n):
                fill(g_blocks[l], j, i * units, lambda at, i=i: raw_g[l, :, i, at])

    def cut_down(l):
        raws[2 * l + 1].wait()
        for j in range(n):
            fill(d_blocks[l], j, 0, lambda at: raw_d[l, :, at])

    cut_gate_up(0)
    for d in range(n):
        attention.arrived(d)
        attention.spread(d)
    forward.scatter(g_first, *sems[8:10])
    cut_down(0)
    back.scatter(d_first, *sems[16:18])
    for d in parts(n, 0, 1):
        attention.forward(d)
    for l in range(1, layers):
        cut_gate_up(l)
        cut_down(l)
    for copy in cuts[4 * n :]:
        copy.wait()
    for d in parts(n, 1, 3):
        attention.forward(d)
    for d in range(n):
        forward.arrived(d)
    for d in parts(n, 0, 1):
        forward.spread(d)
    for d in parts(n, 3, 4):
        attention.forward(d)
    attention.complete()
    forward.complete()
    attention.scatter_sent()
    attention.sent_all()
    forward.scatter_sent()
    forward.sent_all()
    for d in range(n):
        back.arrived(d)
    back.scatter_sent()


class Gather:
    def __init__(self, place, x, send_r, recv_r, send_l, recv_l, core_send, core_recv, lean=False):
        self.place, self.x = place, x
        self.sems = (send_r, recv_r, send_l, recv_l, core_send, core_recv)
        self.lean = lean and place.n == 4
        self.right, self.left, self.across = {}, {}, []

    @staticmethod
    def semaphores(n):
        dma = pltpu.SemaphoreType.DMA
        return [dma((n,))] * 4 + [dma((n,))] * 2

    def _make(self, s):
        place, x = self.place, self.x
        send_r, recv_r, send_l, recv_l = self.sems[:4]
        top = x.shape[2] // 2
        last = s == place.n // 2 - 1
        for i in range(1 if last and not self.lean else 2):
            for made, sign, send, recv in ((self.right, 1, send_r, recv_r), (self.left, -1, send_l, recv_l)):
                piece = i if sign > 0 else 1 - i
                at = x.at[place.ring(-sign * s)[0], place.t, pl.ds(piece * top, top)]
                made[s, i] = pltpu.make_async_remote_copy(
                    src_ref=at, dst_ref=at, send_sem=send.at[2 * s + i], recv_sem=recv.at[2 * s + i],
                    device_id=place.ring(sign)[1], device_id_type=MESH,
                )

    def _cross(self, q):
        core_send, core_recv = self.sems[4:]
        slot, at = len(self.across), self.x.at[q, self.place.t]
        other = {"tp": 1 - self.place.t}
        self.across.append(remote(at, at, core_send.at[slot], core_recv.at[slot], other))

    def begin(self):
        for s in range(self.place.n // 2):
            self._make(s)
        for i in range(2):
            self.right[0, i].start()
            self.left[0, i].start()
        self._cross(self.place.q)

    def _hop(self, s):
        last = self.place.n // 2 - 1
        if not self.lean:
            for i in range(1 if s == last else 2):
                for stream in (self.right, self.left):
                    stream[s, i].wait_recv()
                    if s < last - 1 or (s == last - 1 and i == 0):
                        stream[s + 1, i].start()
            return

        def body(even):
            along_ctx, along_fsdp = (self.left, self.right) if even else (self.right, self.left)
            for i in range(2):
                if s == 0:
                    along_ctx[0, i].wait_recv()
                    along_ctx[1, i].start()
                    along_fsdp[0, i].wait_recv()
                else:
                    along_fsdp[1, i].wait_recv()

        when_even(self.place, body)

    def chunks(self):
        place, half = self.place, self.place.n // 2
        self.across[0].wait_recv()
        yield place.q
        for s in range(half):
            self._hop(s)
            arrived = [place.ring(half)[0]] if s == half - 1 else [place.ring(-s - 1)[0], place.ring(s + 1)[0]]
            first = len(self.across)
            for q in arrived:
                self._cross(q)
            for i, q in enumerate(arrived):
                self.across[first + i].wait_recv()
                yield q

    def finish(self):
        last = self.place.n // 2 - 1
        for s in range(last + 1):
            for i in range(2):
                if s < last:
                    self.right[s, i].wait_send()
                    self.left[s, i].wait_send()
                elif not self.lean and i == 0:
                    self.right[s, 0].wait_send()
                    self.left[s, 0].wait_send()
        if self.lean:

            def body(even):
                for i in range(2):
                    (self.left if even else self.right)[1, i].wait_send()

            when_even(self.place, body)
        for copy in self.across:
            copy.wait_send()


def by_rows(count, body, step=32):
    def one(i, carry):
        body(pl.ds(pl.multiple_of(i * step, step), step))
        return carry

    lax.fori_loop(0, count // step, one, 0)


class Reduce:
    def __init__(self, place, p, from_core, in_r, in_l, send_r, recv_r, send_l, recv_l, core_send, core_recv, lean=False):
        self.place, self.p, self.from_core, self.in_r, self.in_l = place, p, from_core, in_r, in_l
        self.sems = (send_r, recv_r, send_l, recv_l, core_send, core_recv)
        self.lean = lean and place.n == 4
        half = place.n // 2
        self.order = [half] + [k for j in range(half - 1, 0, -1) for k in (j, -j)] + [0]
        self.chips = {k: place.ring(k)[0] for k in self.order}
        self.across, self.copies = {}, {}
        for sign in (1, -1):
            for s in range(half):
                for piece in range(2):
                    if s or self.lean or piece == (sign < 0):
                        self._copy(sign, s, piece)

    @staticmethod
    def scratch(n, rows, width):
        dma = pltpu.SemaphoreType.DMA
        wide = [pltpu.VMEM((n, rows, width), BF)] + [pltpu.VMEM((n // 2, rows, width), BF)] * 2
        return wide + [dma((n // 2, 2))] * 4 + [dma((n,))] * 2

    def offer(self, k):
        core_send, core_recv = self.sems[4:]
        slot, q, t = len(self.across), self.chips[k], self.place.t
        self.across[k] = remote(
            self.p.at[q, 1 - t], self.from_core.at[q], core_send.at[slot], core_recv.at[slot], {"tp": 1 - t}
        )

    def _local(self, k, at):
        q = self.chips[k]
        return self.p[q, self.place.t, at].astype(F32) + self.from_core[q, at].astype(F32)

    def _add(self, k, piece, extra=None):
        top = self.p.shape[2] // 2

        def body(at):
            whole = pl.ds(pl.multiple_of(piece * top + at.start, 16), at.size)
            total = self._local(k, whole)
            if extra is not None:
                total = total + extra[whole].astype(F32)
            self.from_core[self.chips[k], whole] = total.astype(BF)

        by_rows(top, body)

    def _copy(self, sign, s, piece):
        if (sign, s, piece) not in self.copies:
            place, top = self.place, self.p.shape[2] // 2
            send, recv = self.sems[:2] if sign > 0 else self.sems[2:4]
            target = self.in_r if sign > 0 else self.in_l
            k = place.n // 2 - s
            rows = pl.ds(piece * top, top)
            self.copies[sign, s, piece] = pltpu.make_async_remote_copy(
                src_ref=self.from_core.at[self.chips[sign * k if s else k], rows], dst_ref=target.at[s, rows],
                send_sem=send.at[s, piece], recv_sem=recv.at[s, piece],
                device_id=place.ring(sign)[1], device_id_type=MESH,
            )
        return self.copies[sign, s, piece]

    def far(self):
        half = self.place.n // 2
        self.across[half].wait_recv()
        self._add(half, 0)
        self._add(half, 1)
        if self.lean:

            def body(even):
                for piece in range(2):
                    self._copy(-1 if even else 1, 0, piece).start()

            when_even(self.place, body)
        else:
            self._copy(1, 0, 0).start()
            self._copy(-1, 0, 1).start()

    def free(self):
        k = self.place.n // 2 - 1
        if self.lean:
            self.across[1].wait_recv()
            self.across[-1].wait_recv()

            def body(even):
                sign = -1 if even else 1
                for piece in range(2):
                    self._add(sign, piece)
                    self._copy(sign, 1, piece).start()

            when_even(self.place, body)
        elif k:
            for sign, piece in ((1, 1), (-1, 0)):
                self.across[sign * k].wait_recv()
                self._add(sign * k, piece)
                self._copy(sign, 1, piece).start()

    def near(self, s):
        half = self.place.n // 2
        k = half - s
        if self.lean:

            def body(even):
                sign = 1 if even else -1
                for piece in range(2):
                    self._copy(sign, 0, piece).wait_recv()
                    self._add(sign, piece, (self.in_r if even else self.in_l).at[0])
                    self._copy(sign, 1, piece).start()

            when_even(self.place, body)
            return
        if s > 1:
            self.across[k].wait_recv()
            self.across[-k].wait_recv()
        for sign, first, held in ((1, 0, self.in_r), (-1, 1, self.in_l)):
            for piece in (first,) if s == 1 else (first, 1 - first):
                self._copy(sign, s - 1, piece).wait_recv()
                self._add(sign * k, piece, held.at[s - 1])
                self._copy(sign, s, piece).start()

    def end(self, use):
        half = self.place.n // 2
        self.across[0].wait_recv()
        for sign in (1, -1):
            for piece in range(2):
                self._copy(sign, half - 1, piece).wait_recv()

        def body(at):
            use(at, self._local(0, at) + self.in_r[half - 1, at].astype(F32) + self.in_l[half - 1, at].astype(F32))

        by_rows(self.p.shape[2], body)

    def finish(self):
        half = self.place.n // 2
        if self.lean:

            def body(even):
                for piece in range(2):
                    self._copy(-1 if even else 1, 0, piece).wait_send()

            when_even(self.place, body)
        else:
            self._copy(1, 0, 0).wait_send()
            self._copy(-1, 0, 1).wait_send()
        for s in range(1, half):
            for sign in (1, -1):
                for piece in range(2):
                    self._copy(sign, s, piece).wait_send()
        for copy in self.across.values():
            copy.wait_send()

    def run(self, use, before=None, offered=False):
        if not offered:
            for k in self.order:
                self.offer(k)
            self.far()
            self.free()
        for s in range(1, self.place.n // 2):
            self.near(s)
        if before is not None:
            before()
        self.end(use)


def mm(a, b):
    return jnp.dot(a, b, preferred_element_type=F32)


def mm_t(a, b):
    return lax.dot_general(a, b, (((1,), (1,)), ((), ())), preferred_element_type=F32)


def t_mm(a, b):
    return lax.dot_general(a, b, (((0,), (0,)), ((), ())), preferred_element_type=F32)


def rms_scale(values):
    return lax.rsqrt(jnp.mean(values * values, axis=-1, keepdims=True) + EPSILON)


def norm_back(grad_normed, inputs, scale_rows, gain):
    unit = inputs * scale_rows
    scaled = grad_normed * gain
    return scale_rows * (scaled - unit * jnp.mean(scaled * unit, axis=-1, keepdims=True))


def tiles(count, width, body):
    def one(j, carry):
        body(pl.ds(pl.multiple_of(j * width, width), width))
        return carry

    lax.fori_loop(0, count // width, one, 0)


def tile_of(count):
    return 256 if count % 256 == 0 else 128


def turn(v, cosine, sine):
    return v * cosine + pltpu.roll(v, HD // 2, 1) * sine


def block_diagonal(out, parts, rank, width):
    out[...] = jnp.zeros(out.shape, out.dtype)
    for i in range(parts[1]):
        out[i * rank : (i + 1) * rank, i * width : (i + 1) * width] = parts[0][i * rank : (i + 1) * rank, :]


def write_norm(x_rows, source, gain):
    def body(at):
        v = source[at].astype(F32)
        x_rows[at] = (v * rms_scale(v) * gain[...]).astype(BF)

    by_rows(source.shape[0], body)


ROW_BLOCK = 128
KEY_STEP = 256


def row_blocks(tree, body):
    for j in range(tree // KEY_STEP):

        def one(i, carry, j=j):
            body(pl.ds(pl.multiple_of(j * KEY_STEP + i * ROW_BLOCK, ROW_BLOCK), ROW_BLOCK), (j + 1) * KEY_STEP)
            return carry

        lax.fori_loop(0, KEY_STEP // ROW_BLOCK, one, 0)


def seen(rows, keys, query_bits, key_bits):
    shared = (query_bits[rows] & key_bits[:, :keys]) != 0
    i = rows.start + lax.broadcasted_iota(jnp.int32, (ROW_BLOCK, keys), 0)
    j = lax.broadcasted_iota(jnp.int32, (ROW_BLOCK, keys), 1)
    return shared & (j <= i)


def attention_forward(
    n, nf, layer, part, rank, lean, plan,
    residual, gain, w_hbm, a_model, a_head, cosine, sine, query_bits, key_bits, lam, *refs, pace,
):
    jobs, refs = plan.split(refs)
    (middle, x_hbm, queries, keys, values, small, log_total, mixed, headed, side,
     x, p, w, raised, copy_sems, *sems) = refs
    place = Place(n)
    chip_rows, width = 2 * x_hbm.shape[2], x_hbm.shape[3]
    tree = n * chip_rows
    load = pltpu.make_async_copy(w_hbm, w, copy_sems.at[0])
    load.start()
    gather, reduce = Gather(place, x, *sems[:6], lean=lean), Reduce(place, p, *sems[6:], lean=lean)
    write_norm(x.at[place.q, place.t], residual, gain)
    block_diagonal(raised, (a_head[rank : 4 * rank], 3), rank, VD)
    work = plan.work(place, nf, jobs)
    enter(place, nf, bool(plan.scatters))
    gather.begin()
    work.at(0)
    pace.ready()
    load.wait()

    def project(q):
        rows = pl.ds(pl.multiple_of(q * chip_rows, chip_rows), chip_rows)
        v = x[q].reshape(chip_rows, width)
        low = mm_t(v, a_model[: 3 * rank]).astype(BF)
        small[rows] = low
        for i, out in enumerate((queries, keys, values)):
            at = slice(i * VD, (i + 1) * VD)
            made = mm(v, w[:, at]) + ADAPTER_SCALE * mm(low, raised[:, at])
            if i < 2:
                for c in range(2):
                    half = slice(c * HD, (c + 1) * HD)
                    out[rows, half] = turn(made[:, half], cosine[rows], sine[rows]).astype(BF)
            else:
                out[rows] = made.astype(BF)

    for q in gather.chunks():
        project(q)
    work.at(1)
    keep = pltpu.make_async_copy(x, x_hbm, copy_sems.at[1])
    keep.start()
    score_scale = HD ** (-0.5)
    weight = lam[...]

    def attend(rows, count):
        visible = seen(rows, count, query_bits, key_bits)
        both = []
        for c in range(2):
            at = slice(c * HD, (c + 1) * HD)
            scores = mm_t(queries[rows, at], keys[:count, at]) * score_scale
            scores = jnp.where(visible, scores, NEGATIVE_BIG)
            top = jnp.max(scores, axis=-1, keepdims=True)
            raw = jnp.exp(scores - top)
            total = jnp.sum(raw, axis=-1, keepdims=True)
            log_total[rows, c : c + 1] = top + jnp.log(total)
            both.append(raw * (1.0 / total))
        mix = mm((both[0] - weight * both[1]).astype(BF), values[:count])
        mixed[rows] = mix.astype(BF)
        head = (mix * rms_scale(mix) * keep_factor(layer)).astype(BF)
        headed[rows] = head
        side[rows] = mm_t(head, a_head[:rank]).astype(BF)

    row_blocks(tree, attend)
    pace.flush()
    work.at(2)

    for k in reduce.order:
        q = reduce.chips[k]
        rows = pl.ds(pl.multiple_of(q * chip_rows, chip_rows), chip_rows)
        head, low = headed[rows], side[rows]

        def out_tile(at):
            made = mm_t(head, w[at, 3 * VD :]) + ADAPTER_SCALE * mm(low, a_model[9 * rank : 10 * rank, at])
            p[q, :, :, at] = (made * part).astype(BF).reshape(2, chip_rows // 2, at.size)

        tiles(width, 512, out_tile)
        reduce.offer(k)
        if k == reduce.order[0]:
            reduce.far()
        if k == reduce.order[2]:
            reduce.free()
    work.at(3)
    for s in range(1, n // 2):
        reduce.near(s)
    work.at(4)

    def use(at, total):
        middle[at] = residual[at].astype(F32) + total

    reduce.end(use)
    work.at(5)
    keep.wait()
    gather.finish()
    reduce.finish()
    work.settle()


def ffn_forward(
    n, nf, units, rank, last, plan,
    residual, gain, w_hbm, a_model, e_model, *refs, pace,
):
    place = Place(n)
    if last:
        cotangent, *refs = refs
    jobs, refs = plan.split(refs)
    if last:
        all_refs = refs
        next_hbm, *refs, next_x = refs[:-6]
        next_gather = Gather(place, next_x, *all_refs[-6:])
    (following, x_hbm, gates, ups, hidden, small, side,
     x, p, w, raised, copy_sems, *sems) = refs
    chip_rows, width = 2 * x_hbm.shape[2], x_hbm.shape[3]
    tree = n * chip_rows
    load = pltpu.make_async_copy(w_hbm, w.at[:, pl.ds(0, 2 * units)], copy_sems.at[0])
    load.start()
    gather, reduce = Gather(place, x, *sems[:6], lean=not last), Reduce(place, p, *sems[6:], lean=not last)
    write_norm(x.at[place.q, place.t], residual, gain)
    block_diagonal(raised, (e_model, 2), rank, units)
    work = plan.work(place, nf, jobs)
    enter(place, nf, bool(plan.scatters))
    gather.begin()
    work.at(0)
    pace.ready()
    load.wait()
    step = tile_of(units)

    for number, q in enumerate(gather.chunks()):
        if number == n - 1:
            work.at(1)
        rows = pl.ds(pl.multiple_of(q * chip_rows, chip_rows), chip_rows)
        v = x[q].reshape(chip_rows, width)
        low = mm_t(v, a_model[4 * rank : 6 * rank]).astype(BF)
        small[rows] = low

        def unit_tile(at):
            up_at = pl.ds(pl.multiple_of(units + at.start, step), step)
            gate = mm(v, w[:, at]) + ADAPTER_SCALE * mm(low, raised[:, at])
            up = mm(v, w[:, up_at]) + ADAPTER_SCALE * mm(low, raised[:, up_at])
            gates[rows, at] = gate.astype(BF)
            ups[rows, at] = up.astype(BF)
            hidden[rows, at] = (gate / (1.0 + jnp.exp(-gate)) * up).astype(BF)

        tiles(units, step, unit_tile)

    pace.flush()
    if last:
        next_x[place.q, place.t] = cotangent[...]
        next_gather.begin()
    work.at(2)
    keep = pltpu.make_async_copy(x, x_hbm, copy_sems.at[1])
    keep.start()

    work.complete(0)
    load = pltpu.make_async_copy(plan.late(jobs), w.at[:, pl.ds(2 * units, units)], copy_sems.at[0])
    load.start()
    load.wait()
    for k in reduce.order:
        q = reduce.chips[k]
        rows = pl.ds(pl.multiple_of(q * chip_rows, chip_rows), chip_rows)
        made_hidden = hidden[rows]
        low = mm_t(made_hidden, e_model[2 * rank : 3 * rank]).astype(BF)
        side[rows] = low

        def out_tile(at):
            made = mm_t(made_hidden, w[at, 2 * units :])
            made = made + ADAPTER_SCALE * mm(low, a_model[10 * rank : 11 * rank, at])
            p[q, :, :, at] = made.astype(BF).reshape(2, chip_rows // 2, at.size)

        tiles(width, 512, out_tile)
        reduce.offer(k)
        if k == reduce.order[0]:
            reduce.far()
        if k == reduce.order[2]:
            reduce.free()
    if last:
        coming = next_gather.chunks()
        for _ in range(n - 1):
            next(coming)
    work.at(3)
    for s in range(1, n // 2):
        reduce.near(s)
    work.at(4)

    def use(at, total):
        following[at] = residual[at] + total

    reduce.end(use)
    if last:
        for _ in coming:
            pass
        keep_next = pltpu.make_async_copy(next_x, next_hbm, copy_sems.at[2])
        keep_next.start()
    work.at(5)
    keep.wait()
    if last:
        keep_next.wait()
        next_gather.finish()
    gather.finish()
    reduce.finish()
    work.settle((0,))


def ffn_backward(
    n, units, rank, carry,
    grad, middle, gain, w_hbm, w_down_hbm, a_model, e_model, x_hbm, gates, ups, hidden, small, side, *refs, pace,
):
    if carry:
        final, gathered, final_out, *refs = refs
        *refs, final_rows, home_send, home_recv = refs
    else:
        sums, here, sums_out, here_out, *refs = refs
        *refs, home_send, home_recv = refs
    (grad_out, grad_up_down, grad_in, grad_units,
     x, p, w, kept, dgu, dsmall, dside, raised, copy_sems, *sems) = refs
    place = Place(n)
    chip_rows, width = 2 * x_hbm.shape[2], x_hbm.shape[3]
    tree = n * chip_rows
    load = pltpu.make_async_copy(w_hbm, w.at[:, pl.ds(0, 2 * units)], copy_sems.at[0])
    load.start()
    load_down = pltpu.make_async_copy(w_down_hbm, w.at[:, pl.ds(2 * units, units)], copy_sems.at[2])
    load_down.start()
    fetch = pltpu.make_async_copy(x_hbm, kept, copy_sems.at[1])
    gather, reduce = Gather(place, x, *sems[:6]), Reduce(place, p, *sems[6:])

    if carry:
        come = pltpu.make_async_copy(gathered, x, copy_sems.at[3])
        come.start()
    else:

        def own(at):
            x[place.q, place.t, at] = grad[at].astype(BF)

        by_rows(grad.shape[0], own)
    block_diagonal(raised, (e_model, 2), rank, units)
    if carry:

        def last_rows(at):
            final_rows[at] = final[at].astype(BF)

        by_rows(final.shape[0], last_rows)
    enter(place, home=True)
    if not carry:
        gather.begin()
        going = [
            TreeMove(place, source, target, home_send.at[i], home_recv.at[i])
            for i, (source, target) in enumerate(((sums, sums_out), (here, here_out)))
        ]
    else:
        home = Home(place, final_out, home_send, home_recv)
        home.start(final_rows)
    pace.ready()
    load.wait()
    load_down.wait()
    step = tile_of(units)

    if carry:
        come.wait()
    coming = [0] + [k for s in range(1, n // 2) for k in (-s, s)] + [n // 2]
    for q in list(reduce.chips.values()) if carry else gather.chunks():
        rows = pl.ds(pl.multiple_of(q * chip_rows, chip_rows), chip_rows)
        v = x[q].reshape(chip_rows, width)
        low = (ADAPTER_SCALE * mm_t(v, a_model[10 * rank : 11 * rank])).astype(BF)
        dside[rows] = low

        def unit_tile(at):
            up_at = pl.ds(pl.multiple_of(units + at.start, step), step)
            down_at = pl.ds(pl.multiple_of(2 * units + at.start, step), step)
            dhidden = mm(v, w[:, down_at]) + mm(low, e_model[2 * rank : 3 * rank, at])
            gate, up = gates[rows, at].astype(F32), ups[rows, at].astype(F32)
            sig = 1.0 / (1.0 + jnp.exp(-gate))
            dgu[rows, at] = (dhidden * up * sig * (1.0 + gate * (1.0 - sig))).astype(BF)
            dgu[rows, up_at] = (dhidden * gate * sig).astype(BF)

        tiles(units, step, unit_tile)
        back = dgu[rows]
        low_back = (ADAPTER_SCALE * mm_t(back, raised[...])).astype(BF)
        dsmall[rows] = low_back

        def out_tile(at):
            made = mm_t(back, w[at, : 2 * units]) + mm(low_back, a_model[4 * rank : 6 * rank, at])
            p[q, :, :, at] = made.astype(BF).reshape(2, chip_rows // 2, at.size)

        tiles(width, 512, out_tile)
        if carry:
            k = reduce.order[len(reduce.across)]
        else:
            k = coming.pop(0)
        reduce.offer(k)
        if k == n // 2:
            reduce.far()
        if k == (reduce.order[2] if carry else n // 2):
            reduce.free()

    fetch.start()
    if not carry:
        for move in going:
            move.start()

    def use(at, total):
        inputs = middle[at]
        grad_out[at] = grad[at].astype(F32) + norm_back(total, inputs, rms_scale(inputs), gain[...])

    def adapters():
        fetch.wait()

        def model_tile(at):
            flat = x[:, :, :, at].reshape(tree, at.size)
            grad_up_down[:, at] = (ADAPTER_SCALE * t_mm(side[...], flat)).astype(BF)
            flat = kept[:, :, :, at].reshape(tree, at.size)
            grad_in[:, at] = t_mm(dsmall[...], flat).astype(BF)

        tiles(width, 256, model_tile)

        def unit_tile(at):
            up_at = pl.ds(pl.multiple_of(units + at.start, step), step)
            grad_units[:rank, at] = (ADAPTER_SCALE * t_mm(small[...], dgu[:, at])[:rank]).astype(BF)
            grad_units[rank : 2 * rank, at] = (ADAPTER_SCALE * t_mm(small[...], dgu[:, up_at])[rank:]).astype(BF)
            grad_units[2 * rank : 3 * rank, at] = t_mm(dside[...], hidden[:, at]).astype(BF)
            grad_units[3 * rank :, at] = jnp.zeros((rank, at.size), BF)

        tiles(units, step, unit_tile)

    reduce.run(use, adapters, True)
    if not carry:
        gather.finish()
    reduce.finish()
    if carry:
        home.land()
        home.finish()
    else:
        for move in going:
            move.land()


def attention_backward(
    n, layer, share, heads_tp, rank,
    grad, residual, gain, w_hbm, a_model, a_head, cosine, sine, query_bits, key_bits, lam,
    x_hbm, queries, keys, values, small, log_total, mixed, headed, side,
    grad_up_down, grad_ffn_in, grad_units,
    grad_out, own_sum, all_units,
    x, p, w, dmixed, dq, dk, dv, dprojected, dsmall, dside, raised, grad_a9, p_own, copy_sems, *sems, pace,
):
    place = Place(n)
    part = 1.0 / share
    chip_rows, width = 2 * x_hbm.shape[2], x_hbm.shape[3]
    tree = n * chip_rows
    load = pltpu.make_async_copy(w_hbm, w, copy_sems.at[0])
    load.start()
    gather, reduce = Gather(place, x, *sems[:6]), Reduce(place, p, *sems[6:15])
    gather_units, reduce_own = Gather(place, all_units, *sems[15:21]), Reduce(place, p_own, *sems[21:])

    def own(at):
        x[place.q, place.t, at] = grad[at].astype(BF)

    by_rows(grad.shape[0], own)
    block_diagonal(raised, (a_head[rank : 4 * rank], 3), rank, VD)
    all_units[place.q, place.t] = grad_units[...]
    enter(place)
    gather.begin()
    dk[...] = jnp.zeros(dk.shape, F32)
    dv[...] = jnp.zeros(dv.shape, F32)
    pace.ready()
    load.wait()

    score_scale = HD ** (-0.5)
    weight = lam[...]

    def attend(rows, count):
        visible = seen(rows, count, query_bits, key_bits)
        dmix = dmixed[rows]
        dweights = mm_t(dmix, values[:count])
        both = []
        for c in range(2):
            at = slice(c * HD, (c + 1) * HD)
            scores = mm_t(queries[rows, at], keys[:count, at]) * score_scale
            probability = jnp.exp(jnp.where(visible, scores - log_total[rows, c : c + 1], NEGATIVE_BIG))
            both.append(probability)
            weighted = probability * dweights
            dscores = weighted - probability * jnp.sum(weighted, axis=-1, keepdims=True)
            dscores = (dscores * -weight if c else dscores).astype(BF)
            dq[rows, at] = mm(dscores, keys[:count, at])
            dk[:count, at] += t_mm(dscores, queries[rows, at])
        dv[:count] += t_mm((both[0] - weight * both[1]).astype(BF), dmix)

    for q in gather.chunks():
        rows = pl.ds(pl.multiple_of(q * chip_rows, chip_rows), chip_rows)
        v = x[q].reshape(chip_rows, width)
        low = (ADAPTER_SCALE * mm_t(v, a_model[9 * rank : 10 * rank])).astype(BF)
        dside[rows] = low
        dheaded = mm(v, w[:, 3 * VD :]) + mm(low, a_head[:rank])
        inputs = mixed[rows].astype(F32)
        dmixed[rows] = norm_back(dheaded, inputs, rms_scale(inputs), keep_factor(layer)).astype(BF)

        def block(i, carry, q=q):
            attend(pl.ds(pl.multiple_of(q * chip_rows + i * ROW_BLOCK, ROW_BLOCK), ROW_BLOCK), tree)
            return carry

        lax.fori_loop(0, chip_rows // ROW_BLOCK, block, 0)

    gather_units.begin()

    def send_part(k):
        q = reduce.chips[k]
        rows = pl.ds(pl.multiple_of(q * chip_rows, chip_rows), chip_rows)
        for j, source in enumerate((dq, dk)):
            for c in range(2):
                half = slice(c * HD, (c + 1) * HD)
                turned = turn(source[rows, half] * score_scale, cosine[rows], -sine[rows])
                dprojected[rows, j * VD + c * HD : j * VD + (c + 1) * HD] = turned.astype(BF)
        dprojected[rows, 2 * VD :] = dv[rows].astype(BF)
        back = dprojected[rows]
        low_back = (ADAPTER_SCALE * mm_t(back, raised[...])).astype(BF)
        dsmall[rows] = low_back

        def out_tile(at):
            made = mm_t(back, w[at, : 3 * VD]) + mm(low_back, a_model[: 3 * rank, at])
            p[q, :, :, at] = (made * part).astype(BF).reshape(2, chip_rows // 2, at.size)

        tiles(width, 512, out_tile)
        reduce.offer(k)

    for k in reduce.order[:3]:
        send_part(k)
        if k == n // 2:
            reduce.far()
    reduce.free()

    def out_gradient(at):
        flat = x[:, :, :, at].reshape(tree, at.size)
        grad_a9[:, at] = (ADAPTER_SCALE * part * t_mm(side[...], flat)).astype(BF)

    tiles(width, 256, out_gradient)
    gather.finish()
    fetch = pltpu.make_async_copy(x_hbm, x, copy_sems.at[1])
    fetch.start()
    for k in reduce.order[3:]:
        send_part(k)
    for _ in gather_units.chunks():
        pass
    fetch.wait()

    block = width // (2 * n)

    def full_tile(jp, carry):
        at = pl.ds(pl.multiple_of(jp * block, block), block)
        q, t = jp // 2, jp % 2
        flat = x[:, :, :, at].reshape(tree, block)
        p_own[q, t, : 3 * rank] = (part * t_mm(dsmall[...], flat)).astype(BF)
        p_own[q, t, 4 * rank : 6 * rank] = grad_ffn_in[:, at]
        p_own[q, t, 9 * rank : 10 * rank] = grad_a9[:, at]
        p_own[q, t, 10 * rank : 11 * rank] = grad_up_down[:, at]
        p_own[q, t, 11 * rank :] = jnp.zeros((rank, block), BF)
        return carry

    lax.fori_loop(0, 2 * n, full_tile, 0)
    of_head = [part * t_mm(dside[...], headed[...])]
    for i in range(3):
        made = t_mm(small[...], dprojected[:, i * VD : (i + 1) * VD])[i * rank : (i + 1) * rank]
        of_head.append(ADAPTER_SCALE * part * made)
    head = place.t * heads_tp + place.q // share
    for j in range(2 * n):
        start = j * block % VD
        own = (head == j * block // VD).astype(F32)
        for i, k in enumerate((3, 6, 7, 8)):
            made = of_head[i][:, start : start + block] * own
            p_own[j // 2, j % 2, k * rank : (k + 1) * rank] = made.astype(BF)

    for k in reduce.order:
        reduce_own.offer(k)
    reduce_own.far()
    reduce_own.free()
    for s in range(1, n // 2):
        reduce.near(s)
        reduce_own.near(s)

    def use_own(at, total):
        own_sum[at] = total.astype(BF)

    def use(at, total):
        inputs = residual[at].astype(F32)
        grad_out[at] = grad[at].astype(F32) + norm_back(total, inputs, rms_scale(inputs), gain[...])

    reduce.end(use)
    reduce_own.end(use_own)
    gather_units.finish()
    reduce.finish()
    reduce_own.finish()


def finish_kernel(
    n, nf, layers, rank,
    grad, own_sums, own_units, slot, *refs,
):
    earlier, refs = refs[: 2 * layers - 2], refs[2 * layers - 2 :]
    (landed, model_grad, hidden_grad,
     rows_out, passing, sent_sums, all_sums, all_units, home_send, home_recv, tree_send, tree_recv, relay_send, relay_recv) = refs
    place = Place(n)
    own = model_grad.shape[2]
    tall = own_sums.shape[0]

    def cut(at):
        rows_out[at] = grad[at].astype(BF)

    by_rows(grad.shape[0], cut)
    sent_sums[...] = own_sums[...]
    sent_sums[tall - rank :] = jnp.broadcast_to(slot[...], (rank, own_sums.shape[1])).astype(BF)
    enter(place, home=True, ring=False, trees=nf, partner=True)
    top = grad.shape[0] // 2
    low, high = pl.ds(0, top), pl.ds(top, top)
    slot_here = landed.at[place.t]
    partner = {"ctx": (1 - place.c_hi) * place.h + place.c_lo}
    beside = {"fsdp": place.f_hi * 2 + 1 - place.f_lo}

    def make(src, dst, i, device):
        return pltpu.make_async_remote_copy(
            src_ref=src, dst_ref=dst, send_sem=relay_send.at[i], recv_sem=relay_recv.at[i],
            device_id=device, device_id_type=MESH,
        )

    straight = make(rows_out.at[low], slot_here.at[low], 0, place.home)
    to_relay = make(rows_out.at[high], passing, 1, beside)
    from_relay = make(passing, slot_here.at[high], 2, partner)
    stay = pltpu.make_async_copy(rows_out, slot_here, relay_recv.at[3])
    cross = make(slot_here, slot_here, 4, {"tp": 1 - place.t})
    is_away, is_relay = place.away == 1, place.away == 0

    away = {}
    for i, (source, target) in enumerate(((sent_sums, all_sums), (own_units, all_units))):
        away[i] = TreeMove(place, source, target.at[:, 0], home_send.at[i + 1], home_recv.at[i + 1])
        away[i].start()
    copies = []

    def hand_round(source, target, l, i):
        to = target.at[place.f, l]
        for e in range(1, nf):
            sems = tree_send.at[l, i, e], tree_recv.at[l, i, e]
            copies.append(remote(source, to, *sems, {"fsdp": flip(place.f, e)}))

    for l in range(1, layers):
        for i, target in enumerate((all_sums, all_units)):
            source = earlier[2 * l - 2 + i].at[place.f]
            target[place.f, l] = earlier[2 * l - 2 + i][place.f]
            hand_round(source, target, l, i)
    for i, target in enumerate((all_sums, all_units)):
        away[i].land()
        if i == 1:

            @pl.when(is_away)
            def leave():
                straight.start()
                to_relay.start()

            pl.when(is_relay)(stay.start)
        hand_round(target.at[place.f, 0], target, 0, i)
    @pl.when(is_relay)
    def hand_on():
        to_relay.wait_recv()
        from_relay.start()

    for copy in copies:
        copy.wait_recv()
    for b in range(own):
        number = (place.f * own + b).astype(F32)
        keeps = [
            (all_sums[f, 0, tall - rank : tall - rank + 1, :1].astype(F32) == number).astype(F32) for f in range(nf)
        ]
        for l in range(layers):
            for k in range(11):
                at = slice(k * rank, (k + 1) * rank)
                model_grad[l, k, b] = sum(keeps[f] * all_sums[f, l, at].astype(F32) for f in range(nf))
            for k in range(3):
                at = slice(k * rank, (k + 1) * rank)
                hidden_grad[l, k, b] = sum(keeps[f] * all_units[f, l, at].astype(F32) for f in range(nf))

    @pl.when(is_relay)
    def rest():
        stay.wait()
        from_relay.wait_send()

    @pl.when(is_away)
    def arrive():
        straight.wait()
        to_relay.wait_send()
        from_relay.wait_recv()

    cross.start()
    cross.wait()
    for copy in copies:
        copy.wait_send()


class Plan:
    def __init__(self, n, nf, rows, scatters, spreads, schedule):
        self.n, self.nf, self.rows, self.schedule = n, nf, rows, schedule
        self.scatters, self.spreads = scatters, spreads

    def ins(self):
        return [(blocks, True) for blocks, _ in self.scatters] + [(w, True) for w in self.spreads]

    def outs(self):
        made = [(shape, BF, True) for _, shape in self.scatters]
        return made + [(w.shape, BF, True) for w in self.spreads]

    def semaphores(self):
        made = Spread.scatter_semaphores(self.n) * len(self.scatters)
        return made + Spread.spread_semaphores(self.n, self.nf) * len(self.spreads)

    def split(self, refs):
        a, b = len(self.scatters), len(self.spreads)
        count = 2 * a + 6 * b
        refs = list(refs)
        taken = refs[: a + b], refs[a + b : 2 * (a + b)], refs[len(refs) - count :]
        return taken, refs[2 * (a + b) : len(refs) - count]

    def work(self, place, nf, jobs):
        a, b = len(self.scatters), len(self.spreads)
        ins, outs, sems = jobs
        scatters = [(ins[i], outs[i], sems[2 * i : 2 * i + 2]) for i in range(a)]
        spreads = [(outs[a + i], sems[2 * a + 6 * i : 2 * a + 6 * i + 6]) for i in range(b)]
        return Work(place, nf, self.rows, scatters, spreads, self.schedule)

    def late(self, jobs):
        return jobs[1][len(self.scatters)]


class Pace:
    def __init__(self, loads, stores):
        self.loads, self.stores = loads, stores
        for copy in loads:
            copy.start()

    def ready(self):
        for copy in self.loads:
            copy.wait()

    def flush(self):
        for copy in self.stores:
            copy.start()

    def end(self):
        for copy in self.stores:
            copy.wait()


def call(kernel, collective, ins, outs, scratch, plan=None):
    spec = lambda hbm: pl.BlockSpec(memory_space=pl.ANY if hbm else pltpu.VMEM)
    aliases = {}
    if plan is not None:
        first_in, count = len(ins), len(plan.scatters)
        aliases = {first_in + count + i: count + i for i in range(len(plan.spreads))}
        ins, outs, scratch = ins + plan.ins(), plan.outs() + outs, scratch + plan.semaphores()
    late_in = [i for i, (_, hbm) in enumerate(ins) if hbm == "paced"]
    late_out = [i for i, (_, _, hbm) in enumerate(outs) if hbm == "paced"]
    extra = [pltpu.VMEM(ins[i][0].shape, ins[i][0].dtype) for i in late_in]
    extra += [pltpu.VMEM(outs[i][0], outs[i][1]) for i in late_out]
    if late_in or late_out:
        extra.append(pltpu.SemaphoreType.DMA((len(late_in) + len(late_out),)))

        def paced(*refs):
            refs, held = list(refs[: -len(extra)]), refs[-len(extra) :]
            loads, stores = [], []
            for slot, i in enumerate(late_in):
                loads.append(pltpu.make_async_copy(refs[i], held[slot], held[-1].at[slot]))
                refs[i] = held[slot]
            for slot, i in enumerate(late_out, len(late_in)):
                stores.append(pltpu.make_async_copy(held[slot], refs[len(ins) + i], held[-1].at[slot]))
                refs[len(ins) + i] = held[slot]
            pace = Pace(loads, stores)
            kernel(*refs, pace=pace)
            pace.end()

        body = paced
    else:
        body = kernel
    made = pl.pallas_call(
        body,
        out_shape=[jax.ShapeDtypeStruct(shape, kind) for shape, kind, _ in outs],
        in_specs=[spec(hbm) for _, hbm in ins],
        out_specs=[spec(hbm) for _, _, hbm in outs],
        scratch_shapes=scratch + extra,
        input_output_aliases=aliases,
        compiler_params=pltpu.CompilerParams(
            collective_id=collective, has_side_effects=True, vmem_limit_bytes=62 << 20
        ),
    )(*[array for array, _ in ins])
    return list(made)


def line_bits(parent_row, seg):
    number = jnp.arange(NSEG)
    one = lambda x: lax.shift_left(jnp.ones_like(x), x)
    grand = jnp.sum(jnp.where(parent_row[:, None] == number[None, :], parent_row[None, :], 0), axis=1)
    line = one(number) | one(parent_row) | one(grand)
    mine = jnp.sum(jnp.where(seg[:, None] == number[None, :], line[None, :], 0), axis=1)
    return mine, one(seg)


def keep_factor(layer):
    return 0.2 + 0.6 * math.exp(-0.3 * layer)


def chips_of(nf, nc):
    h = nc // 2
    for f in range(nf):
        for c in range(nc):
            yield f * nc + c, (f // 2, f % 2, c // h, c % h)


def permute(x, nf, nc, target):
    h = nc // 2
    pairs = []
    for source, spot in chips_of(nf, nc):
        f_hi, f_lo, c_hi, c_lo = target(*spot)
        pairs.append((source, (f_hi * 2 + f_lo) * nc + c_hi * h + c_lo))
    return lax.ppermute(x, ("fsdp", "ctx"), pairs)


def swap_trees(x, nf, nc):
    return permute(x, nf, nc, lambda f_hi, f_lo, c_hi, c_lo: (f_hi, c_hi, f_lo, c_lo))


def shards(
    nf,
    nc,
    tokens,
    cotangent,
    segments,
    depths,
    parents,
    tree_adapter_index,
    layer_norm_gains,
    difference_lambda,
    query_key_value_weight,
    output_weight,
    gate_up_weight,
    down_weight,
    adapter_model_factors,
    adapter_hidden_factors,
):
    n = nc
    place = Place(n)
    q, t = place.q, place.t
    tokens_dev, width = tokens.shape
    rows = tokens_dev // 2
    tree = tokens_dev * n
    layers, weight_rows = query_key_value_weight.shape[:2]
    heads_tp = difference_lambda.shape[1]
    share = max(1, n // heads_tp)
    head = q // share
    hidden_tp = down_weight.shape[2]
    units = (hidden_tp + n * 128 - 1) // (n * 128) * 128
    rank, adapters = adapter_model_factors.shape[3], adapter_model_factors.shape[2]
    h = n // 2

    notes = jnp.concatenate([segments, depths, parents[0], tree_adapter_index])
    order = jnp.arange(n)
    of_tree = jnp.zeros((n, notes.shape[0]), jnp.int32)
    for d in range(n):

        def hand_out(f_hi, f_lo, c_hi, c_lo, d=d):
            to = (c_hi * (n // 2) + c_lo) ^ d
            return f_hi, to // (n // 2), f_lo, to % (n // 2)

        part_of_tree = permute(notes, nf, nc, hand_out)
        of_tree = of_tree + jnp.where(order[:, None] == flip(q, d), part_of_tree[None], 0)
    seg, dep = of_tree[:, :tokens_dev].reshape(tree), of_tree[:, tokens_dev : 2 * tokens_dev].reshape(tree)
    parent_row, slot = of_tree[0, 2 * tokens_dev : 2 * tokens_dev + NSEG], of_tree[0, 2 * tokens_dev + NSEG]
    own_tokens = lax.dynamic_slice_in_dim(tokens, t * rows, rows, 0)
    own_cotangent = lax.dynamic_slice_in_dim(cotangent, t * rows, rows, 0)
    residual = swap_trees(own_tokens, nf, nc)
    own_cotangent = swap_trees(own_cotangent, nf, nc)

    query_bits, key_bits = line_bits(parent_row, seg)
    query_bits, key_bits = query_bits[:, None], key_bits[None, :]
    frequency = 10000.0 ** (-jnp.arange(HD // 2).astype(F32) / (HD // 2))
    angles = dep.astype(F32)[:, None] * frequency[None, :]
    cosine, sine = jnp.cos(angles), jnp.sin(angles)
    cosine = jnp.concatenate([cosine, cosine], axis=1)
    sine = jnp.concatenate([-sine, sine], axis=1)
    gains = layer_norm_gains

    a_all = lax.dynamic_index_in_dim(adapter_model_factors, slot, 2, keepdims=False)
    e_all = lax.dynamic_index_in_dim(adapter_hidden_factors, slot, 2, keepdims=False)
    a_model = a_all.reshape(layers, 11 * rank, width)
    e_all = e_all.reshape(layers, 3 * rank, -1)
    head_at = (t * heads_tp + head) * VD

    heads_of = lax.dynamic_slice_in_dim(a_all, head_at, VD, 3)
    a_head = jnp.concatenate([heads_of[:, 3:4], heads_of[:, 6:9]], axis=1).reshape(layers, 4 * rank, VD)

    def unit_columns(x):
        x = lax.dynamic_slice_in_dim(x, t * hidden_tp, hidden_tp, x.ndim - 1)
        x = jnp.pad(x, ((0, 0),) * (x.ndim - 1) + ((0, n * units - hidden_tp),))
        return lax.dynamic_slice_in_dim(x, q * units, units, x.ndim - 1)

    e_model = unit_columns(e_all)

    part = 1.0 / share
    vmem = lambda *spec: pltpu.VMEM(*spec)
    calls = [0]
    whole_x = ((n, 2, rows, width), BF)
    sems = Gather.semaphores(n) + Reduce.scratch(n, rows, width)
    pair = pltpu.SemaphoreType.DMA((4,))
    big = [vmem(*whole_x), vmem(*whole_x)]

    def run(kernel, ins, outs, scratch, plan=None):
        calls[0] += 1
        return call(kernel, calls[0], ins, outs, scratch, plan)

    near = lambda *arrays: [(array, False) for array in arrays]
    far = lambda *arrays: [(array, True) for array in arrays]
    paced = lambda *arrays: [(array, "paced") for array in arrays]
    out = lambda shape, kind, hbm=False: (shape, kind, hbm)

    dma = pltpu.SemaphoreType.DMA
    c_a, c_g, c_d = 4 * VD, 2 * units, units
    tall = nf * n * weight_rows
    cut = lambda columns: out((n, weight_rows, columns), BF)
    calls[0] += 1
    made = call(
        functools.partial(weights_kernel, n, nf, units, share, layers),
        calls[0],
        far(jnp.transpose(query_key_value_weight, (0, 2, 1, 3)), output_weight, gate_up_weight, down_weight),
        [out((tall, c_a), BF, True), out((tall, c_g), BF, True), out((tall, c_d), BF, True)]
        + ([cut(c_a)] + [cut(c_g)] + [cut(c_d)]) * (layers - 1),
        [
            vmem((n, weight_rows, c_a), BF),
            vmem((n, weight_rows, c_g), BF),
            vmem((n, weight_rows, c_d), BF),
            vmem((layers, weight_rows, 2, hidden_tp), BF),
            vmem((layers, weight_rows, hidden_tp), BF),
            dma((layers, n, 4)),
            dma((layers, 2)),
        ]
        + (Spread.scatter_semaphores(n) + Spread.spread_semaphores(n, nf)) * 2
        + Spread.scatter_semaphores(n),
    )
    w_a, w_g, w_d = [made[0]], [made[1]], [made[2]]
    a_blocks = [None] + made[3 : 2 + layers]
    g_blocks = [None] + made[2 + layers : 1 + 2 * layers]
    d_blocks = [None] + made[1 + 2 * layers :]

    def plan_of(scatters, spreads, *schedule):
        return Plan(n, nf, weight_rows, scatters, spreads, schedule)

    saved = []
    for l in range(layers):
        last = l == layers - 1
        w_attention = w_a[l]
        lam = lax.dynamic_slice_in_dim(difference_lambda[l], head, 1).reshape(1, 1)
        gain_a, gain_f = gains[l, 0:1], gains[l, 1:2]
        shared = paced(a_model[l]) + near(a_head[l]) + paced(cosine, sine, query_bits) + near(key_bits, lam)
        come = 2 if l else 1
        plan = plan_of(
            [] if last else [(a_blocks[l + 1], (tall, c_a)), (g_blocks[l + 1], (tall, c_g))],
            [w_g[l], w_d[l]],
            moves("forward", 0, parts(n, 0, come)) + moves("spread", 0, parts(n, come, 4)),
            moves("forward", 0, parts(n, come, 2)) + ([] if last else [("scatter", 0)]),
            moves("spread", 1, parts(n, 0, 2)) + moves("forward", 0, parts(n, 2, 3)),
            moves("forward", 0, parts(n, 3, 4)),
            [] if last else [("scatter", 1)],
        )
        got = run(
            functools.partial(attention_forward, n, nf, l, part, rank, True, plan),
            near(residual, gain_a) + far(w_attention) + shared,
            [
                out((rows, width), F32),
                out(*whole_x, True),
                out((tree, VD), BF, "paced"),
                out((tree, VD), BF, "paced"),
                out((tree, VD), BF, "paced"),
                out((tree, 3 * rank), BF, "paced"),
                out((tree, 2), F32, "paced"),
                out((tree, VD), BF, "paced"),
                out((tree, VD), BF, "paced"),
                out((tree, rank), BF, "paced"),
            ],
            big + [vmem((width, 4 * VD), BF), vmem((3 * rank, 3 * VD), BF), pair] + sems,
            plan,
        )
        if not last:
            w_a.append(got[0])
            w_g.append(got[1])
            got = got[2:]
        w_g[l], w_d[l], middle, *kept = got
        plan = plan_of(
            [] if last else [(d_blocks[l + 1], (tall, c_d))],
            [w_d[l]] + ([] if last else [w_a[l + 1], w_g[l + 1]]),
            moves("forward", 0, parts(n, 0, 2)) + moves("spread", 0, parts(n, 2, 4)),
            moves("forward", 0, parts(n, 2, 3)),
            moves("forward", 0, parts(n, 3, 4)) + ([] if last else moves("spread", 1, parts(n, 0, 4)) + [("scatter", 0)]),
            [] if last else moves("forward", 1, parts(n, 0, 1)),
            [] if last else moves("forward", 1, parts(n, 1, 2)) + moves("spread", 2, parts(n, 0, 2)),
            [] if last else moves("forward", 1, parts(n, 2, 4)),
        )
        ffn = run(
            functools.partial(ffn_forward, n, nf, units, rank, last, plan),
            near(middle, gain_f) + far(w_g[l]) + paced(a_model[l]) + near(e_model[l])
            + (near(own_cotangent) if last else []),
            ([out(*whole_x, True)] if last else [])
            + [
                out((rows, width), F32),
                out(*whole_x, True),
                out((tree, units), BF, "paced"),
                out((tree, units), BF, "paced"),
                out((tree, units), BF, "paced"),
                out((tree, 2 * rank), BF, "paced"),
                out((tree, rank), BF),
            ],
            big + [vmem((width, 3 * units), BF), vmem((2 * rank, 2 * units), BF), pair] + sems
            + ([vmem(*whole_x)] + Gather.semaphores(n) if last else []),
            plan,
        )
        if not last:
            w_d.append(ffn[0])
            w_d[l], w_a[l + 1], w_g[l + 1], *ffn = ffn[1:]
        else:
            w_d[l], gathered, *ffn = ffn
        saved.append((residual, middle, gain_a, gain_f, shared, kept, ffn[1:]))
        residual = ffn[0]

    grad = own_cotangent
    units_here, sums_here, earlier, block = [], [], [], width // (2 * n)
    wide = hidden_tp // n
    for l in reversed(range(layers)):
        residual_in, middle, gain_a, gain_f, shared, kept, ffn = saved[l]
        carry = l == layers - 1
        made = run(
            functools.partial(ffn_backward, n, units, rank, carry),
            near(grad) + paced(middle) + near(gain_f) + far(w_g[l], w_d[l]) + paced(a_model[l]) + near(e_model[l])
            + far(ffn[0]) + paced(*ffn[1:])
            + (near(residual) + far(gathered) if carry else near(sums_here[0], units_here[0])),
            ([out((2, rows, width), BF)] if carry else [out((nf, 12 * rank, block), BF), out((nf, 3 * rank, wide), BF)])
            + [
                out((rows, width), F32),
                out((rank, width), BF),
                out((2 * rank, width), BF),
                out((4 * rank, units), BF),
            ],
            big
            + [
                vmem((width, 3 * units), BF),
                vmem(*whole_x),
                vmem((tree, 2 * units), BF),
                vmem((tree, 2 * rank), BF),
                vmem((tree, rank), BF),
                vmem((2 * rank, 2 * units), BF),
                pair,
            ]
            + sems
            + ([vmem((rows, width), BF)] + Home.semaphores() if carry else [dma((2, 2)), dma((2, 2))]),
        )
        if carry:
            outputs, *made = made
        else:
            earlier += made[:2]
            made = made[2:]
        grad, *ffn_grads = made
        grad, own_sum, all_units = run(
            functools.partial(attention_backward, n, l, share, heads_tp, rank),
            near(grad) + paced(residual_in) + near(gain_a) + far(w_a[l]) + shared + far(kept[0])
            + paced(*kept[1:]) + near(*ffn_grads),
            [
                out((rows, width), F32),
                out((12 * rank, block), BF),
                out((n, 2, 4 * rank, units), BF),
            ],
            big
            + [
                vmem((width, 4 * VD), BF),
                vmem((tree, VD), BF),
                vmem((tree, VD), F32),
                vmem((tree, VD), F32),
                vmem((tree, VD), F32),
                vmem((tree, 3 * VD), BF),
                vmem((tree, 3 * rank), BF),
                vmem((tree, rank), BF),
                vmem((3 * rank, 3 * VD), BF),
                vmem((rank, width), BF),
                vmem((n, 2, 12 * rank, block), BF),
                pair,
            ]
            + sems
            + Gather.semaphores(n)
            + Reduce.scratch(n, 12 * rank, block),
        )

        number = (q * 2 + t) * (hidden_tp // n)
        half = lax.dynamic_index_in_dim(all_units, number // hidden_tp, 1, keepdims=False)
        flat = half[:, : 3 * rank].transpose(1, 0, 2).reshape(3 * rank, n * units)
        units_here.insert(0, lax.dynamic_slice_in_dim(flat, number % hidden_tp, hidden_tp // n, 1))
        sums_here.insert(0, own_sum)

    own = adapters // nf
    dma = pltpu.SemaphoreType.DMA
    tokens_grad, grad_model, grad_hidden = run(
        functools.partial(finish_kernel, n, nf, layers, rank),
        near(grad, sums_here[0], units_here[0], slot.astype(F32).reshape(1, 1), *earlier),
        [
            out((2, rows, width), BF),
            out((layers, 11, own, rank, block), F32),
            out((layers, 3, own, rank, wide), F32),
        ],
        [
            vmem((rows, width), BF),
            vmem((rows // 2, width), BF),
            vmem((12 * rank, block), BF),
            vmem((nf, layers, 12 * rank, block), BF),
            vmem((nf, layers, 3 * rank, wide), BF),
            dma((3, 2)),
            dma((3, 2)),
            dma((layers, 2, nf)),
            dma((layers, 2, nf)),
            dma((5,)),
            dma((5,)),
        ],
    )
    return (
        outputs.reshape(2 * rows, width),
        tokens_grad.reshape(2 * rows, width).astype(F32),
        grad_model,
        grad_hidden,
    )


def solution(mesh):
    in_specs = (
        P(("fsdp", "ctx"), None),
        P(("fsdp", "ctx"), None),
        P(("fsdp", "ctx")),
        P(("fsdp", "ctx")),
        P("fsdp", None),
        P("fsdp"),
        P(),
        P(None, "tp"),
        P(None, ("fsdp", "ctx"), None, "tp"),
        P(None, ("fsdp", "ctx"), "tp"),
        P(None, ("fsdp", "ctx"), None, "tp"),
        P(None, ("fsdp", "ctx"), "tp"),
        P(),
        P(),
    )
    out_specs = (
        P(("fsdp", "ctx"), None),
        P(("fsdp", "ctx"), None),
        P(None, None, "fsdp", None, ("ctx", "tp")),
        P(None, None, "fsdp", None, ("ctx", "tp")),
    )
    body = functools.partial(shards, mesh.shape["fsdp"], mesh.shape["ctx"])
    return jax.shard_map(body, mesh=mesh, in_specs=in_specs, out_specs=out_specs, check_vma=False)
```
